32 devices in a mesh: blk: 8 (over z, y), tensor: 4 (over x, core).
Axes of the slice: x: 2, y: 2, z: 4, core: 2. Of those that a mesh axis runs over, the one named last changes fastest.
Arguments:
- tokens: bfloat16 [8, 1024, 2048], P(None, 'blk'), may hold values from -9 to 9
- cotangent: bfloat16 [8, 1024, 2048], P(None, 'blk'), may hold values from -6 to 6
- norm_gain: float32 [2, 2048], replicated, may hold values from 0.5 to 1.5
- in_weight: bfloat16 [2, 2048, 2, 4096], P(None, None, None, 'tensor'), may hold values from -0.125 to 0.125
- conv_weight: float32 [2, 4, 4096], P(None, None, 'tensor'), may hold values from -3 to 3
- conv_bias: float32 [2, 4096], P(None, 'tensor'), may hold values from -3 to 3
- x_weight: bfloat16 [2, 4096, 160], P(None, 'tensor'), may hold values from -0.1875 to 0.1875
- dt_weight: bfloat16 [2, 128, 4096], P(None, None, 'tensor'), may hold values from -0.5 to 0.5
- dt_bias: float32 [2, 4096], P(None, 'tensor'), may hold values from -6.9 to -2.3
- decay_log: float32 [2, 16, 4096], P(None, None, 'tensor'), may hold values from -10 to 4
- skip_weight: float32 [2, 4096], P(None, 'tensor'), may hold values from 0.5 to 1.5
- out_weight: bfloat16 [2, 4096, 2048], P(None, 'tensor'), may hold values from -0.1875 to 0.1875
- scan_init: float32 [2, 8, 16, 4096], P(None, None, None, 'tensor'), may hold values from -6 to 6
- conv_init: float32 [2, 8, 3, 4096], P(None, None, None, 'tensor'), may hold values from -6 to 6
Outputs:
- out: bfloat16 [8, 1024, 2048], P(None, 'blk')
- end_states: float32 [2, 8, 8, 16, 4096], P(None, None, 'blk', None, 'tensor')
- conv_tails: float32 [2, 8, 8, 3, 4096], P(None, None, 'blk', None, 'tensor')
- input_grad: bfloat16 [8, 1024, 2048], P(None, 'blk')
- scan_grads: float32 [2, 8, 8, 16, 4096], P(None, None, 'blk', None, 'tensor')
- conv_grads: float32 [2, 8, 8, 3, 4096], P(None, None, 'blk', None, 'tensor')
- norm_gain_grad: float32 [2, 2048], replicated
- in_weight_grad: float32 [2, 2048, 2, 4096], P(None, 'blk', None, 'tensor')
- conv_weight_grad: float32 [2, 4, 4096], P(None, None, 'tensor')
- conv_bias_grad: float32 [2, 4096], P(None, 'tensor')
- x_weight_grad: float32 [2, 4096, 160], P(None, 'tensor', 'blk')
- dt_weight_grad: float32 [2, 128, 4096], P(None, 'blk', 'tensor')
- dt_bias_grad: float32 [2, 4096], P(None, 'tensor')
- decay_log_grad: float32 [2, 16, 4096], P(None, None, 'tensor')
- skip_weight_grad: float32 [2, 4096], P(None, 'tensor')
- out_weight_grad: float32 [2, 4096, 2048], P(None, 'tensor', 'blk')
- rms_stats: float32 [2, 2], replicated
- input_rms: float32 [1], replicated
The draws below stay inside these ranges and needn't reach their ends.
All inputs are finite; a program needn't handle non-finite values.
Results may differ from the reference program's by a relative error of at most 0.025.
The reference program's roundings to bfloat16 on the way count: a program that leaves them out, or rounds other values in their place, can miss the bound.
Values sent between devices are 32-bit elements; how exact they have to be, the bound alone decides.
A program may use at most 384 MiB of HBM per device.

```python
import math
from functools import partial
import jax
import jax.numpy as jnp
from jax import lax

D = 2048
INNER = 4096
STATE = 16
RANK = 128
KCONV = 4
LAYERS = 2
MICRO = 2
MB_SEQS = 4
GROUP = 128
SEQS = 8
LEN = 1024
XCOLS = 160
N_BLK = 8


def channel_bias(key):
    return jax.random.uniform(key, (LAYERS, INNER), jnp.float32, -6.9, -2.3)


def draw_tokens(key, part):
    key = jax.random.fold_in(key, 11)
    position = jnp.arange(LEN, dtype=jnp.float32) / (LEN - 1)
    noise_values = jnp.clip(jax.random.normal(key, (SEQS, LEN, D), jnp.float32), -6.0, 6.0)
    row_scale = 0.5 * 3.0 ** position
    return (noise_values * row_scale[None, :, None]).astype(jnp.bfloat16)


def draw_dt_bias(key, part):
    shared = channel_bias(key)
    return shared


def draw_decay_log(key, part):
    shared = channel_bias(key)
    key = jax.random.fold_in(key, 7)
    pick_key, slow_key, fast_key = jax.random.split(key, 3)
    slow_share = 0.5
    slow_mask = jax.random.uniform(pick_key, (LAYERS, 1, INNER), jnp.float32) < slow_share
    slow_speed = jnp.exp(jax.random.uniform(slow_key, (LAYERS, STATE, INNER), jnp.float32, math.log(0.3), math.log(1.5))) / LEN
    fast_speed = jnp.exp(jax.random.uniform(fast_key, (LAYERS, STATE, INNER), jnp.float32, math.log(0.02), math.log(0.05)))
    decay_speed = jnp.where(slow_mask, slow_speed, fast_speed)
    return jnp.log(decay_speed / jax.nn.softplus(shared)[:, None, :]).astype(jnp.float32)


def levels(key, dims, cuts, low, largest):
    loudness, own = 1.0, jax.random.fold_in(key, 6)
    for axis_at, parts in cuts:
        heights = jnp.exp(jax.random.uniform(jax.random.fold_in(own, axis_at), (parts,), jnp.float32, low / len(cuts), largest / len(cuts)))
        loudness = loudness * jnp.repeat(heights, dims[axis_at] // parts).reshape([-1 if axis == axis_at else 1 for axis in range(len(dims))])
    return loudness


def centred(stream_key, shape, scale, bound, cuts=(), kind=jnp.bfloat16):
    values = scale * jax.random.normal(stream_key, shape, jnp.float32)
    if cuts:
        values = values * levels(stream_key, shape, cuts, -0.22, 0.18)
    return jnp.clip(values, -bound, bound).astype(kind)


def setup_inputs(seed: int = 0) -> dict:
    seeds = jax.random.split(jax.random.key(seed), 15)
    tokens = draw_tokens(jax.random.fold_in(seeds[14], 71), 0)
    cotangent = centred(seeds[1], (SEQS, LEN, D), 1.0, 6.0, ((1, 8),))
    norm_gain = jnp.clip(1.0 + 0.1 * jax.random.normal(seeds[2], (LAYERS, D), jnp.float32), 0.5, 1.5)
    in_weight = centred(seeds[3], (LAYERS, D, 2, INNER), D ** -0.5, 0.125, ((3, 4),))
    conv_weight = centred(seeds[4], (LAYERS, KCONV, INNER), KCONV ** -0.5, 3.0, ((2, 4),), jnp.float32)
    conv_bias = centred(seeds[5], (LAYERS, INNER), 0.5, 3.0, ((1, 4),), jnp.float32)
    x_weight = centred(seeds[6], (LAYERS, INNER, XCOLS), (INNER // 4) ** -0.5, 0.1875, ((1, 4),))
    dt_weight = centred(seeds[7], (LAYERS, RANK, INNER), RANK ** -0.5, 0.5, ((2, 4),))
    dt_bias = draw_dt_bias(jax.random.fold_in(seeds[14], 71), 0)
    decay_log = draw_decay_log(jax.random.fold_in(seeds[14], 71), 0)
    skip_weight = jnp.clip(0.5 + 1.0 * jax.random.uniform(seeds[10], (LAYERS, INNER), jnp.float32) ** levels(seeds[10], (LAYERS, INNER), ((1, 4),), -0.2, 0.2), 0.5, 1.5)
    out_weight = centred(seeds[11], (LAYERS, INNER, D), (INNER // 4) ** -0.5, 0.1875, ((1, 4),))
    scan_init = centred(seeds[12], (LAYERS, SEQS, STATE, INNER), 1.0, 6.0, ((3, 4),), jnp.float32)
    conv_init = centred(seeds[13], (LAYERS, SEQS, KCONV - 1, INNER), 1.0, 6.0, ((3, 4),), jnp.float32)
    return {"tokens": tokens, "cotangent": cotangent, "norm_gain": norm_gain, "in_weight": in_weight, "conv_weight": conv_weight, "conv_bias": conv_bias, "x_weight": x_weight, "dt_weight": dt_weight, "dt_bias": dt_bias, "decay_log": decay_log, "skip_weight": skip_weight, "out_weight": out_weight, "scan_init": scan_init, "conv_init": conv_init}


EPSILON = 1e-05
TOP_PRECISION = lax.Precision.HIGHEST

@jax.custom_vjp
def low(v):
    return lax.optimization_barrier(v.astype(jnp.bfloat16)).astype(jnp.float32)

@jax.custom_vjp
def low_back(v):
    return v

def low_keep(v):
    return (low(v), None)

def low_pass(kept, grad):
    return (grad,)

def back_keep(v):
    return (v, None)

def back_low(kept, grad):
    return (low(grad),)
low.defvjp(low_keep, low_pass)
low_back.defvjp(back_keep, back_low)

def norm_rows(residual, gain_vector):
    mean_square = lax.optimization_barrier(jnp.mean(residual * residual, axis=-1, keepdims=True))
    return residual * lax.rsqrt(mean_square + EPSILON) * gain_vector

def conv_local(prefix, values, kernel, conv_shift):
    window = jnp.concatenate([prefix, values], axis=1)
    length = values.shape[1]
    summed = conv_shift + kernel[0] * window[:, 0:length]
    for offset in range(1, kernel.shape[0]):
        summed = summed + kernel[offset] * window[:, offset:offset + length]
    return summed

def scan_moment(decay_rate, carried, pieces):
    step_size, inputs, write_coef, read_coef = pieces
    carried = jnp.exp(step_size[:, None, :] * decay_rate) * carried + (step_size * inputs)[:, None, :] * write_coef[:, :, None]
    return (carried, lax.optimization_barrier(jnp.sum(read_coef[:, :, None] * carried, axis=1)))

def run_block(decay_rate, carried, pieces):
    bump_state, step_size, inputs, write_coef, read_coef = pieces
    final_state, outputs = lax.scan(partial(scan_moment, decay_rate), carried + bump_state, (step_size, inputs, write_coef, read_coef))
    return (final_state, (outputs, final_state))

def mamba_layer(residual, weights, scan_start, conv_start, scan_bump, conv_bump):
    gain_vector, input_matrix, kernel, conv_shift, x_matrix, dt_matrix, dt_bias, decay_log, skip_scale, output_matrix = weights
    seq_count, length, model_width = residual.shape
    normalized_rows = low(norm_rows(residual, gain_vector))
    mixer_output = low_back(jnp.einsum('ict,tua->icua', normalized_rows, input_matrix, precision=TOP_PRECISION))
    values = mixer_output[:, :, 0]
    gate_half = mixer_output[:, :, 1]
    inner_width = values.shape[-1]
    blocks = values.reshape(seq_count, N_BLK, GROUP, inner_width)
    rim_width = KCONV - 1
    earlier = jnp.concatenate([conv_start[:, None], blocks[:, :-1, GROUP - rim_width:]], axis=1)
    prefix = earlier + conv_bump
    conv_out = jax.vmap(conv_local, in_axes=(1, 1, None, None), out_axes=1)(prefix, blocks, kernel, conv_shift)
    inputs = low(jax.nn.silu(conv_out.reshape(seq_count, length, inner_width)))
    projected = jnp.einsum('sle,ec->slc', inputs, x_matrix, precision=TOP_PRECISION)
    dt_low = low(projected[..., :RANK])
    write_coef = projected[..., RANK:RANK + STATE]
    read_coef = projected[..., RANK + STATE:]
    step_size = jax.nn.softplus(low_back(jnp.einsum('slr,re->sle', dt_low, dt_matrix, precision=TOP_PRECISION)) + dt_bias)
    decay_rate = -jnp.exp(decay_log)

    def by_block(array_in):
        return array_in.reshape(seq_count, N_BLK, GROUP, array_in.shape[-1]).transpose(1, 2, 0, 3)
    pieces = (jnp.moveaxis(scan_bump, 1, 0), by_block(step_size), by_block(inputs), by_block(write_coef), by_block(read_coef))
    last_state, (outputs, finals) = lax.scan(jax.checkpoint(partial(run_block, decay_rate)), scan_start, pieces)
    scanned = outputs.transpose(2, 0, 1, 3).reshape(seq_count, length, inner_width)
    gated_reduced = low((scanned + skip_scale * inputs) * jax.nn.silu(gate_half))
    side_branch = low_back(jnp.einsum('vyz,zi->vyi', gated_reduced, output_matrix, precision=TOP_PRECISION))
    return (residual + side_branch, side_branch, jnp.moveaxis(finals, 0, 1), blocks[:, :, GROUP - rim_width:])

def reference(tokens, cotangent, norm_gain, in_weight, conv_weight, conv_bias, x_weight, dt_weight, dt_bias, decay_log, skip_weight, out_weight, scan_init, conv_init):
    params = tuple((weight_item.astype(jnp.float32) for weight_item in (norm_gain, in_weight, conv_weight, conv_bias, x_weight, dt_weight, dt_bias, decay_log, skip_weight, out_weight)))
    scan_first = scan_init.astype(jnp.float32)
    conv_first = conv_init.astype(jnp.float32)
    zero_scan = jnp.zeros((LAYERS, MB_SEQS, N_BLK, STATE, INNER), jnp.float32)
    zero_conv = jnp.zeros((LAYERS, MB_SEQS, N_BLK, KCONV - 1, INNER), jnp.float32)
    grad_totals = jax.tree.map(jnp.zeros_like, params)
    square_totals = jnp.zeros((LAYERS, 2), jnp.float32)
    input_total = jnp.zeros((1,), jnp.float32)
    out_parts, state_parts, tail_parts, input_parts, scan_parts, conv_parts = ([], [], [], [], [], [])
    for micro_index in range(MICRO):
        first_seq = micro_index * MB_SEQS
        stop_seq = first_seq + MB_SEQS

        def forward(source, weights, scan_bumps, conv_bumps):
            residual = source
            finals, tail_values, squares = ([], [], [])
            for layer_index in range(LAYERS):
                layer_weights = tuple((weight_item[layer_index] for weight_item in weights))
                next_residual, side_branch, final_states, last_values = mamba_layer(residual, layer_weights, scan_first[layer_index, first_seq:stop_seq], conv_first[layer_index, first_seq:stop_seq], scan_bumps[layer_index], conv_bumps[layer_index])
                squares.append(jnp.stack([jnp.sum(side_branch * side_branch), jnp.sum(next_residual * next_residual)]))
                finals.append(final_states)
                tail_values.append(last_values)
                residual = next_residual
            return (residual, (jnp.stack(finals), jnp.stack(tail_values), jnp.stack(squares)))
        source_values = tokens[first_seq:stop_seq].astype(jnp.float32)
        input_total = input_total + jnp.sum(source_values * source_values)
        result, pullback, extras = jax.vjp(forward, source_values, params, zero_scan, zero_conv, has_aux=True)
        source_grad, weight_grads, scan_grads, conv_grads = pullback(cotangent[first_seq:stop_seq].astype(jnp.float32))
        grad_totals = jax.tree.map(jnp.add, grad_totals, weight_grads)
        square_totals = square_totals + extras[2]
        out_parts.append(result.astype(jnp.bfloat16))
        state_parts.append(extras[0])
        tail_parts.append(extras[1])
        input_parts.append(source_grad.astype(jnp.bfloat16))
        scan_parts.append(scan_grads)
        conv_parts.append(conv_grads)
    rms_stats = jnp.sqrt(square_totals / (SEQS * LEN * D))
    input_rms = jnp.sqrt(input_total / (SEQS * LEN * D))
    return (jnp.concatenate(out_parts, axis=0), jnp.concatenate(state_parts, axis=1), jnp.concatenate(tail_parts, axis=1), jnp.concatenate(input_parts, axis=0), jnp.concatenate(scan_parts, axis=1), jnp.concatenate(conv_parts, axis=1), grad_totals[0], grad_totals[1], grad_totals[2], grad_totals[3], grad_totals[4], grad_totals[5], grad_totals[6], grad_totals[7], grad_totals[8], grad_totals[9], rms_stats, input_rms)
```

```python
import math
from functools import partial
import jax
import jax.numpy as jnp
from jax import lax
from jax.experimental import pallas as pl
from jax.experimental.pallas import tpu as pltpu

from jax.sharding import PartitionSpec as P

STATE = 16
RANK = 128
EPSILON = 1e-05
LANES=128
LOG2E=math.log2(math.e)

def cp(limit):
    return pltpu.CompilerParams(dimension_semantics=("arbitrary",), vmem_limit_bytes=limit)

def spread(ref_value, out, first):
    for t in range(out.shape[0]):
        row = ref_value[t]
        for n in range(STATE):
            out[t, n] = jnp.broadcast_to(row[:, first + n:first + n + 1], out.shape[2:])

def rates(rate_ref, lanes, n):
    return jnp.broadcast_to(rate_ref[pl.ds(n, 1), lanes], (8, LANES))

def end_body(blocks, width, step_ref, push_ref, coef_ref, rate_ref, end_ref, write):
    @pl.when(pl.program_id(0) == 0)
    def _():
        end_ref[...] = jnp.zeros_like(end_ref)
    spread(coef_ref, write, 0)
    def group(g, _):
        cols = [pl.ds(pl.multiple_of((g * width + k) * LANES, LANES), LANES) for k in range(width)]
        for low in range(0, STATE, STATE // width):
            span = range(low, low + STATE // width)
            state = {(k, n): end_ref[n, :, cols[k]] for k in range(width) for n in span}
            rate = {(k, n): rates(rate_ref, cols[k], n) for k in range(width) for n in span}
            for t in range(step_ref.shape[0]):
                step = [step_ref[t, :, c] for c in cols]
                push = [push_ref[t, :, c] for c in cols]
                for n in span:
                    w = write[t, n]
                    for k in range(width):
                        state[k, n] = jnp.exp2(step[k] * rate[k, n]) * state[k, n] + push[k] * w
            for k in range(width):
                for n in span:
                    end_ref[n, :, cols[k]] = state[k, n]
        return 0
    lax.fori_loop(0, blocks // width, group, 0)

def end_states(step, push, coef, rate, tb=8, width=2, limit=40*2**20):
    T, _, C = step.shape
    return pl.pallas_call(
        partial(end_body, C // LANES, width),
        grid=(T // tb,),
        in_specs=[pl.BlockSpec((tb, 8, C), lambda i: (i, 0, 0)), pl.BlockSpec((tb, 8, C), lambda i: (i, 0, 0)),
                  pl.BlockSpec((tb, 8, 2 * STATE), lambda i: (i, 0, 0)), pl.BlockSpec((STATE, C), lambda i: (0, 0))],
        out_specs=pl.BlockSpec((STATE, 8, C), lambda i: (0, 0, 0)),
        out_shape=jax.ShapeDtypeStruct((STATE, 8, C), jnp.float32),
        scratch_shapes=[pltpu.VMEM((tb, STATE, 8, LANES), jnp.float32)],
        compiler_params=cp(limit), name="end_states")(step, push, coef, rate)

def scan_body(blocks, width, step_ref, push_ref, coef_ref, rate_ref, start_ref, out_ref, states_ref, enter_ref, final_ref, write, read):
    @pl.when(pl.program_id(0) == 0)
    def _():
        final_ref[...] = start_ref[...]
    spread(coef_ref, write, 0)
    spread(coef_ref, read, STATE)
    enter_ref[0] = final_ref[...]
    def group(g, _):
        cols = [pl.ds(pl.multiple_of((g * width + k) * LANES, LANES), LANES) for k in range(width)]
        for low in range(0, STATE, STATE // width):
            span = range(low, low + STATE // width)
            state = {(k, n): final_ref[n, :, cols[k]] for k in range(width) for n in span}
            rate = {(k, n): rates(rate_ref, cols[k], n) for k in range(width) for n in span}
            for t in range(step_ref.shape[0]):
                step = [step_ref[t, :, c] for c in cols]
                push = [push_ref[t, :, c] for c in cols]
                total = [None] * width
                for n in span:
                    w, r = write[t, n], read[t, n]
                    for k in range(width):
                        s = jnp.exp2(step[k] * rate[k, n]) * state[k, n] + push[k] * w
                        state[k, n] = s
                        states_ref[t, n, :, cols[k]] = s
                        total[k] = r * s if total[k] is None else total[k] + r * s
                for k in range(width):
                    if low == 0:
                        out_ref[t, :, cols[k]] = total[k]
                    else:
                        out_ref[t, :, cols[k]] += total[k]
            for k in range(width):
                for n in span:
                    final_ref[n, :, cols[k]] = state[k, n]
        return 0
    lax.fori_loop(0, blocks // width, group, 0)

def scan_forward(step, push, coef, rate, start, tb=8, width=2, limit=48*2**20):
    T, _, C = step.shape
    row = pl.BlockSpec((tb, 8, C), lambda i: (i, 0, 0))
    whole = pl.BlockSpec((STATE, 8, C), lambda i: (0, 0, 0))
    f32 = jnp.float32
    return pl.pallas_call(
        partial(scan_body, C // LANES, width),
        grid=(T // tb,),
        in_specs=[row, row, pl.BlockSpec((tb, 8, 2 * STATE), lambda i: (i, 0, 0)), pl.BlockSpec((STATE, C), lambda i: (0, 0)), whole],
        out_specs=[row, pl.BlockSpec((tb, STATE, 8, C), lambda i: (i, 0, 0, 0)), pl.BlockSpec((1, STATE, 8, C), lambda i: (i, 0, 0, 0)), whole],
        out_shape=[jax.ShapeDtypeStruct((T, 8, C), f32), jax.ShapeDtypeStruct((T, STATE, 8, C), f32),
                   jax.ShapeDtypeStruct((T // tb, STATE, 8, C), f32), jax.ShapeDtypeStruct((STATE, 8, C), f32)],
        scratch_shapes=[pltpu.VMEM((tb, STATE, 8, LANES), f32)] * 2,
        compiler_params=cp(limit), name="scan_forward")(step, push, coef, rate, start)

def start_body(blocks, width, step_ref, grad_ref, coef_ref, rate_ref, start_ref, read):
    @pl.when(pl.program_id(0) == 0)
    def _():
        start_ref[...] = jnp.zeros_like(start_ref)
    spread(coef_ref, read, STATE)
    def group(g, _):
        cols = [pl.ds(pl.multiple_of((g * width + k) * LANES, LANES), LANES) for k in range(width)]
        for low in range(0, STATE, STATE // width):
            span = range(low, low + STATE // width)
            state = {(k, n): start_ref[n, :, cols[k]] for k in range(width) for n in span}
            rate = {(k, n): rates(rate_ref, cols[k], n) for k in range(width) for n in span}
            for t in reversed(range(step_ref.shape[0])):
                step = [step_ref[t, :, c] for c in cols]
                grad = [grad_ref[t, :, c] for c in cols]
                for n in span:
                    r = read[t, n]
                    for k in range(width):
                        state[k, n] = jnp.exp2(step[k] * rate[k, n]) * (state[k, n] + r * grad[k])
            for k in range(width):
                for n in span:
                    start_ref[n, :, cols[k]] = state[k, n]
        return 0
    lax.fori_loop(0, blocks // width, group, 0)

def start_grads(step, grad, coef, rate, tb=8, width=2, limit=40*2**20):
    T, _, C = step.shape
    last = T // tb - 1
    row = pl.BlockSpec((tb, 8, C), lambda i: (last - i, 0, 0))
    return pl.pallas_call(
        partial(start_body, C // LANES, width),
        grid=(T // tb,),
        in_specs=[row, row, pl.BlockSpec((tb, 8, 2 * STATE), lambda i: (last - i, 0, 0)), pl.BlockSpec((STATE, C), lambda i: (0, 0))],
        out_specs=pl.BlockSpec((STATE, 8, C), lambda i: (0, 0, 0)),
        out_shape=jax.ShapeDtypeStruct((STATE, 8, C), jnp.float32),
        scratch_shapes=[pltpu.VMEM((tb, STATE, 8, LANES), jnp.float32)],
        compiler_params=cp(limit), name="start_grads")(step, grad, coef, rate)

def back_body(blocks, width, step_ref, push_ref, grad_ref, coef_ref, rate_ref, states_ref, enter_ref, end_ref,
              decay_out, push_out, coef_out, start_ref, speed_ref, write, read, write_sum, read_sum):
    @pl.when(pl.program_id(0) == 0)
    def _():
        start_ref[...] = end_ref[...]
        speed_ref[...] = jnp.zeros_like(speed_ref)
    spread(coef_ref, write, 0)
    spread(coef_ref, read, STATE)
    tb = step_ref.shape[0]
    def group(g, first):
        cols = [pl.ds(pl.multiple_of((g * width + k) * LANES, LANES), LANES) for k in range(width)]
        for low in range(0, STATE, STATE // width):
            span = range(low, low + STATE // width)
            carry = {(k, n): start_ref[n, :, cols[k]] for k in range(width) for n in span}
            speed = {(k, n): speed_ref[n, :, cols[k]] for k in range(width) for n in span}
            rate = {(k, n): rates(rate_ref, cols[k], n) for k in range(width) for n in span}
            for t in reversed(range(tb)):
                step = [step_ref[t, :, c] for c in cols]
                push = [push_ref[t, :, c] for c in cols]
                grad = [grad_ref[t, :, c] for c in cols]
                decays = [None] * width
                pushes = [None] * width
                for n in span:
                    w, r = write[t, n], read[t, n]
                    wsum, rsum = None, None
                    for k in range(width):
                        before = states_ref[t - 1, n, :, cols[k]] if t else enter_ref[0, n, :, cols[k]]
                        back = carry[k, n] + r * grad[k]
                        held = jnp.exp2(step[k] * rate[k, n]) * back
                        carry[k, n] = held
                        q = held * before
                        speed[k, n] = speed[k, n] + step[k] * q
                        rq, bw = rate[k, n] * q, back * w
                        decays[k] = rq if decays[k] is None else decays[k] + rq
                        pushes[k] = bw if pushes[k] is None else pushes[k] + bw
                        bp, gs = back * push[k], grad[k] * states_ref[t, n, :, cols[k]]
                        wsum = bp if wsum is None else wsum + bp
                        rsum = gs if rsum is None else rsum + gs
                    if first:
                        write_sum[t, n] = wsum
                        read_sum[t, n] = rsum
                    else:
                        write_sum[t, n] += wsum
                        read_sum[t, n] += rsum
                for k in range(width):
                    if low == 0:
                        decay_out[t, :, cols[k]] = decays[k]
                        push_out[t, :, cols[k]] = pushes[k]
                    else:
                        decay_out[t, :, cols[k]] += decays[k]
                        push_out[t, :, cols[k]] += pushes[k]
            for k in range(width):
                for n in span:
                    start_ref[n, :, cols[k]] = carry[k, n]
                    speed_ref[n, :, cols[k]] = speed[k, n]
        return 0
    write_sum[...] = jnp.zeros_like(write_sum)
    read_sum[...] = jnp.zeros_like(read_sum)
    lax.fori_loop(0, blocks // width, lambda g, _: group(g, False), 0)
    lane = lax.broadcasted_iota(jnp.int32, (8, 2 * STATE), 1)
    for t in range(tb):
        row = jnp.zeros((8, 2 * STATE), jnp.float32)
        for n in range(STATE):
            row = jnp.where(lane == n, jnp.sum(write_sum[t, n], axis=-1, keepdims=True), row)
            row = jnp.where(lane == STATE + n, jnp.sum(read_sum[t, n], axis=-1, keepdims=True), row)
        coef_out[t] = row

def scan_backward(step, push, grad, coef, rate, states, enter, end, tb=8, width=2, limit=48*2**20):
    T, _, C = step.shape
    last = T // tb - 1
    f32 = jnp.float32
    row = pl.BlockSpec((tb, 8, C), lambda i: (last - i, 0, 0))
    thin = pl.BlockSpec((tb, 8, 2 * STATE), lambda i: (last - i, 0, 0))
    whole = pl.BlockSpec((STATE, 8, C), lambda i: (0, 0, 0))
    return pl.pallas_call(
        partial(back_body, C // LANES, width),
        grid=(T // tb,),
        in_specs=[row, row, row, thin, pl.BlockSpec((STATE, C), lambda i: (0, 0)),
                  pl.BlockSpec((tb, STATE, 8, C), lambda i: (last - i, 0, 0, 0)),
                  pl.BlockSpec((1, STATE, 8, C), lambda i: (last - i, 0, 0, 0)), whole],
        out_specs=[row, row, thin, whole, whole],
        out_shape=[jax.ShapeDtypeStruct((T, 8, C), f32)] * 2 + [jax.ShapeDtypeStruct((T, 8, 2 * STATE), f32)]
          + [jax.ShapeDtypeStruct((STATE, 8, C), f32)] * 2,
        scratch_shapes=[pltpu.VMEM((tb, STATE, 8, LANES), f32)] * 4,
        compiler_params=cp(limit), name="scan_backward")(step, push, grad, coef, rate, states, enter, end)


HALVES_OF_CHIP = 2


def silu_slope(argument):
    sigmoid_value = jax.nn.sigmoid(argument)
    return sigmoid_value * (1.0 + argument * (1.0 - sigmoid_value))


def half_of(array, index):
    size = array.shape[0] // 2
    return lax.dynamic_slice_in_dim(array, index * size, size, 0)


def ordered(index, mine, other):
    first = jnp.where(index == 0, mine, other)
    second = jnp.where(index == 0, other, mine)
    return jnp.concatenate([first, second], axis=0)


def tensor_sum(array):
    if lax.axis_size("tensor") != 4:
        return lax.psum(array, "tensor")
    core = lax.axis_index("tensor") % 2
    beside = [(0, 1), (1, 0), (2, 3), (3, 2)]
    across = [(0, 2), (2, 0), (1, 3), (3, 1)]
    half = half_of(array, core) + lax.ppermute(half_of(array, 1 - core), "tensor", beside)
    half = half + lax.ppermute(half, "tensor", across)
    return ordered(core, half, lax.ppermute(half, "tensor", beside))


def blk_sum(array):
    if lax.axis_size("blk") != 8:
        return lax.psum(array, "blk")
    for bit in (1, 2, 4):
        array = array + lax.ppermute(array, "blk", [(j, j ^ bit) for j in range(8)])
    return array


def blk_scatter(array):
    return lax.psum_scatter(array, "blk", scatter_dimension=0, tiled=True)


def neighbour(value, steps):
    count = lax.axis_size("blk")
    first, last = max(0, -steps), min(count, count - steps)
    return lax.ppermute(value, "blk", [(j, j + steps) for j in range(first, last)])


def entering_any(total, local, rate, first, reverse):
    peers, index = lax.axis_size("blk"), lax.axis_index("blk")
    totals, locals_ = lax.all_gather(total, "blk"), lax.all_gather(local, "blk")

    def step(k, state):
        at = peers - 1 - k if reverse else k
        reached = at > index if reverse else at < index
        return jnp.where(reached, jnp.exp2(totals[at][None] * rate) * state + locals_[at], state)

    return lax.fori_loop(0, peers, step, first)


def entering(total, local, rate, first, reverse):
    if lax.axis_size("blk") != 8:
        return entering_any(total, local, rate, first, reverse)
    index = lax.axis_index("blk")
    y, z = index % 2, index // 2
    pair = [(j, j ^ 1) for j in range(8)]
    if reverse:
        y, z = 1 - y, 3 - z
    sign = -1 if reverse else 1
    at_a = y == 0
    decay = jnp.exp2(total[None] * rate)
    own = local + jnp.where(jnp.logical_and(z == 0, at_a), decay * first, 0.0)
    mine, give = half_of(own, y), half_of(own, 1 - y)
    got = lax.ppermute(jnp.concatenate([give, total[None]], axis=0), "blk", pair)
    got, got_total = got[:-1], got[-1]
    rate_half = half_of(rate, y)
    local_a, local_b = jnp.where(at_a, mine, got), jnp.where(at_a, got, mine)
    total_a, total_b = jnp.where(at_a, total, got_total), jnp.where(at_a, got_total, total)
    joined = local_b + jnp.exp2(total_b[None] * rate_half) * local_a
    message = jnp.concatenate([joined, (total_a + total_b)[None]], axis=0)

    def along(value, pairs):
        if reverse:
            pairs = [(3 - s, 3 - d) for s, d in pairs]
        return lax.ppermute(value, "blk", [(2 * s + k, 2 * d + k) for s, d in pairs for k in (0, 1)])

    one = along(message, [(0, 1), (1, 2), (2, 3)])
    two = along(one, [(1, 2), (2, 3)])
    three = along(one[:-1], [(1, 3)])
    enter = one[:-1] + jnp.exp2(one[-1:] * rate_half) * (
        two[:-1] + jnp.exp2(two[-1:] * rate_half) * three
    )
    after_a = local_a + jnp.exp2(total_a[None] * rate_half) * enter
    other = lax.ppermute(jnp.where(at_a, after_a, enter), "blk", pair)
    state = ordered(y, jnp.where(at_a, enter, after_a), other)
    return jnp.where(jnp.logical_and(z == 0, at_a), first, state)


def rows(array):
    return array.reshape(-1, array.shape[-1])


def by_step(array):
    return array.reshape(-1, 8, array.shape[-1])


def dot32(left, right):
    return jnp.dot(left, right, preferred_element_type=jnp.float32)


def dot_t(left, right):
    return lax.dot_general(left, right, (((0,), (0,)), ((), ())), preferred_element_type=jnp.float32)


def dot_n(left, right):
    return lax.dot_general(left, right, (((1,), (1,)), ((), ())), preferred_element_type=jnp.float32)


def two_parts(array):
    high = lax.optimization_barrier(array.astype(jnp.bfloat16))
    return high, (array - high.astype(jnp.float32)).astype(jnp.bfloat16)


def split_parts(array, parts):
    return array.reshape(array.shape[:-2] + (parts, 8 // parts) + array.shape[-1:])


class Layer:
    def __init__(self, index, args):
        (norm_gain, in_weight, conv_weight, conv_bias, x_weight, dt_weight, dt_bias, decay_log,
         skip_weight, out_weight) = args
        self.gain = norm_gain[index]
        self.into = in_weight[index].reshape(in_weight.shape[1], -1)
        self.taps = conv_weight[index]
        self.shift = conv_bias[index]
        self.x = x_weight[index]
        self.dt = dt_weight[index]
        self.dt_bias = dt_bias[index]
        self.rate = -jnp.exp(decay_log[index])
        self.rate2 = self.rate * LOG2E
        self.skip = skip_weight[index]
        self.out = out_weight[index]


def forward_layer(layer, residual, scan_first, conv_first, parts, at_first):
    width = residual.shape[1]
    q = lax.rsqrt(jnp.mean(residual * residual, axis=-1, keepdims=True) + EPSILON)
    normed = (residual * q * layer.gain).astype(jnp.bfloat16)
    mixed = dot32(normed, layer.into)
    inner = mixed.shape[-1] // 2
    values, gate = mixed[:, :inner], mixed[:, inner:]
    count = values.shape[0]
    rim = layer.taps.shape[0] - 1
    tails = split_parts(by_step(values[count - 8 * rim:]), parts)
    arrived = jnp.where(at_first, conv_first, neighbour(tails[:, -1], 1))
    prefix = jnp.concatenate([arrived[:, None], tails[:, :-1]], axis=1).reshape(rim * 8, inner)
    window = jnp.concatenate([prefix, values], axis=0)
    conv_out = layer.shift + sum(layer.taps[k] * window[8 * k:8 * k + count] for k in range(rim + 1))
    inputs = lax.optimization_barrier(jax.nn.silu(conv_out).astype(jnp.bfloat16))
    projected = tensor_sum(dot32(inputs, layer.x))
    dt_low = projected[:, :RANK].astype(jnp.bfloat16)
    coef = by_step(projected[:, RANK:])
    before = dot32(dt_low, layer.dt) + layer.dt_bias
    step = jax.nn.softplus(before)
    push = step * inputs.astype(jnp.float32)
    rate = layer.rate2[:, None]
    local = split_parts(end_states(by_step(step), by_step(push), coef, layer.rate2), parts)
    totals = split_parts(jnp.sum(by_step(step), axis=0), parts)
    joined, total = local[:, 0], totals[0]
    for p in range(1, parts):
        joined = local[:, p] + jnp.exp2(totals[p][None] * rate) * joined
        total = total + totals[p]
    start = entering(total, joined, rate, scan_first, False)
    starts = [start]
    for p in range(1, parts):
        starts.append(local[:, p - 1] + jnp.exp2(totals[p - 1][None] * rate) * starts[-1])
    start = jnp.stack(starts, axis=1).reshape(STATE, 8, inner)
    scanned, states, enter, final = scan_forward(by_step(step), by_step(push), coef, layer.rate2, start)
    result = rows(scanned) + layer.skip * inputs.astype(jnp.float32)
    gated = (result * jax.nn.silu(gate)).astype(jnp.bfloat16)
    branch = tensor_sum(dot32(gated, layer.out))
    following = residual + branch
    squares = jnp.stack([jnp.sum(branch * branch), jnp.sum(following * following)])
    kept = (residual, q, normed, window, gate, conv_out, inputs, dt_low, coef, before, step, push, totals,
            result, gated, states, enter)
    return following, squares, split_parts(final, parts)[:, -1], tails[:, -1], kept


def backward_layer(layer, grad, kept, parts):
    (residual, q, normed, window, gate, conv_out, inputs, dt_low, coef, before, step, push, totals,
     result, gated, states, enter) = kept
    count, inner = gate.shape
    rim = layer.taps.shape[0] - 1
    wide = inputs.astype(jnp.float32)
    grad_low = grad.astype(jnp.bfloat16)
    grad_gated = dot_n(grad_low, layer.out)
    out_grad = dot_t(grad_low, gated)
    grad_result = grad_gated * jax.nn.silu(gate)
    grad_gate = (grad_gated * result * silu_slope(gate)).astype(jnp.bfloat16)
    skip_grad = jnp.sum(grad_result * wide, axis=0)
    gate_grad = dot_t(normed, grad_gate)
    rate = layer.rate2[:, None]
    local = split_parts(start_grads(by_step(step), by_step(grad_result), coef, layer.rate2), parts)
    joined, total = local[:, -1], totals[-1]
    for p in reversed(range(parts - 1)):
        joined = local[:, p] + jnp.exp2(totals[p][None] * rate) * joined
        total = total + totals[p]
    end = entering(total, joined, rate, jnp.zeros_like(joined), True)
    ends = [end]
    for p in reversed(range(1, parts)):
        ends.insert(0, local[:, p] + jnp.exp2(totals[p][None] * rate) * ends[0])
    end = jnp.stack(ends, axis=1).reshape(STATE, 8, inner)
    decays, pushes, coef_grad, start_grad, speed = scan_backward(
        by_step(step), by_step(push), by_step(grad_result), coef, layer.rate2, states, enter, end)
    pushes = rows(pushes)
    step_grad = rows(decays) * (1.0 / LOG2E) + wide * pushes
    before_grad = step_grad * jax.nn.sigmoid(before)
    bias_grad = jnp.sum(before_grad, axis=0)
    decay_grad = layer.rate * jnp.sum(speed, axis=1)
    before_low = before_grad.astype(jnp.bfloat16)
    dt_grad = dot_t(dt_low, before_low)
    projected_grad = tensor_sum(jnp.concatenate([dot_n(before_low, layer.dt), rows(coef_grad)], axis=-1))
    high, low = two_parts(projected_grad)
    x_grad = dot_t(high, inputs) + dot_t(low, inputs)
    through = dot_n(jnp.concatenate([high, low], axis=-1), jnp.concatenate([layer.x, layer.x], axis=-1))
    inputs_grad = grad_result * layer.skip + step * pushes + through
    conv_grad = inputs_grad * silu_slope(conv_out)
    taps_grad = jnp.stack([jnp.sum(conv_grad * window[8 * k:8 * k + count], axis=0) for k in range(rim + 1)])
    shift_grad = jnp.sum(conv_grad, axis=0)
    margin = jnp.zeros((8 * rim, inner), jnp.float32)
    padded = jnp.concatenate([margin, conv_grad, margin], axis=0)
    window_grad = sum(
        layer.taps[k] * padded[8 * (rim - k):8 * (rim - k) + count + 8 * rim] for k in range(rim + 1))
    prefix_grad = split_parts(by_step(window_grad[:8 * rim]), parts)
    arrived = neighbour(prefix_grad[:, 0], -1)
    tail_grad = jnp.concatenate([prefix_grad[:, 1:], arrived[:, None]], axis=1).reshape(8 * rim, inner)
    values_grad = jnp.concatenate([window_grad[8 * rim:count], window_grad[count:] + tail_grad], axis=0)
    values_grad = values_grad.astype(jnp.bfloat16)
    into_grad = dot_t(normed, values_grad)
    mixed_grad = jnp.concatenate([values_grad, grad_gate], axis=-1)
    normed_grad = tensor_sum(dot_n(mixed_grad, layer.into))
    gain_grad = jnp.sum(normed_grad * (residual * q), axis=0)
    scaled = normed_grad * layer.gain
    inner_mean = jnp.mean(scaled * residual, axis=-1, keepdims=True)
    passed = grad + q * scaled - residual * (q * q * q * inner_mean)
    grads = (gain_grad, into_grad, gate_grad, taps_grad, shift_grad, x_grad, dt_grad, bias_grad, decay_grad,
             skip_grad, out_grad)
    start_first = split_parts(start_grad, parts)[:, 0]
    return passed, grads, start_first, prefix_grad[:, 0]


MICRO = 1


def on_device(tokens, cotangent, *args):
    scan_init, conv_init = args[-2:]
    weights = args[:-2]
    blocks, index = lax.axis_size("blk"), lax.axis_index("blk")
    at_first = index == 0
    layer_total = weights[1].shape[0]
    seqs = tokens.shape[0] // MICRO
    parts = 8 // seqs
    length = tokens.shape[1] // parts
    width = tokens.shape[2]
    layers = [Layer(l, weights) for l in range(layer_total)]

    def arrange(array):
        return array.reshape(seqs, parts, length, width).transpose(2, 1, 0, 3).reshape(length * 8, width)

    def restore(array):
        array = array.reshape(length, parts, seqs, width).transpose(2, 1, 0, 3)
        return array.reshape(seqs, parts * length, width)

    outs, ins = [], []
    finals, tails, starts, prefixes = ([[None] * MICRO for _ in range(layer_total)] for _ in range(4))
    sums = [None] * layer_total
    squares = [0.0] * layer_total
    input_square = 0.0
    for m in range(MICRO):
        part = slice(m * seqs, (m + 1) * seqs)
        residual = arrange(tokens[part]).astype(jnp.float32)
        input_square = input_square + jnp.sum(residual * residual)
        kept = []
        for l in range(layer_total):
            residual, square, finals[l][m], tails[l][m], saved = forward_layer(
                layers[l], residual, jnp.moveaxis(scan_init[l, part], 1, 0),
                jnp.moveaxis(conv_init[l, part], 1, 0), parts, at_first)
            squares[l] = squares[l] + square
            kept.append(saved)
        outs.append(restore(residual.astype(jnp.bfloat16)))
        grad = arrange(cotangent[part]).astype(jnp.float32)
        for l in reversed(range(layer_total)):
            grad, grads, starts[l][m], prefixes[l][m] = backward_layer(layers[l], grad, kept[l], parts)
            sums[l] = grads if sums[l] is None else jax.tree.map(jnp.add, sums[l], grads)
        ins.append(restore(grad.astype(jnp.bfloat16)))

    big, small = [], []
    for l in reversed(range(layer_total)):
        (gain_grad, into_grad, gate_grad, taps_grad, shift_grad, x_grad, dt_grad, bias_grad, decay_grad,
         skip_grad, out_grad) = sums[l]
        into_part, gate_part, out_part = blk_scatter(into_grad), blk_scatter(gate_grad), blk_scatter(out_grad)
        thin = jnp.concatenate([x_grad.reshape(blocks, -1, x_grad.shape[-1]),
                                dt_grad.reshape(blocks, -1, dt_grad.shape[-1])], axis=1)
        thin = blk_scatter(thin)[0]
        cut = x_grad.shape[0] // blocks
        big.insert(0, (jnp.stack([into_part, gate_part], axis=1), out_part.T, thin[:cut].T, thin[cut:]))
        inner = taps_grad.shape[-1]
        packed = jnp.concatenate([gain_grad.reshape(-1, inner), taps_grad, shift_grad[None], bias_grad[None],
                                  skip_grad[None], decay_grad], axis=0)
        if l == 0:
            extra = jnp.concatenate([jnp.stack(squares).reshape(-1), input_square.reshape(1)])
            extra = jnp.pad(extra, (0, inner - extra.shape[0]))[None]
            packed = jnp.concatenate([packed, extra], axis=0)
        small.insert(0, blk_sum(packed))
    rows_gain = width // weights[2].shape[-1]
    taps = weights[2].shape[1]

    def unpack(first, count):
        return jnp.stack([part[first:first + count] for part in small])

    row_total = tokens.shape[0] * tokens.shape[1] * width * blocks
    last = jnp.sqrt(small[0][-1] / row_total)
    rms_stats = last[:2 * layer_total].reshape(layer_total, 2)
    input_rms = last[2 * layer_total:2 * layer_total + 1]
    gain_grad = unpack(0, rows_gain).reshape(layer_total, width)
    at = rows_gain + taps

    def stacked(lists):
        return jnp.stack([jnp.moveaxis(jnp.concatenate(parts_, axis=1), 0, 1) for parts_ in lists])[:, :, None]

    return (
        jnp.concatenate(outs, axis=0),
        stacked(finals),
        stacked(tails),
        jnp.concatenate(ins, axis=0),
        stacked(starts),
        stacked(prefixes),
        gain_grad,
        jnp.stack([part[0] for part in big]),
        unpack(rows_gain, taps),
        unpack(at, 1)[:, 0],
        jnp.stack([part[2] for part in big]),
        jnp.stack([part[3] for part in big]),
        unpack(at + 1, 1)[:, 0],
        unpack(at + 3, STATE),
        unpack(at + 2, 1)[:, 0],
        jnp.stack([part[1] for part in big]),
        rms_stats,
        input_rms,
    )


def solution(mesh):
    placed = (
        P(None, "blk", None),
        P(None, "blk", None),
        P(),
        P(None, None, None, "tensor"),
        P(None, None, "tensor"),
        P(None, "tensor"),
        P(None, "tensor", None),
        P(None, None, "tensor"),
        P(None, "tensor"),
        P(None, None, "tensor"),
        P(None, "tensor"),
        P(None, "tensor", None),
        P(None, None, None, "tensor"),
        P(None, None, None, "tensor"),
    )
    return jax.shard_map(
        on_device,
        mesh=mesh,
        in_specs=placed,
        out_specs=(
            P(None, "blk", None),
            P(None, None, "blk", None, "tensor"),
            P(None, None, "blk", None, "tensor"),
            P(None, "blk", None),
            P(None, None, "blk", None, "tensor"),
            P(None, None, "blk", None, "tensor"),
            P(),
            P(None, "blk", None, "tensor"),
            P(None, None, "tensor"),
            P(None, "tensor"),
            P(None, "tensor", "blk"),
            P(None, "blk", "tensor"),
            P(None, "tensor"),
            P(None, None, "tensor"),
            P(None, "tensor"),
            P(None, "tensor", "blk"),
            P(),
            P(),
        ),
        check_vma=False,
    )
```

```python
import math
from functools import partial
import jax
import jax.numpy as jnp
from jax import lax
from jax.experimental import pallas as pl
from jax.experimental.pallas import tpu as pltpu

from jax.sharding import PartitionSpec as P

STATE = 16
RANK = 128
EPSILON = 1e-05
LANES=128
LOG2E=math.log2(math.e)

def cp(limit):
    return pltpu.CompilerParams(dimension_semantics=("arbitrary",), vmem_limit_bytes=limit)

def spread(ref_value, out, first):
    for t in range(out.shape[0]):
        row = ref_value[t]
        for n in range(STATE):
            out[t, n] = jnp.broadcast_to(row[:, first + n:first + n + 1], out.shape[2:])

def rates(rate_ref, lanes, n):
    return jnp.broadcast_to(rate_ref[pl.ds(n, 1), lanes], (8, LANES))

def end_body(blocks, width, step_ref, push_ref, coef_ref, rate_ref, end_ref, write):
    @pl.when(pl.program_id(0) == 0)
    def _():
        end_ref[...] = jnp.zeros_like(end_ref)
    spread(coef_ref, write, 0)
    def group(g, _):
        cols = [pl.ds(pl.multiple_of((g * width + k) * LANES, LANES), LANES) for k in range(width)]
        for low in range(0, STATE, STATE // width):
            span = range(low, low + STATE // width)
            state = {(k, n): end_ref[n, :, cols[k]] for k in range(width) for n in span}
            rate = {(k, n): rates(rate_ref, cols[k], n) for k in range(width) for n in span}
            for t in range(step_ref.shape[0]):
                step = [step_ref[t, :, c] for c in cols]
                push = [push_ref[t, :, c] for c in cols]
                for n in span:
                    w = write[t, n]
                    for k in range(width):
                        state[k, n] = jnp.exp2(step[k] * rate[k, n]) * state[k, n] + push[k] * w
            for k in range(width):
                for n in span:
                    end_ref[n, :, cols[k]] = state[k, n]
        return 0
    lax.fori_loop(0, blocks // width, group, 0)

def end_states(step, push, coef, rate, tb=8, width=2, limit=40*2**20):
    T, _, C = step.shape
    return pl.pallas_call(
        partial(end_body, C // LANES, width),
        grid=(T // tb,),
        in_specs=[pl.BlockSpec((tb, 8, C), lambda i: (i, 0, 0)), pl.BlockSpec((tb, 8, C), lambda i: (i, 0, 0)),
                  pl.BlockSpec((tb, 8, 2 * STATE), lambda i: (i, 0, 0)), pl.BlockSpec((STATE, C), lambda i: (0, 0))],
        out_specs=pl.BlockSpec((STATE, 8, C), lambda i: (0, 0, 0)),
        out_shape=jax.ShapeDtypeStruct((STATE, 8, C), jnp.float32),
        scratch_shapes=[pltpu.VMEM((tb, STATE, 8, LANES), jnp.float32)],
        compiler_params=cp(limit), name="end_states")(step, push, coef, rate)

def scan_body(blocks, width, step_ref, push_ref, coef_ref, rate_ref, start_ref, out_ref, states_ref, enter_ref, final_ref, write, read):
    @pl.when(pl.program_id(0) == 0)
    def _():
        final_ref[...] = start_ref[...]
    spread(coef_ref, write, 0)
    spread(coef_ref, read, STATE)
    enter_ref[0] = final_ref[...]
    def group(g, _):
        cols = [pl.ds(pl.multiple_of((g * width + k) * LANES, LANES), LANES) for k in range(width)]
        for low in range(0, STATE, STATE // width):
            span = range(low, low + STATE // width)
            state = {(k, n): final_ref[n, :, cols[k]] for k in range(width) for n in span}
            rate = {(k, n): rates(rate_ref, cols[k], n) for k in range(width) for n in span}
            for t in range(step_ref.shape[0]):
                step = [step_ref[t, :, c] for c in cols]
                push = [push_ref[t, :, c] for c in cols]
                total = [None] * width
                for n in span:
                    w, r = write[t, n], read[t, n]
                    for k in range(width):
                        s = jnp.exp2(step[k] * rate[k, n]) * state[k, n] + push[k] * w
                        state[k, n] = s
                        states_ref[t, n, :, cols[k]] = s
                        total[k] = r * s if total[k] is None else total[k] + r * s
                for k in range(width):
                    if low == 0:
                        out_ref[t, :, cols[k]] = total[k]
                    else:
                        out_ref[t, :, cols[k]] += total[k]
            for k in range(width):
                for n in span:
                    final_ref[n, :, cols[k]] = state[k, n]
        return 0
    lax.fori_loop(0, blocks // width, group, 0)

def scan_forward(step, push, coef, rate, start, tb=8, width=2, limit=48*2**20):
    T, _, C = step.shape
    row = pl.BlockSpec((tb, 8, C), lambda i: (i, 0, 0))
    whole = pl.BlockSpec((STATE, 8, C), lambda i: (0, 0, 0))
    f32 = jnp.float32
    return pl.pallas_call(
        partial(scan_body, C // LANES, width),
        grid=(T // tb,),
        in_specs=[row, row, pl.BlockSpec((tb, 8, 2 * STATE), lambda i: (i, 0, 0)), pl.BlockSpec((STATE, C), lambda i: (0, 0)), whole],
        out_specs=[row, pl.BlockSpec((tb, STATE, 8, C), lambda i: (i, 0, 0, 0)), pl.BlockSpec((1, STATE, 8, C), lambda i: (i, 0, 0, 0)), whole],
        out_shape=[jax.ShapeDtypeStruct((T, 8, C), f32), jax.ShapeDtypeStruct((T, STATE, 8, C), f32),
                   jax.ShapeDtypeStruct((T // tb, STATE, 8, C), f32), jax.ShapeDtypeStruct((STATE, 8, C), f32)],
        scratch_shapes=[pltpu.VMEM((tb, STATE, 8, LANES), f32)] * 2,
        compiler_params=cp(limit), name="scan_forward")(step, push, coef, rate, start)

def start_body(blocks, width, step_ref, grad_ref, coef_ref, rate_ref, start_ref, read):
    @pl.when(pl.program_id(0) == 0)
    def _():
        start_ref[...] = jnp.zeros_like(start_ref)
    spread(coef_ref, read, STATE)
    def group(g, _):
        cols = [pl.ds(pl.multiple_of((g * width + k) * LANES, LANES), LANES) for k in range(width)]
        for low in range(0, STATE, STATE // width):
            span = range(low, low + STATE // width)
            state = {(k, n): start_ref[n, :, cols[k]] for k in range(width) for n in span}
            rate = {(k, n): rates(rate_ref, cols[k], n) for k in range(width) for n in span}
            for t in reversed(range(step_ref.shape[0])):
                step = [step_ref[t, :, c] for c in cols]
                grad = [grad_ref[t, :, c] for c in cols]
                for n in span:
                    r = read[t, n]
                    for k in range(width):
                        state[k, n] = jnp.exp2(step[k] * rate[k, n]) * (state[k, n] + r * grad[k])
            for k in range(width):
                for n in span:
                    start_ref[n, :, cols[k]] = state[k, n]
        return 0
    lax.fori_loop(0, blocks // width, group, 0)

def start_grads(step, grad, coef, rate, tb=8, width=2, limit=40*2**20):
    T, _, C = step.shape
    last = T // tb - 1
    row = pl.BlockSpec((tb, 8, C), lambda i: (last - i, 0, 0))
    return pl.pallas_call(
        partial(start_body, C // LANES, width),
        grid=(T // tb,),
        in_specs=[row, row, pl.BlockSpec((tb, 8, 2 * STATE), lambda i: (last - i, 0, 0)), pl.BlockSpec((STATE, C), lambda i: (0, 0))],
        out_specs=pl.BlockSpec((STATE, 8, C), lambda i: (0, 0, 0)),
        out_shape=jax.ShapeDtypeStruct((STATE, 8, C), jnp.float32),
        scratch_shapes=[pltpu.VMEM((tb, STATE, 8, LANES), jnp.float32)],
        compiler_params=cp(limit), name="start_grads")(step, grad, coef, rate)

def back_body(blocks, width, step_ref, push_ref, grad_ref, coef_ref, rate_ref, states_ref, enter_ref, end_ref,
              decay_out, push_out, coef_out, start_ref, speed_ref, write, read, write_sum, read_sum):
    @pl.when(pl.program_id(0) == 0)
    def _():
        start_ref[...] = end_ref[...]
        speed_ref[...] = jnp.zeros_like(speed_ref)
    spread(coef_ref, write, 0)
    spread(coef_ref, read, STATE)
    tb = step_ref.shape[0]
    def group(g, first):
        cols = [pl.ds(pl.multiple_of((g * width + k) * LANES, LANES), LANES) for k in range(width)]
        for low in range(0, STATE, STATE // width):
            span = range(low, low + STATE // width)
            carry = {(k, n): start_ref[n, :, cols[k]] for k in range(width) for n in span}
            speed = {(k, n): speed_ref[n, :, cols[k]] for k in range(width) for n in span}
            rate = {(k, n): rates(rate_ref, cols[k], n) for k in range(width) for n in span}
            for t in reversed(range(tb)):
                step = [step_ref[t, :, c] for c in cols]
                push = [push_ref[t, :, c] for c in cols]
                grad = [grad_ref[t, :, c] for c in cols]
                decays = [None] * width
                pushes = [None] * width
                for n in span:
                    w, r = write[t, n], read[t, n]
                    wsum, rsum = None, None
                    for k in range(width):
                        before = states_ref[t - 1, n, :, cols[k]] if t else enter_ref[0, n, :, cols[k]]
                        back = carry[k, n] + r * grad[k]
                        held = jnp.exp2(step[k] * rate[k, n]) * back
                        carry[k, n] = held
                        q = held * before
                        speed[k, n] = speed[k, n] + step[k] * q
                        rq, bw = rate[k, n] * q, back * w
                        decays[k] = rq if decays[k] is None else decays[k] + rq
                        pushes[k] = bw if pushes[k] is None else pushes[k] + bw
                        bp, gs = back * push[k], grad[k] * states_ref[t, n, :, cols[k]]
                        wsum = bp if wsum is None else wsum + bp
                        rsum = gs if rsum is None else rsum + gs
                    if first:
                        write_sum[t, n] = wsum
                        read_sum[t, n] = rsum
                    else:
                        write_sum[t, n] += wsum
                        read_sum[t, n] += rsum
                for k in range(width):
                    if low == 0:
                        decay_out[t, :, cols[k]] = decays[k]
                        push_out[t, :, cols[k]] = pushes[k]
                    else:
                        decay_out[t, :, cols[k]] += decays[k]
                        push_out[t, :, cols[k]] += pushes[k]
            for k in range(width):
                for n in span:
                    start_ref[n, :, cols[k]] = carry[k, n]
                    speed_ref[n, :, cols[k]] = speed[k, n]
        return 0
    write_sum[...] = jnp.zeros_like(write_sum)
    read_sum[...] = jnp.zeros_like(read_sum)
    lax.fori_loop(0, blocks // width, lambda g, _: group(g, False), 0)
    lane = lax.broadcasted_iota(jnp.int32, (8, 2 * STATE), 1)
    for t in range(tb):
        row = jnp.zeros((8, 2 * STATE), jnp.float32)
        for n in range(STATE):
            row = jnp.where(lane == n, jnp.sum(write_sum[t, n], axis=-1, keepdims=True), row)
            row = jnp.where(lane == STATE + n, jnp.sum(read_sum[t, n], axis=-1, keepdims=True), row)
        coef_out[t] = row

def scan_backward(step, push, grad, coef, rate, states, enter, end, tb=8, width=2, limit=48*2**20):
    T, _, C = step.shape
    last = T // tb - 1
    f32 = jnp.float32
    row = pl.BlockSpec((tb, 8, C), lambda i: (last - i, 0, 0))
    thin = pl.BlockSpec((tb, 8, 2 * STATE), lambda i: (last - i, 0, 0))
    whole = pl.BlockSpec((STATE, 8, C), lambda i: (0, 0, 0))
    return pl.pallas_call(
        partial(back_body, C // LANES, width),
        grid=(T // tb,),
        in_specs=[row, row, row, thin, pl.BlockSpec((STATE, C), lambda i: (0, 0)),
                  pl.BlockSpec((tb, STATE, 8, C), lambda i: (last - i, 0, 0, 0)),
                  pl.BlockSpec((1, STATE, 8, C), lambda i: (last - i, 0, 0, 0)), whole],
        out_specs=[row, row, thin, whole, whole],
        out_shape=[jax.ShapeDtypeStruct((T, 8, C), f32)] * 2 + [jax.ShapeDtypeStruct((T, 8, 2 * STATE), f32)]
          + [jax.ShapeDtypeStruct((STATE, 8, C), f32)] * 2,
        scratch_shapes=[pltpu.VMEM((tb, STATE, 8, LANES), f32)] * 4,
        compiler_params=cp(limit), name="scan_backward")(step, push, grad, coef, rate, states, enter, end)


HALVES_OF_CHIP = 2


def silu_slope(argument):
    sigmoid_value = jax.nn.sigmoid(argument)
    return sigmoid_value * (1.0 + argument * (1.0 - sigmoid_value))


def half_of(array, index):
    size = array.shape[0] // 2
    return lax.dynamic_slice_in_dim(array, index * size, size, 0)


def ordered(index, mine, other):
    first = jnp.where(index == 0, mine, other)
    second = jnp.where(index == 0, other, mine)
    return jnp.concatenate([first, second], axis=0)


BESIDE = [(0, 1), (1, 0), (2, 3), (3, 2)]
ACROSS = [(0, 2), (2, 0), (1, 3), (3, 1)]


def paired():
    return lax.axis_size("tensor") == 4


def tensor_sum(array):
    if not paired():
        return lax.psum(array, "tensor")
    core = lax.axis_index("tensor") % 2
    half = half_of(array, core) + lax.ppermute(half_of(array, 1 - core), "tensor", BESIDE)
    half = half + lax.ppermute(half, "tensor", ACROSS)
    return ordered(core, half, lax.ppermute(half, "tensor", BESIDE))


def own_rows(array):
    if not paired():
        size = array.shape[0] // lax.axis_size("tensor")
        return lax.dynamic_slice_in_dim(array, lax.axis_index("tensor") * size, size, 0)
    return half_of(array, lax.axis_index("tensor") % 2)


def own_sum(array, beside):
    if not paired():
        return lax.psum_scatter(array, "tensor", scatter_dimension=0, tiled=True), beside
    core = lax.axis_index("tensor") % 2
    half = half_of(array, core) + lax.ppermute(half_of(array, 1 - core), "tensor", BESIDE)
    got = lax.ppermute(half, "tensor", ACROSS)
    got, beside = lax.optimization_barrier((got, beside))
    return half + got, beside


def all_rows(array):
    if not paired():
        return lax.optimization_barrier(lax.all_gather(array, "tensor", tiled=True))
    other = lax.optimization_barrier(lax.ppermute(array, "tensor", BESIDE))
    return ordered(lax.axis_index("tensor") % 2, array, other)


def rows_sum(array):
    if not paired():
        return lax.psum(array, "tensor")
    return array + lax.ppermute(array, "tensor", BESIDE)


def chosen(array, axis, index):
    return lax.dynamic_index_in_dim(array, index, axis, keepdims=False)


def blk_sum(array):
    if lax.axis_size("blk") != 8:
        return lax.psum(array, "blk")
    for bit in (1, 2, 4):
        array = array + lax.ppermute(array, "blk", [(j, j ^ bit) for j in range(8)])
    return array


def blk_scatter(array):
    return lax.psum_scatter(array, "blk", scatter_dimension=0, tiled=True)


def halved(array, bits):
    axes = [4, 2, 1]
    for bit in bits:
        axis = axes.index(bit)
        axes.remove(bit)
        mine = (lax.axis_index("blk") // bit) % 2
        give = chosen(array, axis, 1 - mine)
        array = chosen(array, axis, mine) + lax.ppermute(give, "blk", [(j, j ^ bit) for j in range(8)])
    return array


def split_scatter(array):
    if lax.axis_size("blk") != 8:
        return blk_scatter(array)
    array = array.reshape((2, 2, 2, array.shape[0] // 8, array.shape[1]))
    middle = array.shape[-1] // 2
    return jnp.concatenate([halved(array[..., :middle], (1, 2, 4)), halved(array[..., middle:], (2, 4, 1))], axis=-1)


def neighbour(value, steps):
    count = lax.axis_size("blk")
    first, last = max(0, -steps), min(count, count - steps)
    return lax.ppermute(value, "blk", [(j, j + steps) for j in range(first, last)])


def entering_any(total, local, rate, first, reverse):
    peers, index = lax.axis_size("blk"), lax.axis_index("blk")
    totals, locals_ = lax.all_gather(total, "blk"), lax.all_gather(local, "blk")

    def step(k, state):
        at = peers - 1 - k if reverse else k
        reached = at > index if reverse else at < index
        return jnp.where(reached, jnp.exp2(totals[at][None] * rate) * state + locals_[at], state)

    return lax.fori_loop(0, peers, step, first)


def entering(total, local, rate, first, reverse):
    if lax.axis_size("blk") != 8:
        return entering_any(total, local, rate, first, reverse)
    index = lax.axis_index("blk")
    y, z = index % 2, index // 2
    pair = [(j, j ^ 1) for j in range(8)]
    if reverse:
        y, z = 1 - y, 3 - z
    sign = -1 if reverse else 1
    at_a = y == 0
    decay = jnp.exp2(total[None] * rate)
    own = local + jnp.where(jnp.logical_and(z == 0, at_a), decay * first, 0.0)
    mine, give = half_of(own, y), half_of(own, 1 - y)
    got = lax.ppermute(jnp.concatenate([give, total[None]], axis=0), "blk", pair)
    got, got_total = got[:-1], got[-1]
    rate_half = half_of(rate, y)
    local_a, local_b = jnp.where(at_a, mine, got), jnp.where(at_a, got, mine)
    total_a, total_b = jnp.where(at_a, total, got_total), jnp.where(at_a, got_total, total)
    joined = local_b + jnp.exp2(total_b[None] * rate_half) * local_a
    message = jnp.concatenate([joined, (total_a + total_b)[None]], axis=0)

    def along(value, pairs):
        if reverse:
            pairs = [(3 - s, 3 - d) for s, d in pairs]
        return lax.ppermute(value, "blk", [(2 * s + k, 2 * d + k) for s, d in pairs for k in (0, 1)])

    one = along(message, [(0, 1), (1, 2), (2, 3)])
    two = along(one, [(1, 2), (2, 3)])
    three = along(one[:-1], [(1, 3)])
    enter = one[:-1] + jnp.exp2(one[-1:] * rate_half) * (
        two[:-1] + jnp.exp2(two[-1:] * rate_half) * three
    )
    after_a = local_a + jnp.exp2(total_a[None] * rate_half) * enter
    other = lax.ppermute(jnp.where(at_a, after_a, enter), "blk", pair)
    state = ordered(y, jnp.where(at_a, enter, after_a), other)
    return jnp.where(jnp.logical_and(z == 0, at_a), first, state)


def rows(array):
    return array.reshape(-1, array.shape[-1])


def by_step(array):
    return array.reshape(-1, 8, array.shape[-1])


def dot32(left, right):
    return jnp.dot(left, right, preferred_element_type=jnp.float32)


def dot_t(left, right):
    return lax.dot_general(left, right, (((0,), (0,)), ((), ())), preferred_element_type=jnp.float32)


def dot_n(left, right):
    return lax.dot_general(left, right, (((1,), (1,)), ((), ())), preferred_element_type=jnp.float32)


def two_parts(array):
    high = lax.optimization_barrier(array.astype(jnp.bfloat16))
    return high, (array - high.astype(jnp.float32)).astype(jnp.bfloat16)


def split_parts(array, parts):
    return array.reshape(array.shape[:-2] + (parts, 8 // parts) + array.shape[-1:])


class Layer:
    def __init__(self, index, args):
        (norm_gain, in_weight, conv_weight, conv_bias, x_weight, dt_weight, dt_bias, decay_log,
         skip_weight, out_weight) = args
        self.gain = norm_gain[index]
        self.into = in_weight[index].reshape(in_weight.shape[1], -1)
        self.taps = conv_weight[index]
        self.shift = conv_bias[index]
        self.x = x_weight[index]
        self.dt = dt_weight[index]
        self.dt_bias = dt_bias[index]
        self.rate = -jnp.exp(decay_log[index])
        self.rate2 = self.rate * LOG2E
        self.skip = skip_weight[index]
        self.out = out_weight[index]


def inverse_rms(residual):
    return lax.rsqrt(jnp.mean(residual * residual, axis=-1, keepdims=True) + EPSILON)


def front(layer, normed, conv_first, parts, at_first):
    mixed = dot32(normed, layer.into)
    inner = mixed.shape[-1] // 2
    values, gate = mixed[:, :inner], mixed[:, inner:]
    count = values.shape[0]
    rim = layer.taps.shape[0] - 1
    tails = split_parts(by_step(values[count - 8 * rim:]), parts)
    arrived = jnp.where(at_first, conv_first, neighbour(tails[:, -1], 1))
    prefix = jnp.concatenate([arrived[:, None], tails[:, :-1]], axis=1).reshape(rim * 8, inner)
    window = jnp.concatenate([prefix, values], axis=0)
    conv_out = layer.shift + sum(layer.taps[k] * window[8 * k:8 * k + count] for k in range(rim + 1))
    inputs = lax.optimization_barrier(jax.nn.silu(conv_out).astype(jnp.bfloat16))
    projected = tensor_sum(dot32(inputs, layer.x))
    dt_low = projected[:, :RANK].astype(jnp.bfloat16)
    coef = by_step(projected[:, RANK:])
    before = dot32(dt_low, layer.dt) + layer.dt_bias
    step = jax.nn.softplus(before)
    push = step * inputs.astype(jnp.float32)
    local = split_parts(end_states(by_step(step), by_step(push), coef, layer.rate2), parts)
    totals = split_parts(jnp.sum(by_step(step), axis=0), parts)
    return (window, gate, conv_out, inputs, dt_low, coef, before, step, push, totals), local, tails[:, -1]


def join(local, totals, rate, reverse):
    order = range(local.shape[1])
    order = list(reversed(order)) if reverse else list(order)
    joined, total = local[:, order[0]], totals[order[0]]
    for p in order[1:]:
        joined = local[:, p] + jnp.exp2(totals[p][None] * rate) * joined
        total = total + totals[p]
    return total, joined


def each_part(state, local, totals, rate, reverse):
    order = range(local.shape[1])
    order = list(reversed(order)) if reverse else list(order)
    states = {order[0]: state}
    for p, following in zip(order[:-1], order[1:]):
        states[following] = local[:, p] + jnp.exp2(totals[p][None] * rate) * states[p]
    state = jnp.stack([states[p] for p in range(local.shape[1])], axis=1)
    return state.reshape(STATE, 8, state.shape[-1])


def exchange(layer, local, totals, first, reverse):
    rate = layer.rate2[:, None]
    total, joined = join(local, totals, rate, reverse)
    state = entering(total, joined, rate, first, reverse)
    return each_part(state, local, totals, rate, reverse)


def scanning(layer, kept, start):
    window, gate, conv_out, inputs, dt_low, coef, before, step, push, totals = kept
    scanned, states, enter, final = scan_forward(by_step(step), by_step(push), coef, layer.rate2, start)
    result = rows(scanned) + layer.skip * inputs.astype(jnp.float32)
    gated = (result * jax.nn.silu(gate)).astype(jnp.bfloat16)
    return dot32(gated, layer.out), (result, gated, states, enter), final


def back_front(layer, kept, grad_low):
    window, gate, conv_out, inputs, dt_low, coef, before, step, push, totals = kept
    grad_gated = dot_n(grad_low, layer.out)
    grad_result = grad_gated * jax.nn.silu(gate)
    local = start_grads(by_step(step), by_step(grad_result), coef, layer.rate2)
    return (grad_gated, grad_result), split_parts(local, totals.shape[0])


def back_side(layer, kept, normed, scans, grads, grad_low):
    window, gate, conv_out, inputs, dt_low, coef, before, step, push, totals = kept
    result, gated, states, enter = scans
    grad_gated, grad_result = grads
    inner = gate.shape[1]
    out_grad = dot_t(grad_low, gated)
    grad_gate = (grad_gated * result * silu_slope(gate)).astype(jnp.bfloat16)
    gate_grad = dot_t(normed, grad_gate)
    gate_through = dot_n(grad_gate, layer.into[:, inner:])
    skip_grad = jnp.sum(grad_result * inputs.astype(jnp.float32), axis=0)
    return out_grad, gate_grad, gate_through, skip_grad


def back_scan(layer, kept, normed, scans, grads, end, gate_through):
    window, gate, conv_out, inputs, dt_low, coef, before, step, push, totals = kept
    result, gated, states, enter = scans
    grad_gated, grad_result = grads
    count, inner = gate.shape
    parts = totals.shape[0]
    rim = layer.taps.shape[0] - 1
    wide = inputs.astype(jnp.float32)
    decays, pushes, coef_grad, start_grad, speed = scan_backward(
        by_step(step), by_step(push), by_step(grad_result), coef, layer.rate2, states, enter, end)
    pushes = rows(pushes)
    step_grad = rows(decays) * (1.0 / LOG2E) + wide * pushes
    before_grad = step_grad * jax.nn.sigmoid(before)
    bias_grad = jnp.sum(before_grad, axis=0)
    decay_grad = layer.rate * jnp.sum(speed, axis=1)
    before_low = before_grad.astype(jnp.bfloat16)
    projected_grad = tensor_sum(jnp.concatenate([dot_n(before_low, layer.dt), rows(coef_grad)], axis=-1))
    dt_grad = dot_t(dt_low, before_low)
    high, low = two_parts(projected_grad)
    x_grad = dot_t(high, inputs) + dot_t(low, inputs)
    through = dot_n(jnp.concatenate([high, low], axis=-1), jnp.concatenate([layer.x, layer.x], axis=-1))
    inputs_grad = grad_result * layer.skip + step * pushes + through
    conv_grad = inputs_grad * silu_slope(conv_out)
    taps_grad = jnp.stack([jnp.sum(conv_grad * window[8 * k:8 * k + count], axis=0) for k in range(rim + 1)])
    shift_grad = jnp.sum(conv_grad, axis=0)
    margin = jnp.zeros((8 * rim, inner), jnp.float32)
    padded = jnp.concatenate([margin, conv_grad, margin], axis=0)
    window_grad = sum(
        layer.taps[k] * padded[8 * (rim - k):8 * (rim - k) + count + 8 * rim] for k in range(rim + 1))
    prefix_grad = split_parts(by_step(window_grad[:8 * rim]), parts)
    arrived = neighbour(prefix_grad[:, 0], -1)
    tail_grad = jnp.concatenate([prefix_grad[:, 1:], arrived[:, None]], axis=1).reshape(8 * rim, inner)
    values_grad = jnp.concatenate([window_grad[8 * rim:count], window_grad[count:] + tail_grad], axis=0)
    values_grad = values_grad.astype(jnp.bfloat16)
    into_grad = dot_t(normed, values_grad)
    normed_part = dot_n(values_grad, layer.into[:, :inner]) + gate_through
    grads = (into_grad, taps_grad, shift_grad, x_grad, dt_grad, bias_grad, decay_grad)
    return normed_part, grads, split_parts(start_grad, parts)[:, 0], prefix_grad[:, 0]


def norm_back(layer, normed_grad, residual, q):
    gain_grad = jnp.sum(normed_grad * (residual * q), axis=0)
    scaled = normed_grad * layer.gain
    inner_mean = jnp.mean(scaled * residual, axis=-1, keepdims=True)
    return gain_grad, q * scaled - residual * (q * q * q * inner_mean)


def on_device(tokens, cotangent, *args):
    scan_init, conv_init = args[-2:]
    weights = args[:-2]
    blocks, index = lax.axis_size("blk"), lax.axis_index("blk")
    at_first = index == 0
    layer_total = weights[1].shape[0]
    seqs = tokens.shape[0]
    parts = 8 // seqs
    length = tokens.shape[1] // parts
    width = tokens.shape[2]
    layers = [Layer(l, weights) for l in range(layer_total)]
    last = layer_total - 1

    def arrange(array):
        return array.reshape(seqs, parts, length, width).transpose(2, 1, 0, 3).reshape(length * 8, width)

    def restore(array):
        array = array.reshape(length, parts, seqs, width).transpose(2, 1, 0, 3)
        return array.reshape(seqs, parts * length, width)

    residual = arrange(tokens).astype(jnp.float32)
    normed = (residual * inverse_rms(residual) * layers[0].gain).astype(jnp.bfloat16)
    residual = own_rows(residual)
    input_square = jnp.sum(residual * residual)
    grad = arrange(cotangent).astype(jnp.float32)
    grad_low = grad.astype(jnp.bfloat16)

    kept, scans, norms, finals, tails, squares = ([None] * layer_total for _ in range(6))
    starts, prefixes, sums = ([None] * layer_total for _ in range(3))
    for l, layer in enumerate(layers):
        norms[l] = (normed, residual)
        kept[l], local, tails[l] = front(
            layer, normed, jnp.moveaxis(conv_init[l], 1, 0), parts, at_first)
        totals = kept[l][-1]
        if l == last:
            grads, back_local = back_front(layer, kept[l], grad_low)
            local, back_local = lax.optimization_barrier((local, back_local))
            end = exchange(layer, back_local, totals, jnp.zeros_like(back_local[:, 0]), True)
        start = exchange(layer, local, totals, jnp.moveaxis(scan_init[l], 1, 0), False)
        partial_sum, scans[l], final = scanning(layer, kept[l], start)
        finals[l] = split_parts(final, parts)[:, -1]
        if l < last:
            branch, layers[l + 1].into = own_sum(partial_sum, layers[l + 1].into)
        else:
            branch, _ = own_sum(partial_sum, ())
        following = residual + branch
        squares[l] = jnp.stack([jnp.sum(branch * branch), jnp.sum(following * following)])
        residual = following
        if l < last:
            unscaled = all_rows(residual * inverse_rms(residual))
            normed = (unscaled * layers[l + 1].gain).astype(jnp.bfloat16)
    out = restore((2.0 * all_rows(0.5 * residual)).astype(jnp.bfloat16))

    for l in reversed(range(layer_total)):
        layer = layers[l]
        normed, residual = norms[l]
        if l < last:
            grads, back_local = back_front(layer, kept[l], grad_low)
            end = exchange(layer, back_local, kept[l][-1], jnp.zeros_like(back_local[:, 0]), True)
        side = back_side(layer, kept[l], normed, scans[l], grads, grad_low)
        end, side = lax.optimization_barrier((end, side))
        out_grad, gate_grad, gate_through, skip_grad = side
        normed_part, layer_grads, starts[l], prefixes[l] = back_scan(
            layer, kept[l], normed, scans[l], grads, end, gate_through)
        if l == last:
            normed_part, out = lax.optimization_barrier((normed_part, out))
        normed_grad, _ = own_sum(normed_part, ())
        gain_grad, change = norm_back(layer, normed_grad, residual, inverse_rms(residual))
        grad = grad + all_rows(change)
        grad_low = grad.astype(jnp.bfloat16)
        sums[l] = (gain_grad, gate_grad, skip_grad, out_grad) + layer_grads
    input_grad = restore(grad_low)

    big, small, shared = [], [], []
    for l in reversed(range(layer_total)):
        (gain_grad, gate_grad, skip_grad, out_grad, into_grad, taps_grad, shift_grad, x_grad, dt_grad, bias_grad,
         decay_grad) = sums[l]
        scatter = blk_scatter if l else split_scatter
        into_part, gate_part, out_part = scatter(into_grad), scatter(gate_grad), blk_scatter(out_grad)
        thin = jnp.concatenate([x_grad.reshape(blocks, -1, x_grad.shape[-1]),
                                dt_grad.reshape(blocks, -1, dt_grad.shape[-1])], axis=1)
        thin = split_scatter(thin.reshape(-1, thin.shape[-1]))
        cut = x_grad.shape[0] // blocks
        big.insert(0, (jnp.stack([into_part, gate_part], axis=1), out_part.T, thin[:cut].T, thin[cut:]))
        small.insert(0, jnp.concatenate(
            [taps_grad, shift_grad[None], bias_grad[None], skip_grad[None], decay_grad], axis=0))
        shared.insert(0, gain_grad)
    inner = small[0].shape[-1]
    extra = jnp.concatenate([jnp.stack(squares).reshape(-1), input_square.reshape(1)])
    extra = jnp.pad(extra, (0, inner - extra.shape[0]))[None]
    shared = rows_sum(jnp.concatenate([jnp.stack(shared).reshape(-1, inner), extra], axis=0))
    gain_rows = shared.shape[0] - 1
    sizes = [part.shape[0] for part in small]
    packed = blk_sum(jnp.concatenate(small + [shared], axis=0))
    rest = packed[sum(sizes):]
    small = packed[:sum(sizes)].reshape(layer_total, sizes[0], inner)
    taps = weights[2].shape[1]
    row_total = tokens.shape[0] * tokens.shape[1] * width * blocks
    squares = rest[-1] / row_total
    rms_stats = jnp.sqrt(squares[:2 * layer_total]).reshape(layer_total, 2)
    input_rms = jnp.sqrt(squares[2 * layer_total:2 * layer_total + 1])

    def stacked(parts_):
        return jnp.stack([jnp.moveaxis(part, 0, 1) for part in parts_])[:, :, None]

    return (
        out,
        stacked(finals),
        stacked(tails),
        input_grad,
        stacked(starts),
        stacked(prefixes),
        rest[:gain_rows].reshape(layer_total, width),
        jnp.stack([part[0] for part in big]),
        small[:, :taps],
        small[:, taps],
        jnp.stack([part[2] for part in big]),
        jnp.stack([part[3] for part in big]),
        small[:, taps + 1],
        small[:, taps + 3:],
        small[:, taps + 2],
        jnp.stack([part[1] for part in big]),
        rms_stats,
        input_rms,
    )


def solution(mesh):
    placed = (
        P(None, "blk", None),
        P(None, "blk", None),
        P(),
        P(None, None, None, "tensor"),
        P(None, None, "tensor"),
        P(None, "tensor"),
        P(None, "tensor", None),
        P(None, None, "tensor"),
        P(None, "tensor"),
        P(None, None, "tensor"),
        P(None, "tensor"),
        P(None, "tensor", None),
        P(None, None, None, "tensor"),
        P(None, None, None, "tensor"),
    )
    return jax.shard_map(
        on_device,
        mesh=mesh,
        in_specs=placed,
        out_specs=(
            P(None, "blk", None),
            P(None, None, "blk", None, "tensor"),
            P(None, None, "blk", None, "tensor"),
            P(None, "blk", None),
            P(None, None, "blk", None, "tensor"),
            P(None, None, "blk", None, "tensor"),
            P(),
            P(None, "blk", None, "tensor"),
            P(None, None, "tensor"),
            P(None, "tensor"),
            P(None, "tensor", "blk"),
            P(None, "blk", "tensor"),
            P(None, "tensor"),
            P(None, None, "tensor"),
            P(None, "tensor"),
            P(None, "tensor", "blk"),
            P(),
            P(),
        ),
        check_vma=False,
    )
```

```python
import math
from functools import partial
import jax
import jax.numpy as jnp
from jax import lax
from jax.experimental import pallas as pl
from jax.experimental.pallas import tpu as pltpu

from jax.sharding import PartitionSpec as P

STATE = 16
RANK = 128
EPSILON = 1e-05
LANES=128
LOG2E=math.log2(math.e)

def cost(step, passes):
    return pl.CostEstimate(flops=passes * STATE * step.size, bytes_accessed=passes * STATE * step.size, transcendentals=0)

def cp(limit):
    return pltpu.CompilerParams(dimension_semantics=("arbitrary",), vmem_limit_bytes=limit)

def spread(ref_value, out, first):
    for t in range(out.shape[0]):
        row = ref_value[t]
        for n in range(STATE):
            out[t, n] = jnp.broadcast_to(row[:, first + n:first + n + 1], out.shape[2:])

def rates(rate_ref, lanes, n):
    return jnp.broadcast_to(rate_ref[pl.ds(n, 1), lanes], (8, LANES))

def end_body(blocks, width, step_ref, push_ref, coef_ref, rate_ref, end_ref, write):
    @pl.when(pl.program_id(0) == 0)
    def _():
        end_ref[...] = jnp.zeros_like(end_ref)
    spread(coef_ref, write, 0)
    def group(g, _):
        cols = [pl.ds(pl.multiple_of((g * width + k) * LANES, LANES), LANES) for k in range(width)]
        for low in range(0, STATE, STATE // width):
            span = range(low, low + STATE // width)
            state = {(k, n): end_ref[n, :, cols[k]] for k in range(width) for n in span}
            rate = {(k, n): rates(rate_ref, cols[k], n) for k in range(width) for n in span}
            for t in range(step_ref.shape[0]):
                step = [step_ref[t, :, c] for c in cols]
                push = [push_ref[t, :, c] for c in cols]
                for n in span:
                    w = write[t, n]
                    for k in range(width):
                        state[k, n] = jnp.exp2(step[k] * rate[k, n]) * state[k, n] + push[k] * w
            for k in range(width):
                for n in span:
                    end_ref[n, :, cols[k]] = state[k, n]
        return 0
    lax.fori_loop(0, blocks // width, group, 0)

def end_states(step, push, coef, rate, tb=8, width=2, limit=40*2**20):
    T, _, C = step.shape
    return pl.pallas_call(
        partial(end_body, C // LANES, width),
        grid=(T // tb,),
        in_specs=[pl.BlockSpec((tb, 8, C), lambda i: (i, 0, 0)), pl.BlockSpec((tb, 8, C), lambda i: (i, 0, 0)),
                  pl.BlockSpec((tb, 8, 2 * STATE), lambda i: (i, 0, 0)), pl.BlockSpec((STATE, C), lambda i: (0, 0))],
        out_specs=pl.BlockSpec((STATE, 8, C), lambda i: (0, 0, 0)),
        out_shape=jax.ShapeDtypeStruct((STATE, 8, C), jnp.float32),
        scratch_shapes=[pltpu.VMEM((tb, STATE, 8, LANES), jnp.float32)],
        compiler_params=cp(limit), cost_estimate=cost(step, 4), name="end_states")(step, push, coef, rate)

def scan_body(blocks, width, step_ref, push_ref, coef_ref, rate_ref, start_ref, out_ref, states_ref, final_ref, write, read):
    @pl.when(pl.program_id(0) == 0)
    def _():
        final_ref[...] = start_ref[...]
    spread(coef_ref, write, 0)
    spread(coef_ref, read, STATE)
    def group(g, _):
        cols = [pl.ds(pl.multiple_of((g * width + k) * LANES, LANES), LANES) for k in range(width)]
        for low in range(0, STATE, STATE // width):
            span = range(low, low + STATE // width)
            state = {(k, n): final_ref[n, :, cols[k]] for k in range(width) for n in span}
            rate = {(k, n): rates(rate_ref, cols[k], n) for k in range(width) for n in span}
            for t in range(step_ref.shape[0]):
                step = [step_ref[t, :, c] for c in cols]
                push = [push_ref[t, :, c] for c in cols]
                total = [None] * width
                for n in span:
                    w, r = write[t, n], read[t, n]
                    for k in range(width):
                        s = jnp.exp2(step[k] * rate[k, n]) * state[k, n] + push[k] * w
                        state[k, n] = s
                        states_ref[t, n, :, cols[k]] = s
                        total[k] = r * s if total[k] is None else total[k] + r * s
                for k in range(width):
                    if low == 0:
                        out_ref[t, :, cols[k]] = total[k]
                    else:
                        out_ref[t, :, cols[k]] += total[k]
            for k in range(width):
                for n in span:
                    final_ref[n, :, cols[k]] = state[k, n]
        return 0
    lax.fori_loop(0, blocks // width, group, 0)

def scan_forward(step, push, coef, rate, start, tb=8, width=2, limit=48*2**20):
    T, _, C = step.shape
    row = pl.BlockSpec((tb, 8, C), lambda i: (i, 0, 0))
    whole = pl.BlockSpec((STATE, 8, C), lambda i: (0, 0, 0))
    f32 = jnp.float32
    return pl.pallas_call(
        partial(scan_body, C // LANES, width),
        grid=(T // tb,),
        in_specs=[row, row, pl.BlockSpec((tb, 8, 2 * STATE), lambda i: (i, 0, 0)), pl.BlockSpec((STATE, C), lambda i: (0, 0)), whole],
        out_specs=[row, pl.BlockSpec((tb, STATE, 8, C), lambda i: (i, 0, 0, 0)), whole],
        out_shape=[jax.ShapeDtypeStruct((T, 8, C), f32), jax.ShapeDtypeStruct((T, STATE, 8, C), f32),
                   jax.ShapeDtypeStruct((STATE, 8, C), f32)],
        scratch_shapes=[pltpu.VMEM((tb, STATE, 8, LANES), f32)] * 2,
        compiler_params=cp(limit), cost_estimate=cost(step, 7), name="scan_forward")(step, push, coef, rate, start)

def start_body(blocks, width, step_ref, grad_ref, coef_ref, rate_ref, start_ref, read):
    @pl.when(pl.program_id(0) == 0)
    def _():
        start_ref[...] = jnp.zeros_like(start_ref)
    spread(coef_ref, read, STATE)
    def group(g, _):
        cols = [pl.ds(pl.multiple_of((g * width + k) * LANES, LANES), LANES) for k in range(width)]
        for low in range(0, STATE, STATE // width):
            span = range(low, low + STATE // width)
            state = {(k, n): start_ref[n, :, cols[k]] for k in range(width) for n in span}
            rate = {(k, n): rates(rate_ref, cols[k], n) for k in range(width) for n in span}
            for t in reversed(range(step_ref.shape[0])):
                step = [step_ref[t, :, c] for c in cols]
                grad = [grad_ref[t, :, c] for c in cols]
                for n in span:
                    r = read[t, n]
                    for k in range(width):
                        state[k, n] = jnp.exp2(step[k] * rate[k, n]) * (state[k, n] + r * grad[k])
            for k in range(width):
                for n in span:
                    start_ref[n, :, cols[k]] = state[k, n]
        return 0
    lax.fori_loop(0, blocks // width, group, 0)

def start_grads(step, grad, coef, rate, tb=8, width=2, limit=40*2**20):
    T, _, C = step.shape
    last = T // tb - 1
    row = pl.BlockSpec((tb, 8, C), lambda i: (last - i, 0, 0))
    return pl.pallas_call(
        partial(start_body, C // LANES, width),
        grid=(T // tb,),
        in_specs=[row, row, pl.BlockSpec((tb, 8, 2 * STATE), lambda i: (last - i, 0, 0)), pl.BlockSpec((STATE, C), lambda i: (0, 0))],
        out_specs=pl.BlockSpec((STATE, 8, C), lambda i: (0, 0, 0)),
        out_shape=jax.ShapeDtypeStruct((STATE, 8, C), jnp.float32),
        scratch_shapes=[pltpu.VMEM((tb, STATE, 8, LANES), jnp.float32)],
        compiler_params=cp(limit), cost_estimate=cost(step, 4), name="start_grads")(step, grad, coef, rate)

def back_body(blocks, width, step_ref, push_ref, grad_ref, coef_ref, rate_ref, states_ref, prior_ref, begin_ref, end_ref,
              decay_out, push_out, coef_out, start_ref, speed_ref, write, read, write_sum, read_sum):
    @pl.when(pl.program_id(0) == 0)
    def _():
        start_ref[...] = end_ref[...]
        speed_ref[...] = jnp.zeros_like(speed_ref)
    spread(coef_ref, write, 0)
    spread(coef_ref, read, STATE)
    tb = step_ref.shape[0]
    begins = pl.program_id(0) == pl.num_programs(0) - 1
    def group(g, first):
        cols = [pl.ds(pl.multiple_of((g * width + k) * LANES, LANES), LANES) for k in range(width)]
        for low in range(0, STATE, STATE // width):
            span = range(low, low + STATE // width)
            carry = {(k, n): start_ref[n, :, cols[k]] for k in range(width) for n in span}
            speed = {(k, n): speed_ref[n, :, cols[k]] for k in range(width) for n in span}
            rate = {(k, n): rates(rate_ref, cols[k], n) for k in range(width) for n in span}
            enter = {(k, n): jnp.where(begins, begin_ref[n, :, cols[k]], prior_ref[0, n, :, cols[k]])
                     for k in range(width) for n in span}
            for t in reversed(range(tb)):
                step = [step_ref[t, :, c] for c in cols]
                push = [push_ref[t, :, c] for c in cols]
                grad = [grad_ref[t, :, c] for c in cols]
                decays = [None] * width
                pushes = [None] * width
                for n in span:
                    w, r = write[t, n], read[t, n]
                    wsum, rsum = None, None
                    for k in range(width):
                        before = states_ref[t - 1, n, :, cols[k]] if t else enter[k, n]
                        back = carry[k, n] + r * grad[k]
                        held = jnp.exp2(step[k] * rate[k, n]) * back
                        carry[k, n] = held
                        q = held * before
                        speed[k, n] = speed[k, n] + step[k] * q
                        rq, bw = rate[k, n] * q, back * w
                        decays[k] = rq if decays[k] is None else decays[k] + rq
                        pushes[k] = bw if pushes[k] is None else pushes[k] + bw
                        bp, gs = back * push[k], grad[k] * states_ref[t, n, :, cols[k]]
                        wsum = bp if wsum is None else wsum + bp
                        rsum = gs if rsum is None else rsum + gs
                    if first:
                        write_sum[t, n] = wsum
                        read_sum[t, n] = rsum
                    else:
                        write_sum[t, n] += wsum
                        read_sum[t, n] += rsum
                for k in range(width):
                    if low == 0:
                        decay_out[t, :, cols[k]] = decays[k]
                        push_out[t, :, cols[k]] = pushes[k]
                    else:
                        decay_out[t, :, cols[k]] += decays[k]
                        push_out[t, :, cols[k]] += pushes[k]
            for k in range(width):
                for n in span:
                    start_ref[n, :, cols[k]] = carry[k, n]
                    speed_ref[n, :, cols[k]] = speed[k, n]
        return 0
    write_sum[...] = jnp.zeros_like(write_sum)
    read_sum[...] = jnp.zeros_like(read_sum)
    lax.fori_loop(0, blocks // width, lambda g, _: group(g, False), 0)
    lane = lax.broadcasted_iota(jnp.int32, (8, 2 * STATE), 1)
    for t in range(tb):
        row = jnp.zeros((8, 2 * STATE), jnp.float32)
        for n in range(STATE):
            row = jnp.where(lane == n, jnp.sum(write_sum[t, n], axis=-1, keepdims=True), row)
            row = jnp.where(lane == STATE + n, jnp.sum(read_sum[t, n], axis=-1, keepdims=True), row)
        coef_out[t] = row

def scan_backward(step, push, grad, coef, rate, states, begin, end, tb=8, width=2, limit=48*2**20):
    T, _, C = step.shape
    last = T // tb - 1
    f32 = jnp.float32
    row = pl.BlockSpec((tb, 8, C), lambda i: (last - i, 0, 0))
    thin = pl.BlockSpec((tb, 8, 2 * STATE), lambda i: (last - i, 0, 0))
    whole = pl.BlockSpec((STATE, 8, C), lambda i: (0, 0, 0))
    return pl.pallas_call(
        partial(back_body, C // LANES, width),
        grid=(T // tb,),
        in_specs=[row, row, row, thin, pl.BlockSpec((STATE, C), lambda i: (0, 0)),
                  pl.BlockSpec((tb, STATE, 8, C), lambda i: (last - i, 0, 0, 0)),
                  pl.BlockSpec((1, STATE, 8, C), lambda i: (jnp.maximum((last - i) * tb - 1, 0), 0, 0, 0)), whole, whole],
        out_specs=[row, row, thin, whole, whole],
        out_shape=[jax.ShapeDtypeStruct((T, 8, C), f32)] * 2 + [jax.ShapeDtypeStruct((T, 8, 2 * STATE), f32)]
          + [jax.ShapeDtypeStruct((STATE, 8, C), f32)] * 2,
        scratch_shapes=[pltpu.VMEM((tb, STATE, 8, LANES), f32)] * 4,
        compiler_params=cp(limit), cost_estimate=cost(step, 13), name="scan_backward")(step, push, grad, coef, rate, states, states, begin, end)


HALVES_OF_CHIP = 2


def silu_slope(argument):
    sigmoid_value = jax.nn.sigmoid(argument)
    return sigmoid_value * (1.0 + argument * (1.0 - sigmoid_value))


def half_of(array, index):
    size = array.shape[0] // 2
    return lax.dynamic_slice_in_dim(array, index * size, size, 0)


def ordered(index, mine, other):
    first = jnp.where(index == 0, mine, other)
    second = jnp.where(index == 0, other, mine)
    return jnp.concatenate([first, second], axis=0)


BESIDE = [(0, 1), (1, 0), (2, 3), (3, 2)]
ACROSS = [(0, 2), (2, 0), (1, 3), (3, 1)]


def paired():
    return lax.axis_size("tensor") == 4


def tensor_sum(array):
    if not paired():
        return lax.psum(array, "tensor")
    core = lax.axis_index("tensor") % 2
    half = half_of(array, core) + lax.ppermute(half_of(array, 1 - core), "tensor", BESIDE)
    half = half + lax.ppermute(half, "tensor", ACROSS)
    return ordered(core, half, lax.ppermute(half, "tensor", BESIDE))


def own_rows(array):
    if not paired():
        size = array.shape[0] // lax.axis_size("tensor")
        return lax.dynamic_slice_in_dim(array, lax.axis_index("tensor") * size, size, 0)
    return half_of(array, lax.axis_index("tensor") % 2)


def ordered_after(value, *others):
    return lax.optimization_barrier((value,) + others)[0]


def core_sum(array):
    if not paired():
        return lax.psum_scatter(array, "tensor", scatter_dimension=0, tiled=True)
    core = lax.axis_index("tensor") % 2
    return half_of(array, core) + lax.ppermute(half_of(array, 1 - core), "tensor", BESIDE)


def across(half):
    if not paired():
        return jnp.zeros_like(half)
    return lax.ppermute(half, "tensor", ACROSS)


def all_rows(array):
    if not paired():
        return lax.optimization_barrier(lax.all_gather(array, "tensor", tiled=True))
    other = lax.optimization_barrier(lax.ppermute(array, "tensor", BESIDE))
    return ordered(lax.axis_index("tensor") % 2, array, other)


def rows_sum(array):
    if not paired():
        return lax.psum(array, "tensor")
    return array + lax.ppermute(array, "tensor", BESIDE)


def chosen(array, axis, index):
    return lax.dynamic_index_in_dim(array, index, axis, keepdims=False)


def blk_sum(array):
    if lax.axis_size("blk") != 8:
        return lax.psum(array, "blk")
    for bit in (1, 2, 4):
        array = array + lax.ppermute(array, "blk", [(j, j ^ bit) for j in range(8)])
    return array


def blk_scatter(array):
    return lax.psum_scatter(array, "blk", scatter_dimension=0, tiled=True)


def add_rows(total, other, count):
    slab = 8

    def body(i, _):
        at = pl.ds(pl.multiple_of(i * slab, slab), slab)
        total[at, :] = total[at, :] + other[at, :]
        return 0

    lax.fori_loop(0, count // slab, body, 0)


def remote(src, dst, sends, recvs, at, device):
    return pltpu.make_async_remote_copy(
        src_ref=src, dst_ref=dst, send_sem=sends.at[at], recv_sem=recvs.at[at], device_id=device,
        device_id_type=pl.DeviceIdType.MESH)


def joint_body(plan, chunks, sum_ref, *refs):
    count = 1 + max(job[0] for job in plan)
    thick_refs, small_ref, refs = refs[:count], refs[count], refs[count + 1:]
    half_out, thick_outs, small_out, refs = refs[0], refs[1:1 + count], refs[1 + count], refs[2 + count:]
    own_half, core_half, far_half, small_in, refs = refs[0], refs[1], refs[2], refs[3], refs[4:]
    core_send, core_recv, far_send, far_recv, local_sem, out_sem, small_send, small_recv = refs[:8]
    refs = refs[8:]
    blk, tensor = lax.axis_index("blk"), lax.axis_index("tensor")
    bits = {1: blk % 2, 2: (blk // 2) % 2, 4: blk // 4}
    core = tensor % 2
    beside = (blk, tensor + 1 - 2 * core)
    far = (blk, (tensor + 2) % 4)
    peers = {bit: (blk + bit - 2 * bit * bits[bit], tensor) for bit in bits}
    barrier = pltpu.get_barrier_semaphore()
    for device in (beside, far, peers[1], peers[2], peers[4]):
        pl.semaphore_signal(barrier, inc=1, device_id=device, device_id_type=pl.DeviceIdType.MESH)
    pl.semaphore_wait(barrier, 5)

    rows_each = half_out.shape[0] // chunks
    smalls, core_copies, local_copies, far_copies, outs = [], [], [], [], []

    def small_step(i):
        copy = remote(small_out, small_in.at[i], small_send, small_recv, i, peers[1 << i])
        copy.start()
        smalls.append(copy)

    def small_end(i):
        smalls[i].wait()
        small_out[...] = small_out[...] + small_in[i]

    small_out[...] = small_ref[...]
    small_step(0)
    for k in range(chunks):
        give = pl.ds(pl.multiple_of((1 - core) * rows_each * chunks + k * rows_each, rows_each), rows_each)
        keep = pl.ds(pl.multiple_of(core * rows_each * chunks + k * rows_each, rows_each), rows_each)
        copy = remote(sum_ref.at[give], core_half.at[k], core_send, core_recv, k, beside)
        copy.start()
        core_copies.append(copy)
        copy = pltpu.make_async_copy(sum_ref.at[keep], own_half.at[k], local_sem.at[k])
        copy.start()
        local_copies.append(copy)

    class Job:
        def __init__(self, which, low, wide, order, refs):
            (self.own, self.first, self.second, self.third, self.sems) = refs[0], refs[1], refs[2], refs[3], refs[4:]
            self.order = order
            self.count = thick_refs[which].shape[3]
            self.out = thick_outs[which].at[:, pl.ds(low, wide)]
            lead, (u, v) = bits[order[0]], (bits[order[1]], bits[order[2]])
            self.parts = [(1 - u, 1 - v), (1 - u, v), (u, 1 - v), (u, v)]
            self.firsts, self.owns, self.seconds = [], [], []
            for i, part in enumerate(self.parts):
                at = {order[1]: part[0], order[2]: part[1]}

                def source(mine):
                    index = dict(at)
                    index[order[0]] = mine
                    return thick_refs[which].at[index[4], index[2], index[1], :, pl.ds(low, wide)]

                copy = remote(source(1 - lead), self.first.at[part], self.sems[0], self.sems[1], i, peers[order[0]])
                copy.start()
                self.firsts.append(copy)
                copy = pltpu.make_async_copy(source(lead), self.own.at[part], self.sems[2].at[i])
                copy.start()
                self.owns.append(copy)

        def first_end(self, i):
            self.owns[i].wait()
            self.firsts[i].wait_recv()
            add_rows(self.own.at[self.parts[i]], self.first.at[self.parts[i]], self.count)
            if i < 2:
                copy = remote(self.own.at[self.parts[i]], self.second.at[i], self.sems[3], self.sems[4], i,
                              peers[self.order[1]])
                copy.start()
                self.seconds.append(copy)
                return
            self.seconds[i - 2].wait_recv()
            add_rows(self.own.at[self.parts[i]], self.second.at[i - 2], self.count)
            if i == 2:
                self.last = remote(self.own.at[self.parts[i]], self.third, self.sems[5], self.sems[6], 0,
                                   peers[self.order[2]])
                self.last.start()

        def end(self):
            self.last.wait_recv()
            add_rows(self.own.at[self.parts[3]], self.third, self.count)
            copy = pltpu.make_async_copy(self.own.at[self.parts[3]], self.out, self.sems[7].at[0])
            copy.start()
            outs.append(copy)

        def sent(self):
            return self.firsts + self.seconds + [self.last]

    jobs = [Job(*job, refs[12 * i:12 * i + 12]) for i, job in enumerate(plan)]

    def core_end(k):
        local_copies[k].wait()
        core_copies[k].wait()
        add_rows(own_half.at[k], core_half.at[k], rows_each)
        copy = remote(own_half.at[k], far_half.at[k], far_send, far_recv, k, far)
        copy.start()
        far_copies.append(copy)

    def far_end(k):
        far_copies[k].wait_recv()
        add_rows(far_half.at[k], own_half.at[k], rows_each)
        copy = pltpu.make_async_copy(
            far_half.at[k], half_out.at[pl.ds(k * rows_each, rows_each)], out_sem.at[k])
        copy.start()
        outs.append(copy)

    for k in range(chunks):
        core_end(k)
    small_end(0)
    small_step(1)
    for i in range(4):
        for job in jobs:
            job.first_end(i)
        if i in (0, 1):
            small_end(i + 1)
            if i == 0:
                small_step(2)
        far_end(i)
    for job in jobs:
        job.end()
    for copy in far_copies + [each for job in jobs for each in job.sent()]:
        copy.wait_send()
    for copy in outs:
        copy.wait()


def joint_sums(array, thick, small, collective_id):
    if not paired() or lax.axis_size("blk") != 8:
        return (lax.psum_scatter(array, "tensor", scatter_dimension=0, tiled=True),
                [blk_scatter(part) for part in thick], lax.psum(small, "blk"))
    R, N = array.shape
    C = thick[0].shape[1]
    chunks = 4
    f32 = jnp.float32
    dma = pltpu.SemaphoreType.DMA
    any_spec = pl.BlockSpec(memory_space=pl.ANY)
    vmem_spec = pl.BlockSpec(memory_space=pltpu.VMEM)
    cut = C - 128 if len(thick) == 1 else C
    plan = [(0, 0, cut, (1, 2, 4))]
    if cut < C:
        plan.append((0, cut, C - cut, (2, 4, 1)))
    plan += [(i, 0, C, (2, 4, 1)) for i in range(1, len(thick))]
    scratch = []
    for which, _, wide, _ in plan:
        count = thick[which].shape[0] // 8
        scratch += [pltpu.VMEM((2, 2, count, wide), f32), pltpu.VMEM((2, 2, count, wide), f32),
                    pltpu.VMEM((2, count, wide), f32), pltpu.VMEM((count, wide), f32),
                    dma((4,)), dma((4,)), dma((4,)), dma((2,)), dma((2,)), dma((1,)), dma((1,)), dma((1,))]
    half = pltpu.VMEM((chunks, R // 2 // chunks, N), f32)
    out = pl.pallas_call(
        partial(joint_body, plan, chunks),
        in_specs=[any_spec] * (1 + len(thick)) + [vmem_spec],
        out_specs=[any_spec] * (1 + len(thick)) + [vmem_spec],
        out_shape=[jax.ShapeDtypeStruct((R // 2, N), f32)]
        + [jax.ShapeDtypeStruct((part.shape[0] // 8, C), f32) for part in thick]
        + [jax.ShapeDtypeStruct(small.shape, f32)],
        scratch_shapes=[half, half, half, pltpu.VMEM((3,) + small.shape, f32)]
        + [dma((chunks,))] * 5 + [dma((chunks,)), dma((3,)), dma((3,))] + scratch,
        compiler_params=pltpu.CompilerParams(
            collective_id=collective_id, has_side_effects=True, vmem_limit_bytes=52 * 2**20),
        cost_estimate=pl.CostEstimate(flops=0, bytes_accessed=50 * R * N * 4, transcendentals=0),
        name="joint_sums",
    )(array, *[part.reshape(2, 2, 2, part.shape[0] // 8, C) for part in thick], small)
    return out[0], list(out[1:-1]), out[-1]


def neighbour(value, steps):
    count = lax.axis_size("blk")
    first, last = max(0, -steps), min(count, count - steps)
    return lax.ppermute(value, "blk", [(j, j + steps) for j in range(first, last)])


def entering_any(total, local, rate, first, reverse):
    peers, index = lax.axis_size("blk"), lax.axis_index("blk")
    totals, locals_ = lax.all_gather(total, "blk"), lax.all_gather(local, "blk")

    def step(k, state):
        at = peers - 1 - k if reverse else k
        reached = at > index if reverse else at < index
        return jnp.where(reached, jnp.exp2(totals[at][None] * rate) * state + locals_[at], state)

    return lax.fori_loop(0, peers, step, first)


def entering(total, local, rate, first, reverse):
    if lax.axis_size("blk") != 8:
        return entering_any(total, local, rate, first, reverse)
    index = lax.axis_index("blk")
    y, z = index % 2, index // 2
    pair = [(j, j ^ 1) for j in range(8)]
    if reverse:
        y, z = 1 - y, 3 - z
    sign = -1 if reverse else 1
    at_a = y == 0
    decay = jnp.exp2(total[None] * rate)
    own = local + jnp.where(jnp.logical_and(z == 0, at_a), decay * first, 0.0)
    mine, give = half_of(own, y), half_of(own, 1 - y)
    got = lax.ppermute(jnp.concatenate([give, total[None]], axis=0), "blk", pair)
    got, got_total = got[:-1], got[-1]
    rate_half = half_of(rate, y)
    local_a, local_b = jnp.where(at_a, mine, got), jnp.where(at_a, got, mine)
    total_a, total_b = jnp.where(at_a, total, got_total), jnp.where(at_a, got_total, total)
    joined = local_b + jnp.exp2(total_b[None] * rate_half) * local_a
    message = jnp.concatenate([joined, (total_a + total_b)[None]], axis=0)

    def along(value, pairs):
        if reverse:
            pairs = [(3 - s, 3 - d) for s, d in pairs]
        return lax.ppermute(value, "blk", [(2 * s + k, 2 * d + k) for s, d in pairs for k in (0, 1)])

    one = along(message, [(0, 1), (1, 2), (2, 3)])
    two = along(one, [(1, 2), (2, 3)])
    three = along(one[:-1], [(1, 3)])
    enter = one[:-1] + jnp.exp2(one[-1:] * rate_half) * (
        two[:-1] + jnp.exp2(two[-1:] * rate_half) * three
    )
    after_a = local_a + jnp.exp2(total_a[None] * rate_half) * enter
    other = lax.ppermute(jnp.where(at_a, after_a, enter), "blk", pair)
    state = ordered(y, jnp.where(at_a, enter, after_a), other)
    return jnp.where(jnp.logical_and(z == 0, at_a), first, state)


def rows(array):
    return array.reshape(-1, array.shape[-1])


def by_step(array):
    return array.reshape(-1, 8, array.shape[-1])


def dot32(left, right):
    return jnp.dot(left, right, preferred_element_type=jnp.float32)


def dot_t(left, right):
    return lax.dot_general(left, right, (((0,), (0,)), ((), ())), preferred_element_type=jnp.float32)


def dot_n(left, right):
    return lax.dot_general(left, right, (((1,), (1,)), ((), ())), preferred_element_type=jnp.float32)


def two_parts(array):
    high = lax.optimization_barrier(array.astype(jnp.bfloat16))
    return high, (array - high.astype(jnp.float32)).astype(jnp.bfloat16)


def split_parts(array, parts):
    return array.reshape(array.shape[:-2] + (parts, 8 // parts) + array.shape[-1:])


class Layer:
    def __init__(self, index, args):
        (norm_gain, in_weight, conv_weight, conv_bias, x_weight, dt_weight, dt_bias, decay_log,
         skip_weight, out_weight) = args
        self.gain = norm_gain[index]
        self.raw = in_weight[index]
        self.taps = conv_weight[index]
        self.shift = conv_bias[index]
        self.x = x_weight[index]
        self.dt = dt_weight[index]
        self.dt_bias = dt_bias[index]
        self.rate = -jnp.exp(decay_log[index])
        self.rate2 = self.rate * LOG2E
        self.skip = skip_weight[index]
        self.out = out_weight[index]


def inverse_rms(residual):
    return lax.rsqrt(jnp.mean(residual * residual, axis=-1, keepdims=True) + EPSILON)


def front(layer, normed, conv_first, parts, at_first):
    mixed = jnp.einsum("rd,dkc->krc", normed, layer.raw, preferred_element_type=jnp.float32)
    values, gate = mixed[0], mixed[1]
    inner = values.shape[-1]
    count = values.shape[0]
    rim = layer.taps.shape[0] - 1
    tails = split_parts(by_step(values[count - 8 * rim:]), parts)
    arrived = jnp.where(at_first, conv_first, neighbour(tails[:, -1], 1))
    prefix = jnp.concatenate([arrived[:, None], tails[:, :-1]], axis=1).reshape(rim * 8, inner)
    window = jnp.concatenate([prefix, values], axis=0)
    conv_out = layer.shift + sum(layer.taps[k] * window[8 * k:8 * k + count] for k in range(rim + 1))
    inputs = lax.optimization_barrier(jax.nn.silu(conv_out).astype(jnp.bfloat16))
    projected = tensor_sum(dot32(inputs, layer.x))
    dt_low = projected[:, :RANK].astype(jnp.bfloat16)
    coef = by_step(projected[:, RANK:])
    step = jax.nn.softplus(dot32(dt_low, layer.dt) + layer.dt_bias)
    push = step * inputs.astype(jnp.float32)
    local = split_parts(end_states(by_step(step), by_step(push), coef, layer.rate2), parts)
    totals = split_parts(jnp.sum(by_step(step), axis=0), parts)
    return (window, gate, conv_out, inputs, dt_low, coef, step, push, totals), local, tails[:, -1]


def join(local, totals, rate, reverse):
    order = range(local.shape[1])
    order = list(reversed(order)) if reverse else list(order)
    joined, total = local[:, order[0]], totals[order[0]]
    for p in order[1:]:
        joined = local[:, p] + jnp.exp2(totals[p][None] * rate) * joined
        total = total + totals[p]
    return total, joined


def each_part(state, local, totals, rate, reverse):
    order = range(local.shape[1])
    order = list(reversed(order)) if reverse else list(order)
    states = {order[0]: state}
    for p, following in zip(order[:-1], order[1:]):
        states[following] = local[:, p] + jnp.exp2(totals[p][None] * rate) * states[p]
    state = jnp.stack([states[p] for p in range(local.shape[1])], axis=1)
    return state.reshape(STATE, 8, state.shape[-1])


def exchange(layer, local, totals, first, reverse):
    rate = layer.rate2[:, None]
    total, joined = join(local, totals, rate, reverse)
    state = entering(total, joined, rate, first, reverse)
    return each_part(state, local, totals, rate, reverse)


def scanning(layer, kept, start):
    window, gate, conv_out, inputs, dt_low, coef, step, push, totals = kept
    scanned, states, final = scan_forward(by_step(step), by_step(push), coef, layer.rate2, start)
    result = rows(scanned) + layer.skip * inputs.astype(jnp.float32)
    gated = (result * jax.nn.silu(gate)).astype(jnp.bfloat16)
    return dot32(gated, layer.out), (result, gated, states, start), final


def back_gated(layer, kept, grad_low):
    gate = kept[1]
    grad_gated = dot_n(grad_low, layer.out)
    return grad_gated, grad_gated * jax.nn.silu(gate)


def back_local(layer, kept, grad_result):
    window, gate, conv_out, inputs, dt_low, coef, step, push, totals = kept
    local = start_grads(by_step(step), by_step(grad_result), coef, layer.rate2)
    return split_parts(local, totals.shape[0])


def back_side(layer, kept, normed, scans, grads, grad_low):
    window, gate, conv_out, inputs, dt_low, coef, step, push, totals = kept
    result, gated, states, start = scans
    grad_gated, grad_result = grads
    inner = gate.shape[1]
    grad_gate = (grad_gated * result * silu_slope(gate)).astype(jnp.bfloat16)
    gate_grad = dot_t(normed, grad_gate)
    gate_through = dot_n(grad_gate, layer.into[:, inner:])
    skip_grad = jnp.sum(grad_result * inputs.astype(jnp.float32), axis=0)
    return gate_grad, gate_through, skip_grad


def back_scan(layer, kept, scans, grads, end):
    window, gate, conv_out, inputs, dt_low, coef, step, push, totals = kept
    result, gated, states, start = scans
    grad_gated, grad_result = grads
    return scan_backward(
        by_step(step), by_step(push), by_step(grad_result), coef, layer.rate2, states, start, end)


def back_rest(layer, kept, grads, scan_out, gate_through):
    window, gate, conv_out, inputs, dt_low, coef, step, push, totals = kept
    grad_gated, grad_result = grads
    count, inner = gate.shape
    parts = totals.shape[0]
    rim = layer.taps.shape[0] - 1
    wide = inputs.astype(jnp.float32)
    decays, pushes, coef_grad, start_grad, speed = scan_out
    pushes = rows(pushes)
    step_grad = rows(decays) * (1.0 / LOG2E) + wide * pushes
    before_grad = step_grad * -jnp.expm1(-step)
    bias_grad = jnp.sum(before_grad, axis=0)
    decay_grad = layer.rate * jnp.sum(speed, axis=1)
    before_low = before_grad.astype(jnp.bfloat16)
    projected_grad = tensor_sum(jnp.concatenate([dot_n(before_low, layer.dt), rows(coef_grad)], axis=-1))
    high, low = two_parts(projected_grad)
    through = dot_n(jnp.concatenate([high, low], axis=-1), jnp.concatenate([layer.x, layer.x], axis=-1))
    inputs_grad = grad_result * layer.skip + step * pushes + through
    conv_grad = inputs_grad * silu_slope(conv_out)
    taps_grad = jnp.stack([jnp.sum(conv_grad * window[8 * k:8 * k + count], axis=0) for k in range(rim + 1)])
    shift_grad = jnp.sum(conv_grad, axis=0)
    margin = jnp.zeros((8 * rim, inner), jnp.float32)
    padded = jnp.concatenate([margin, conv_grad, margin], axis=0)
    window_grad = sum(
        layer.taps[k] * padded[8 * (rim - k):8 * (rim - k) + count + 8 * rim] for k in range(rim + 1))
    prefix_grad = split_parts(by_step(window_grad[:8 * rim]), parts)
    arrived = neighbour(prefix_grad[:, 0], -1)
    tail_grad = jnp.concatenate([prefix_grad[:, 1:], arrived[:, None]], axis=1).reshape(8 * rim, inner)
    values_grad = jnp.concatenate([window_grad[8 * rim:count], window_grad[count:] + tail_grad], axis=0)
    values_grad = values_grad.astype(jnp.bfloat16)
    normed_part = dot_n(values_grad, layer.into[:, :inner]) + gate_through
    small = jnp.concatenate([taps_grad, shift_grad[None], bias_grad[None], decay_grad], axis=0)
    return normed_part, small, (values_grad, before_low, high, low), split_parts(start_grad, parts)[:, 0], prefix_grad[:, 0]


def thick_grads(kept, normed, lows):
    inputs, dt_low = kept[3], kept[4]
    values_grad, before_low, high, low = lows
    blocks = lax.axis_size("blk")
    x_grad = dot_t(high, inputs) + dot_t(low, inputs)
    return [eights(part.reshape(blocks, -1, part.shape[-1]))
            for part in (dot_t(normed, values_grad), x_grad, dot_t(dt_low, before_low))]


def eights(array):
    return jnp.pad(array, ((0, 0), (0, -array.shape[1] % 8), (0, 0)))


def norm_back(layer, normed_grad, residual, q):
    gain_grad = jnp.sum(normed_grad * (residual * q), axis=0)
    scaled = normed_grad * layer.gain
    inner_mean = jnp.mean(scaled * residual, axis=-1, keepdims=True)
    return gain_grad, q * scaled - residual * (q * q * q * inner_mean)


def on_device(tokens, cotangent, *args):
    scan_init, conv_init = args[-2:]
    weights = args[:-2]
    blocks, index = lax.axis_size("blk"), lax.axis_index("blk")
    at_first = index == 0
    layer_total = weights[1].shape[0]
    seqs = tokens.shape[0]
    parts = 8 // seqs
    length = tokens.shape[1] // parts
    width = tokens.shape[2]
    layers = [Layer(l, weights) for l in range(layer_total)]
    last = layer_total - 1

    def arrange(array):
        return array.reshape(seqs, parts, length, width).transpose(2, 1, 0, 3).reshape(length * 8, width)

    def restore(array):
        array = array.reshape(length, parts, seqs, width).transpose(2, 1, 0, 3)
        return array.reshape(seqs, parts * length, width)

    residual = arrange(tokens).astype(jnp.float32)
    normed = (residual * inverse_rms(residual) * layers[0].gain).astype(jnp.bfloat16)
    residual = own_rows(residual)
    input_square = jnp.sum(residual * residual)
    grad = arrange(cotangent).astype(jnp.float32)
    grad_low = grad.astype(jnp.bfloat16)

    kept, scans, norms, finals, tails, squares = ([None] * layer_total for _ in range(6))
    starts, prefixes, smalls, gains = ([None] * layer_total for _ in range(4))
    for l, layer in enumerate(layers):
        norms[l] = (normed, residual)
        kept[l], local, tails[l] = front(
            layer, normed, jnp.moveaxis(conv_init[l], 1, 0), parts, at_first)
        totals = kept[l][-1]
        if l == last:
            grads = back_gated(layer, kept[l], grad_low)
            local, late = lax.optimization_barrier((local, back_local(layer, kept[l], grads[1])))
            end = exchange(layer, late, totals, jnp.zeros_like(late[:, 0]), True)
        start = exchange(layer, local, totals, jnp.moveaxis(scan_init[l], 1, 0), False)
        partial_sum, scans[l], final = scanning(layer, kept[l], start)
        finals[l] = split_parts(final, parts)[:, -1]
        half = core_sum(partial_sum)
        if l < last:
            half, stored = lax.optimization_barrier((half, weights[1]))
            into = [stored[k].reshape(width, -1) for k in range(layer_total)]
            got, into, grad_low = lax.optimization_barrier((across(half), into, grad_low))
            for each, array in zip(layers, into):
                each.into = array
            branch = half + got
            following = residual + branch
            squares[l] = jnp.stack([jnp.sum(branch * branch), jnp.sum(following * following)])
            residual = following
            unscaled = all_rows(residual * inverse_rms(residual))
            normed = (unscaled * layers[l + 1].gain).astype(jnp.bfloat16)

    thins, scattered = [], [None] * layer_total
    for l in reversed(range(layer_total)):
        layer = layers[l]
        normed, base = norms[l]
        if l < last:
            grads = back_gated(layer, kept[l], grad_low)
            late = back_local(layer, kept[l], grads[1])
            end = exchange(layer, late, kept[l][-1], jnp.zeros_like(late[:, 0]), True)
        out_grad = dot_t(grad_low, scans[l][1])
        side = back_side(layer, kept[l], normed, scans[l], grads, grad_low)
        middle = half.shape[0] // 2
        if l == last:
            end, side, out_grad, half = lax.optimization_barrier((end, side, out_grad, half))
            scattered[l] = [blk_scatter(out_grad), blk_scatter(side[0])]
            scan_out, got = lax.optimization_barrier(
                (back_scan(layer, kept[l], scans[l], grads, end), across(half[:middle])))
        else:
            end, side, out_grad, half, scattered[last] = lax.optimization_barrier(
                (end, side, out_grad, half, scattered[last]))
            scattered[l] = [blk_scatter(out_grad), blk_scatter(side[0])]
            scan_out, got_rest = lax.optimization_barrier(
                (back_scan(layer, kept[l], scans[l], grads, end), across(half[middle:])))
            branch = half + jnp.concatenate([got, got_rest], axis=0)
            following = residual + branch
            squares[last] = jnp.stack([jnp.sum(branch * branch), jnp.sum(following * following)])
            out = restore((2.0 * all_rows(0.5 * following)).astype(jnp.bfloat16))
        gate_grad, gate_through, skip_grad = side
        normed_part, smalls[l], lows, starts[l], prefixes[l] = back_rest(
            layer, kept[l], grads, scan_out, gate_through)
        smalls[l] = jnp.concatenate([smalls[l], skip_grad[None]], axis=0)
        thick = thick_grads(kept[l], normed, lows)
        inner = smalls[l].shape[-1]
        if l == last:
            thins = thick[1:] + thins
            normed_grad, thick, smalls[l] = joint_sums(normed_part, [rows(thick[0])], smalls[l], l)
            scattered[l].append(thick[0])
        else:
            thins = thick[1:] + thins
            cuts = [part.shape[1] for part in thins]
            extra = jnp.concatenate([jnp.stack(squares).reshape(-1), input_square.reshape(1)])
            extra = jnp.pad(extra, (0, inner - extra.shape[0]))[None]
            shared = rows_sum(jnp.concatenate(
                [extra] + [gain.reshape(-1, inner) for gain in gains[1:]], axis=0))
            own_count = smalls[l].shape[0]
            small = jnp.concatenate([smalls[l], shared], axis=0)
            small = jnp.pad(small, ((0, -small.shape[0] % 8), (0, 0)))
            normed_part, thins, out = lax.optimization_barrier((normed_part, thins, out))
            normed_grad, thick, small = joint_sums(
                normed_part, [rows(thick[0]), rows(jnp.concatenate(thins, axis=1))], small, l)
            scattered[l].append(thick[0])
            smalls[l], rest = small[:own_count], small[own_count:]
        gains[l], change = norm_back(layer, normed_grad, base, inverse_rms(base))
        grad = grad + all_rows(change)
        grad_low = grad.astype(jnp.bfloat16)
    first_gain = blk_sum(rows_sum(gains[0].reshape(-1, inner)))
    input_grad = restore(grad_low)

    small = jnp.stack(smalls)
    gain_rows = first_gain.shape[0] * layer_total
    gain_grad = jnp.concatenate([first_gain, rest[1:1 + gain_rows - first_gain.shape[0]]], axis=0)
    gain_grad = gain_grad.reshape(layer_total, width)
    taps = weights[2].shape[1]
    row_total = tokens.shape[0] * tokens.shape[1] * width * blocks
    squares = rest[0] / row_total
    rms_stats = jnp.sqrt(squares[:2 * layer_total]).reshape(layer_total, 2)
    input_rms = jnp.sqrt(squares[2 * layer_total:2 * layer_total + 1])
    pieces, at = [], 0
    for cut in cuts:
        pieces.append(thick[1][at:at + cut])
        at += cut
    into_out = jnp.stack([jnp.stack([part[2], part[1]], axis=1) for part in scattered])

    def stacked(parts_):
        return jnp.stack([jnp.moveaxis(part, 0, 1) for part in parts_])[:, :, None]

    return (
        out,
        stacked(finals),
        stacked(tails),
        input_grad,
        stacked(starts),
        stacked(prefixes),
        gain_grad,
        into_out,
        small[:, :taps],
        small[:, taps],
        jnp.stack([part[:weights[4].shape[-1] // blocks].T for part in pieces[0::2]]),
        jnp.stack([part[:RANK // blocks] for part in pieces[1::2]]),
        small[:, taps + 1],
        small[:, taps + 2:-1],
        small[:, -1],
        jnp.stack([part[0].T for part in scattered]),
        rms_stats,
        input_rms,
    )


def solution(mesh):
    placed = (
        P(None, "blk", None),
        P(None, "blk", None),
        P(),
        P(None, None, None, "tensor"),
        P(None, None, "tensor"),
        P(None, "tensor"),
        P(None, "tensor", None),
        P(None, None, "tensor"),
        P(None, "tensor"),
        P(None, None, "tensor"),
        P(None, "tensor"),
        P(None, "tensor", None),
        P(None, None, None, "tensor"),
        P(None, None, None, "tensor"),
    )
    return jax.shard_map(
        on_device,
        mesh=mesh,
        in_specs=placed,
        out_specs=(
            P(None, "blk", None),
            P(None, None, "blk", None, "tensor"),
            P(None, None, "blk", None, "tensor"),
            P(None, "blk", None),
            P(None, None, "blk", None, "tensor"),
            P(None, None, "blk", None, "tensor"),
            P(),
            P(None, "blk", None, "tensor"),
            P(None, None, "tensor"),
            P(None, "tensor"),
            P(None, "tensor", "blk"),
            P(None, "blk", "tensor"),
            P(None, "tensor"),
            P(None, None, "tensor"),
            P(None, "tensor"),
            P(None, "tensor", "blk"),
            P(),
            P(),
        ),
        check_vma=False,
    )
```

```python
import math
from functools import partial
import jax
import jax.numpy as jnp
from jax import lax
from jax.experimental import pallas as pl
from jax.experimental.pallas import tpu as pltpu

from jax.sharding import PartitionSpec as P

STATE = 16
RANK = 128
EPSILON = 1e-05
LANES=128
LOG2E=math.log2(math.e)

def cost(step, passes):
    return pl.CostEstimate(flops=passes * STATE * step.size, bytes_accessed=passes * STATE * step.size, transcendentals=0)

def cp(limit):
    return pltpu.CompilerParams(dimension_semantics=("arbitrary",), vmem_limit_bytes=limit)

def spread(ref_value, out, first):
    for t in range(out.shape[0]):
        row = ref_value[t]
        for n in range(STATE):
            out[t, n] = jnp.broadcast_to(row[:, first + n:first + n + 1], out.shape[2:])

def rates(rate_ref, lanes, n):
    return jnp.broadcast_to(rate_ref[pl.ds(n, 1), lanes], (8, LANES))

def end_body(blocks, width, step_ref, push_ref, coef_ref, rate_ref, end_ref, write):
    @pl.when(pl.program_id(0) == 0)
    def _():
        end_ref[...] = jnp.zeros_like(end_ref)
    spread(coef_ref, write, 0)
    def group(g, _):
        cols = [pl.ds(pl.multiple_of((g * width + k) * LANES, LANES), LANES) for k in range(width)]
        for low in range(0, STATE, STATE // width):
            span = range(low, low + STATE // width)
            state = {(k, n): end_ref[n, :, cols[k]] for k in range(width) for n in span}
            rate = {(k, n): rates(rate_ref, cols[k], n) for k in range(width) for n in span}
            for t in range(step_ref.shape[0]):
                step = [step_ref[t, :, c] for c in cols]
                push = [push_ref[t, :, c] for c in cols]
                for n in span:
                    w = write[t, n]
                    for k in range(width):
                        state[k, n] = jnp.exp2(step[k] * rate[k, n]) * state[k, n] + push[k] * w
            for k in range(width):
                for n in span:
                    end_ref[n, :, cols[k]] = state[k, n]
        return 0
    lax.fori_loop(0, blocks // width, group, 0)

def end_states(step, push, coef, rate, tb=8, width=2, limit=40*2**20):
    T, _, C = step.shape
    return pl.pallas_call(
        partial(end_body, C // LANES, width),
        grid=(T // tb,),
        in_specs=[pl.BlockSpec((tb, 8, C), lambda i: (i, 0, 0)), pl.BlockSpec((tb, 8, C), lambda i: (i, 0, 0)),
                  pl.BlockSpec((tb, 8, 2 * STATE), lambda i: (i, 0, 0)), pl.BlockSpec((STATE, C), lambda i: (0, 0))],
        out_specs=pl.BlockSpec((STATE, 8, C), lambda i: (0, 0, 0)),
        out_shape=jax.ShapeDtypeStruct((STATE, 8, C), jnp.float32),
        scratch_shapes=[pltpu.VMEM((tb, STATE, 8, LANES), jnp.float32)],
        compiler_params=cp(limit), cost_estimate=cost(step, 4), name="end_states")(step, push, coef, rate)

def scan_body(blocks, width, step_ref, push_ref, coef_ref, rate_ref, start_ref, out_ref, states_ref, final_ref, write, read):
    @pl.when(pl.program_id(0) == 0)
    def _():
        final_ref[...] = start_ref[...]
    spread(coef_ref, write, 0)
    spread(coef_ref, read, STATE)
    def group(g, _):
        cols = [pl.ds(pl.multiple_of((g * width + k) * LANES, LANES), LANES) for k in range(width)]
        for low in range(0, STATE, STATE // width):
            span = range(low, low + STATE // width)
            state = {(k, n): final_ref[n, :, cols[k]] for k in range(width) for n in span}
            rate = {(k, n): rates(rate_ref, cols[k], n) for k in range(width) for n in span}
            for t in range(step_ref.shape[0]):
                step = [step_ref[t, :, c] for c in cols]
                push = [push_ref[t, :, c] for c in cols]
                total = [None] * width
                for n in span:
                    w, r = write[t, n], read[t, n]
                    for k in range(width):
                        s = jnp.exp2(step[k] * rate[k, n]) * state[k, n] + push[k] * w
                        state[k, n] = s
                        states_ref[t, n, :, cols[k]] = s
                        total[k] = r * s if total[k] is None else total[k] + r * s
                for k in range(width):
                    if low == 0:
                        out_ref[t, :, cols[k]] = total[k]
                    else:
                        out_ref[t, :, cols[k]] += total[k]
            for k in range(width):
                for n in span:
                    final_ref[n, :, cols[k]] = state[k, n]
        return 0
    lax.fori_loop(0, blocks // width, group, 0)

def scan_forward(step, push, coef, rate, start, tb=8, width=2, limit=48*2**20):
    T, _, C = step.shape
    row = pl.BlockSpec((tb, 8, C), lambda i: (i, 0, 0))
    whole = pl.BlockSpec((STATE, 8, C), lambda i: (0, 0, 0))
    f32 = jnp.float32
    return pl.pallas_call(
        partial(scan_body, C // LANES, width),
        grid=(T // tb,),
        in_specs=[row, row, pl.BlockSpec((tb, 8, 2 * STATE), lambda i: (i, 0, 0)), pl.BlockSpec((STATE, C), lambda i: (0, 0)), whole],
        out_specs=[row, pl.BlockSpec((tb, STATE, 8, C), lambda i: (i, 0, 0, 0)), whole],
        out_shape=[jax.ShapeDtypeStruct((T, 8, C), f32), jax.ShapeDtypeStruct((T, STATE, 8, C), f32),
                   jax.ShapeDtypeStruct((STATE, 8, C), f32)],
        scratch_shapes=[pltpu.VMEM((tb, STATE, 8, LANES), f32)] * 2,
        compiler_params=cp(limit), cost_estimate=cost(step, 7), name="scan_forward")(step, push, coef, rate, start)

def start_body(blocks, width, step_ref, grad_ref, coef_ref, rate_ref, start_ref, read):
    @pl.when(pl.program_id(0) == 0)
    def _():
        start_ref[...] = jnp.zeros_like(start_ref)
    spread(coef_ref, read, STATE)
    def group(g, _):
        cols = [pl.ds(pl.multiple_of((g * width + k) * LANES, LANES), LANES) for k in range(width)]
        for low in range(0, STATE, STATE // width):
            span = range(low, low + STATE // width)
            state = {(k, n): start_ref[n, :, cols[k]] for k in range(width) for n in span}
            rate = {(k, n): rates(rate_ref, cols[k], n) for k in range(width) for n in span}
            for t in reversed(range(step_ref.shape[0])):
                step = [step_ref[t, :, c] for c in cols]
                grad = [grad_ref[t, :, c] for c in cols]
                for n in span:
                    r = read[t, n]
                    for k in range(width):
                        state[k, n] = jnp.exp2(step[k] * rate[k, n]) * (state[k, n] + r * grad[k])
            for k in range(width):
                for n in span:
                    start_ref[n, :, cols[k]] = state[k, n]
        return 0
    lax.fori_loop(0, blocks // width, group, 0)

def start_grads(step, grad, coef, rate, tb=8, width=2, limit=40*2**20):
    T, _, C = step.shape
    last = T // tb - 1
    row = pl.BlockSpec((tb, 8, C), lambda i: (last - i, 0, 0))
    return pl.pallas_call(
        partial(start_body, C // LANES, width),
        grid=(T // tb,),
        in_specs=[row, row, pl.BlockSpec((tb, 8, 2 * STATE), lambda i: (last - i, 0, 0)), pl.BlockSpec((STATE, C), lambda i: (0, 0))],
        out_specs=pl.BlockSpec((STATE, 8, C), lambda i: (0, 0, 0)),
        out_shape=jax.ShapeDtypeStruct((STATE, 8, C), jnp.float32),
        scratch_shapes=[pltpu.VMEM((tb, STATE, 8, LANES), jnp.float32)],
        compiler_params=cp(limit), cost_estimate=cost(step, 4), name="start_grads")(step, grad, coef, rate)

def back_body(blocks, width, step_ref, push_ref, grad_ref, coef_ref, rate_ref, states_ref, prior_ref, begin_ref, end_ref,
              decay_out, push_out, coef_out, start_ref, speed_ref, write, read, write_sum, read_sum):
    @pl.when(pl.program_id(0) == 0)
    def _():
        start_ref[...] = end_ref[...]
        speed_ref[...] = jnp.zeros_like(speed_ref)
    spread(coef_ref, write, 0)
    spread(coef_ref, read, STATE)
    tb = step_ref.shape[0]
    begins = pl.program_id(0) == pl.num_programs(0) - 1
    def group(g, first):
        cols = [pl.ds(pl.multiple_of((g * width + k) * LANES, LANES), LANES) for k in range(width)]
        for low in range(0, STATE, STATE // width):
            span = range(low, low + STATE // width)
            carry = {(k, n): start_ref[n, :, cols[k]] for k in range(width) for n in span}
            speed = {(k, n): speed_ref[n, :, cols[k]] for k in range(width) for n in span}
            rate = {(k, n): rates(rate_ref, cols[k], n) for k in range(width) for n in span}
            enter = {(k, n): jnp.where(begins, begin_ref[n, :, cols[k]], prior_ref[0, n, :, cols[k]])
                     for k in range(width) for n in span}
            for t in reversed(range(tb)):
                step = [step_ref[t, :, c] for c in cols]
                push = [push_ref[t, :, c] for c in cols]
                grad = [grad_ref[t, :, c] for c in cols]
                decays = [None] * width
                pushes = [None] * width
                for n in span:
                    w, r = write[t, n], read[t, n]
                    wsum, rsum = None, None
                    for k in range(width):
                        before = states_ref[t - 1, n, :, cols[k]] if t else enter[k, n]
                        back = carry[k, n] + r * grad[k]
                        held = jnp.exp2(step[k] * rate[k, n]) * back
                        carry[k, n] = held
                        q = held * before
                        speed[k, n] = speed[k, n] + step[k] * q
                        rq, bw = rate[k, n] * q, back * w
                        decays[k] = rq if decays[k] is None else decays[k] + rq
                        pushes[k] = bw if pushes[k] is None else pushes[k] + bw
                        bp, gs = back * push[k], grad[k] * states_ref[t, n, :, cols[k]]
                        wsum = bp if wsum is None else wsum + bp
                        rsum = gs if rsum is None else rsum + gs
                    if first:
                        write_sum[t, n] = wsum
                        read_sum[t, n] = rsum
                    else:
                        write_sum[t, n] += wsum
                        read_sum[t, n] += rsum
                for k in range(width):
                    if low == 0:
                        decay_out[t, :, cols[k]] = decays[k]
                        push_out[t, :, cols[k]] = pushes[k]
                    else:
                        decay_out[t, :, cols[k]] += decays[k]
                        push_out[t, :, cols[k]] += pushes[k]
            for k in range(width):
                for n in span:
                    start_ref[n, :, cols[k]] = carry[k, n]
                    speed_ref[n, :, cols[k]] = speed[k, n]
        return 0
    write_sum[...] = jnp.zeros_like(write_sum)
    read_sum[...] = jnp.zeros_like(read_sum)
    lax.fori_loop(0, blocks // width, lambda g, _: group(g, False), 0)
    lane = lax.broadcasted_iota(jnp.int32, (8, 2 * STATE), 1)
    for t in range(tb):
        row = jnp.zeros((8, 2 * STATE), jnp.float32)
        for n in range(STATE):
            row = jnp.where(lane == n, jnp.sum(write_sum[t, n], axis=-1, keepdims=True), row)
            row = jnp.where(lane == STATE + n, jnp.sum(read_sum[t, n], axis=-1, keepdims=True), row)
        coef_out[t] = row

def scan_backward(step, push, grad, coef, rate, states, begin, end, tb=8, width=2, limit=48*2**20):
    T, _, C = step.shape
    last = T // tb - 1
    f32 = jnp.float32
    row = pl.BlockSpec((tb, 8, C), lambda i: (last - i, 0, 0))
    thin = pl.BlockSpec((tb, 8, 2 * STATE), lambda i: (last - i, 0, 0))
    whole = pl.BlockSpec((STATE, 8, C), lambda i: (0, 0, 0))
    return pl.pallas_call(
        partial(back_body, C // LANES, width),
        grid=(T // tb,),
        in_specs=[row, row, row, thin, pl.BlockSpec((STATE, C), lambda i: (0, 0)),
                  pl.BlockSpec((tb, STATE, 8, C), lambda i: (last - i, 0, 0, 0)),
                  pl.BlockSpec((1, STATE, 8, C), lambda i: (jnp.maximum((last - i) * tb - 1, 0), 0, 0, 0)), whole, whole],
        out_specs=[row, row, thin, whole, whole],
        out_shape=[jax.ShapeDtypeStruct((T, 8, C), f32)] * 2 + [jax.ShapeDtypeStruct((T, 8, 2 * STATE), f32)]
          + [jax.ShapeDtypeStruct((STATE, 8, C), f32)] * 2,
        scratch_shapes=[pltpu.VMEM((tb, STATE, 8, LANES), f32)] * 4,
        compiler_params=cp(limit), cost_estimate=cost(step, 13), name="scan_backward")(step, push, grad, coef, rate, states, states, begin, end)


HALVES_OF_CHIP = 2


def silu_slope(argument):
    sigmoid_value = jax.nn.sigmoid(argument)
    return sigmoid_value * (1.0 + argument * (1.0 - sigmoid_value))


def half_of(array, index):
    size = array.shape[0] // 2
    return lax.dynamic_slice_in_dim(array, index * size, size, 0)


def ordered(index, mine, other):
    first = jnp.where(index == 0, mine, other)
    second = jnp.where(index == 0, other, mine)
    return jnp.concatenate([first, second], axis=0)


BESIDE = [(0, 1), (1, 0), (2, 3), (3, 2)]
ACROSS = [(0, 2), (2, 0), (1, 3), (3, 1)]


def paired():
    return lax.axis_size("tensor") == 4


def tensor_sum(array):
    if not paired():
        return lax.psum(array, "tensor")
    core = lax.axis_index("tensor") % 2
    half = half_of(array, core) + lax.ppermute(half_of(array, 1 - core), "tensor", BESIDE)
    half = half + lax.ppermute(half, "tensor", ACROSS)
    return ordered(core, half, lax.ppermute(half, "tensor", BESIDE))


def own_rows(array):
    if not paired():
        size = array.shape[0] // lax.axis_size("tensor")
        return lax.dynamic_slice_in_dim(array, lax.axis_index("tensor") * size, size, 0)
    return half_of(array, lax.axis_index("tensor") % 2)


def core_sum(array):
    if not paired():
        return lax.psum_scatter(array, "tensor", scatter_dimension=0, tiled=True)
    core = lax.axis_index("tensor") % 2
    return half_of(array, core) + lax.ppermute(half_of(array, 1 - core), "tensor", BESIDE)


def across(half):
    if not paired():
        return jnp.zeros_like(half)
    return lax.ppermute(half, "tensor", ACROSS)


def all_rows(array):
    if not paired():
        return lax.optimization_barrier(lax.all_gather(array, "tensor", tiled=True))
    other = lax.optimization_barrier(lax.ppermute(array, "tensor", BESIDE))
    return ordered(lax.axis_index("tensor") % 2, array, other)


def rows_sum(array):
    if not paired():
        return lax.psum(array, "tensor")
    return array + lax.ppermute(array, "tensor", BESIDE)


def blk_sum(array):
    if lax.axis_size("blk") != 8:
        return lax.psum(array, "blk")
    for bit in (1, 2, 4):
        array = array + lax.ppermute(array, "blk", [(j, j ^ bit) for j in range(8)])
    return array


def blk_scatter(array):
    return lax.psum_scatter(array, "blk", scatter_dimension=0, tiled=True)


def add_rows(total, other, count):
    slab = 8

    def body(i, _):
        at = pl.ds(pl.multiple_of(i * slab, slab), slab)
        total[at, :] = total[at, :] + other[at, :]
        return 0

    lax.fori_loop(0, count // slab, body, 0)


def remote(src, dst, sends, recvs, at, device):
    return pltpu.make_async_remote_copy(
        src_ref=src, dst_ref=dst, send_sem=sends.at[at], recv_sem=recvs.at[at], device_id=device,
        device_id_type=pl.DeviceIdType.MESH)


def joint_body(plan, chunks, sum_ref, *refs):
    count = 1 + max(job[0] for job in plan)
    thick_refs, small_ref, refs = refs[:count], refs[count], refs[count + 1:]
    half_out, thick_outs, small_out, refs = refs[0], refs[1:1 + count], refs[1 + count], refs[2 + count:]
    own_half, core_half, far_half, small_in, refs = refs[0], refs[1], refs[2], refs[3], refs[4:]
    core_send, core_recv, far_send, far_recv, local_sem, out_sem, small_send, small_recv = refs[:8]
    refs = refs[8:]
    blk, tensor = lax.axis_index("blk"), lax.axis_index("tensor")
    bits = {1: blk % 2, 2: (blk // 2) % 2, 4: blk // 4}
    core = tensor % 2
    beside = (blk, tensor + 1 - 2 * core)
    far = (blk, (tensor + 2) % 4)
    peers = {bit: (blk + bit - 2 * bit * bits[bit], tensor) for bit in bits}
    barrier = pltpu.get_barrier_semaphore()
    for device in (beside, far, peers[1], peers[2], peers[4]):
        pl.semaphore_signal(barrier, inc=1, device_id=device, device_id_type=pl.DeviceIdType.MESH)
    pl.semaphore_wait(barrier, 5)

    rows_each = half_out.shape[0] // chunks
    smalls, core_copies, local_copies, far_copies, outs = [], [], [], [], []

    def small_step(i):
        copy = remote(small_out, small_in.at[i], small_send, small_recv, i, peers[1 << i])
        copy.start()
        smalls.append(copy)

    def small_end(i):
        smalls[i].wait()
        small_out[...] = small_out[...] + small_in[i]

    small_out[...] = small_ref[...]
    small_step(0)
    for k in range(chunks):
        give = pl.ds(pl.multiple_of((1 - core) * rows_each * chunks + k * rows_each, rows_each), rows_each)
        keep = pl.ds(pl.multiple_of(core * rows_each * chunks + k * rows_each, rows_each), rows_each)
        copy = remote(sum_ref.at[give], core_half.at[k], core_send, core_recv, k, beside)
        copy.start()
        core_copies.append(copy)
        copy = pltpu.make_async_copy(sum_ref.at[keep], own_half.at[k], local_sem.at[k])
        copy.start()
        local_copies.append(copy)

    class Job:
        def __init__(self, which, low, wide, order, refs):
            (self.own, self.first, self.second, self.third, self.sems) = refs[0], refs[1], refs[2], refs[3], refs[4:]
            self.order = order
            self.count = thick_refs[which].shape[3]
            self.out = thick_outs[which].at[:, pl.ds(low, wide)]
            lead, (u, v) = bits[order[0]], (bits[order[1]], bits[order[2]])
            self.parts = [(1 - u, 1 - v), (1 - u, v), (u, 1 - v), (u, v)]
            self.firsts, self.owns, self.seconds = [], [], []
            for i, part in enumerate(self.parts):
                at = {order[1]: part[0], order[2]: part[1]}

                def source(mine):
                    index = dict(at)
                    index[order[0]] = mine
                    return thick_refs[which].at[index[4], index[2], index[1], :, pl.ds(low, wide)]

                copy = remote(source(1 - lead), self.first.at[part], self.sems[0], self.sems[1], i, peers[order[0]])
                copy.start()
                self.firsts.append(copy)
                copy = pltpu.make_async_copy(source(lead), self.own.at[part], self.sems[2].at[i])
                copy.start()
                self.owns.append(copy)

        def first_end(self, i):
            self.owns[i].wait()
            self.firsts[i].wait_recv()
            add_rows(self.own.at[self.parts[i]], self.first.at[self.parts[i]], self.count)
            if i < 2:
                copy = remote(self.own.at[self.parts[i]], self.second.at[i], self.sems[3], self.sems[4], i,
                              peers[self.order[1]])
                copy.start()
                self.seconds.append(copy)
                return
            self.seconds[i - 2].wait_recv()
            add_rows(self.own.at[self.parts[i]], self.second.at[i - 2], self.count)
            if i == 2:
                self.last = remote(self.own.at[self.parts[i]], self.third, self.sems[5], self.sems[6], 0,
                                   peers[self.order[2]])
                self.last.start()

        def end(self):
            self.last.wait_recv()
            add_rows(self.own.at[self.parts[3]], self.third, self.count)
            copy = pltpu.make_async_copy(self.own.at[self.parts[3]], self.out, self.sems[7].at[0])
            copy.start()
            outs.append(copy)

        def sent(self):
            return self.firsts + self.seconds + [self.last]

    jobs = [Job(*job, refs[12 * i:12 * i + 12]) for i, job in enumerate(plan)]

    def core_end(k):
        local_copies[k].wait()
        core_copies[k].wait()
        add_rows(own_half.at[k], core_half.at[k], rows_each)
        copy = remote(own_half.at[k], far_half.at[k], far_send, far_recv, k, far)
        copy.start()
        far_copies.append(copy)

    def far_end(k):
        far_copies[k].wait_recv()
        add_rows(far_half.at[k], own_half.at[k], rows_each)
        copy = pltpu.make_async_copy(
            far_half.at[k], half_out.at[pl.ds(k * rows_each, rows_each)], out_sem.at[k])
        copy.start()
        outs.append(copy)

    for k in range(chunks):
        core_end(k)
    small_end(0)
    small_step(1)
    for i in range(4):
        for job in jobs:
            job.first_end(i)
        if i in (0, 1):
            small_end(i + 1)
            if i == 0:
                small_step(2)
        far_end(i)
    for job in jobs:
        job.end()
    for copy in far_copies + [each for job in jobs for each in job.sent()]:
        copy.wait_send()
    for copy in outs:
        copy.wait()


def joint_sums(array, thick, late, small, collective_id):
    if not paired() or lax.axis_size("blk") != 8:
        return (lax.psum_scatter(array, "tensor", scatter_dimension=0, tiled=True),
                [blk_scatter(part) for part in thick], lax.psum(small, "blk"))
    R, N = array.shape
    C = thick[0].shape[1]
    chunks = 4
    f32 = jnp.float32
    dma = pltpu.SemaphoreType.DMA
    any_spec = pl.BlockSpec(memory_space=pl.ANY)
    vmem_spec = pl.BlockSpec(memory_space=pltpu.VMEM)
    plan = [(i, 0, C - each, (1, 2, 4)) for i, each in enumerate(late) if each < C]
    plan += [(i, C - each, each, (2, 4, 1)) for i, each in enumerate(late) if each]
    scratch = []
    for which, _, wide, _ in plan:
        count = thick[which].shape[0] // 8
        scratch += [pltpu.VMEM((2, 2, count, wide), f32), pltpu.VMEM((2, 2, count, wide), f32),
                    pltpu.VMEM((2, count, wide), f32), pltpu.VMEM((count, wide), f32),
                    dma((4,)), dma((4,)), dma((4,)), dma((2,)), dma((2,)), dma((1,)), dma((1,)), dma((1,))]
    half = pltpu.VMEM((chunks, R // 2 // chunks, N), f32)
    out = pl.pallas_call(
        partial(joint_body, plan, chunks),
        in_specs=[any_spec] * (1 + len(thick)) + [vmem_spec],
        out_specs=[any_spec] * (1 + len(thick)) + [vmem_spec],
        out_shape=[jax.ShapeDtypeStruct((R // 2, N), f32)]
        + [jax.ShapeDtypeStruct((part.shape[0] // 8, C), f32) for part in thick]
        + [jax.ShapeDtypeStruct(small.shape, f32)],
        scratch_shapes=[half, half, half, pltpu.VMEM((3,) + small.shape, f32)]
        + [dma((chunks,))] * 5 + [dma((chunks,)), dma((3,)), dma((3,))] + scratch,
        compiler_params=pltpu.CompilerParams(
            collective_id=collective_id, has_side_effects=True, vmem_limit_bytes=52 * 2**20),
        cost_estimate=pl.CostEstimate(flops=0, bytes_accessed=50 * R * N * 4, transcendentals=0),
        name="joint_sums",
    )(array, *[part.reshape(2, 2, 2, part.shape[0] // 8, C) for part in thick], small)
    return out[0], list(out[1:-1]), out[-1]


def neighbour(value, steps):
    count = lax.axis_size("blk")
    first, last = max(0, -steps), min(count, count - steps)
    return lax.ppermute(value, "blk", [(j, j + steps) for j in range(first, last)])


def entering_any(total, local, rate, first, reverse):
    peers, index = lax.axis_size("blk"), lax.axis_index("blk")
    totals, locals_ = lax.all_gather(total, "blk"), lax.all_gather(local, "blk")

    def step(k, state):
        at = peers - 1 - k if reverse else k
        reached = at > index if reverse else at < index
        return jnp.where(reached, jnp.exp2(totals[at][None] * rate) * state + locals_[at], state)

    return lax.fori_loop(0, peers, step, first)


def hop_body(reverses, groups, total_ref, rate_ref, *refs):
    ways = len(reverses)
    locals_, first_ref, refs = refs[:ways], refs[ways], refs[ways + 1:]
    outs, refs = refs[:ways], refs[ways:]
    beside_total, total_send, total_recv, refs = refs[0], refs[1], refs[2], refs[3:]
    blk, tensor = lax.axis_index("blk"), lax.axis_index("tensor")
    y, z = blk % 2, blk // 2
    beside = (blk + 1 - 2 * y, tensor)
    up, down = ((blk + 2) % 8, tensor), ((blk + 6) % 8, tensor)
    barrier = pltpu.get_barrier_semaphore()

    def greet(device):
        pl.semaphore_signal(barrier, inc=1, device_id=device, device_id_type=pl.DeviceIdType.MESH)

    greet(beside)
    pl.when(z < 3)(lambda: greet(up))
    pl.when(z > 0)(lambda: greet(down))
    pl.semaphore_wait(barrier, 3 - z // 3 - (3 - z) // 3)

    total = total_ref[...]
    copy_total = remote(total_ref, beside_total, total_send, total_recv, 0, beside)
    copy_total.start()
    size = STATE // 2 // groups

    class Way:
        def __init__(self, reverse, local, out, refs):
            self.own, self.other, self.came, self.goes, self.gives, self.gets = refs[:6]
            self.sems, self.out, self.reverse = refs[6:], out, reverse
            self.y, self.z = (1 - y, 3 - z) if reverse else (y, z)
            self.following = down if reverse else up
            self.at_a, self.begins = self.y == 0, self.z == 0
            self.firsts = []
            for n in range(STATE):
                value = local[n]
                if not reverse:
                    decay = jnp.exp2(total * rate_ref[pl.ds(n, 1), :])
                    value = value + jnp.where(jnp.logical_and(self.begins, self.at_a), decay * first_ref[n], 0.0)
                self.own[n] = value
            for k in range(groups):
                give = pl.ds((1 - self.y) * (STATE // 2) + k * size, size)
                copy = remote(self.own.at[give], self.other.at[pl.ds(k * size, size)], self.sems[0], self.sems[1], k, beside)
                copy.start()
                self.firsts.append(copy)

        def chain(self, k):
            part = pl.ds(k * size, size)
            return remote(self.goes.at[part], self.came.at[part], self.sems[2], self.sems[3], k, self.following)

        def middle(self, k, total_a, total_b):
            self.firsts[k].wait()
            pl.when(self.z > 0)(lambda: self.chain(k).wait_recv())
            for i in range(k * size, k * size + size):
                n = self.y * (STATE // 2) + i
                rate = rate_ref[pl.ds(n, 1), :]
                mine, got = self.own[n], self.other[i]
                local_a, local_b = jnp.where(self.at_a, mine, got), jnp.where(self.at_a, got, mine)
                enter = jnp.where(self.begins, 0.0, self.came[i])
                after_a = local_a + jnp.exp2(total_a * rate) * enter
                self.goes[i] = local_b + jnp.exp2(total_b * rate) * after_a
                self.gives[i] = jnp.where(self.at_a, after_a, enter)
                self.out[n] = jnp.where(self.at_a, enter, after_a)
            pl.when(self.z < 3)(lambda: self.chain(k).start())
            self.last(k).start()

        def last(self, k):
            part = pl.ds(k * size, size)
            return remote(self.gives.at[part], self.gets.at[part], self.sems[4], self.sems[5], k, beside)

        def all(self):
            other_total = beside_total[...]
            total_a, total_b = jnp.where(self.at_a, total, other_total), jnp.where(self.at_a, other_total, total)
            for k in range(groups):
                self.middle(k, total_a, total_b)

        def end(self, k):
            self.last(k).wait()
            for i in range(k * size, k * size + size):
                self.out[(1 - self.y) * (STATE // 2) + i] = self.gets[i]
            pl.when(self.z < 3)(lambda: self.chain(k).wait_send())

        def begin(self):
            starts = jnp.logical_and(self.begins, self.at_a)
            for n in range(STATE):
                first = 0.0 if self.reverse else first_ref[n]
                self.out[n] = jnp.where(starts, first, self.out[n])

    each = 6 + 6
    jobs = [Way(reverse, locals_[i], outs[i], refs[each * i:each * i + each]) for i, reverse in enumerate(reverses)]
    copy_total.wait()
    if ways == 1:
        jobs[0].all()
    else:

        def in_turn(order):
            for job in order:
                job.all()

        pl.when(z < 2)(lambda: in_turn(jobs))
        pl.when(z >= 2)(lambda: in_turn(jobs[::-1]))
    for k in range(groups):
        for job in jobs:
            job.end(k)
    for job in jobs:
        job.begin()


def hops(total, locals_, rate, first, reverses, collective_id):
    C = total.shape[-1]
    groups = 4
    f32 = jnp.float32
    dma = pltpu.SemaphoreType.DMA
    spec = pl.BlockSpec(memory_space=pltpu.VMEM)
    whole, half = pltpu.VMEM((STATE, 8, C), f32), pltpu.VMEM((STATE // 2, 8, C), f32)
    return pl.pallas_call(
        partial(hop_body, reverses, groups),
        in_specs=[spec] * (3 + len(locals_)),
        out_specs=[spec] * len(locals_),
        out_shape=[jax.ShapeDtypeStruct((STATE, 8, C), f32)] * len(locals_),
        scratch_shapes=[pltpu.VMEM((8, C), f32), dma((1,)), dma((1,))]
        + ([whole] + [half] * 5 + [dma((groups,))] * 6) * len(locals_),
        compiler_params=pltpu.CompilerParams(
            collective_id=collective_id, has_side_effects=True, vmem_limit_bytes=32 * 2**20),
        cost_estimate=pl.CostEstimate(flops=0, bytes_accessed=100 * total.size * 32, transcendentals=0),
        name="hops",
    )(total, rate, *locals_, first)


def rows(array):
    return array.reshape(-1, array.shape[-1])


def by_step(array):
    return array.reshape(-1, 8, array.shape[-1])


def dot32(left, right):
    return jnp.dot(left, right, preferred_element_type=jnp.float32)


def dot_t(left, right):
    return lax.dot_general(left, right, (((0,), (0,)), ((), ())), preferred_element_type=jnp.float32)


def dot_n(left, right):
    return lax.dot_general(left, right, (((1,), (1,)), ((), ())), preferred_element_type=jnp.float32)


def two_parts(array):
    high = lax.optimization_barrier(array.astype(jnp.bfloat16))
    return high, (array - high.astype(jnp.float32)).astype(jnp.bfloat16)


def split_parts(array, parts):
    return array.reshape(array.shape[:-2] + (parts, 8 // parts) + array.shape[-1:])


class Layer:
    def __init__(self, index, args):
        (norm_gain, in_weight, conv_weight, conv_bias, x_weight, dt_weight, dt_bias, decay_log,
         skip_weight, out_weight) = args
        self.gain = norm_gain[index]
        self.raw = in_weight[index] if index == 0 else None
        self.taps = conv_weight[index]
        self.shift = conv_bias[index]
        self.x = x_weight[index]
        self.dt = dt_weight[index]
        self.dt_bias = dt_bias[index]
        self.rate = -jnp.exp(decay_log[index])
        self.rate2 = self.rate * LOG2E
        self.skip = skip_weight[index]
        self.out = out_weight[index]


def inverse_rms(residual):
    return lax.rsqrt(jnp.mean(residual * residual, axis=-1, keepdims=True) + EPSILON)


def front(layer, normed, conv_first, parts, at_first):
    mixed = jnp.einsum("rd,dkc->krc", normed, layer.raw, preferred_element_type=jnp.float32)
    values, gate = mixed[0], mixed[1]
    inner = values.shape[-1]
    count = values.shape[0]
    rim = layer.taps.shape[0] - 1
    tails = split_parts(by_step(values[count - 8 * rim:]), parts)
    arrived = jnp.where(at_first, conv_first, neighbour(tails[:, -1], 1))
    prefix = jnp.concatenate([arrived[:, None], tails[:, :-1]], axis=1).reshape(rim * 8, inner)
    window = jnp.concatenate([prefix, values], axis=0)
    conv_out = layer.shift + sum(layer.taps[k] * window[8 * k:8 * k + count] for k in range(rim + 1))
    inputs = lax.optimization_barrier(jax.nn.silu(conv_out).astype(jnp.bfloat16))
    projected = tensor_sum(dot32(inputs, layer.x))
    dt_low = projected[:, :RANK].astype(jnp.bfloat16)
    coef = by_step(projected[:, RANK:])
    step = jax.nn.softplus(dot32(dt_low, layer.dt) + layer.dt_bias)
    push = step * inputs.astype(jnp.float32)
    local = split_parts(end_states(by_step(step), by_step(push), coef, layer.rate2), parts)
    totals = split_parts(jnp.sum(by_step(step), axis=0), parts)
    return (window, gate, conv_out, inputs, dt_low, coef, step, push, totals), local, tails[:, -1]


def join(local, totals, rate, reverse):
    order = range(local.shape[1])
    order = list(reversed(order)) if reverse else list(order)
    joined, total = local[:, order[0]], totals[order[0]]
    for p in order[1:]:
        joined = local[:, p] + jnp.exp2(totals[p][None] * rate) * joined
        total = total + totals[p]
    return total, joined


def each_part(state, local, totals, rate, reverse):
    order = range(local.shape[1])
    order = list(reversed(order)) if reverse else list(order)
    states = {order[0]: state}
    for p, following in zip(order[:-1], order[1:]):
        states[following] = local[:, p] + jnp.exp2(totals[p][None] * rate) * states[p]
    state = jnp.stack([states[p] for p in range(local.shape[1])], axis=1)
    return state.reshape(STATE, 8, state.shape[-1])


def exchange(layer, locals_, totals, first, reverses, collective_id):
    rate = layer.rate2[:, None]
    if lax.axis_size("blk") == 8 and totals.shape[0] == 1:
        return hops(totals[0], [local[:, 0] for local in locals_], layer.rate2, first, reverses, collective_id)
    states = []
    for local, reverse in zip(locals_, reverses):
        total, joined = join(local, totals, rate, reverse)
        state = entering_any(total, joined, rate, jnp.zeros_like(first) if reverse else first, reverse)
        states.append(each_part(state, local, totals, rate, reverse))
    return states


def scanning(layer, kept, start):
    window, gate, conv_out, inputs, dt_low, coef, step, push, totals = kept
    scanned, states, final = scan_forward(by_step(step), by_step(push), coef, layer.rate2, start)
    result = rows(scanned) + layer.skip * inputs.astype(jnp.float32)
    gated = (result * jax.nn.silu(gate)).astype(jnp.bfloat16)
    return dot32(gated, layer.out), (result, gated, states, start), final


def back_gated(layer, kept, grad_low):
    gate = kept[1]
    grad_gated = dot_n(grad_low, layer.out)
    return grad_gated, grad_gated * jax.nn.silu(gate)


def back_local(layer, kept, grad_result):
    window, gate, conv_out, inputs, dt_low, coef, step, push, totals = kept
    local = start_grads(by_step(step), by_step(grad_result), coef, layer.rate2)
    return split_parts(local, totals.shape[0])


def back_side(layer, kept, normed, scans, grads, grad_low):
    window, gate, conv_out, inputs, dt_low, coef, step, push, totals = kept
    result, gated, states, start = scans
    grad_gated, grad_result = grads
    inner = gate.shape[1]
    grad_gate = (grad_gated * result * silu_slope(gate)).astype(jnp.bfloat16)
    gate_grad = dot_t(normed, grad_gate)
    gate_through = dot_n(grad_gate, layer.into[:, inner:])
    skip_grad = jnp.sum(grad_result * inputs.astype(jnp.float32), axis=0)
    return gate_grad, gate_through, skip_grad


def back_scan(layer, kept, scans, grads, end):
    window, gate, conv_out, inputs, dt_low, coef, step, push, totals = kept
    result, gated, states, start = scans
    grad_gated, grad_result = grads
    return scan_backward(
        by_step(step), by_step(push), by_step(grad_result), coef, layer.rate2, states, start, end)


def back_rest(layer, kept, grads, scan_out, gate_through):
    window, gate, conv_out, inputs, dt_low, coef, step, push, totals = kept
    grad_gated, grad_result = grads
    count, inner = gate.shape
    parts = totals.shape[0]
    rim = layer.taps.shape[0] - 1
    wide = inputs.astype(jnp.float32)
    decays, pushes, coef_grad, start_grad, speed = scan_out
    pushes = rows(pushes)
    step_grad = rows(decays) * (1.0 / LOG2E) + wide * pushes
    before_grad = step_grad * -jnp.expm1(-step)
    bias_grad = jnp.sum(before_grad, axis=0)
    decay_grad = layer.rate * jnp.sum(speed, axis=1)
    before_low = before_grad.astype(jnp.bfloat16)
    projected_grad = tensor_sum(jnp.concatenate([dot_n(before_low, layer.dt), rows(coef_grad)], axis=-1))
    high, low = two_parts(projected_grad)
    through = dot_n(jnp.concatenate([high, low], axis=-1), jnp.concatenate([layer.x, layer.x], axis=-1))
    inputs_grad = grad_result * layer.skip + step * pushes + through
    conv_grad = inputs_grad * silu_slope(conv_out)
    taps_grad = jnp.stack([jnp.sum(conv_grad * window[8 * k:8 * k + count], axis=0) for k in range(rim + 1)])
    shift_grad = jnp.sum(conv_grad, axis=0)
    margin = jnp.zeros((8 * rim, inner), jnp.float32)
    padded = jnp.concatenate([margin, conv_grad, margin], axis=0)
    window_grad = sum(
        layer.taps[k] * padded[8 * (rim - k):8 * (rim - k) + count + 8 * rim] for k in range(rim + 1))
    prefix_grad = split_parts(by_step(window_grad[:8 * rim]), parts)
    arrived = neighbour(prefix_grad[:, 0], -1)
    tail_grad = jnp.concatenate([prefix_grad[:, 1:], arrived[:, None]], axis=1).reshape(8 * rim, inner)
    values_grad = jnp.concatenate([window_grad[8 * rim:count], window_grad[count:] + tail_grad], axis=0)
    values_grad = values_grad.astype(jnp.bfloat16)
    normed_part = dot_n(values_grad, layer.into[:, :inner]) + gate_through
    small = jnp.concatenate([taps_grad, shift_grad[None], bias_grad[None], decay_grad], axis=0)
    return normed_part, small, (values_grad, before_low, high, low), split_parts(start_grad, parts)[:, 0], prefix_grad[:, 0]


def thick_grads(kept, normed, lows):
    inputs, dt_low = kept[3], kept[4]
    values_grad, before_low, high, low = lows
    blocks = lax.axis_size("blk")
    x_grad = dot_t(high, inputs) + dot_t(low, inputs)
    return [eights(part.reshape(blocks, -1, part.shape[-1]))
            for part in (dot_t(normed, values_grad), x_grad, dot_t(dt_low, before_low))]


def eights(array):
    return jnp.pad(array, ((0, 0), (0, -array.shape[1] % 8), (0, 0)))


def norm_back(layer, normed_grad, residual, q):
    gain_grad = jnp.sum(normed_grad * (residual * q), axis=0)
    scaled = normed_grad * layer.gain
    inner_mean = jnp.mean(scaled * residual, axis=-1, keepdims=True)
    return gain_grad, q * scaled - residual * (q * q * q * inner_mean)


def on_device(tokens, cotangent, *args):
    scan_init, conv_init = args[-2:]
    weights = args[:-2]
    blocks, index = lax.axis_size("blk"), lax.axis_index("blk")
    at_first = index == 0
    layer_total = weights[1].shape[0]
    seqs = tokens.shape[0]
    parts = 8 // seqs
    length = tokens.shape[1] // parts
    width = tokens.shape[2]
    layers = [Layer(l, weights) for l in range(layer_total)]
    last = layer_total - 1

    def arrange(array):
        return array.reshape(seqs, parts, length, width).transpose(2, 1, 0, 3).reshape(length * 8, width)

    def restore(array):
        array = array.reshape(length, parts, seqs, width).transpose(2, 1, 0, 3)
        return array.reshape(seqs, parts * length, width)

    residual = arrange(tokens).astype(jnp.float32)
    normed = (residual * inverse_rms(residual) * layers[0].gain).astype(jnp.bfloat16)
    residual = own_rows(residual)
    input_square = jnp.sum(residual * residual)
    grad = arrange(cotangent).astype(jnp.float32)
    grad_low = grad.astype(jnp.bfloat16)

    kept, scans, norms, finals, tails, squares = ([None] * layer_total for _ in range(6))
    starts, prefixes, smalls, gains = ([None] * layer_total for _ in range(4))
    for l, layer in enumerate(layers):
        norms[l] = (normed, residual)
        kept[l], local, tails[l] = front(
            layer, normed, jnp.moveaxis(conv_init[l], 1, 0), parts, at_first)
        totals = kept[l][-1]
        first = jnp.moveaxis(scan_init[l], 1, 0)
        if l == last:
            grads = back_gated(layer, kept[l], grad_low)
            late = back_local(layer, kept[l], grads[1])
            start, end = exchange(layer, [local, late], totals, first, (False, True), layer_total + l)
        else:
            start, = exchange(layer, [local], totals, first, (False,), layer_total + l)
        partial_sum, scans[l], final = scanning(layer, kept[l], start)
        finals[l] = split_parts(final, parts)[:, -1]
        half = core_sum(partial_sum)
        if l < last:
            half, stored = lax.optimization_barrier((half, weights[1]))
            into = [stored[k].reshape(width, -1) for k in range(layer_total)]
            layers[l + 1].raw = stored[l + 1]
            got, into, grad_low = lax.optimization_barrier((across(half), into, grad_low))
            for each, array in zip(layers, into):
                each.into = array
            branch = half + got
            following = residual + branch
            squares[l] = jnp.stack([jnp.sum(branch * branch), jnp.sum(following * following)])
            residual = following
            unscaled = all_rows(residual * inverse_rms(residual))
            normed = (unscaled * layers[l + 1].gain).astype(jnp.bfloat16)

    thins, scattered = [], [None] * layer_total
    for l in reversed(range(layer_total)):
        layer = layers[l]
        normed, base = norms[l]
        if l < last:
            grads, out_grad, scattered[last] = lax.optimization_barrier(
                (back_gated(layer, kept[l], grad_low), dot_t(grad_low, scans[l][1]), scattered[last]))
            scattered[l] = [blk_scatter(out_grad)]
            late = back_local(layer, kept[l], grads[1])
            end, = exchange(layer, [late], kept[l][-1], jnp.zeros_like(late[:, 0]), (True,), 2 + 2 * layer_total + l)
        else:
            out_grad = dot_t(grad_low, scans[l][1])
        side = back_side(layer, kept[l], normed, scans[l], grads, grad_low)
        middle = half.shape[0] // 2
        if l == last:
            end, side, out_grad, half = lax.optimization_barrier((end, side, out_grad, half))
            scattered[l] = [blk_scatter(out_grad)]
            scan_out, got = lax.optimization_barrier(
                (back_scan(layer, kept[l], scans[l], grads, end), across(half[:middle])))
        else:
            end, side, half = lax.optimization_barrier((end, side, half))
            scattered[l].append(blk_scatter(side[0]))
            scan_out, got_rest = lax.optimization_barrier(
                (back_scan(layer, kept[l], scans[l], grads, end), across(half[middle:])))
            branch = half + jnp.concatenate([got, got_rest], axis=0)
            following = residual + branch
            squares[last] = jnp.stack([jnp.sum(branch * branch), jnp.sum(following * following)])
            out = restore((2.0 * all_rows(0.5 * following)).astype(jnp.bfloat16))
        gate_grad, gate_through, skip_grad = side
        normed_part, smalls[l], lows, starts[l], prefixes[l] = back_rest(
            layer, kept[l], grads, scan_out, gate_through)
        smalls[l] = jnp.concatenate([smalls[l], skip_grad[None]], axis=0)
        thick = thick_grads(kept[l], normed, lows)
        inner = smalls[l].shape[-1]
        if l == last:
            thins = thick[1:] + thins
            normed_grad, thick, smalls[l] = joint_sums(
                normed_part, [rows(thick[0]), side[0]], (128, 128), smalls[l], l)
            scattered[l] += [thick[1], thick[0]]
        else:
            thins = thick[1:] + thins
            cuts = [part.shape[1] for part in thins]
            extra = jnp.concatenate([jnp.stack(squares).reshape(-1), input_square.reshape(1)])
            extra = jnp.pad(extra, (0, inner - extra.shape[0]))[None]
            shared = rows_sum(jnp.concatenate(
                [extra] + [gain.reshape(-1, inner) for gain in gains[1:]], axis=0))
            own_count = smalls[l].shape[0]
            small = jnp.concatenate([smalls[l], shared], axis=0)
            small = jnp.pad(small, ((0, -small.shape[0] % 8), (0, 0)))
            normed_part, thins, out = lax.optimization_barrier((normed_part, thins, out))
            normed_grad, thick, small = joint_sums(
                normed_part, [rows(thick[0]), rows(jnp.concatenate(thins, axis=1))], (0, inner), small, l)
            scattered[l].append(thick[0])
            smalls[l], rest = small[:own_count], small[own_count:]
        gains[l], change = norm_back(layer, normed_grad, base, inverse_rms(base))
        grad = grad + all_rows(change)
        grad_low = grad.astype(jnp.bfloat16)
    first_gain = blk_sum(rows_sum(gains[0].reshape(-1, inner)))
    input_grad = restore(grad_low)

    small = jnp.stack(smalls)
    gain_rows = first_gain.shape[0] * layer_total
    gain_grad = jnp.concatenate([first_gain, rest[1:1 + gain_rows - first_gain.shape[0]]], axis=0)
    gain_grad = gain_grad.reshape(layer_total, width)
    taps = weights[2].shape[1]
    row_total = tokens.shape[0] * tokens.shape[1] * width * blocks
    squares = rest[0] / row_total
    rms_stats = jnp.sqrt(squares[:2 * layer_total]).reshape(layer_total, 2)
    input_rms = jnp.sqrt(squares[2 * layer_total:2 * layer_total + 1])
    pieces, at = [], 0
    for cut in cuts:
        pieces.append(thick[1][at:at + cut])
        at += cut
    into_out = jnp.stack([jnp.stack([part[2], part[1]], axis=1) for part in scattered])

    def stacked(parts_):
        return jnp.stack([jnp.moveaxis(part, 0, 1) for part in parts_])[:, :, None]

    return (
        out,
        stacked(finals),
        stacked(tails),
        input_grad,
        stacked(starts),
        stacked(prefixes),
        gain_grad,
        into_out,
        small[:, :taps],
        small[:, taps],
        jnp.stack([part[:weights[4].shape[-1] // blocks].T for part in pieces[0::2]]),
        jnp.stack([part[:RANK // blocks] for part in pieces[1::2]]),
        small[:, taps + 1],
        small[:, taps + 2:-1],
        small[:, -1],
        jnp.stack([part[0].T for part in scattered]),
        rms_stats,
        input_rms,
    )


def solution(mesh):
    placed = (
        P(None, "blk", None),
        P(None, "blk", None),
        P(),
        P(None, None, None, "tensor"),
        P(None, None, "tensor"),
        P(None, "tensor"),
        P(None, "tensor", None),
        P(None, None, "tensor"),
        P(None, "tensor"),
        P(None, None, "tensor"),
        P(None, "tensor"),
        P(None, "tensor", None),
        P(None, None, None, "tensor"),
        P(None, None, None, "tensor"),
    )
    return jax.shard_map(
        on_device,
        mesh=mesh,
        in_specs=placed,
        out_specs=(
            P(None, "blk", None),
            P(None, None, "blk", None, "tensor"),
            P(None, None, "blk", None, "tensor"),
            P(None, "blk", None),
            P(None, None, "blk", None, "tensor"),
            P(None, None, "blk", None, "tensor"),
            P(),
            P(None, "blk", None, "tensor"),
            P(None, None, "tensor"),
            P(None, "tensor"),
            P(None, "tensor", "blk"),
            P(None, "blk", "tensor"),
            P(None, "tensor"),
            P(None, None, "tensor"),
            P(None, "tensor"),
            P(None, "tensor", "blk"),
            P(),
            P(),
        ),
        check_vma=False,
    )
```

```python
import math
from functools import partial
import jax
import jax.numpy as jnp
from jax import lax
from jax.experimental import pallas as pl
from jax.experimental.pallas import tpu as pltpu

from jax.sharding import PartitionSpec as P

STATE = 16
RANK = 128
EPSILON = 1e-05
LANES=128
LOG2E=math.log2(math.e)

def cost(step, passes):
    return pl.CostEstimate(flops=passes * STATE * step.size, bytes_accessed=passes * STATE * step.size, transcendentals=0)

def cp(limit):
    return pltpu.CompilerParams(dimension_semantics=("arbitrary",), vmem_limit_bytes=limit)

def spread(ref_value, out, first):
    for t in range(out.shape[0]):
        row = ref_value[t]
        for n in range(STATE):
            out[t, n] = jnp.broadcast_to(row[:, first + n:first + n + 1], out.shape[2:])

def rates(rate_ref, lanes, n):
    return jnp.broadcast_to(rate_ref[pl.ds(n, 1), lanes], (8, LANES))

def end_body(blocks, width, step_ref, push_ref, coef_ref, rate_ref, end_ref, write):
    @pl.when(pl.program_id(0) == 0)
    def _():
        end_ref[...] = jnp.zeros_like(end_ref)
    spread(coef_ref, write, 0)
    def group(g, _):
        cols = [pl.ds(pl.multiple_of((g * width + k) * LANES, LANES), LANES) for k in range(width)]
        for low in range(0, STATE, STATE // width):
            span = range(low, low + STATE // width)
            state = {(k, n): end_ref[n, :, cols[k]] for k in range(width) for n in span}
            rate = {(k, n): rates(rate_ref, cols[k], n) for k in range(width) for n in span}
            for t in range(step_ref.shape[0]):
                step = [step_ref[t, :, c] for c in cols]
                push = [push_ref[t, :, c] for c in cols]
                for n in span:
                    w = write[t, n]
                    for k in range(width):
                        state[k, n] = jnp.exp2(step[k] * rate[k, n]) * state[k, n] + push[k] * w
            for k in range(width):
                for n in span:
                    end_ref[n, :, cols[k]] = state[k, n]
        return 0
    lax.fori_loop(0, blocks // width, group, 0)

def end_states(step, push, coef, rate, tb=8, width=2, limit=40*2**20):
    T, _, C = step.shape
    return pl.pallas_call(
        partial(end_body, C // LANES, width),
        grid=(T // tb,),
        in_specs=[pl.BlockSpec((tb, 8, C), lambda i: (i, 0, 0)), pl.BlockSpec((tb, 8, C), lambda i: (i, 0, 0)),
                  pl.BlockSpec((tb, 8, 2 * STATE), lambda i: (i, 0, 0)), pl.BlockSpec((STATE, C), lambda i: (0, 0))],
        out_specs=pl.BlockSpec((STATE, 8, C), lambda i: (0, 0, 0)),
        out_shape=jax.ShapeDtypeStruct((STATE, 8, C), jnp.float32),
        scratch_shapes=[pltpu.VMEM((tb, STATE, 8, LANES), jnp.float32)],
        compiler_params=cp(limit), cost_estimate=cost(step, 4), name="end_states")(step, push, coef, rate)

def scan_body(blocks, width, step_ref, push_ref, coef_ref, rate_ref, start_ref, out_ref, states_ref, final_ref, write, read):
    @pl.when(pl.program_id(0) == 0)
    def _():
        final_ref[...] = start_ref[...]
    spread(coef_ref, write, 0)
    spread(coef_ref, read, STATE)
    def group(g, _):
        cols = [pl.ds(pl.multiple_of((g * width + k) * LANES, LANES), LANES) for k in range(width)]
        for low in range(0, STATE, STATE // width):
            span = range(low, low + STATE // width)
            state = {(k, n): final_ref[n, :, cols[k]] for k in range(width) for n in span}
            rate = {(k, n): rates(rate_ref, cols[k], n) for k in range(width) for n in span}
            for t in range(step_ref.shape[0]):
                step = [step_ref[t, :, c] for c in cols]
                push = [push_ref[t, :, c] for c in cols]
                total = [None] * width
                for n in span:
                    w, r = write[t, n], read[t, n]
                    for k in range(width):
                        s = jnp.exp2(step[k] * rate[k, n]) * state[k, n] + push[k] * w
                        state[k, n] = s
                        states_ref[t, n, :, cols[k]] = s
                        total[k] = r * s if total[k] is None else total[k] + r * s
                for k in range(width):
                    if low == 0:
                        out_ref[t, :, cols[k]] = total[k]
                    else:
                        out_ref[t, :, cols[k]] += total[k]
            for k in range(width):
                for n in span:
                    final_ref[n, :, cols[k]] = state[k, n]
        return 0
    lax.fori_loop(0, blocks // width, group, 0)

def scan_forward(step, push, coef, rate, start, tb=8, width=2, limit=48*2**20):
    T, _, C = step.shape
    row = pl.BlockSpec((tb, 8, C), lambda i: (i, 0, 0))
    whole = pl.BlockSpec((STATE, 8, C), lambda i: (0, 0, 0))
    f32 = jnp.float32
    return pl.pallas_call(
        partial(scan_body, C // LANES, width),
        grid=(T // tb,),
        in_specs=[row, row, pl.BlockSpec((tb, 8, 2 * STATE), lambda i: (i, 0, 0)), pl.BlockSpec((STATE, C), lambda i: (0, 0)), whole],
        out_specs=[row, pl.BlockSpec((tb, STATE, 8, C), lambda i: (i, 0, 0, 0)), whole],
        out_shape=[jax.ShapeDtypeStruct((T, 8, C), f32), jax.ShapeDtypeStruct((T, STATE, 8, C), f32),
                   jax.ShapeDtypeStruct((STATE, 8, C), f32)],
        scratch_shapes=[pltpu.VMEM((tb, STATE, 8, LANES), f32)] * 2,
        compiler_params=cp(limit), cost_estimate=cost(step, 7), name="scan_forward")(step, push, coef, rate, start)

def start_body(blocks, width, step_ref, grad_ref, coef_ref, rate_ref, start_ref, read):
    @pl.when(pl.program_id(0) == 0)
    def _():
        start_ref[...] = jnp.zeros_like(start_ref)
    spread(coef_ref, read, STATE)
    def group(g, _):
        cols = [pl.ds(pl.multiple_of((g * width + k) * LANES, LANES), LANES) for k in range(width)]
        for low in range(0, STATE, STATE // width):
            span = range(low, low + STATE // width)
            state = {(k, n): start_ref[n, :, cols[k]] for k in range(width) for n in span}
            rate = {(k, n): rates(rate_ref, cols[k], n) for k in range(width) for n in span}
            for t in reversed(range(step_ref.shape[0])):
                step = [step_ref[t, :, c] for c in cols]
                grad = [grad_ref[t, :, c] for c in cols]
                for n in span:
                    r = read[t, n]
                    for k in range(width):
                        state[k, n] = jnp.exp2(step[k] * rate[k, n]) * (state[k, n] + r * grad[k])
            for k in range(width):
                for n in span:
                    start_ref[n, :, cols[k]] = state[k, n]
        return 0
    lax.fori_loop(0, blocks // width, group, 0)

def start_grads(step, grad, coef, rate, tb=8, width=2, limit=40*2**20):
    T, _, C = step.shape
    last = T // tb - 1
    row = pl.BlockSpec((tb, 8, C), lambda i: (last - i, 0, 0))
    return pl.pallas_call(
        partial(start_body, C // LANES, width),
        grid=(T // tb,),
        in_specs=[row, row, pl.BlockSpec((tb, 8, 2 * STATE), lambda i: (last - i, 0, 0)), pl.BlockSpec((STATE, C), lambda i: (0, 0))],
        out_specs=pl.BlockSpec((STATE, 8, C), lambda i: (0, 0, 0)),
        out_shape=jax.ShapeDtypeStruct((STATE, 8, C), jnp.float32),
        scratch_shapes=[pltpu.VMEM((tb, STATE, 8, LANES), jnp.float32)],
        compiler_params=cp(limit), cost_estimate=cost(step, 4), name="start_grads")(step, grad, coef, rate)

def back_body(blocks, width, step_ref, push_ref, grad_ref, coef_ref, rate_ref, states_ref, prior_ref, begin_ref, end_ref,
              decay_out, push_out, coef_out, start_ref, speed_ref, write, read, write_sum, read_sum):
    @pl.when(pl.program_id(0) == 0)
    def _():
        start_ref[...] = end_ref[...]
        speed_ref[...] = jnp.zeros_like(speed_ref)
    spread(coef_ref, write, 0)
    spread(coef_ref, read, STATE)
    tb = step_ref.shape[0]
    begins = pl.program_id(0) == pl.num_programs(0) - 1
    def group(g, first):
        cols = [pl.ds(pl.multiple_of((g * width + k) * LANES, LANES), LANES) for k in range(width)]
        for low in range(0, STATE, STATE // width):
            span = range(low, low + STATE // width)
            carry = {(k, n): start_ref[n, :, cols[k]] for k in range(width) for n in span}
            speed = {(k, n): speed_ref[n, :, cols[k]] for k in range(width) for n in span}
            rate = {(k, n): rates(rate_ref, cols[k], n) for k in range(width) for n in span}
            enter = {(k, n): jnp.where(begins, begin_ref[n, :, cols[k]], prior_ref[0, n, :, cols[k]])
                     for k in range(width) for n in span}
            for t in reversed(range(tb)):
                step = [step_ref[t, :, c] for c in cols]
                push = [push_ref[t, :, c] for c in cols]
                grad = [grad_ref[t, :, c] for c in cols]
                decays = [None] * width
                pushes = [None] * width
                for n in span:
                    w, r = write[t, n], read[t, n]
                    wsum, rsum = None, None
                    for k in range(width):
                        before = states_ref[t - 1, n, :, cols[k]] if t else enter[k, n]
                        back = carry[k, n] + r * grad[k]
                        held = jnp.exp2(step[k] * rate[k, n]) * back
                        carry[k, n] = held
                        q = held * before
                        speed[k, n] = speed[k, n] + step[k] * q
                        rq, bw = rate[k, n] * q, back * w
                        decays[k] = rq if decays[k] is None else decays[k] + rq
                        pushes[k] = bw if pushes[k] is None else pushes[k] + bw
                        bp, gs = back * push[k], grad[k] * states_ref[t, n, :, cols[k]]
                        wsum = bp if wsum is None else wsum + bp
                        rsum = gs if rsum is None else rsum + gs
                    if first:
                        write_sum[t, n] = wsum
                        read_sum[t, n] = rsum
                    else:
                        write_sum[t, n] += wsum
                        read_sum[t, n] += rsum
                for k in range(width):
                    if low == 0:
                        decay_out[t, :, cols[k]] = decays[k]
                        push_out[t, :, cols[k]] = pushes[k]
                    else:
                        decay_out[t, :, cols[k]] += decays[k]
                        push_out[t, :, cols[k]] += pushes[k]
            for k in range(width):
                for n in span:
                    start_ref[n, :, cols[k]] = carry[k, n]
                    speed_ref[n, :, cols[k]] = speed[k, n]
        return 0
    write_sum[...] = jnp.zeros_like(write_sum)
    read_sum[...] = jnp.zeros_like(read_sum)
    lax.fori_loop(0, blocks // width, lambda g, _: group(g, False), 0)
    lane = lax.broadcasted_iota(jnp.int32, (8, 2 * STATE), 1)
    for t in range(tb):
        row = jnp.zeros((8, 2 * STATE), jnp.float32)
        for n in range(STATE):
            row = jnp.where(lane == n, jnp.sum(write_sum[t, n], axis=-1, keepdims=True), row)
            row = jnp.where(lane == STATE + n, jnp.sum(read_sum[t, n], axis=-1, keepdims=True), row)
        coef_out[t] = row

def scan_backward(step, push, grad, coef, rate, states, begin, end, tb=8, width=2, limit=48*2**20):
    T, _, C = step.shape
    last = T // tb - 1
    f32 = jnp.float32
    row = pl.BlockSpec((tb, 8, C), lambda i: (last - i, 0, 0))
    thin = pl.BlockSpec((tb, 8, 2 * STATE), lambda i: (last - i, 0, 0))
    whole = pl.BlockSpec((STATE, 8, C), lambda i: (0, 0, 0))
    return pl.pallas_call(
        partial(back_body, C // LANES, width),
        grid=(T // tb,),
        in_specs=[row, row, row, thin, pl.BlockSpec((STATE, C), lambda i: (0, 0)),
                  pl.BlockSpec((tb, STATE, 8, C), lambda i: (last - i, 0, 0, 0)),
                  pl.BlockSpec((1, STATE, 8, C), lambda i: (jnp.maximum((last - i) * tb - 1, 0), 0, 0, 0)), whole, whole],
        out_specs=[row, row, thin, whole, whole],
        out_shape=[jax.ShapeDtypeStruct((T, 8, C), f32)] * 2 + [jax.ShapeDtypeStruct((T, 8, 2 * STATE), f32)]
          + [jax.ShapeDtypeStruct((STATE, 8, C), f32)] * 2,
        scratch_shapes=[pltpu.VMEM((tb, STATE, 8, LANES), f32)] * 4,
        compiler_params=cp(limit), cost_estimate=cost(step, 13), name="scan_backward")(step, push, grad, coef, rate, states, states, begin, end)


HALVES_OF_CHIP = 2


def silu_slope(argument):
    sigmoid_value = jax.nn.sigmoid(argument)
    return sigmoid_value * (1.0 + argument * (1.0 - sigmoid_value))


def half_of(array, index):
    size = array.shape[0] // 2
    return lax.dynamic_slice_in_dim(array, index * size, size, 0)


def ordered(index, mine, other):
    first = jnp.where(index == 0, mine, other)
    second = jnp.where(index == 0, other, mine)
    return jnp.concatenate([first, second], axis=0)


BESIDE = [(0, 1), (1, 0), (2, 3), (3, 2)]
ACROSS = [(0, 2), (2, 0), (1, 3), (3, 1)]


def paired():
    return lax.axis_size("tensor") == 4


def tensor_sum(array):
    if not paired():
        return lax.psum(array, "tensor")
    core = lax.axis_index("tensor") % 2
    half = half_of(array, core) + lax.ppermute(half_of(array, 1 - core), "tensor", BESIDE)
    half = half + lax.ppermute(half, "tensor", ACROSS)
    return ordered(core, half, lax.ppermute(half, "tensor", BESIDE))


def own_rows(array):
    if not paired():
        size = array.shape[0] // lax.axis_size("tensor")
        return lax.dynamic_slice_in_dim(array, lax.axis_index("tensor") * size, size, 0)
    return half_of(array, lax.axis_index("tensor") % 2)


def core_sum(array):
    if not paired():
        return lax.psum_scatter(array, "tensor", scatter_dimension=0, tiled=True)
    core = lax.axis_index("tensor") % 2
    return half_of(array, core) + lax.ppermute(half_of(array, 1 - core), "tensor", BESIDE)


def across(half):
    if not paired():
        return jnp.zeros_like(half)
    return lax.ppermute(half, "tensor", ACROSS)


def all_rows(array):
    if not paired():
        return lax.optimization_barrier(lax.all_gather(array, "tensor", tiled=True))
    other = lax.optimization_barrier(lax.ppermute(array, "tensor", BESIDE))
    return ordered(lax.axis_index("tensor") % 2, array, other)


def rows_sum(array):
    if not paired():
        return lax.psum(array, "tensor")
    return array + lax.ppermute(array, "tensor", BESIDE)


def blk_sum(array):
    if lax.axis_size("blk") != 8:
        return lax.psum(array, "blk")
    for bit in (1, 2, 4):
        array = array + lax.ppermute(array, "blk", [(j, j ^ bit) for j in range(8)])
    return array


def blk_scatter(array):
    return lax.psum_scatter(array, "blk", scatter_dimension=0, tiled=True)


def chosen(array, axis, index):
    return lax.dynamic_index_in_dim(array, index, axis, keepdims=False)


class Halving:
    def __init__(self, array, bits=(1, 2, 4)):
        self.got = None
        if lax.axis_size("blk") != 8:
            self.array, self.bits = blk_scatter(array), []
            return
        self.array = array.reshape((2, 2, 2, array.shape[0] // 8, array.shape[1]))
        self.axes, self.bits = [4, 2, 1], list(bits)

    def start(self):
        if self.bits:
            bit = self.bits.pop(0)
            axis = self.axes.index(bit)
            self.axes.remove(bit)
            mine = (lax.axis_index("blk") // bit) % 2
            self.keep = chosen(self.array, axis, mine)
            give = chosen(self.array, axis, 1 - mine)
            self.got = lax.ppermute(give, "blk", [(j, j ^ bit) for j in range(8)])
        return self


def meet(jobs, values, more=True):
    jobs = [job for job in jobs if job.got is not None]
    gots, values = lax.optimization_barrier((tuple(job.got for job in jobs), values))
    for job, got in zip(jobs, gots):
        job.array, job.got = job.keep + got, None
        if more:
            job.start()
    return values


def halvings(array):
    middle = array.shape[1] // 2
    return [Halving(array[:, :middle]).start(), Halving(array[:, middle:], (2, 4, 1)).start()]


def add_rows(total, other, count):
    slab = 8

    def body(i, _):
        at = pl.ds(pl.multiple_of(i * slab, slab), slab)
        total[at, :] = total[at, :] + other[at, :]
        return 0

    lax.fori_loop(0, count // slab, body, 0)


def remote(src, dst, sends, recvs, at, device):
    return pltpu.make_async_remote_copy(
        src_ref=src, dst_ref=dst, send_sem=sends.at[at], recv_sem=recvs.at[at], device_id=device,
        device_id_type=pl.DeviceIdType.MESH)


def joint_body(plan, chunks, sum_ref, *refs):
    count = 1 + max(job[0] for job in plan)
    thick_refs, small_ref, refs = refs[:count], refs[count], refs[count + 1:]
    half_out, thick_outs, small_out, refs = refs[0], refs[1:1 + count], refs[1 + count], refs[2 + count:]
    own_half, core_half, far_half, small_in, refs = refs[0], refs[1], refs[2], refs[3], refs[4:]
    core_send, core_recv, far_send, far_recv, local_sem, out_sem, small_send, small_recv = refs[:8]
    refs = refs[8:]
    blk, tensor = lax.axis_index("blk"), lax.axis_index("tensor")
    bits = {1: blk % 2, 2: (blk // 2) % 2, 4: blk // 4}
    core = tensor % 2
    beside = (blk, tensor + 1 - 2 * core)
    far = (blk, (tensor + 2) % 4)
    peers = {bit: (blk + bit - 2 * bit * bits[bit], tensor) for bit in bits}
    barrier = pltpu.get_barrier_semaphore()
    for device in (beside, far, peers[1], peers[2], peers[4]):
        pl.semaphore_signal(barrier, inc=1, device_id=device, device_id_type=pl.DeviceIdType.MESH)
    pl.semaphore_wait(barrier, 5)

    rows_each = half_out.shape[0] // chunks
    smalls, core_copies, local_copies, far_copies, outs = [], [], [], [], []

    def small_step(i):
        copy = remote(small_out, small_in.at[i], small_send, small_recv, i, peers[1 << i])
        copy.start()
        smalls.append(copy)

    def small_end(i):
        smalls[i].wait()
        small_out[...] = small_out[...] + small_in[i]

    small_out[...] = small_ref[...]
    small_step(0)
    for k in range(chunks):
        give = pl.ds(pl.multiple_of((1 - core) * rows_each * chunks + k * rows_each, rows_each), rows_each)
        keep = pl.ds(pl.multiple_of(core * rows_each * chunks + k * rows_each, rows_each), rows_each)
        copy = remote(sum_ref.at[give], core_half.at[k], core_send, core_recv, k, beside)
        copy.start()
        core_copies.append(copy)
        copy = pltpu.make_async_copy(sum_ref.at[keep], own_half.at[k], local_sem.at[k])
        copy.start()
        local_copies.append(copy)

    class Job:
        def __init__(self, which, low, wide, order, refs):
            (self.own, self.first, self.second, self.third, self.sems) = refs[0], refs[1], refs[2], refs[3], refs[4:]
            self.order = order
            self.count = thick_refs[which].shape[3]
            self.out = thick_outs[which].at[:, pl.ds(low, wide)]
            lead, (u, v) = bits[order[0]], (bits[order[1]], bits[order[2]])
            self.parts = [(1 - u, 1 - v), (1 - u, v), (u, 1 - v), (u, v)]
            self.firsts, self.owns, self.seconds = [], [], []
            for i, part in enumerate(self.parts):
                at = {order[1]: part[0], order[2]: part[1]}

                def source(mine):
                    index = dict(at)
                    index[order[0]] = mine
                    return thick_refs[which].at[index[4], index[2], index[1], :, pl.ds(low, wide)]

                copy = remote(source(1 - lead), self.first.at[part], self.sems[0], self.sems[1], i, peers[order[0]])
                copy.start()
                self.firsts.append(copy)
                copy = pltpu.make_async_copy(source(lead), self.own.at[part], self.sems[2].at[i])
                copy.start()
                self.owns.append(copy)

        def first_end(self, i):
            self.owns[i].wait()
            self.firsts[i].wait_recv()
            add_rows(self.own.at[self.parts[i]], self.first.at[self.parts[i]], self.count)
            if i < 2:
                copy = remote(self.own.at[self.parts[i]], self.second.at[i], self.sems[3], self.sems[4], i,
                              peers[self.order[1]])
                copy.start()
                self.seconds.append(copy)
                return
            self.seconds[i - 2].wait_recv()
            add_rows(self.own.at[self.parts[i]], self.second.at[i - 2], self.count)
            if i == 2:
                self.last = remote(self.own.at[self.parts[i]], self.third, self.sems[5], self.sems[6], 0,
                                   peers[self.order[2]])
                self.last.start()

        def end(self):
            self.last.wait_recv()
            add_rows(self.own.at[self.parts[3]], self.third, self.count)
            copy = pltpu.make_async_copy(self.own.at[self.parts[3]], self.out, self.sems[7].at[0])
            copy.start()
            outs.append(copy)

        def sent(self):
            return self.firsts + self.seconds + [self.last]

    jobs = [Job(*job, refs[12 * i:12 * i + 12]) for i, job in enumerate(plan)]

    def core_end(k):
        local_copies[k].wait()
        core_copies[k].wait()
        add_rows(own_half.at[k], core_half.at[k], rows_each)
        copy = remote(own_half.at[k], far_half.at[k], far_send, far_recv, k, far)
        copy.start()
        far_copies.append(copy)

    def far_end(k):
        far_copies[k].wait_recv()
        add_rows(far_half.at[k], own_half.at[k], rows_each)
        copy = pltpu.make_async_copy(
            far_half.at[k], half_out.at[pl.ds(k * rows_each, rows_each)], out_sem.at[k])
        copy.start()
        outs.append(copy)

    for k in range(chunks):
        core_end(k)
    small_end(0)
    small_step(1)
    for i in range(4):
        for job in jobs:
            job.first_end(i)
        if i in (0, 1):
            small_end(i + 1)
            if i == 0:
                small_step(2)
        far_end(i)
    for job in jobs:
        job.end()
    for copy in far_copies + [each for job in jobs for each in job.sent()]:
        copy.wait_send()
    for copy in outs:
        copy.wait()


def joint_sums(array, thick, late, small, collective_id):
    if not paired() or lax.axis_size("blk") != 8:
        return (lax.psum_scatter(array, "tensor", scatter_dimension=0, tiled=True),
                [blk_scatter(part) for part in thick], lax.psum(small, "blk"))
    R, N = array.shape
    C = thick[0].shape[1]
    chunks = 4
    f32 = jnp.float32
    dma = pltpu.SemaphoreType.DMA
    any_spec = pl.BlockSpec(memory_space=pl.ANY)
    vmem_spec = pl.BlockSpec(memory_space=pltpu.VMEM)
    plan = [(i, 0, C - each, (1, 2, 4)) for i, each in enumerate(late) if each < C]
    plan += [(i, C - each, each, (2, 4, 1)) for i, each in enumerate(late) if each]
    scratch = []
    for which, _, wide, _ in plan:
        count = thick[which].shape[0] // 8
        scratch += [pltpu.VMEM((2, 2, count, wide), f32), pltpu.VMEM((2, 2, count, wide), f32),
                    pltpu.VMEM((2, count, wide), f32), pltpu.VMEM((count, wide), f32),
                    dma((4,)), dma((4,)), dma((4,)), dma((2,)), dma((2,)), dma((1,)), dma((1,)), dma((1,))]
    half = pltpu.VMEM((chunks, R // 2 // chunks, N), f32)
    out = pl.pallas_call(
        partial(joint_body, plan, chunks),
        in_specs=[any_spec] * (1 + len(thick)) + [vmem_spec],
        out_specs=[any_spec] * (1 + len(thick)) + [vmem_spec],
        out_shape=[jax.ShapeDtypeStruct((R // 2, N), f32)]
        + [jax.ShapeDtypeStruct((part.shape[0] // 8, C), f32) for part in thick]
        + [jax.ShapeDtypeStruct(small.shape, f32)],
        scratch_shapes=[half, half, half, pltpu.VMEM((3,) + small.shape, f32)]
        + [dma((chunks,))] * 5 + [dma((chunks,)), dma((3,)), dma((3,))] + scratch,
        compiler_params=pltpu.CompilerParams(
            collective_id=collective_id, has_side_effects=True, vmem_limit_bytes=52 * 2**20),
        cost_estimate=pl.CostEstimate(flops=0, bytes_accessed=50 * R * N * 4, transcendentals=0),
        name="joint_sums",
    )(array, *[part.reshape(2, 2, 2, part.shape[0] // 8, C) for part in thick], small)
    return out[0], list(out[1:-1]), out[-1]


def neighbour(value, steps):
    count = lax.axis_size("blk")
    first, last = max(0, -steps), min(count, count - steps)
    return lax.ppermute(value, "blk", [(j, j + steps) for j in range(first, last)])


def entering_any(total, local, rate, first, reverse):
    peers, index = lax.axis_size("blk"), lax.axis_index("blk")
    totals, locals_ = lax.all_gather(total, "blk"), lax.all_gather(local, "blk")

    def step(k, state):
        at = peers - 1 - k if reverse else k
        reached = at > index if reverse else at < index
        return jnp.where(reached, jnp.exp2(totals[at][None] * rate) * state + locals_[at], state)

    return lax.fori_loop(0, peers, step, first)


def hop_body(reverses, groups, total_ref, rate_ref, *refs):
    ways = len(reverses)
    locals_, first_ref, refs = refs[:ways], refs[ways], refs[ways + 1:]
    outs, refs = refs[:ways], refs[ways:]
    beside_total, total_send, total_recv, refs = refs[0], refs[1], refs[2], refs[3:]
    blk, tensor = lax.axis_index("blk"), lax.axis_index("tensor")
    y, z = blk % 2, blk // 2
    beside = (blk + 1 - 2 * y, tensor)
    up, down = ((blk + 2) % 8, tensor), ((blk + 6) % 8, tensor)
    barrier = pltpu.get_barrier_semaphore()

    def greet(device):
        pl.semaphore_signal(barrier, inc=1, device_id=device, device_id_type=pl.DeviceIdType.MESH)

    greet(beside)
    pl.when(z < 3)(lambda: greet(up))
    pl.when(z > 0)(lambda: greet(down))
    pl.semaphore_wait(barrier, 3 - z // 3 - (3 - z) // 3)

    total = total_ref[...]
    copy_total = remote(total_ref, beside_total, total_send, total_recv, 0, beside)
    copy_total.start()
    size = STATE // 2 // groups

    class Way:
        def __init__(self, reverse, local, out, refs):
            self.own, self.other, self.came, self.goes, self.gives, self.gets = refs[:6]
            self.sems, self.out, self.reverse = refs[6:], out, reverse
            self.y, self.z = (1 - y, 3 - z) if reverse else (y, z)
            self.following = down if reverse else up
            self.at_a, self.begins = self.y == 0, self.z == 0
            self.firsts = []
            for n in range(STATE):
                value = local[n]
                if not reverse:
                    decay = jnp.exp2(total * rate_ref[pl.ds(n, 1), :])
                    value = value + jnp.where(jnp.logical_and(self.begins, self.at_a), decay * first_ref[n], 0.0)
                self.own[n] = value
            for k in range(groups):
                give = pl.ds((1 - self.y) * (STATE // 2) + k * size, size)
                copy = remote(self.own.at[give], self.other.at[pl.ds(k * size, size)], self.sems[0], self.sems[1], k, beside)
                copy.start()
                self.firsts.append(copy)

        def chain(self, k):
            part = pl.ds(k * size, size)
            return remote(self.goes.at[part], self.came.at[part], self.sems[2], self.sems[3], k, self.following)

        def middle(self, k, total_a, total_b):
            self.firsts[k].wait()
            pl.when(self.z > 0)(lambda: self.chain(k).wait_recv())
            for i in range(k * size, k * size + size):
                n = self.y * (STATE // 2) + i
                rate = rate_ref[pl.ds(n, 1), :]
                mine, got = self.own[n], self.other[i]
                local_a, local_b = jnp.where(self.at_a, mine, got), jnp.where(self.at_a, got, mine)
                enter = jnp.where(self.begins, 0.0, self.came[i])
                after_a = local_a + jnp.exp2(total_a * rate) * enter
                self.goes[i] = local_b + jnp.exp2(total_b * rate) * after_a
                self.gives[i] = jnp.where(self.at_a, after_a, enter)
                self.out[n] = jnp.where(self.at_a, enter, after_a)
            pl.when(self.z < 3)(lambda: self.chain(k).start())
            self.last(k).start()

        def last(self, k):
            part = pl.ds(k * size, size)
            return remote(self.gives.at[part], self.gets.at[part], self.sems[4], self.sems[5], k, beside)

        def all(self):
            other_total = beside_total[...]
            total_a, total_b = jnp.where(self.at_a, total, other_total), jnp.where(self.at_a, other_total, total)
            for k in range(groups):
                self.middle(k, total_a, total_b)

        def end(self, k):
            self.last(k).wait()
            for i in range(k * size, k * size + size):
                self.out[(1 - self.y) * (STATE // 2) + i] = self.gets[i]
            pl.when(self.z < 3)(lambda: self.chain(k).wait_send())

        def begin(self):
            starts = jnp.logical_and(self.begins, self.at_a)
            for n in range(STATE):
                first = 0.0 if self.reverse else first_ref[n]
                self.out[n] = jnp.where(starts, first, self.out[n])

    each = 6 + 6
    jobs = [Way(reverse, locals_[i], outs[i], refs[each * i:each * i + each]) for i, reverse in enumerate(reverses)]
    copy_total.wait()
    if ways == 1:
        jobs[0].all()
    else:

        def in_turn(order):
            for job in order:
                job.all()

        pl.when(z < 2)(lambda: in_turn(jobs))
        pl.when(z >= 2)(lambda: in_turn(jobs[::-1]))
    for k in range(groups):
        for job in jobs:
            job.end(k)
    for job in jobs:
        job.begin()


def hops(total, locals_, rate, first, reverses, collective_id):
    C = total.shape[-1]
    groups = 4
    f32 = jnp.float32
    dma = pltpu.SemaphoreType.DMA
    spec = pl.BlockSpec(memory_space=pltpu.VMEM)
    whole, half = pltpu.VMEM((STATE, 8, C), f32), pltpu.VMEM((STATE // 2, 8, C), f32)
    return pl.pallas_call(
        partial(hop_body, reverses, groups),
        in_specs=[spec] * (3 + len(locals_)),
        out_specs=[spec] * len(locals_),
        out_shape=[jax.ShapeDtypeStruct((STATE, 8, C), f32)] * len(locals_),
        scratch_shapes=[pltpu.VMEM((8, C), f32), dma((1,)), dma((1,))]
        + ([whole] + [half] * 5 + [dma((groups,))] * 6) * len(locals_),
        compiler_params=pltpu.CompilerParams(
            collective_id=collective_id, has_side_effects=True, vmem_limit_bytes=32 * 2**20),
        cost_estimate=pl.CostEstimate(flops=0, bytes_accessed=100 * total.size * 32, transcendentals=0),
        name="hops",
    )(total, rate, *locals_, first)


def rows(array):
    return array.reshape(-1, array.shape[-1])


def by_step(array):
    return array.reshape(-1, 8, array.shape[-1])


def dot32(left, right):
    return jnp.dot(left, right, preferred_element_type=jnp.float32)


def dot_t(left, right):
    return lax.dot_general(left, right, (((0,), (0,)), ((), ())), preferred_element_type=jnp.float32)


def dot_n(left, right):
    return lax.dot_general(left, right, (((1,), (1,)), ((), ())), preferred_element_type=jnp.float32)


def two_parts(array):
    high = lax.optimization_barrier(array.astype(jnp.bfloat16))
    return high, (array - high.astype(jnp.float32)).astype(jnp.bfloat16)


def split_parts(array, parts):
    return array.reshape(array.shape[:-2] + (parts, 8 // parts) + array.shape[-1:])


class Layer:
    def __init__(self, index, args):
        (norm_gain, in_weight, conv_weight, conv_bias, x_weight, dt_weight, dt_bias, decay_log,
         skip_weight, out_weight) = args
        self.gain = norm_gain[index]
        self.raw = in_weight[index] if index == 0 else None
        self.taps = conv_weight[index]
        self.shift = conv_bias[index]
        self.x = x_weight[index]
        self.dt = dt_weight[index]
        self.dt_bias = dt_bias[index]
        self.rate = -jnp.exp(decay_log[index])
        self.rate2 = self.rate * LOG2E
        self.skip = skip_weight[index]
        self.out = out_weight[index]


def inverse_rms(residual):
    return lax.rsqrt(jnp.mean(residual * residual, axis=-1, keepdims=True) + EPSILON)


def front(layer, normed, conv_first, parts, at_first):
    mixed = jnp.einsum("rd,dkc->krc", normed, layer.raw, preferred_element_type=jnp.float32)
    values, gate = mixed[0], mixed[1]
    inner = values.shape[-1]
    count = values.shape[0]
    rim = layer.taps.shape[0] - 1
    tails = split_parts(by_step(values[count - 8 * rim:]), parts)
    arrived = jnp.where(at_first, conv_first, neighbour(tails[:, -1], 1))
    prefix = jnp.concatenate([arrived[:, None], tails[:, :-1]], axis=1).reshape(rim * 8, inner)
    window = jnp.concatenate([prefix, values], axis=0)
    conv_out = layer.shift + sum(layer.taps[k] * window[8 * k:8 * k + count] for k in range(rim + 1))
    inputs = lax.optimization_barrier(jax.nn.silu(conv_out).astype(jnp.bfloat16))
    projected = tensor_sum(dot32(inputs, layer.x))
    dt_low = projected[:, :RANK].astype(jnp.bfloat16)
    coef = by_step(projected[:, RANK:])
    step = jax.nn.softplus(dot32(dt_low, layer.dt) + layer.dt_bias)
    push = step * inputs.astype(jnp.float32)
    local = split_parts(end_states(by_step(step), by_step(push), coef, layer.rate2), parts)
    totals = split_parts(jnp.sum(by_step(step), axis=0), parts)
    return (window, gate, conv_out, inputs, dt_low, coef, step, push, totals), local, tails[:, -1]


def join(local, totals, rate, reverse):
    order = range(local.shape[1])
    order = list(reversed(order)) if reverse else list(order)
    joined, total = local[:, order[0]], totals[order[0]]
    for p in order[1:]:
        joined = local[:, p] + jnp.exp2(totals[p][None] * rate) * joined
        total = total + totals[p]
    return total, joined


def each_part(state, local, totals, rate, reverse):
    order = range(local.shape[1])
    order = list(reversed(order)) if reverse else list(order)
    states = {order[0]: state}
    for p, following in zip(order[:-1], order[1:]):
        states[following] = local[:, p] + jnp.exp2(totals[p][None] * rate) * states[p]
    state = jnp.stack([states[p] for p in range(local.shape[1])], axis=1)
    return state.reshape(STATE, 8, state.shape[-1])


def exchange(layer, locals_, totals, first, reverses, collective_id):
    rate = layer.rate2[:, None]
    if lax.axis_size("blk") == 8 and totals.shape[0] == 1:
        return hops(totals[0], [local[:, 0] for local in locals_], layer.rate2, first, reverses, collective_id)
    states = []
    for local, reverse in zip(locals_, reverses):
        total, joined = join(local, totals, rate, reverse)
        state = entering_any(total, joined, rate, jnp.zeros_like(first) if reverse else first, reverse)
        states.append(each_part(state, local, totals, rate, reverse))
    return states


def scanning(layer, kept, start):
    window, gate, conv_out, inputs, dt_low, coef, step, push, totals = kept
    scanned, states, final = scan_forward(by_step(step), by_step(push), coef, layer.rate2, start)
    result = rows(scanned) + layer.skip * inputs.astype(jnp.float32)
    gated = (result * jax.nn.silu(gate)).astype(jnp.bfloat16)
    return dot32(gated, layer.out), (result, gated, states, start), final


def back_gated(layer, kept, grad_low):
    gate = kept[1]
    grad_gated = dot_n(grad_low, layer.out)
    return grad_gated, grad_gated * jax.nn.silu(gate)


def back_local(layer, kept, grad_result):
    window, gate, conv_out, inputs, dt_low, coef, step, push, totals = kept
    local = start_grads(by_step(step), by_step(grad_result), coef, layer.rate2)
    return split_parts(local, totals.shape[0])


def back_side(layer, kept, normed, scans, grads, grad_low):
    window, gate, conv_out, inputs, dt_low, coef, step, push, totals = kept
    result, gated, states, start = scans
    grad_gated, grad_result = grads
    inner = gate.shape[1]
    grad_gate = (grad_gated * result * silu_slope(gate)).astype(jnp.bfloat16)
    gate_grad = dot_t(normed, grad_gate)
    gate_through = dot_n(grad_gate, layer.into[:, inner:])
    skip_grad = jnp.sum(grad_result * inputs.astype(jnp.float32), axis=0)
    return gate_grad, gate_through, skip_grad


def back_scan(layer, kept, scans, grads, end):
    window, gate, conv_out, inputs, dt_low, coef, step, push, totals = kept
    result, gated, states, start = scans
    grad_gated, grad_result = grads
    return scan_backward(
        by_step(step), by_step(push), by_step(grad_result), coef, layer.rate2, states, start, end)


def back_rest(layer, kept, grads, scan_out, gate_through):
    window, gate, conv_out, inputs, dt_low, coef, step, push, totals = kept
    grad_gated, grad_result = grads
    count, inner = gate.shape
    parts = totals.shape[0]
    rim = layer.taps.shape[0] - 1
    wide = inputs.astype(jnp.float32)
    decays, pushes, coef_grad, start_grad, speed = scan_out
    pushes = rows(pushes)
    step_grad = rows(decays) * (1.0 / LOG2E) + wide * pushes
    before_grad = step_grad * -jnp.expm1(-step)
    bias_grad = jnp.sum(before_grad, axis=0)
    decay_grad = layer.rate * jnp.sum(speed, axis=1)
    before_low = before_grad.astype(jnp.bfloat16)
    projected_grad = tensor_sum(jnp.concatenate([dot_n(before_low, layer.dt), rows(coef_grad)], axis=-1))
    high, low = two_parts(projected_grad)
    through = dot_n(jnp.concatenate([high, low], axis=-1), jnp.concatenate([layer.x, layer.x], axis=-1))
    inputs_grad = grad_result * layer.skip + step * pushes + through
    conv_grad = inputs_grad * silu_slope(conv_out)
    taps_grad = jnp.stack([jnp.sum(conv_grad * window[8 * k:8 * k + count], axis=0) for k in range(rim + 1)])
    shift_grad = jnp.sum(conv_grad, axis=0)
    margin = jnp.zeros((8 * rim, inner), jnp.float32)
    padded = jnp.concatenate([margin, conv_grad, margin], axis=0)
    window_grad = sum(
        layer.taps[k] * padded[8 * (rim - k):8 * (rim - k) + count + 8 * rim] for k in range(rim + 1))
    prefix_grad = split_parts(by_step(window_grad[:8 * rim]), parts)
    arrived = neighbour(prefix_grad[:, 0], -1)
    tail_grad = jnp.concatenate([prefix_grad[:, 1:], arrived[:, None]], axis=1).reshape(8 * rim, inner)
    values_grad = jnp.concatenate([window_grad[8 * rim:count], window_grad[count:] + tail_grad], axis=0)
    values_grad = values_grad.astype(jnp.bfloat16)
    normed_part = dot_n(values_grad, layer.into[:, :inner]) + gate_through
    small = jnp.concatenate([taps_grad, shift_grad[None], bias_grad[None], decay_grad], axis=0)
    return normed_part, small, (values_grad, before_low, high, low), split_parts(start_grad, parts)[:, 0], prefix_grad[:, 0]


def thick_grads(kept, normed, lows):
    inputs, dt_low = kept[3], kept[4]
    values_grad, before_low, high, low = lows
    blocks = lax.axis_size("blk")
    x_grad = dot_t(high, inputs) + dot_t(low, inputs)
    return [eights(part.reshape(blocks, -1, part.shape[-1]))
            for part in (dot_t(normed, values_grad), x_grad, dot_t(dt_low, before_low))]


def eights(array):
    return jnp.pad(array, ((0, 0), (0, -array.shape[1] % 8), (0, 0)))


def norm_back(layer, normed_grad, residual, q):
    gain_grad = jnp.sum(normed_grad * (residual * q), axis=0)
    scaled = normed_grad * layer.gain
    inner_mean = jnp.mean(scaled * residual, axis=-1, keepdims=True)
    return gain_grad, q * scaled - residual * (q * q * q * inner_mean)


def on_device(tokens, cotangent, *args):
    scan_init, conv_init = args[-2:]
    weights = args[:-2]
    blocks, index = lax.axis_size("blk"), lax.axis_index("blk")
    at_first = index == 0
    layer_total = weights[1].shape[0]
    seqs = tokens.shape[0]
    parts = 8 // seqs
    length = tokens.shape[1] // parts
    width = tokens.shape[2]
    layers = [Layer(l, weights) for l in range(layer_total)]
    last = layer_total - 1

    def arrange(array):
        return array.reshape(seqs, parts, length, width).transpose(2, 1, 0, 3).reshape(length * 8, width)

    def restore(array):
        array = array.reshape(length, parts, seqs, width).transpose(2, 1, 0, 3)
        return array.reshape(seqs, parts * length, width)

    residual = arrange(tokens).astype(jnp.float32)
    normed = (residual * inverse_rms(residual) * layers[0].gain).astype(jnp.bfloat16)
    residual = own_rows(residual)
    input_square = jnp.sum(residual * residual)
    grad = arrange(cotangent).astype(jnp.float32)
    grad_low = grad.astype(jnp.bfloat16)

    kept, scans, norms, finals, tails, squares = ([None] * layer_total for _ in range(6))
    starts, prefixes, smalls, gains = ([None] * layer_total for _ in range(4))
    for l, layer in enumerate(layers):
        norms[l] = (normed, residual)
        kept[l], local, tails[l] = front(
            layer, normed, jnp.moveaxis(conv_init[l], 1, 0), parts, at_first)
        totals = kept[l][-1]
        first = jnp.moveaxis(scan_init[l], 1, 0)
        if l == last:
            grads = back_gated(layer, kept[l], grad_low)
            late = back_local(layer, kept[l], grads[1])
            start, end = exchange(layer, [local, late], totals, first, (False, True), layer_total + l)
        else:
            start, = exchange(layer, [local], totals, first, (False,), layer_total + l)
        partial_sum, scans[l], final = scanning(layer, kept[l], start)
        finals[l] = split_parts(final, parts)[:, -1]
        half = core_sum(partial_sum)
        if l < last:
            half, stored = lax.optimization_barrier((half, weights[1]))
            into = [stored[k].reshape(width, -1) for k in range(layer_total)]
            layers[l + 1].raw = stored[l + 1]
            got, into, grad_low = lax.optimization_barrier((across(half), into, grad_low))
            for each, array in zip(layers, into):
                each.into = array
            branch = half + got
            following = residual + branch
            squares[l] = jnp.stack([jnp.sum(branch * branch), jnp.sum(following * following)])
            residual = following
            unscaled = all_rows(residual * inverse_rms(residual))
            normed = (unscaled * layers[l + 1].gain).astype(jnp.bfloat16)

    thins, scattered = [], [None] * layer_total
    for l in reversed(range(layer_total)):
        layer = layers[l]
        normed, base = norms[l]
        if l < last:
            grads = back_gated(layer, kept[l], grad_low)
            out_grad = dot_t(grad_low, scans[l][1])
            late = back_local(layer, kept[l], grads[1])
            end, = exchange(layer, [late], kept[l][-1], jnp.zeros_like(late[:, 0]), (True,), 2 + 2 * layer_total + l)
        else:
            out_grad = dot_t(grad_low, scans[l][1])
        side = back_side(layer, kept[l], normed, scans[l], grads, grad_low)
        middle = half.shape[0] // 2
        if l == last:
            end, side, out_grad, half = lax.optimization_barrier((end, side, out_grad, half))
            jobs = [halvings(out_grad)]
            scattered[l] = [blk_scatter(side[0])]
            scan_out, got = meet(jobs[0], (back_scan(layer, kept[l], scans[l], grads, end), across(half[:middle])))
        else:
            end, side, out_grad, half = lax.optimization_barrier((end, side, out_grad, half))
            jobs.append(halvings(out_grad))
            scattered[l] = [blk_scatter(side[0])]
            scan_out, got_rest = meet(
                jobs[0] + jobs[1], (back_scan(layer, kept[l], scans[l], grads, end), across(half[middle:])))
            branch = half + jnp.concatenate([got, got_rest], axis=0)
            following = residual + branch
            squares[last] = jnp.stack([jnp.sum(branch * branch), jnp.sum(following * following)])
            out = restore((2.0 * all_rows(0.5 * following)).astype(jnp.bfloat16))
        gate_grad, gate_through, skip_grad = side
        normed_part, smalls[l], lows, starts[l], prefixes[l] = back_rest(
            layer, kept[l], grads, scan_out, gate_through)
        smalls[l] = jnp.concatenate([smalls[l], skip_grad[None]], axis=0)
        thick = thick_grads(kept[l], normed, lows)
        inner = smalls[l].shape[-1]
        if l == last:
            thins = thick[1:] + thins
            normed_part, scattered[l] = lax.optimization_barrier((normed_part, scattered[l]))
            normed_grad, thick, smalls[l] = meet(
                jobs[0], joint_sums(normed_part, [rows(thick[0])], (128,), smalls[l], l))
            scattered[l].append(thick[0])
        else:
            thins = thick[1:] + thins
            cuts = [part.shape[1] for part in thins]
            extra = jnp.concatenate([jnp.stack(squares).reshape(-1), input_square.reshape(1)])
            extra = jnp.pad(extra, (0, inner - extra.shape[0]))[None]
            shared = rows_sum(jnp.concatenate(
                [extra] + [gain.reshape(-1, inner) for gain in gains[1:]], axis=0))
            own_count = smalls[l].shape[0]
            small = jnp.concatenate([smalls[l], shared], axis=0)
            small = jnp.pad(small, ((0, -small.shape[0] % 8), (0, 0)))
            normed_part, thins, out = lax.optimization_barrier((normed_part, thins, out))
            normed_grad, thick, small = meet(jobs[1], joint_sums(
                normed_part, [rows(thick[0]), rows(jnp.concatenate(thins, axis=1))], (0, inner), small, l))
            scattered[l].append(thick[0])
            smalls[l], rest = small[:own_count], small[own_count:]
        gains[l], change = norm_back(layer, normed_grad, base, inverse_rms(base))
        grad = grad + all_rows(change)
        grad_low = grad.astype(jnp.bfloat16)
    meet(jobs[1], ())
    out_grads = [jnp.concatenate([job.array.T for job in each], axis=0) for each in reversed(jobs)]
    first_gain = blk_sum(rows_sum(gains[0].reshape(-1, inner)))
    input_grad = restore(grad_low)

    small = jnp.stack(smalls)
    gain_rows = first_gain.shape[0] * layer_total
    gain_grad = jnp.concatenate([first_gain, rest[1:1 + gain_rows - first_gain.shape[0]]], axis=0)
    gain_grad = gain_grad.reshape(layer_total, width)
    taps = weights[2].shape[1]
    row_total = tokens.shape[0] * tokens.shape[1] * width * blocks
    squares = rest[0] / row_total
    rms_stats = jnp.sqrt(squares[:2 * layer_total]).reshape(layer_total, 2)
    input_rms = jnp.sqrt(squares[2 * layer_total:2 * layer_total + 1])
    pieces, at = [], 0
    for cut in cuts:
        pieces.append(thick[1][at:at + cut])
        at += cut
    into_out = jnp.stack([jnp.stack([part[1], part[0]], axis=1) for part in scattered])

    def stacked(parts_):
        return jnp.stack([jnp.moveaxis(part, 0, 1) for part in parts_])[:, :, None]

    return (
        out,
        stacked(finals),
        stacked(tails),
        input_grad,
        stacked(starts),
        stacked(prefixes),
        gain_grad,
        into_out,
        small[:, :taps],
        small[:, taps],
        jnp.stack([part[:weights[4].shape[-1] // blocks].T for part in pieces[0::2]]),
        jnp.stack([part[:RANK // blocks] for part in pieces[1::2]]),
        small[:, taps + 1],
        small[:, taps + 2:-1],
        small[:, -1],
        jnp.stack(out_grads),
        rms_stats,
        input_rms,
    )


def solution(mesh):
    placed = (
        P(None, "blk", None),
        P(None, "blk", None),
        P(),
        P(None, None, None, "tensor"),
        P(None, None, "tensor"),
        P(None, "tensor"),
        P(None, "tensor", None),
        P(None, None, "tensor"),
        P(None, "tensor"),
        P(None, None, "tensor"),
        P(None, "tensor"),
        P(None, "tensor", None),
        P(None, None, None, "tensor"),
        P(None, None, None, "tensor"),
    )
    return jax.shard_map(
        on_device,
        mesh=mesh,
        in_specs=placed,
        out_specs=(
            P(None, "blk", None),
            P(None, None, "blk", None, "tensor"),
            P(None, None, "blk", None, "tensor"),
            P(None, "blk", None),
            P(None, None, "blk", None, "tensor"),
            P(None, None, "blk", None, "tensor"),
            P(),
            P(None, "blk", None, "tensor"),
            P(None, None, "tensor"),
            P(None, "tensor"),
            P(None, "tensor", "blk"),
            P(None, "blk", "tensor"),
            P(None, "tensor"),
            P(None, None, "tensor"),
            P(None, "tensor"),
            P(None, "tensor", "blk"),
            P(),
            P(),
        ),
        check_vma=False,
    )
```

```python
import math
from functools import partial
import jax
import jax.numpy as jnp
from jax import lax
from jax.experimental import pallas as pl
from jax.experimental.pallas import tpu as pltpu

from jax.sharding import PartitionSpec as P

STATE = 16
RANK = 128
EPSILON = 1e-05
LANES=128
LOG2E=math.log2(math.e)

def cost(step, passes):
    return pl.CostEstimate(flops=passes * STATE * step.size, bytes_accessed=passes * STATE * step.size, transcendentals=0)

def cp(limit):
    return pltpu.CompilerParams(dimension_semantics=("arbitrary",), vmem_limit_bytes=limit)

def spread(ref_value, out, first):
    for t in range(out.shape[0]):
        row = ref_value[t]
        for n in range(STATE):
            out[t, n] = jnp.broadcast_to(row[:, first + n:first + n + 1], out.shape[2:])

def rates(rate_ref, lanes, n):
    return jnp.broadcast_to(rate_ref[pl.ds(n, 1), lanes], (8, LANES))

def end_body(blocks, width, step_ref, push_ref, coef_ref, rate_ref, end_ref, write):
    @pl.when(pl.program_id(0) == 0)
    def _():
        end_ref[...] = jnp.zeros_like(end_ref)
    spread(coef_ref, write, 0)
    def group(g, _):
        cols = [pl.ds(pl.multiple_of((g * width + k) * LANES, LANES), LANES) for k in range(width)]
        for low in range(0, STATE, STATE // width):
            span = range(low, low + STATE // width)
            state = {(k, n): end_ref[n, :, cols[k]] for k in range(width) for n in span}
            rate = {(k, n): rates(rate_ref, cols[k], n) for k in range(width) for n in span}
            for t in range(step_ref.shape[0]):
                step = [step_ref[t, :, c] for c in cols]
                push = [push_ref[t, :, c] for c in cols]
                for n in span:
                    w = write[t, n]
                    for k in range(width):
                        state[k, n] = jnp.exp2(step[k] * rate[k, n]) * state[k, n] + push[k] * w
            for k in range(width):
                for n in span:
                    end_ref[n, :, cols[k]] = state[k, n]
        return 0
    lax.fori_loop(0, blocks // width, group, 0)

def end_states(step, push, coef, rate, tb=8, width=2, limit=40*2**20):
    T, _, C = step.shape
    return pl.pallas_call(
        partial(end_body, C // LANES, width),
        grid=(T // tb,),
        in_specs=[pl.BlockSpec((tb, 8, C), lambda i: (i, 0, 0)), pl.BlockSpec((tb, 8, C), lambda i: (i, 0, 0)),
                  pl.BlockSpec((tb, 8, 2 * STATE), lambda i: (i, 0, 0)), pl.BlockSpec((STATE, C), lambda i: (0, 0))],
        out_specs=pl.BlockSpec((STATE, 8, C), lambda i: (0, 0, 0)),
        out_shape=jax.ShapeDtypeStruct((STATE, 8, C), jnp.float32),
        scratch_shapes=[pltpu.VMEM((tb, STATE, 8, LANES), jnp.float32)],
        compiler_params=cp(limit), cost_estimate=cost(step, 4), name="end_states")(step, push, coef, rate)

def scan_body(blocks, width, step_ref, push_ref, coef_ref, rate_ref, start_ref, out_ref, states_ref, final_ref, write, read):
    @pl.when(pl.program_id(0) == 0)
    def _():
        final_ref[...] = start_ref[...]
    spread(coef_ref, write, 0)
    spread(coef_ref, read, STATE)
    def group(g, _):
        cols = [pl.ds(pl.multiple_of((g * width + k) * LANES, LANES), LANES) for k in range(width)]
        for low in range(0, STATE, STATE // width):
            span = range(low, low + STATE // width)
            state = {(k, n): final_ref[n, :, cols[k]] for k in range(width) for n in span}
            rate = {(k, n): rates(rate_ref, cols[k], n) for k in range(width) for n in span}
            for t in range(step_ref.shape[0]):
                step = [step_ref[t, :, c] for c in cols]
                push = [push_ref[t, :, c] for c in cols]
                total = [None] * width
                for n in span:
                    w, r = write[t, n], read[t, n]
                    for k in range(width):
                        s = jnp.exp2(step[k] * rate[k, n]) * state[k, n] + push[k] * w
                        state[k, n] = s
                        states_ref[t, n, :, cols[k]] = s
                        total[k] = r * s if total[k] is None else total[k] + r * s
                for k in range(width):
                    if low == 0:
                        out_ref[t, :, cols[k]] = total[k]
                    else:
                        out_ref[t, :, cols[k]] += total[k]
            for k in range(width):
                for n in span:
                    final_ref[n, :, cols[k]] = state[k, n]
        return 0
    lax.fori_loop(0, blocks // width, group, 0)

def scan_forward(step, push, coef, rate, start, tb=8, width=2, limit=48*2**20):
    T, _, C = step.shape
    row = pl.BlockSpec((tb, 8, C), lambda i: (i, 0, 0))
    whole = pl.BlockSpec((STATE, 8, C), lambda i: (0, 0, 0))
    f32 = jnp.float32
    return pl.pallas_call(
        partial(scan_body, C // LANES, width),
        grid=(T // tb,),
        in_specs=[row, row, pl.BlockSpec((tb, 8, 2 * STATE), lambda i: (i, 0, 0)), pl.BlockSpec((STATE, C), lambda i: (0, 0)), whole],
        out_specs=[row, pl.BlockSpec((tb, STATE, 8, C), lambda i: (i, 0, 0, 0)), whole],
        out_shape=[jax.ShapeDtypeStruct((T, 8, C), f32), jax.ShapeDtypeStruct((T, STATE, 8, C), f32),
                   jax.ShapeDtypeStruct((STATE, 8, C), f32)],
        scratch_shapes=[pltpu.VMEM((tb, STATE, 8, LANES), f32)] * 2,
        compiler_params=cp(limit), cost_estimate=cost(step, 7), name="scan_forward")(step, push, coef, rate, start)

def start_body(blocks, width, step_ref, grad_ref, coef_ref, rate_ref, start_ref, read):
    @pl.when(pl.program_id(0) == 0)
    def _():
        start_ref[...] = jnp.zeros_like(start_ref)
    spread(coef_ref, read, STATE)
    def group(g, _):
        cols = [pl.ds(pl.multiple_of((g * width + k) * LANES, LANES), LANES) for k in range(width)]
        for low in range(0, STATE, STATE // width):
            span = range(low, low + STATE // width)
            state = {(k, n): start_ref[n, :, cols[k]] for k in range(width) for n in span}
            rate = {(k, n): rates(rate_ref, cols[k], n) for k in range(width) for n in span}
            for t in reversed(range(step_ref.shape[0])):
                step = [step_ref[t, :, c] for c in cols]
                grad = [grad_ref[t, :, c] for c in cols]
                for n in span:
                    r = read[t, n]
                    for k in range(width):
                        state[k, n] = jnp.exp2(step[k] * rate[k, n]) * (state[k, n] + r * grad[k])
            for k in range(width):
                for n in span:
                    start_ref[n, :, cols[k]] = state[k, n]
        return 0
    lax.fori_loop(0, blocks // width, group, 0)

def start_grads(step, grad, coef, rate, tb=8, width=2, limit=40*2**20):
    T, _, C = step.shape
    last = T // tb - 1
    row = pl.BlockSpec((tb, 8, C), lambda i: (last - i, 0, 0))
    return pl.pallas_call(
        partial(start_body, C // LANES, width),
        grid=(T // tb,),
        in_specs=[row, row, pl.BlockSpec((tb, 8, 2 * STATE), lambda i: (last - i, 0, 0)), pl.BlockSpec((STATE, C), lambda i: (0, 0))],
        out_specs=pl.BlockSpec((STATE, 8, C), lambda i: (0, 0, 0)),
        out_shape=jax.ShapeDtypeStruct((STATE, 8, C), jnp.float32),
        scratch_shapes=[pltpu.VMEM((tb, STATE, 8, LANES), jnp.float32)],
        compiler_params=cp(limit), cost_estimate=cost(step, 4), name="start_grads")(step, grad, coef, rate)

def back_body(blocks, width, step_ref, push_ref, grad_ref, coef_ref, rate_ref, states_ref, prior_ref, begin_ref, end_ref,
              decay_out, push_out, coef_out, start_ref, speed_ref, write, read, write_sum, read_sum):
    @pl.when(pl.program_id(0) == 0)
    def _():
        start_ref[...] = end_ref[...]
        speed_ref[...] = jnp.zeros_like(speed_ref)
    spread(coef_ref, write, 0)
    spread(coef_ref, read, STATE)
    tb = step_ref.shape[0]
    begins = pl.program_id(0) == pl.num_programs(0) - 1
    def group(g, first):
        cols = [pl.ds(pl.multiple_of((g * width + k) * LANES, LANES), LANES) for k in range(width)]
        for low in range(0, STATE, STATE // width):
            span = range(low, low + STATE // width)
            carry = {(k, n): start_ref[n, :, cols[k]] for k in range(width) for n in span}
            speed = {(k, n): speed_ref[n, :, cols[k]] for k in range(width) for n in span}
            rate = {(k, n): rates(rate_ref, cols[k], n) for k in range(width) for n in span}
            enter = {(k, n): jnp.where(begins, begin_ref[n, :, cols[k]], prior_ref[0, n, :, cols[k]])
                     for k in range(width) for n in span}
            for t in reversed(range(tb)):
                step = [step_ref[t, :, c] for c in cols]
                push = [push_ref[t, :, c] for c in cols]
                grad = [grad_ref[t, :, c] for c in cols]
                decays = [None] * width
                pushes = [None] * width
                for n in span:
                    w, r = write[t, n], read[t, n]
                    wsum, rsum = None, None
                    for k in range(width):
                        before = states_ref[t - 1, n, :, cols[k]] if t else enter[k, n]
                        back = carry[k, n] + r * grad[k]
                        held = jnp.exp2(step[k] * rate[k, n]) * back
                        carry[k, n] = held
                        q = held * before
                        speed[k, n] = speed[k, n] + step[k] * q
                        rq, bw = rate[k, n] * q, back * w
                        decays[k] = rq if decays[k] is None else decays[k] + rq
                        pushes[k] = bw if pushes[k] is None else pushes[k] + bw
                        bp, gs = back * push[k], grad[k] * states_ref[t, n, :, cols[k]]
                        wsum = bp if wsum is None else wsum + bp
                        rsum = gs if rsum is None else rsum + gs
                    if first:
                        write_sum[t, n] = wsum
                        read_sum[t, n] = rsum
                    else:
                        write_sum[t, n] += wsum
                        read_sum[t, n] += rsum
                for k in range(width):
                    if low == 0:
                        decay_out[t, :, cols[k]] = decays[k]
                        push_out[t, :, cols[k]] = pushes[k]
                    else:
                        decay_out[t, :, cols[k]] += decays[k]
                        push_out[t, :, cols[k]] += pushes[k]
            for k in range(width):
                for n in span:
                    start_ref[n, :, cols[k]] = carry[k, n]
                    speed_ref[n, :, cols[k]] = speed[k, n]
        return 0
    write_sum[...] = jnp.zeros_like(write_sum)
    read_sum[...] = jnp.zeros_like(read_sum)
    lax.fori_loop(0, blocks // width, lambda g, _: group(g, False), 0)
    lane = lax.broadcasted_iota(jnp.int32, (8, 2 * STATE), 1)
    for t in range(tb):
        row = jnp.zeros((8, 2 * STATE), jnp.float32)
        for n in range(STATE):
            row = jnp.where(lane == n, jnp.sum(write_sum[t, n], axis=-1, keepdims=True), row)
            row = jnp.where(lane == STATE + n, jnp.sum(read_sum[t, n], axis=-1, keepdims=True), row)
        coef_out[t] = row

def scan_backward(step, push, grad, coef, rate, states, begin, end, tb=8, width=2, limit=48*2**20):
    T, _, C = step.shape
    last = T // tb - 1
    f32 = jnp.float32
    row = pl.BlockSpec((tb, 8, C), lambda i: (last - i, 0, 0))
    thin = pl.BlockSpec((tb, 8, 2 * STATE), lambda i: (last - i, 0, 0))
    whole = pl.BlockSpec((STATE, 8, C), lambda i: (0, 0, 0))
    return pl.pallas_call(
        partial(back_body, C // LANES, width),
        grid=(T // tb,),
        in_specs=[row, row, row, thin, pl.BlockSpec((STATE, C), lambda i: (0, 0)),
                  pl.BlockSpec((tb, STATE, 8, C), lambda i: (last - i, 0, 0, 0)),
                  pl.BlockSpec((1, STATE, 8, C), lambda i: (jnp.maximum((last - i) * tb - 1, 0), 0, 0, 0)), whole, whole],
        out_specs=[row, row, thin, whole, whole],
        out_shape=[jax.ShapeDtypeStruct((T, 8, C), f32)] * 2 + [jax.ShapeDtypeStruct((T, 8, 2 * STATE), f32)]
          + [jax.ShapeDtypeStruct((STATE, 8, C), f32)] * 2,
        scratch_shapes=[pltpu.VMEM((tb, STATE, 8, LANES), f32)] * 4,
        compiler_params=cp(limit), cost_estimate=cost(step, 13), name="scan_backward")(step, push, grad, coef, rate, states, states, begin, end)


HALVES_OF_CHIP = 2


def silu_slope(argument):
    sigmoid_value = jax.nn.sigmoid(argument)
    return sigmoid_value * (1.0 + argument * (1.0 - sigmoid_value))


def half_of(array, index):
    size = array.shape[0] // 2
    return lax.dynamic_slice_in_dim(array, index * size, size, 0)


def ordered(index, mine, other):
    first = jnp.where(index == 0, mine, other)
    second = jnp.where(index == 0, other, mine)
    return jnp.concatenate([first, second], axis=0)


BESIDE = [(0, 1), (1, 0), (2, 3), (3, 2)]
ACROSS = [(0, 2), (2, 0), (1, 3), (3, 1)]


def paired():
    return lax.axis_size("tensor") == 4


def tensor_sum(array):
    if not paired():
        return lax.psum(array, "tensor")
    core = lax.axis_index("tensor") % 2
    half = half_of(array, core) + lax.ppermute(half_of(array, 1 - core), "tensor", BESIDE)
    half = half + lax.ppermute(half, "tensor", ACROSS)
    return ordered(core, half, lax.ppermute(half, "tensor", BESIDE))


def own_rows(array):
    if not paired():
        size = array.shape[0] // lax.axis_size("tensor")
        return lax.dynamic_slice_in_dim(array, lax.axis_index("tensor") * size, size, 0)
    return half_of(array, lax.axis_index("tensor") % 2)


def core_sum(array):
    if not paired():
        return lax.psum_scatter(array, "tensor", scatter_dimension=0, tiled=True)
    core = lax.axis_index("tensor") % 2
    return half_of(array, core) + lax.ppermute(half_of(array, 1 - core), "tensor", BESIDE)


def across(half):
    if not paired():
        return jnp.zeros_like(half)
    return lax.ppermute(half, "tensor", ACROSS)


def all_rows(array):
    if not paired():
        return lax.optimization_barrier(lax.all_gather(array, "tensor", tiled=True))
    other = lax.optimization_barrier(lax.ppermute(array, "tensor", BESIDE))
    return ordered(lax.axis_index("tensor") % 2, array, other)


def rows_sum(array):
    if not paired():
        return lax.psum(array, "tensor")
    return array + lax.ppermute(array, "tensor", BESIDE)


def blk_sum(array):
    if lax.axis_size("blk") != 8:
        return lax.psum(array, "blk")
    for bit in (1, 2, 4):
        array = array + lax.ppermute(array, "blk", [(j, j ^ bit) for j in range(8)])
    return array


def blk_scatter(array):
    return lax.psum_scatter(array, "blk", scatter_dimension=0, tiled=True)


def add_rows(total, other, count):
    slab = 8

    def body(i, _):
        at = pl.ds(pl.multiple_of(i * slab, slab), slab)
        total[at, :] = total[at, :] + other[at, :]
        return 0

    lax.fori_loop(0, count // slab, body, 0)


def remote(src, dst, sends, recvs, at, device):
    return pltpu.make_async_remote_copy(
        src_ref=src, dst_ref=dst, send_sem=sends.at[at], recv_sem=recvs.at[at], device_id=device,
        device_id_type=pl.DeviceIdType.MESH)


def joint_body(plan, chunks, sum_ref, base_ref, gain_ref, *refs):
    count = 1 + max(job[0] for job in plan)
    thick_refs, small_ref, refs = refs[:count], refs[count], refs[count + 1:]
    change_out, gain_out, refs = refs[0], refs[1], refs[2:]
    thick_outs, small_out, refs = refs[:count], refs[count], refs[1 + count:]
    own_half, core_half, far_half, base, came, small_in, refs = refs[0], refs[1], refs[2], refs[3], refs[4], refs[5], refs[6:]
    core_send, core_recv, far_send, far_recv, back_send, back_recv, local_sem, base_sem, out_sem, came_sem = refs[:10]
    small_send, small_recv = refs[10:12]
    refs = refs[12:]
    blk, tensor = lax.axis_index("blk"), lax.axis_index("tensor")
    bits = {1: blk % 2, 2: (blk // 2) % 2, 4: blk // 4}
    core = tensor % 2
    beside = (blk, tensor + 1 - 2 * core)
    far = (blk, (tensor + 2) % 4)
    peers = {bit: (blk + bit - 2 * bit * bits[bit], tensor) for bit in bits}
    barrier = pltpu.get_barrier_semaphore()
    for device in (beside, far, peers[1], peers[2], peers[4]):
        pl.semaphore_signal(barrier, inc=1, device_id=device, device_id_type=pl.DeviceIdType.MESH)
    pl.semaphore_wait(barrier, 5)

    rows_each, width = own_half.shape[1:]
    smalls, core_copies, local_copies, base_copies, far_copies, back_copies, outs = [], [], [], [], [], [], []

    def small_step(i):
        copy = remote(small_out, small_in.at[i], small_send, small_recv, i, peers[1 << i])
        copy.start()
        smalls.append(copy)

    def small_end(i):
        smalls[i].wait()
        small_out[...] = small_out[...] + small_in[i]

    small_out[...] = small_ref[...]
    small_step(0)
    for k in range(chunks):
        give = pl.ds(pl.multiple_of((1 - core) * rows_each * chunks + k * rows_each, rows_each), rows_each)
        keep = pl.ds(pl.multiple_of(core * rows_each * chunks + k * rows_each, rows_each), rows_each)
        copy = remote(sum_ref.at[give], core_half.at[k], core_send, core_recv, k, beside)
        copy.start()
        core_copies.append(copy)
        copy = pltpu.make_async_copy(sum_ref.at[keep], own_half.at[k], local_sem.at[k])
        copy.start()
        local_copies.append(copy)
        copy = pltpu.make_async_copy(base_ref.at[pl.ds(k * rows_each, rows_each)], base.at[k], base_sem.at[k])
        copy.start()
        base_copies.append(copy)
    gain_out[...] = jnp.zeros_like(gain_out)

    class Job:
        def __init__(self, which, low, wide, order, refs):
            (self.own, self.first, self.second, self.third, self.sems) = refs[0], refs[1], refs[2], refs[3], refs[4:]
            self.order = order
            self.count = thick_refs[which].shape[3]
            self.out = thick_outs[which].at[:, pl.ds(low, wide)]
            lead, (u, v) = bits[order[0]], (bits[order[1]], bits[order[2]])
            self.parts = [(1 - u, 1 - v), (1 - u, v), (u, 1 - v), (u, v)]
            self.firsts, self.owns, self.seconds = [], [], []
            for i, part in enumerate(self.parts):
                at = {order[1]: part[0], order[2]: part[1]}

                def source(mine):
                    index = dict(at)
                    index[order[0]] = mine
                    return thick_refs[which].at[index[4], index[2], index[1], :, pl.ds(low, wide)]

                copy = remote(source(1 - lead), self.first.at[part], self.sems[0], self.sems[1], i, peers[order[0]])
                copy.start()
                self.firsts.append(copy)
                copy = pltpu.make_async_copy(source(lead), self.own.at[part], self.sems[2].at[i])
                copy.start()
                self.owns.append(copy)

        def first_end(self, i):
            self.owns[i].wait()
            self.firsts[i].wait_recv()
            add_rows(self.own.at[self.parts[i]], self.first.at[self.parts[i]], self.count)
            if i < 2:
                copy = remote(self.own.at[self.parts[i]], self.second.at[i], self.sems[3], self.sems[4], i,
                              peers[self.order[1]])
                copy.start()
                self.seconds.append(copy)
                return
            self.seconds[i - 2].wait_recv()
            add_rows(self.own.at[self.parts[i]], self.second.at[i - 2], self.count)
            if i == 2:
                self.last = remote(self.own.at[self.parts[i]], self.third, self.sems[5], self.sems[6], 0,
                                   peers[self.order[2]])
                self.last.start()

        def end(self):
            self.last.wait_recv()
            add_rows(self.own.at[self.parts[3]], self.third, self.count)
            copy = pltpu.make_async_copy(self.own.at[self.parts[3]], self.out, self.sems[7].at[0])
            copy.start()
            outs.append(copy)

        def sent(self):
            return self.firsts + self.seconds + [self.last]

    jobs = [Job(*job, refs[12 * i:12 * i + 12]) for i, job in enumerate(plan)]

    def core_end(k):
        local_copies[k].wait()
        core_copies[k].wait()
        add_rows(own_half.at[k], core_half.at[k], rows_each)
        copy = remote(own_half.at[k], far_half.at[k], far_send, far_recv, k, far)
        copy.start()
        far_copies.append(copy)

    def far_end(k):
        far_copies[k].wait_recv()
        base_copies[k].wait()

        def slab(i, _):
            at = pl.ds(pl.multiple_of(i * 8, 8), 8)
            residual = base[k, at, :]
            normed_grad = far_half[k, at, :] + own_half[k, at, :]
            q = lax.rsqrt(jnp.sum(residual * residual, axis=-1, keepdims=True) * (1.0 / width) + EPSILON)
            part = residual * q
            gain_out[...] += normed_grad * part
            scaled = normed_grad * gain_ref[...]
            inner = jnp.sum(scaled * part, axis=-1, keepdims=True) * (1.0 / width)
            far_half[k, at, :] = q * (scaled - part * inner)
            return 0

        lax.fori_loop(0, rows_each // 8, slab, 0)
        copy = remote(far_half.at[k], came.at[k], back_send, back_recv, k, beside)
        copy.start()
        back_copies.append(copy)
        own_rows_at = pl.ds(pl.multiple_of((core * chunks + k) * rows_each, rows_each), rows_each)
        copy = pltpu.make_async_copy(far_half.at[k], change_out.at[own_rows_at], out_sem.at[k])
        copy.start()
        outs.append(copy)

    def back_end(k):
        back_copies[k].wait_recv()
        other_rows_at = pl.ds(pl.multiple_of(((1 - core) * chunks + k) * rows_each, rows_each), rows_each)
        copy = pltpu.make_async_copy(came.at[k], change_out.at[other_rows_at], came_sem.at[k])
        copy.start()
        outs.append(copy)

    for k in range(chunks):
        core_end(k)
    small_end(0)
    small_step(1)
    for i in range(4):
        for job in jobs:
            job.first_end(i)
        if i in (0, 1):
            small_end(i + 1)
            if i == 0:
                small_step(2)
        far_end(i)
    for k in range(chunks):
        back_end(k)
    for job in jobs:
        job.end()
    for copy in far_copies + back_copies + [each for job in jobs for each in job.sent()]:
        copy.wait_send()
    for copy in outs:
        copy.wait()


def joint_sums(array, base, gain, thick, late, small, collective_id):
    if not paired() or lax.axis_size("blk") != 8:
        normed_grad = lax.psum_scatter(array, "tensor", scatter_dimension=0, tiled=True)
        gain_grad, change = norm_back(gain, normed_grad, base, inverse_rms(base))
        return all_rows(change), gain_grad, [blk_scatter(part) for part in thick], lax.psum(small, "blk")
    R, N = array.shape
    C = thick[0].shape[1]
    chunks = 4
    f32 = jnp.float32
    dma = pltpu.SemaphoreType.DMA
    any_spec = pl.BlockSpec(memory_space=pl.ANY)
    vmem_spec = pl.BlockSpec(memory_space=pltpu.VMEM)
    plan = [(i, 0, C - each, (1, 2, 4)) for i, each in enumerate(late) if each < C]
    plan += [(i, C - each, each, (2, 4, 1)) for i, each in enumerate(late) if each]
    scratch = []
    for which, _, wide, _ in plan:
        count = thick[which].shape[0] // 8
        scratch += [pltpu.VMEM((2, 2, count, wide), f32), pltpu.VMEM((2, 2, count, wide), f32),
                    pltpu.VMEM((2, count, wide), f32), pltpu.VMEM((count, wide), f32),
                    dma((4,)), dma((4,)), dma((4,)), dma((2,)), dma((2,)), dma((1,)), dma((1,)), dma((1,))]
    half = pltpu.VMEM((chunks, R // 2 // chunks, N), f32)
    out = pl.pallas_call(
        partial(joint_body, plan, chunks),
        in_specs=[any_spec, any_spec, vmem_spec] + [any_spec] * len(thick) + [vmem_spec],
        out_specs=[any_spec, vmem_spec] + [any_spec] * len(thick) + [vmem_spec],
        out_shape=[jax.ShapeDtypeStruct((R, N), f32), jax.ShapeDtypeStruct((8, N), f32)]
        + [jax.ShapeDtypeStruct((part.shape[0] // 8, C), f32) for part in thick]
        + [jax.ShapeDtypeStruct(small.shape, f32)],
        scratch_shapes=[half] * 5 + [pltpu.VMEM((3,) + small.shape, f32)]
        + [dma((chunks,))] * 10 + [dma((3,)), dma((3,))] + scratch,
        compiler_params=pltpu.CompilerParams(
            collective_id=collective_id, has_side_effects=True, vmem_limit_bytes=52 * 2**20),
        cost_estimate=pl.CostEstimate(flops=0, bytes_accessed=50 * R * N * 4, transcendentals=0),
        name="joint_sums",
    )(array, base, gain[None], *[part.reshape(2, 2, 2, part.shape[0] // 8, C) for part in thick], small)
    return out[0], jnp.sum(out[1], axis=0), list(out[2:-1]), out[-1]


def neighbour(value, steps):
    count = lax.axis_size("blk")
    first, last = max(0, -steps), min(count, count - steps)
    return lax.ppermute(value, "blk", [(j, j + steps) for j in range(first, last)])


def entering_any(total, local, rate, first, reverse):
    peers, index = lax.axis_size("blk"), lax.axis_index("blk")
    totals, locals_ = lax.all_gather(total, "blk"), lax.all_gather(local, "blk")

    def step(k, state):
        at = peers - 1 - k if reverse else k
        reached = at > index if reverse else at < index
        return jnp.where(reached, jnp.exp2(totals[at][None] * rate) * state + locals_[at], state)

    return lax.fori_loop(0, peers, step, first)


def hop_body(reverses, groups, total_ref, rate_ref, *refs):
    ways = len(reverses)
    locals_, first_ref, refs = refs[:ways], refs[ways], refs[ways + 1:]
    outs, refs = refs[:ways], refs[ways:]
    beside_total, total_send, total_recv, refs = refs[0], refs[1], refs[2], refs[3:]
    blk, tensor = lax.axis_index("blk"), lax.axis_index("tensor")
    y, z = blk % 2, blk // 2
    beside = (blk + 1 - 2 * y, tensor)
    up, down = ((blk + 2) % 8, tensor), ((blk + 6) % 8, tensor)
    barrier = pltpu.get_barrier_semaphore()

    def greet(device):
        pl.semaphore_signal(barrier, inc=1, device_id=device, device_id_type=pl.DeviceIdType.MESH)

    greet(beside)
    pl.when(z < 3)(lambda: greet(up))
    pl.when(z > 0)(lambda: greet(down))
    pl.semaphore_wait(barrier, 3 - z // 3 - (3 - z) // 3)

    total = total_ref[...]
    copy_total = remote(total_ref, beside_total, total_send, total_recv, 0, beside)
    copy_total.start()
    size = STATE // 2 // groups

    class Way:
        def __init__(self, reverse, local, out, refs):
            self.own, self.other, self.came, self.goes, self.gives, self.gets = refs[:6]
            self.sems, self.out, self.reverse = refs[6:], out, reverse
            self.y, self.z = (1 - y, 3 - z) if reverse else (y, z)
            self.following = down if reverse else up
            self.at_a, self.begins = self.y == 0, self.z == 0
            self.firsts = []
            for n in range(STATE):
                value = local[n]
                if not reverse:
                    decay = jnp.exp2(total * rate_ref[pl.ds(n, 1), :])
                    value = value + jnp.where(jnp.logical_and(self.begins, self.at_a), decay * first_ref[n], 0.0)
                self.own[n] = value
            for k in range(groups):
                give = pl.ds((1 - self.y) * (STATE // 2) + k * size, size)
                copy = remote(self.own.at[give], self.other.at[pl.ds(k * size, size)], self.sems[0], self.sems[1], k, beside)
                copy.start()
                self.firsts.append(copy)

        def chain(self, k):
            part = pl.ds(k * size, size)
            return remote(self.goes.at[part], self.came.at[part], self.sems[2], self.sems[3], k, self.following)

        def middle(self, k, total_a, total_b):
            self.firsts[k].wait()
            pl.when(self.z > 0)(lambda: self.chain(k).wait_recv())
            for i in range(k * size, k * size + size):
                n = self.y * (STATE // 2) + i
                rate = rate_ref[pl.ds(n, 1), :]
                mine, got = self.own[n], self.other[i]
                local_a, local_b = jnp.where(self.at_a, mine, got), jnp.where(self.at_a, got, mine)
                enter = jnp.where(self.begins, 0.0, self.came[i])
                after_a = local_a + jnp.exp2(total_a * rate) * enter
                self.goes[i] = local_b + jnp.exp2(total_b * rate) * after_a
                self.gives[i] = jnp.where(self.at_a, after_a, enter)
                self.out[n] = jnp.where(self.at_a, enter, after_a)
            pl.when(self.z < 3)(lambda: self.chain(k).start())
            self.last(k).start()

        def last(self, k):
            part = pl.ds(k * size, size)
            return remote(self.gives.at[part], self.gets.at[part], self.sems[4], self.sems[5], k, beside)

        def all(self):
            other_total = beside_total[...]
            total_a, total_b = jnp.where(self.at_a, total, other_total), jnp.where(self.at_a, other_total, total)
            for k in range(groups):
                self.middle(k, total_a, total_b)

        def end(self, k):
            self.last(k).wait()
            for i in range(k * size, k * size + size):
                self.out[(1 - self.y) * (STATE // 2) + i] = self.gets[i]
            pl.when(self.z < 3)(lambda: self.chain(k).wait_send())

        def begin(self):
            starts = jnp.logical_and(self.begins, self.at_a)
            for n in range(STATE):
                first = 0.0 if self.reverse else first_ref[n]
                self.out[n] = jnp.where(starts, first, self.out[n])

    each = 6 + 6
    jobs = [Way(reverse, locals_[i], outs[i], refs[each * i:each * i + each]) for i, reverse in enumerate(reverses)]
    copy_total.wait()
    if ways == 1:
        jobs[0].all()
    else:

        def in_turn(order):
            for job in order:
                job.all()

        pl.when(z < 2)(lambda: in_turn(jobs))
        pl.when(z >= 2)(lambda: in_turn(jobs[::-1]))
    for k in range(groups):
        for job in jobs:
            job.end(k)
    for job in jobs:
        job.begin()


def hops(total, locals_, rate, first, reverses, collective_id):
    C = total.shape[-1]
    groups = 4
    f32 = jnp.float32
    dma = pltpu.SemaphoreType.DMA
    spec = pl.BlockSpec(memory_space=pltpu.VMEM)
    whole, half = pltpu.VMEM((STATE, 8, C), f32), pltpu.VMEM((STATE // 2, 8, C), f32)
    return pl.pallas_call(
        partial(hop_body, reverses, groups),
        in_specs=[spec] * (3 + len(locals_)),
        out_specs=[spec] * len(locals_),
        out_shape=[jax.ShapeDtypeStruct((STATE, 8, C), f32)] * len(locals_),
        scratch_shapes=[pltpu.VMEM((8, C), f32), dma((1,)), dma((1,))]
        + ([whole] + [half] * 5 + [dma((groups,))] * 6) * len(locals_),
        compiler_params=pltpu.CompilerParams(
            collective_id=collective_id, has_side_effects=True, vmem_limit_bytes=32 * 2**20),
        cost_estimate=pl.CostEstimate(flops=0, bytes_accessed=100 * total.size * 32, transcendentals=0),
        name="hops",
    )(total, rate, *locals_, first)


def rows(array):
    return array.reshape(-1, array.shape[-1])


def by_step(array):
    return array.reshape(-1, 8, array.shape[-1])


def dot32(left, right):
    return jnp.dot(left, right, preferred_element_type=jnp.float32)


def dot_t(left, right):
    return lax.dot_general(left, right, (((0,), (0,)), ((), ())), preferred_element_type=jnp.float32)


def dot_n(left, right):
    return lax.dot_general(left, right, (((1,), (1,)), ((), ())), preferred_element_type=jnp.float32)


def two_parts(array):
    high = lax.optimization_barrier(array.astype(jnp.bfloat16))
    return high, (array - high.astype(jnp.float32)).astype(jnp.bfloat16)


def split_parts(array, parts):
    return array.reshape(array.shape[:-2] + (parts, 8 // parts) + array.shape[-1:])


class Layer:
    def __init__(self, index, args):
        (norm_gain, in_weight, conv_weight, conv_bias, x_weight, dt_weight, dt_bias, decay_log,
         skip_weight, out_weight) = args
        self.gain = norm_gain[index]
        self.raw = in_weight[index] if index == 0 else None
        self.taps = conv_weight[index]
        self.shift = conv_bias[index]
        self.x = x_weight[index]
        self.dt = dt_weight[index]
        self.dt_bias = dt_bias[index]
        self.rate = -jnp.exp(decay_log[index])
        self.rate2 = self.rate * LOG2E
        self.skip = skip_weight[index]
        self.out = out_weight[index]


def inverse_rms(residual):
    return lax.rsqrt(jnp.mean(residual * residual, axis=-1, keepdims=True) + EPSILON)


def front(layer, normed, conv_first, parts, at_first):
    mixed = jnp.einsum("rd,dkc->krc", normed, layer.raw, preferred_element_type=jnp.float32)
    values, gate = mixed[0], mixed[1]
    inner = values.shape[-1]
    count = values.shape[0]
    rim = layer.taps.shape[0] - 1
    tails = split_parts(by_step(values[count - 8 * rim:]), parts)
    arrived = jnp.where(at_first, conv_first, neighbour(tails[:, -1], 1))
    prefix = jnp.concatenate([arrived[:, None], tails[:, :-1]], axis=1).reshape(rim * 8, inner)
    window = jnp.concatenate([prefix, values], axis=0)
    conv_out = layer.shift + sum(layer.taps[k] * window[8 * k:8 * k + count] for k in range(rim + 1))
    inputs = lax.optimization_barrier(jax.nn.silu(conv_out).astype(jnp.bfloat16))
    projected = tensor_sum(dot32(inputs, layer.x))
    dt_low = projected[:, :RANK].astype(jnp.bfloat16)
    coef = by_step(projected[:, RANK:])
    step = jax.nn.softplus(dot32(dt_low, layer.dt) + layer.dt_bias)
    push = step * inputs.astype(jnp.float32)
    local = split_parts(end_states(by_step(step), by_step(push), coef, layer.rate2), parts)
    totals = split_parts(jnp.sum(by_step(step), axis=0), parts)
    return (window, gate, conv_out, inputs, dt_low, coef, step, push, totals), local, tails[:, -1]


def join(local, totals, rate, reverse):
    order = range(local.shape[1])
    order = list(reversed(order)) if reverse else list(order)
    joined, total = local[:, order[0]], totals[order[0]]
    for p in order[1:]:
        joined = local[:, p] + jnp.exp2(totals[p][None] * rate) * joined
        total = total + totals[p]
    return total, joined


def each_part(state, local, totals, rate, reverse):
    order = range(local.shape[1])
    order = list(reversed(order)) if reverse else list(order)
    states = {order[0]: state}
    for p, following in zip(order[:-1], order[1:]):
        states[following] = local[:, p] + jnp.exp2(totals[p][None] * rate) * states[p]
    state = jnp.stack([states[p] for p in range(local.shape[1])], axis=1)
    return state.reshape(STATE, 8, state.shape[-1])


def exchange(layer, locals_, totals, first, reverses, collective_id):
    rate = layer.rate2[:, None]
    if lax.axis_size("blk") == 8 and totals.shape[0] == 1:
        return hops(totals[0], [local[:, 0] for local in locals_], layer.rate2, first, reverses, collective_id)
    states = []
    for local, reverse in zip(locals_, reverses):
        total, joined = join(local, totals, rate, reverse)
        state = entering_any(total, joined, rate, jnp.zeros_like(first) if reverse else first, reverse)
        states.append(each_part(state, local, totals, rate, reverse))
    return states


def scanning(layer, kept, start):
    window, gate, conv_out, inputs, dt_low, coef, step, push, totals = kept
    scanned, states, final = scan_forward(by_step(step), by_step(push), coef, layer.rate2, start)
    result = rows(scanned) + layer.skip * inputs.astype(jnp.float32)
    gated = (result * jax.nn.silu(gate)).astype(jnp.bfloat16)
    return dot32(gated, layer.out), (result, gated, states, start), final


def back_gated(kept, grad_gated):
    gate = kept[1]
    return grad_gated, grad_gated * jax.nn.silu(gate)


def back_local(layer, kept, grad_result):
    window, gate, conv_out, inputs, dt_low, coef, step, push, totals = kept
    local = start_grads(by_step(step), by_step(grad_result), coef, layer.rate2)
    return split_parts(local, totals.shape[0])


def back_side(layer, kept, normed, scans, grads, grad_low):
    window, gate, conv_out, inputs, dt_low, coef, step, push, totals = kept
    result, gated, states, start = scans
    grad_gated, grad_result = grads
    inner = gate.shape[1]
    grad_gate = (grad_gated * result * silu_slope(gate)).astype(jnp.bfloat16)
    gate_grad = dot_t(normed, grad_gate)
    gate_through = dot_n(grad_gate, layer.into[:, inner:])
    skip_grad = jnp.sum(grad_result * inputs.astype(jnp.float32), axis=0)
    return gate_grad, gate_through, skip_grad


def back_scan(layer, kept, scans, grads, end):
    window, gate, conv_out, inputs, dt_low, coef, step, push, totals = kept
    result, gated, states, start = scans
    grad_gated, grad_result = grads
    return scan_backward(
        by_step(step), by_step(push), by_step(grad_result), coef, layer.rate2, states, start, end)


def back_rest(layer, kept, grads, scan_out, gate_through):
    window, gate, conv_out, inputs, dt_low, coef, step, push, totals = kept
    grad_gated, grad_result = grads
    count, inner = gate.shape
    parts = totals.shape[0]
    rim = layer.taps.shape[0] - 1
    wide = inputs.astype(jnp.float32)
    decays, pushes, coef_grad, start_grad, speed = scan_out
    pushes = rows(pushes)
    step_grad = rows(decays) * (1.0 / LOG2E) + wide * pushes
    before_grad = step_grad * -jnp.expm1(-step)
    bias_grad = jnp.sum(before_grad, axis=0)
    decay_grad = layer.rate * jnp.sum(speed, axis=1)
    before_low = before_grad.astype(jnp.bfloat16)
    projected_grad = tensor_sum(jnp.concatenate([dot_n(before_low, layer.dt), rows(coef_grad)], axis=-1))
    high, low = two_parts(projected_grad)
    through = dot_n(jnp.concatenate([high, low], axis=-1), jnp.concatenate([layer.x, layer.x], axis=-1))
    inputs_grad = grad_result * layer.skip + step * pushes + through
    conv_grad = inputs_grad * silu_slope(conv_out)
    taps_grad = jnp.stack([jnp.sum(conv_grad * window[8 * k:8 * k + count], axis=0) for k in range(rim + 1)])
    shift_grad = jnp.sum(conv_grad, axis=0)
    margin = jnp.zeros((8 * rim, inner), jnp.float32)
    padded = jnp.concatenate([margin, conv_grad, margin], axis=0)
    window_grad = sum(
        layer.taps[k] * padded[8 * (rim - k):8 * (rim - k) + count + 8 * rim] for k in range(rim + 1))
    prefix_grad = split_parts(by_step(window_grad[:8 * rim]), parts)
    arrived = neighbour(prefix_grad[:, 0], -1)
    tail_grad = jnp.concatenate([prefix_grad[:, 1:], arrived[:, None]], axis=1).reshape(8 * rim, inner)
    values_grad = jnp.concatenate([window_grad[8 * rim:count], window_grad[count:] + tail_grad], axis=0)
    values_grad = values_grad.astype(jnp.bfloat16)
    normed_part = dot_n(values_grad, layer.into[:, :inner]) + gate_through
    small = jnp.concatenate([taps_grad, shift_grad[None], bias_grad[None], decay_grad], axis=0)
    return normed_part, small, (values_grad, before_low, high, low), split_parts(start_grad, parts)[:, 0], prefix_grad[:, 0]


def thick_grads(kept, normed, lows):
    inputs, dt_low = kept[3], kept[4]
    values_grad, before_low, high, low = lows
    blocks = lax.axis_size("blk")
    x_grad = dot_t(high, inputs) + dot_t(low, inputs)
    return [eights(part.reshape(blocks, -1, part.shape[-1]))
            for part in (dot_t(normed, values_grad), x_grad, dot_t(dt_low, before_low))]


def eights(array):
    return jnp.pad(array, ((0, 0), (0, -array.shape[1] % 8), (0, 0)))


def norm_back(gain, normed_grad, residual, q):
    gain_grad = jnp.sum(normed_grad * (residual * q), axis=0)
    scaled = normed_grad * gain
    inner_mean = jnp.mean(scaled * residual, axis=-1, keepdims=True)
    return gain_grad, q * scaled - residual * (q * q * q * inner_mean)


def on_device(tokens, cotangent, *args):
    scan_init, conv_init = args[-2:]
    weights = args[:-2]
    blocks, index = lax.axis_size("blk"), lax.axis_index("blk")
    at_first = index == 0
    layer_total = weights[1].shape[0]
    seqs = tokens.shape[0]
    parts = 8 // seqs
    length = tokens.shape[1] // parts
    width = tokens.shape[2]
    layers = [Layer(l, weights) for l in range(layer_total)]
    last = layer_total - 1

    def arrange(array):
        return array.reshape(seqs, parts, length, width).transpose(2, 1, 0, 3).reshape(length * 8, width)

    def restore(array):
        array = array.reshape(length, parts, seqs, width).transpose(2, 1, 0, 3)
        return array.reshape(seqs, parts * length, width)

    residual = arrange(tokens).astype(jnp.float32)
    normed = lax.optimization_barrier((residual * inverse_rms(residual) * layers[0].gain).astype(jnp.bfloat16))
    residual = own_rows(residual)
    input_square = jnp.sum(residual * residual)
    grad = arrange(cotangent).astype(jnp.float32)
    grad_low = grad.astype(jnp.bfloat16)

    kept, scans, norms, finals, tails, squares = ([None] * layer_total for _ in range(6))
    starts, prefixes, smalls, gains = ([None] * layer_total for _ in range(4))
    for l, layer in enumerate(layers):
        norms[l] = (normed, residual)
        kept[l], local, tails[l] = front(
            layer, normed, jnp.moveaxis(conv_init[l], 1, 0), parts, at_first)
        totals = kept[l][-1]
        first = jnp.moveaxis(scan_init[l], 1, 0)
        if l == last:
            grads = back_gated(kept[l], late_gated)
            late = back_local(layer, kept[l], grads[1])
            start, end = exchange(layer, [local, late], totals, first, (False, True), layer_total + l)
        else:
            start, = exchange(layer, [local], totals, first, (False,), layer_total + l)
        partial_sum, scans[l], final = scanning(layer, kept[l], start)
        finals[l] = split_parts(final, parts)[:, -1]
        half = core_sum(partial_sum)
        if l < last:
            half, stored = lax.optimization_barrier((half, weights[1]))
            into = [stored[k].reshape(width, -1) for k in range(layer_total)]
            layers[l + 1].raw = stored[l + 1]
            late_gated = dot_n(grad_low, layers[last].out)
            got, into, grad_low, late_gated = lax.optimization_barrier((across(half), into, grad_low, late_gated))
            for each, array in zip(layers, into):
                each.into = array
            branch = half + got
            following = residual + branch
            squares[l] = jnp.stack([jnp.sum(branch * branch), jnp.sum(following * following)])
            residual = following
            unscaled = all_rows(residual * inverse_rms(residual))
            normed = (unscaled * layers[l + 1].gain).astype(jnp.bfloat16)

    thins, scattered = [], [None] * layer_total
    for l in reversed(range(layer_total)):
        layer = layers[l]
        normed, base = norms[l]
        if l < last:
            grads, out_grad = lax.optimization_barrier(
                (back_gated(kept[l], dot_n(grad_low, layer.out)), dot_t(grad_low, scans[l][1])))
            scattered[l] = [blk_scatter(out_grad)]
            late = back_local(layer, kept[l], grads[1])
            end, = exchange(layer, [late], kept[l][-1], jnp.zeros_like(late[:, 0]), (True,), 2 + 2 * layer_total + l)
        else:
            out_grad = dot_t(grad_low, scans[l][1])
        side = back_side(layer, kept[l], normed, scans[l], grads, grad_low)
        middle = half.shape[0] // 2
        if l == last:
            end, side, out_grad, half = lax.optimization_barrier((end, side, out_grad, half))
            scattered[l] = [blk_scatter(out_grad), blk_scatter(side[0])]
            scan_out, got = lax.optimization_barrier(
                (back_scan(layer, kept[l], scans[l], grads, end), across(half[:middle])))
        else:
            end, side, half, scattered[last] = lax.optimization_barrier((end, side, half, scattered[last]))
            scattered[l].append(blk_scatter(side[0]))
            scan_out, got_rest = lax.optimization_barrier(
                (back_scan(layer, kept[l], scans[l], grads, end), across(half[middle:])))
            branch = half + jnp.concatenate([got, got_rest], axis=0)
            following = residual + branch
            squares[last] = jnp.stack([jnp.sum(branch * branch), jnp.sum(following * following)])
            out = restore((2.0 * all_rows(0.5 * following)).astype(jnp.bfloat16))
        gate_grad, gate_through, skip_grad = side
        normed_part, smalls[l], lows, starts[l], prefixes[l] = back_rest(
            layer, kept[l], grads, scan_out, gate_through)
        smalls[l] = jnp.concatenate([smalls[l], skip_grad[None]], axis=0)
        thick = thick_grads(kept[l], normed, lows)
        inner = smalls[l].shape[-1]
        if l == last:
            thins = thick[1:] + thins
            joint, scattered[l][0] = lax.optimization_barrier((joint_sums(
                normed_part, base, layer.gain, [rows(thick[0])], (128,), smalls[l], l), scattered[l][0]))
            change, gains[l], thick, smalls[l] = joint
            scattered[l].append(thick[0])
        else:
            thins = thick[1:] + thins
            cuts = [part.shape[1] for part in thins]
            extra = jnp.concatenate([jnp.stack(squares).reshape(-1), input_square.reshape(1)])
            extra = jnp.pad(extra, (0, inner - extra.shape[0]))[None]
            shared = rows_sum(jnp.concatenate(
                [extra] + [gain.reshape(-1, inner) for gain in gains[1:]], axis=0))
            own_count = smalls[l].shape[0]
            small = jnp.concatenate([smalls[l], shared], axis=0)
            small = jnp.pad(small, ((0, -small.shape[0] % 8), (0, 0)))
            normed_part, thins, out = lax.optimization_barrier((normed_part, thins, out))
            change, gains[l], thick, small = joint_sums(
                normed_part, base, layer.gain, [rows(thick[0]), rows(jnp.concatenate(thins, axis=1))], (0, inner),
                small, l)
            scattered[l].append(thick[0])
            smalls[l], rest = small[:own_count], small[own_count:]
        grad = grad + change
        grad_low = grad.astype(jnp.bfloat16)
    first_gain = blk_sum(rows_sum(gains[0].reshape(-1, inner)))
    input_grad = restore(grad_low)

    small = jnp.stack(smalls)
    gain_rows = first_gain.shape[0] * layer_total
    gain_grad = jnp.concatenate([first_gain, rest[1:1 + gain_rows - first_gain.shape[0]]], axis=0)
    gain_grad = gain_grad.reshape(layer_total, width)
    taps = weights[2].shape[1]
    row_total = tokens.shape[0] * tokens.shape[1] * width * blocks
    squares = rest[0] / row_total
    rms_stats = jnp.sqrt(squares[:2 * layer_total]).reshape(layer_total, 2)
    input_rms = jnp.sqrt(squares[2 * layer_total:2 * layer_total + 1])
    pieces, at = [], 0
    for cut in cuts:
        pieces.append(thick[1][at:at + cut])
        at += cut
    into_out = jnp.stack([jnp.stack([part[2], part[1]], axis=1) for part in scattered])

    def stacked(parts_):
        return jnp.stack([jnp.moveaxis(part, 0, 1) for part in parts_])[:, :, None]

    return (
        out,
        stacked(finals),
        stacked(tails),
        input_grad,
        stacked(starts),
        stacked(prefixes),
        gain_grad,
        into_out,
        small[:, :taps],
        small[:, taps],
        jnp.stack([part[:weights[4].shape[-1] // blocks].T for part in pieces[0::2]]),
        jnp.stack([part[:RANK // blocks] for part in pieces[1::2]]),
        small[:, taps + 1],
        small[:, taps + 2:-1],
        small[:, -1],
        jnp.stack([part[0].T for part in scattered]),
        rms_stats,
        input_rms,
    )


def solution(mesh):
    placed = (
        P(None, "blk", None),
        P(None, "blk", None),
        P(),
        P(None, None, None, "tensor"),
        P(None, None, "tensor"),
        P(None, "tensor"),
        P(None, "tensor", None),
        P(None, None, "tensor"),
        P(None, "tensor"),
        P(None, None, "tensor"),
        P(None, "tensor"),
        P(None, "tensor", None),
        P(None, None, None, "tensor"),
        P(None, None, None, "tensor"),
    )
    return jax.shard_map(
        on_device,
        mesh=mesh,
        in_specs=placed,
        out_specs=(
            P(None, "blk", None),
            P(None, None, "blk", None, "tensor"),
            P(None, None, "blk", None, "tensor"),
            P(None, "blk", None),
            P(None, None, "blk", None, "tensor"),
            P(None, None, "blk", None, "tensor"),
            P(),
            P(None, "blk", None, "tensor"),
            P(None, None, "tensor"),
            P(None, "tensor"),
            P(None, "tensor", "blk"),
            P(None, "blk", "tensor"),
            P(None, "tensor"),
            P(None, None, "tensor"),
            P(None, "tensor"),
            P(None, "tensor", "blk"),
            P(),
            P(),
        ),
        check_vma=False,
    )
```

```python
import math
from functools import partial
import jax
import jax.numpy as jnp
from jax import lax
from jax.experimental import pallas as pl
from jax.experimental.pallas import tpu as pltpu

from jax.sharding import PartitionSpec as P

STATE = 16
RANK = 128
EPSILON = 1e-05
LANES=128
LOG2E=math.log2(math.e)

def cost(step, passes):
    return pl.CostEstimate(flops=passes * STATE * step.size, bytes_accessed=passes * STATE * step.size, transcendentals=0)

def cp(limit):
    return pltpu.CompilerParams(dimension_semantics=("arbitrary",), vmem_limit_bytes=limit)

def spread(ref_value, out, first):
    for n in range(STATE):
        for t in range(out.shape[0]):
            out[t, n] = jnp.broadcast_to(ref_value[t, :, first + n:first + n + 1], out.shape[2:])

def rates(rate_ref, lanes, n):
    return jnp.broadcast_to(rate_ref[pl.ds(n, 1), lanes], (8, LANES))

def end_body(blocks, width, held, step_ref, push_ref, coef_ref, rate_ref, end_ref, write):
    @pl.when(pl.program_id(0) == 0)
    def _():
        end_ref[...] = jnp.zeros_like(end_ref)
    spread(coef_ref, write, 0)
    def group(g, _):
        cols = [pl.ds(pl.multiple_of((g * width + k) * LANES, LANES), LANES) for k in range(width)]
        for low in range(0, STATE, held):
            span = range(low, low + held)
            state = {(k, n): end_ref[n, :, cols[k]] for k in range(width) for n in span}
            rate = {(k, n): rates(rate_ref, cols[k], n) for k in range(width) for n in span}
            for t in range(step_ref.shape[0]):
                step = [step_ref[t, :, c] for c in cols]
                push = [push_ref[t, :, c] for c in cols]
                for n in span:
                    w = write[t, n]
                    for k in range(width):
                        state[k, n] = jnp.exp2(step[k] * rate[k, n]) * state[k, n] + push[k] * w
            for k in range(width):
                for n in span:
                    end_ref[n, :, cols[k]] = state[k, n]
        return 0
    lax.fori_loop(0, blocks // width, group, 0)

def end_states(step, push, coef, rate, tb=16, width=2, held=8, limit=48*2**20):
    T, _, C = step.shape
    return pl.pallas_call(
        partial(end_body, C // LANES, width, held),
        grid=(T // tb,),
        in_specs=[pl.BlockSpec((tb, 8, C), lambda i: (i, 0, 0)), pl.BlockSpec((tb, 8, C), lambda i: (i, 0, 0)),
                  pl.BlockSpec((tb, 8, 2 * STATE), lambda i: (i, 0, 0)), pl.BlockSpec((STATE, C), lambda i: (0, 0))],
        out_specs=pl.BlockSpec((STATE, 8, C), lambda i: (0, 0, 0)),
        out_shape=jax.ShapeDtypeStruct((STATE, 8, C), jnp.float32),
        scratch_shapes=[pltpu.VMEM((tb, STATE, 8, LANES), jnp.float32)],
        compiler_params=cp(limit), cost_estimate=cost(step, 4), name="end_states")(step, push, coef, rate)

def scan_body(blocks, width, held, step_ref, push_ref, coef_ref, rate_ref, start_ref, out_ref, states_ref, final_ref, write, read):
    @pl.when(pl.program_id(0) == 0)
    def _():
        final_ref[...] = start_ref[...]
    spread(coef_ref, write, 0)
    spread(coef_ref, read, STATE)
    def group(g, _):
        cols = [pl.ds(pl.multiple_of((g * width + k) * LANES, LANES), LANES) for k in range(width)]
        for low in range(0, STATE, held):
            span = range(low, low + held)
            state = {(k, n): final_ref[n, :, cols[k]] for k in range(width) for n in span}
            rate = {(k, n): rates(rate_ref, cols[k], n) for k in range(width) for n in span}
            for t in range(step_ref.shape[0]):
                step = [step_ref[t, :, c] for c in cols]
                push = [push_ref[t, :, c] for c in cols]
                total = [None] * width
                for n in span:
                    w, r = write[t, n], read[t, n]
                    for k in range(width):
                        s = jnp.exp2(step[k] * rate[k, n]) * state[k, n] + push[k] * w
                        state[k, n] = s
                        states_ref[t, n, :, cols[k]] = s
                        total[k] = r * s if total[k] is None else total[k] + r * s
                for k in range(width):
                    if low == 0:
                        out_ref[t, :, cols[k]] = total[k]
                    else:
                        out_ref[t, :, cols[k]] += total[k]
            for k in range(width):
                for n in span:
                    final_ref[n, :, cols[k]] = state[k, n]
        return 0
    lax.fori_loop(0, blocks // width, group, 0)

def scan_forward(step, push, coef, rate, start, tb=16, width=2, held=8, limit=48*2**20):
    T, _, C = step.shape
    row = pl.BlockSpec((tb, 8, C), lambda i: (i, 0, 0))
    whole = pl.BlockSpec((STATE, 8, C), lambda i: (0, 0, 0))
    f32 = jnp.float32
    return pl.pallas_call(
        partial(scan_body, C // LANES, width, held),
        grid=(T // tb,),
        in_specs=[row, row, pl.BlockSpec((tb, 8, 2 * STATE), lambda i: (i, 0, 0)), pl.BlockSpec((STATE, C), lambda i: (0, 0)), whole],
        out_specs=[row, pl.BlockSpec((tb, STATE, 8, C), lambda i: (i, 0, 0, 0)), whole],
        out_shape=[jax.ShapeDtypeStruct((T, 8, C), f32), jax.ShapeDtypeStruct((T, STATE, 8, C), f32),
                   jax.ShapeDtypeStruct((STATE, 8, C), f32)],
        scratch_shapes=[pltpu.VMEM((tb, STATE, 8, LANES), f32)] * 2,
        compiler_params=cp(limit), cost_estimate=cost(step, 7), name="scan_forward")(step, push, coef, rate, start)

def start_body(blocks, width, held, step_ref, grad_ref, coef_ref, rate_ref, start_ref, read):
    @pl.when(pl.program_id(0) == 0)
    def _():
        start_ref[...] = jnp.zeros_like(start_ref)
    spread(coef_ref, read, STATE)
    def group(g, _):
        cols = [pl.ds(pl.multiple_of((g * width + k) * LANES, LANES), LANES) for k in range(width)]
        for low in range(0, STATE, held):
            span = range(low, low + held)
            state = {(k, n): start_ref[n, :, cols[k]] for k in range(width) for n in span}
            rate = {(k, n): rates(rate_ref, cols[k], n) for k in range(width) for n in span}
            for t in reversed(range(step_ref.shape[0])):
                step = [step_ref[t, :, c] for c in cols]
                grad = [grad_ref[t, :, c] for c in cols]
                for n in span:
                    r = read[t, n]
                    for k in range(width):
                        state[k, n] = jnp.exp2(step[k] * rate[k, n]) * (state[k, n] + r * grad[k])
            for k in range(width):
                for n in span:
                    start_ref[n, :, cols[k]] = state[k, n]
        return 0
    lax.fori_loop(0, blocks // width, group, 0)

def start_grads(step, grad, coef, rate, tb=16, width=2, held=8, limit=48*2**20):
    T, _, C = step.shape
    last = T // tb - 1
    row = pl.BlockSpec((tb, 8, C), lambda i: (last - i, 0, 0))
    return pl.pallas_call(
        partial(start_body, C // LANES, width, held),
        grid=(T // tb,),
        in_specs=[row, row, pl.BlockSpec((tb, 8, 2 * STATE), lambda i: (last - i, 0, 0)), pl.BlockSpec((STATE, C), lambda i: (0, 0))],
        out_specs=pl.BlockSpec((STATE, 8, C), lambda i: (0, 0, 0)),
        out_shape=jax.ShapeDtypeStruct((STATE, 8, C), jnp.float32),
        scratch_shapes=[pltpu.VMEM((tb, STATE, 8, LANES), jnp.float32)],
        compiler_params=cp(limit), cost_estimate=cost(step, 4), name="start_grads")(step, grad, coef, rate)

def back_body(blocks, width, held, step_ref, push_ref, grad_ref, coef_ref, rate_ref, states_ref, prior_ref, begin_ref, end_ref,
              decay_out, push_out, coef_out, start_ref, speed_ref, write, read, write_sum, read_sum):
    @pl.when(pl.program_id(0) == 0)
    def _():
        start_ref[...] = end_ref[...]
        speed_ref[...] = jnp.zeros_like(speed_ref)
    spread(coef_ref, write, 0)
    spread(coef_ref, read, STATE)
    tb = step_ref.shape[0]
    begins = pl.program_id(0) == pl.num_programs(0) - 1
    def group(g, first):
        cols = [pl.ds((g * width + k) * LANES if first else pl.multiple_of((g * width + k) * LANES, LANES), LANES)
                for k in range(width)]
        for low in range(0, STATE, held):
            span = range(low, low + held)
            carry = {(k, n): start_ref[n, :, cols[k]] for k in range(width) for n in span}
            speed = {(k, n): speed_ref[n, :, cols[k]] for k in range(width) for n in span}
            rate = {(k, n): rates(rate_ref, cols[k], n) for k in range(width) for n in span}
            enter = {(k, n): jnp.where(begins, begin_ref[n, :, cols[k]], prior_ref[0, n, :, cols[k]])
                     for k in range(width) for n in span}
            for t in reversed(range(tb)):
                step = [step_ref[t, :, c] for c in cols]
                push = [push_ref[t, :, c] for c in cols]
                grad = [grad_ref[t, :, c] for c in cols]
                decays = [None] * width
                pushes = [None] * width
                for n in span:
                    w, r = write[t, n], read[t, n]
                    wsum, rsum = None, None
                    for k in range(width):
                        before = states_ref[t - 1, n, :, cols[k]] if t else enter[k, n]
                        back = carry[k, n] + r * grad[k]
                        onward = jnp.exp2(step[k] * rate[k, n]) * back
                        carry[k, n] = onward
                        q = onward * before
                        speed[k, n] = speed[k, n] + step[k] * q
                        rq, bw = rate[k, n] * q, back * w
                        decays[k] = rq if decays[k] is None else decays[k] + rq
                        pushes[k] = bw if pushes[k] is None else pushes[k] + bw
                        bp, gs = back * push[k], grad[k] * states_ref[t, n, :, cols[k]]
                        wsum = bp if wsum is None else wsum + bp
                        rsum = gs if rsum is None else rsum + gs
                    if first:
                        write_sum[t, n] = wsum
                        read_sum[t, n] = rsum
                    else:
                        write_sum[t, n] += wsum
                        read_sum[t, n] += rsum
                for k in range(width):
                    if low == 0:
                        decay_out[t, :, cols[k]] = decays[k]
                        push_out[t, :, cols[k]] = pushes[k]
                    else:
                        decay_out[t, :, cols[k]] += decays[k]
                        push_out[t, :, cols[k]] += pushes[k]
            for k in range(width):
                for n in span:
                    start_ref[n, :, cols[k]] = carry[k, n]
                    speed_ref[n, :, cols[k]] = speed[k, n]
        return 0
    group(0, True)
    lax.fori_loop(1, blocks // width, lambda g, _: group(g, False), 0)
    lane = lax.broadcasted_iota(jnp.int32, (8, 2 * STATE), 1)
    for t in range(tb):
        row = jnp.zeros((8, 2 * STATE), jnp.float32)
        for n in range(STATE):
            row = jnp.where(lane == n, jnp.sum(write_sum[t, n], axis=-1, keepdims=True), row)
            row = jnp.where(lane == STATE + n, jnp.sum(read_sum[t, n], axis=-1, keepdims=True), row)
        coef_out[t] = row

def scan_backward(step, push, grad, coef, rate, states, begin, end, tb=8, width=2, held=4, limit=48*2**20):
    T, _, C = step.shape
    last = T // tb - 1
    f32 = jnp.float32
    row = pl.BlockSpec((tb, 8, C), lambda i: (last - i, 0, 0))
    thin = pl.BlockSpec((tb, 8, 2 * STATE), lambda i: (last - i, 0, 0))
    whole = pl.BlockSpec((STATE, 8, C), lambda i: (0, 0, 0))
    return pl.pallas_call(
        partial(back_body, C // LANES, width, held),
        grid=(T // tb,),
        in_specs=[row, row, row, thin, pl.BlockSpec((STATE, C), lambda i: (0, 0)),
                  pl.BlockSpec((tb, STATE, 8, C), lambda i: (last - i, 0, 0, 0)),
                  pl.BlockSpec((1, STATE, 8, C), lambda i: (jnp.maximum((last - i) * tb - 1, 0), 0, 0, 0)), whole, whole],
        out_specs=[row, row, thin, whole, whole],
        out_shape=[jax.ShapeDtypeStruct((T, 8, C), f32)] * 2 + [jax.ShapeDtypeStruct((T, 8, 2 * STATE), f32)]
          + [jax.ShapeDtypeStruct((STATE, 8, C), f32)] * 2,
        scratch_shapes=[pltpu.VMEM((tb, STATE, 8, LANES), f32)] * 4,
        compiler_params=cp(limit), cost_estimate=cost(step, 13), name="scan_backward")(step, push, grad, coef, rate, states, states, begin, end)


HALVES_OF_CHIP = 2


def silu_slope(argument):
    sigmoid_value = jax.nn.sigmoid(argument)
    return sigmoid_value * (1.0 + argument * (1.0 - sigmoid_value))


def half_of(array, index):
    size = array.shape[0] // 2
    return lax.dynamic_slice_in_dim(array, index * size, size, 0)


def ordered(index, mine, other):
    first = jnp.where(index == 0, mine, other)
    second = jnp.where(index == 0, other, mine)
    return jnp.concatenate([first, second], axis=0)


BESIDE = [(0, 1), (1, 0), (2, 3), (3, 2)]
ACROSS = [(0, 2), (2, 0), (1, 3), (3, 1)]


def paired():
    return lax.axis_size("tensor") == 4


def tensor_sum(array):
    if not paired():
        return lax.psum(array, "tensor")
    core = lax.axis_index("tensor") % 2
    half = half_of(array, core) + lax.ppermute(half_of(array, 1 - core), "tensor", BESIDE)
    half = half + lax.ppermute(half, "tensor", ACROSS)
    return ordered(core, half, lax.ppermute(half, "tensor", BESIDE))


def own_rows(array):
    if not paired():
        size = array.shape[0] // lax.axis_size("tensor")
        return lax.dynamic_slice_in_dim(array, lax.axis_index("tensor") * size, size, 0)
    return half_of(array, lax.axis_index("tensor") % 2)


def core_sum(array):
    if not paired():
        return lax.psum_scatter(array, "tensor", scatter_dimension=0, tiled=True)
    core = lax.axis_index("tensor") % 2
    return half_of(array, core) + lax.ppermute(half_of(array, 1 - core), "tensor", BESIDE)


def across(half):
    if not paired():
        return jnp.zeros_like(half)
    return lax.ppermute(half, "tensor", ACROSS)


def all_rows(array):
    if not paired():
        return lax.optimization_barrier(lax.all_gather(array, "tensor", tiled=True))
    other = lax.optimization_barrier(lax.ppermute(array, "tensor", BESIDE))
    return ordered(lax.axis_index("tensor") % 2, array, other)


def rows_sum(array):
    if not paired():
        return lax.psum(array, "tensor")
    return array + lax.ppermute(array, "tensor", BESIDE)


def blk_sum(array):
    if lax.axis_size("blk") != 8:
        return lax.psum(array, "blk")
    for bit in (1, 2, 4):
        array = array + lax.ppermute(array, "blk", [(j, j ^ bit) for j in range(8)])
    return array


def blk_scatter(array):
    return lax.psum_scatter(array, "blk", scatter_dimension=0, tiled=True)


def add_rows(total, other, count):
    slab = 8

    def body(i, _):
        at = pl.ds(pl.multiple_of(i * slab, slab), slab)
        total[at, :] = total[at, :] + other[at, :]
        return 0

    lax.fori_loop(0, count // slab, body, 0)


def remote(src, dst, sends, recvs, at, device):
    return pltpu.make_async_remote_copy(
        src_ref=src, dst_ref=dst, send_sem=sends.at[at], recv_sem=recvs.at[at], device_id=device,
        device_id_type=pl.DeviceIdType.MESH)


def joint_body(plan, chunks, sum_ref, base_ref, gain_ref, *refs):
    count = 1 + max(job[0] for job in plan)
    thick_refs, small_ref, refs = refs[:count], refs[count], refs[count + 1:]
    change_out, gain_out, refs = refs[0], refs[1], refs[2:]
    thick_outs, small_out, refs = refs[:count], refs[count], refs[1 + count:]
    own_half, core_half, far_half, base, came, small_in, refs = refs[0], refs[1], refs[2], refs[3], refs[4], refs[5], refs[6:]
    core_send, core_recv, far_send, far_recv, back_send, back_recv, local_sem, base_sem, out_sem, came_sem = refs[:10]
    small_send, small_recv = refs[10:12]
    refs = refs[12:]
    blk, tensor = lax.axis_index("blk"), lax.axis_index("tensor")
    bits = {1: blk % 2, 2: (blk // 2) % 2, 4: blk // 4}
    core = tensor % 2
    beside = (blk, tensor + 1 - 2 * core)
    far = (blk, (tensor + 2) % 4)
    peers = {bit: (blk + bit - 2 * bit * bits[bit], tensor) for bit in bits}
    barrier = pltpu.get_barrier_semaphore()
    for device in (beside, far, peers[1], peers[2], peers[4]):
        pl.semaphore_signal(barrier, inc=1, device_id=device, device_id_type=pl.DeviceIdType.MESH)
    pl.semaphore_wait(barrier, 5)

    rows_each, width = own_half.shape[1:]
    smalls, core_copies, local_copies, base_copies, far_copies, back_copies, outs = [], [], [], [], [], [], []

    def small_step(i):
        copy = remote(small_out, small_in.at[i], small_send, small_recv, i, peers[1 << i])
        copy.start()
        smalls.append(copy)

    def small_end(i):
        smalls[i].wait()
        small_out[...] = small_out[...] + small_in[i]

    small_out[...] = small_ref[...]
    small_step(0)
    for k in range(chunks):
        give = pl.ds(pl.multiple_of((1 - core) * rows_each * chunks + k * rows_each, rows_each), rows_each)
        keep = pl.ds(pl.multiple_of(core * rows_each * chunks + k * rows_each, rows_each), rows_each)
        copy = remote(sum_ref.at[give], core_half.at[k], core_send, core_recv, k, beside)
        copy.start()
        core_copies.append(copy)
        copy = pltpu.make_async_copy(sum_ref.at[keep], own_half.at[k], local_sem.at[k])
        copy.start()
        local_copies.append(copy)
        copy = pltpu.make_async_copy(base_ref.at[pl.ds(k * rows_each, rows_each)], base.at[k], base_sem.at[k])
        copy.start()
        base_copies.append(copy)
    gain_out[...] = jnp.zeros_like(gain_out)

    class Job:
        def __init__(self, which, low, wide, order, refs):
            (self.own, self.first, self.second, self.third, self.sems) = refs[0], refs[1], refs[2], refs[3], refs[4:]
            self.order = order
            self.count = thick_refs[which].shape[3]
            self.out = thick_outs[which].at[:, pl.ds(low, wide)]
            lead, (u, v) = bits[order[0]], (bits[order[1]], bits[order[2]])
            self.parts = [(1 - u, 1 - v), (1 - u, v), (u, 1 - v), (u, v)]
            self.firsts, self.owns, self.seconds = [], [], []
            for i, part in enumerate(self.parts):
                at = {order[1]: part[0], order[2]: part[1]}

                def source(mine):
                    index = dict(at)
                    index[order[0]] = mine
                    return thick_refs[which].at[index[4], index[2], index[1], :, pl.ds(low, wide)]

                copy = remote(source(1 - lead), self.first.at[part], self.sems[0], self.sems[1], i, peers[order[0]])
                copy.start()
                self.firsts.append(copy)
                copy = pltpu.make_async_copy(source(lead), self.own.at[part], self.sems[2].at[i])
                copy.start()
                self.owns.append(copy)

        def first_end(self, i):
            self.owns[i].wait()
            self.firsts[i].wait_recv()
            add_rows(self.own.at[self.parts[i]], self.first.at[self.parts[i]], self.count)
            if i < 2:
                copy = remote(self.own.at[self.parts[i]], self.second.at[i], self.sems[3], self.sems[4], i,
                              peers[self.order[1]])
                copy.start()
                self.seconds.append(copy)
                return
            self.seconds[i - 2].wait_recv()
            add_rows(self.own.at[self.parts[i]], self.second.at[i - 2], self.count)
            if i == 2:
                self.last = remote(self.own.at[self.parts[i]], self.third, self.sems[5], self.sems[6], 0,
                                   peers[self.order[2]])
                self.last.start()

        def end(self):
            self.last.wait_recv()
            add_rows(self.own.at[self.parts[3]], self.third, self.count)
            copy = pltpu.make_async_copy(self.own.at[self.parts[3]], self.out, self.sems[7].at[0])
            copy.start()
            outs.append(copy)

        def sent(self):
            return self.firsts + self.seconds + [self.last]

    jobs = [Job(*job, refs[12 * i:12 * i + 12]) for i, job in enumerate(plan)]

    def core_end(k):
        local_copies[k].wait()
        core_copies[k].wait()
        add_rows(own_half.at[k], core_half.at[k], rows_each)
        copy = remote(own_half.at[k], far_half.at[k], far_send, far_recv, k, far)
        copy.start()
        far_copies.append(copy)

    def far_end(k):
        far_copies[k].wait_recv()
        base_copies[k].wait()

        def slab(i, _):
            at = pl.ds(pl.multiple_of(i * 8, 8), 8)
            residual = base[k, at, :]
            normed_grad = far_half[k, at, :] + own_half[k, at, :]
            q = lax.rsqrt(jnp.sum(residual * residual, axis=-1, keepdims=True) * (1.0 / width) + EPSILON)
            part = residual * q
            gain_out[...] += normed_grad * part
            scaled = normed_grad * gain_ref[...]
            inner = jnp.sum(scaled * part, axis=-1, keepdims=True) * (1.0 / width)
            far_half[k, at, :] = q * (scaled - part * inner)
            return 0

        lax.fori_loop(0, rows_each // 8, slab, 0)
        copy = remote(far_half.at[k], came.at[k], back_send, back_recv, k, beside)
        copy.start()
        back_copies.append(copy)
        own_rows_at = pl.ds(pl.multiple_of((core * chunks + k) * rows_each, rows_each), rows_each)
        copy = pltpu.make_async_copy(far_half.at[k], change_out.at[own_rows_at], out_sem.at[k])
        copy.start()
        outs.append(copy)

    def back_end(k):
        back_copies[k].wait_recv()
        other_rows_at = pl.ds(pl.multiple_of(((1 - core) * chunks + k) * rows_each, rows_each), rows_each)
        copy = pltpu.make_async_copy(came.at[k], change_out.at[other_rows_at], came_sem.at[k])
        copy.start()
        outs.append(copy)

    for k in range(chunks):
        core_end(k)
    small_end(0)
    small_step(1)
    for i in range(4):
        for job in jobs:
            job.first_end(i)
        if i in (0, 1):
            small_end(i + 1)
            if i == 0:
                small_step(2)
        far_end(i)
    for k in range(chunks):
        back_end(k)
    for job in jobs:
        job.end()
    for copy in far_copies + back_copies + [each for job in jobs for each in job.sent()]:
        copy.wait_send()
    for copy in outs:
        copy.wait()


def joint_sums(array, base, gain, thick, late, small, collective_id):
    if not paired() or lax.axis_size("blk") != 8:
        normed_grad = lax.psum_scatter(array, "tensor", scatter_dimension=0, tiled=True)
        gain_grad, change = norm_back(gain, normed_grad, base, inverse_rms(base))
        return all_rows(change), gain_grad, [blk_scatter(part) for part in thick], lax.psum(small, "blk")
    R, N = array.shape
    C = thick[0].shape[1]
    chunks = 4
    f32 = jnp.float32
    dma = pltpu.SemaphoreType.DMA
    any_spec = pl.BlockSpec(memory_space=pl.ANY)
    vmem_spec = pl.BlockSpec(memory_space=pltpu.VMEM)
    plan = [(i, 0, C - each, (1, 2, 4)) for i, each in enumerate(late) if each < C]
    plan += [(i, C - each, each, (2, 4, 1)) for i, each in enumerate(late) if each]
    scratch = []
    for which, _, wide, _ in plan:
        count = thick[which].shape[0] // 8
        scratch += [pltpu.VMEM((2, 2, count, wide), f32), pltpu.VMEM((2, 2, count, wide), f32),
                    pltpu.VMEM((2, count, wide), f32), pltpu.VMEM((count, wide), f32),
                    dma((4,)), dma((4,)), dma((4,)), dma((2,)), dma((2,)), dma((1,)), dma((1,)), dma((1,))]
    half = pltpu.VMEM((chunks, R // 2 // chunks, N), f32)
    out = pl.pallas_call(
        partial(joint_body, plan, chunks),
        in_specs=[any_spec, any_spec, vmem_spec] + [any_spec] * len(thick) + [vmem_spec],
        out_specs=[any_spec, vmem_spec] + [any_spec] * len(thick) + [vmem_spec],
        out_shape=[jax.ShapeDtypeStruct((R, N), f32), jax.ShapeDtypeStruct((8, N), f32)]
        + [jax.ShapeDtypeStruct((part.shape[0] // 8, C), f32) for part in thick]
        + [jax.ShapeDtypeStruct(small.shape, f32)],
        scratch_shapes=[half] * 5 + [pltpu.VMEM((3,) + small.shape, f32)]
        + [dma((chunks,))] * 10 + [dma((3,)), dma((3,))] + scratch,
        compiler_params=pltpu.CompilerParams(
            collective_id=collective_id, has_side_effects=True, vmem_limit_bytes=52 * 2**20),
        cost_estimate=pl.CostEstimate(flops=0, bytes_accessed=50 * R * N * 4, transcendentals=0),
        name="joint_sums",
    )(array, base, gain[None], *[part.reshape(2, 2, 2, part.shape[0] // 8, C) for part in thick], small)
    return out[0], jnp.sum(out[1], axis=0), list(out[2:-1]), out[-1]


def neighbour(value, steps):
    count = lax.axis_size("blk")
    first, last = max(0, -steps), min(count, count - steps)
    return lax.ppermute(value, "blk", [(j, j + steps) for j in range(first, last)])


def entering_any(total, local, rate, first, reverse):
    peers, index = lax.axis_size("blk"), lax.axis_index("blk")
    totals, locals_ = lax.all_gather(total, "blk"), lax.all_gather(local, "blk")

    def step(k, state):
        at = peers - 1 - k if reverse else k
        reached = at > index if reverse else at < index
        return jnp.where(reached, jnp.exp2(totals[at][None] * rate) * state + locals_[at], state)

    return lax.fori_loop(0, peers, step, first)


def hop_body(reverses, groups, total_ref, rate_ref, *refs):
    ways = len(reverses)
    locals_, first_ref, refs = refs[:ways], refs[ways], refs[ways + 1:]
    outs, refs = refs[:ways], refs[ways:]
    beside_total, total_send, total_recv, refs = refs[0], refs[1], refs[2], refs[3:]
    blk, tensor = lax.axis_index("blk"), lax.axis_index("tensor")
    y, z = blk % 2, blk // 2
    beside = (blk + 1 - 2 * y, tensor)
    up, down = ((blk + 2) % 8, tensor), ((blk + 6) % 8, tensor)
    barrier = pltpu.get_barrier_semaphore()

    def greet(device):
        pl.semaphore_signal(barrier, inc=1, device_id=device, device_id_type=pl.DeviceIdType.MESH)

    greet(beside)
    pl.when(z < 3)(lambda: greet(up))
    pl.when(z > 0)(lambda: greet(down))
    pl.semaphore_wait(barrier, 3 - z // 3 - (3 - z) // 3)

    total = total_ref[...]
    copy_total = remote(total_ref, beside_total, total_send, total_recv, 0, beside)
    copy_total.start()
    size = STATE // 2 // groups

    class Way:
        def __init__(self, reverse, local, out, refs):
            self.own, self.other, self.came, self.goes, self.gives, self.gets = refs[:6]
            self.sems, self.out, self.reverse = refs[6:], out, reverse
            self.y, self.z = (1 - y, 3 - z) if reverse else (y, z)
            self.following = down if reverse else up
            self.at_a, self.begins = self.y == 0, self.z == 0
            self.firsts = []
            for n in range(STATE):
                value = local[n]
                if not reverse:
                    decay = jnp.exp2(total * rate_ref[pl.ds(n, 1), :])
                    value = value + jnp.where(jnp.logical_and(self.begins, self.at_a), decay * first_ref[n], 0.0)
                self.own[n] = value
            for k in range(groups):
                give = pl.ds((1 - self.y) * (STATE // 2) + k * size, size)
                copy = remote(self.own.at[give], self.other.at[pl.ds(k * size, size)], self.sems[0], self.sems[1], k, beside)
                copy.start()
                self.firsts.append(copy)

        def chain(self, k):
            part = pl.ds(k * size, size)
            return remote(self.goes.at[part], self.came.at[part], self.sems[2], self.sems[3], k, self.following)

        def middle(self, k, total_a, total_b):
            self.firsts[k].wait()
            pl.when(self.z > 0)(lambda: self.chain(k).wait_recv())
            for i in range(k * size, k * size + size):
                n = self.y * (STATE // 2) + i
                rate = rate_ref[pl.ds(n, 1), :]
                mine, got = self.own[n], self.other[i]
                local_a, local_b = jnp.where(self.at_a, mine, got), jnp.where(self.at_a, got, mine)
                enter = jnp.where(self.begins, 0.0, self.came[i])
                after_a = local_a + jnp.exp2(total_a * rate) * enter
                self.goes[i] = local_b + jnp.exp2(total_b * rate) * after_a
                self.gives[i] = jnp.where(self.at_a, after_a, enter)
                self.out[n] = jnp.where(self.at_a, enter, after_a)
            pl.when(self.z < 3)(lambda: self.chain(k).start())
            self.last(k).start()

        def last(self, k):
            part = pl.ds(k * size, size)
            return remote(self.gives.at[part], self.gets.at[part], self.sems[4], self.sems[5], k, beside)

        def all(self):
            other_total = beside_total[...]
            total_a, total_b = jnp.where(self.at_a, total, other_total), jnp.where(self.at_a, other_total, total)
            for k in range(groups):
                self.middle(k, total_a, total_b)

        def end(self, k):
            self.last(k).wait()
            for i in range(k * size, k * size + size):
                self.out[(1 - self.y) * (STATE // 2) + i] = self.gets[i]
            pl.when(self.z < 3)(lambda: self.chain(k).wait_send())

        def begin(self):
            starts = jnp.logical_and(self.begins, self.at_a)
            for n in range(STATE):
                first = 0.0 if self.reverse else first_ref[n]
                self.out[n] = jnp.where(starts, first, self.out[n])

    each = 6 + 6
    jobs = [Way(reverse, locals_[i], outs[i], refs[each * i:each * i + each]) for i, reverse in enumerate(reverses)]
    copy_total.wait()
    if ways == 1:
        jobs[0].all()
    else:

        def in_turn(order):
            for job in order:
                job.all()

        pl.when(z < 2)(lambda: in_turn(jobs))
        pl.when(z >= 2)(lambda: in_turn(jobs[::-1]))
    for k in range(groups):
        for job in jobs:
            job.end(k)
    for job in jobs:
        job.begin()


def hops(total, locals_, rate, first, reverses, collective_id):
    C = total.shape[-1]
    groups = 4
    f32 = jnp.float32
    dma = pltpu.SemaphoreType.DMA
    spec = pl.BlockSpec(memory_space=pltpu.VMEM)
    whole, half = pltpu.VMEM((STATE, 8, C), f32), pltpu.VMEM((STATE // 2, 8, C), f32)
    return pl.pallas_call(
        partial(hop_body, reverses, groups),
        in_specs=[spec] * (3 + len(locals_)),
        out_specs=[spec] * len(locals_),
        out_shape=[jax.ShapeDtypeStruct((STATE, 8, C), f32)] * len(locals_),
        scratch_shapes=[pltpu.VMEM((8, C), f32), dma((1,)), dma((1,))]
        + ([whole] + [half] * 5 + [dma((groups,))] * 6) * len(locals_),
        compiler_params=pltpu.CompilerParams(
            collective_id=collective_id, has_side_effects=True, vmem_limit_bytes=32 * 2**20),
        cost_estimate=pl.CostEstimate(flops=0, bytes_accessed=100 * total.size * 32, transcendentals=0),
        name="hops",
    )(total, rate, *locals_, first)


def rows(array):
    return array.reshape(-1, array.shape[-1])


def by_step(array):
    return array.reshape(-1, 8, array.shape[-1])


def dot32(left, right):
    return jnp.dot(left, right, preferred_element_type=jnp.float32)


def dot_t(left, right):
    return lax.dot_general(left, right, (((0,), (0,)), ((), ())), preferred_element_type=jnp.float32)


def dot_n(left, right):
    return lax.dot_general(left, right, (((1,), (1,)), ((), ())), preferred_element_type=jnp.float32)


def two_parts(array):
    high = lax.optimization_barrier(array.astype(jnp.bfloat16))
    return high, (array - high.astype(jnp.float32)).astype(jnp.bfloat16)


def split_parts(array, parts):
    return array.reshape(array.shape[:-2] + (parts, 8 // parts) + array.shape[-1:])


class Layer:
    def __init__(self, index, args):
        (norm_gain, in_weight, conv_weight, conv_bias, x_weight, dt_weight, dt_bias, decay_log,
         skip_weight, out_weight) = args
        self.gain = norm_gain[index]
        self.raw = in_weight[index] if index == 0 else None
        self.taps = conv_weight[index]
        self.shift = conv_bias[index]
        self.x = x_weight[index]
        self.dt = dt_weight[index]
        self.dt_bias = dt_bias[index]
        self.rate = -jnp.exp(decay_log[index])
        self.rate2 = self.rate * LOG2E
        self.skip = skip_weight[index]
        self.out = out_weight[index]


def inverse_rms(residual):
    return lax.rsqrt(jnp.mean(residual * residual, axis=-1, keepdims=True) + EPSILON)


def front(layer, normed, conv_first, parts, at_first):
    mixed = jnp.einsum("rd,dkc->krc", normed, layer.raw, preferred_element_type=jnp.float32)
    values, gate = mixed[0], mixed[1]
    inner = values.shape[-1]
    count = values.shape[0]
    rim = layer.taps.shape[0] - 1
    tails = split_parts(by_step(values[count - 8 * rim:]), parts)
    arrived = jnp.where(at_first, conv_first, neighbour(tails[:, -1], 1))
    prefix = jnp.concatenate([arrived[:, None], tails[:, :-1]], axis=1).reshape(rim * 8, inner)
    window = jnp.concatenate([prefix, values], axis=0)
    conv_out = layer.shift + sum(layer.taps[k] * window[8 * k:8 * k + count] for k in range(rim + 1))
    inputs = lax.optimization_barrier(jax.nn.silu(conv_out).astype(jnp.bfloat16))
    projected = tensor_sum(dot32(inputs, layer.x))
    dt_low = projected[:, :RANK].astype(jnp.bfloat16)
    coef = by_step(projected[:, RANK:])
    step = jax.nn.softplus(dot32(dt_low, layer.dt) + layer.dt_bias)
    push = step * inputs.astype(jnp.float32)
    local = split_parts(end_states(by_step(step), by_step(push), coef, layer.rate2), parts)
    totals = split_parts(jnp.sum(by_step(step), axis=0), parts)
    return (window, gate, conv_out, inputs, dt_low, coef, step, push, totals), local, tails[:, -1]


def join(local, totals, rate, reverse):
    order = range(local.shape[1])
    order = list(reversed(order)) if reverse else list(order)
    joined, total = local[:, order[0]], totals[order[0]]
    for p in order[1:]:
        joined = local[:, p] + jnp.exp2(totals[p][None] * rate) * joined
        total = total + totals[p]
    return total, joined


def each_part(state, local, totals, rate, reverse):
    order = range(local.shape[1])
    order = list(reversed(order)) if reverse else list(order)
    states = {order[0]: state}
    for p, following in zip(order[:-1], order[1:]):
        states[following] = local[:, p] + jnp.exp2(totals[p][None] * rate) * states[p]
    state = jnp.stack([states[p] for p in range(local.shape[1])], axis=1)
    return state.reshape(STATE, 8, state.shape[-1])


def exchange(layer, locals_, totals, first, reverses, collective_id):
    rate = layer.rate2[:, None]
    if lax.axis_size("blk") == 8 and totals.shape[0] == 1:
        return hops(totals[0], [local[:, 0] for local in locals_], layer.rate2, first, reverses, collective_id)
    states = []
    for local, reverse in zip(locals_, reverses):
        total, joined = join(local, totals, rate, reverse)
        state = entering_any(total, joined, rate, jnp.zeros_like(first) if reverse else first, reverse)
        states.append(each_part(state, local, totals, rate, reverse))
    return states


def scanning(layer, kept, start):
    window, gate, conv_out, inputs, dt_low, coef, step, push, totals = kept
    scanned, states, final = scan_forward(by_step(step), by_step(push), coef, layer.rate2, start)
    result = rows(scanned) + layer.skip * inputs.astype(jnp.float32)
    gated = (result * jax.nn.silu(gate)).astype(jnp.bfloat16)
    return (result, gated, states, start), final


def back_gated(kept, grad_gated):
    gate = kept[1]
    return grad_gated, grad_gated * jax.nn.silu(gate)


def back_local(layer, kept, grad_result):
    window, gate, conv_out, inputs, dt_low, coef, step, push, totals = kept
    local = start_grads(by_step(step), by_step(grad_result), coef, layer.rate2)
    return split_parts(local, totals.shape[0])


def back_side(layer, kept, normed, scans, grads, grad_low):
    window, gate, conv_out, inputs, dt_low, coef, step, push, totals = kept
    result, gated, states, start = scans
    grad_gated, grad_result = grads
    inner = gate.shape[1]
    grad_gate = (grad_gated * result * silu_slope(gate)).astype(jnp.bfloat16)
    gate_grad = dot_t(normed, grad_gate)
    gate_through = dot_n(grad_gate, layer.into[:, inner:])
    skip_grad = jnp.sum(grad_result * inputs.astype(jnp.float32), axis=0)
    return gate_grad, gate_through, skip_grad


def back_scan(layer, kept, scans, grads, end):
    window, gate, conv_out, inputs, dt_low, coef, step, push, totals = kept
    result, gated, states, start = scans
    grad_gated, grad_result = grads
    return scan_backward(
        by_step(step), by_step(push), by_step(grad_result), coef, layer.rate2, states, start, end)


def back_rest(layer, kept, grads, scan_out, gate_through):
    window, gate, conv_out, inputs, dt_low, coef, step, push, totals = kept
    grad_gated, grad_result = grads
    count, inner = gate.shape
    parts = totals.shape[0]
    rim = layer.taps.shape[0] - 1
    wide = inputs.astype(jnp.float32)
    decays, pushes, coef_grad, start_grad, speed = scan_out
    pushes = rows(pushes)
    step_grad = rows(decays) * (1.0 / LOG2E) + wide * pushes
    before_grad = step_grad * -jnp.expm1(-step)
    bias_grad = jnp.sum(before_grad, axis=0)
    decay_grad = layer.rate * jnp.sum(speed, axis=1)
    before_low = before_grad.astype(jnp.bfloat16)
    projected_grad = tensor_sum(jnp.concatenate([dot_n(before_low, layer.dt), rows(coef_grad)], axis=-1))
    high, low = two_parts(projected_grad)
    through = dot_n(jnp.concatenate([high, low], axis=-1), jnp.concatenate([layer.x, layer.x], axis=-1))
    inputs_grad = grad_result * layer.skip + step * pushes + through
    conv_grad = inputs_grad * silu_slope(conv_out)
    taps_grad = jnp.stack([jnp.sum(conv_grad * window[8 * k:8 * k + count], axis=0) for k in range(rim + 1)])
    shift_grad = jnp.sum(conv_grad, axis=0)
    margin = jnp.zeros((8 * rim, inner), jnp.float32)
    padded = jnp.concatenate([margin, conv_grad, margin], axis=0)
    window_grad = sum(
        layer.taps[k] * padded[8 * (rim - k):8 * (rim - k) + count + 8 * rim] for k in range(rim + 1))
    prefix_grad = split_parts(by_step(window_grad[:8 * rim]), parts)
    arrived = neighbour(prefix_grad[:, 0], -1)
    tail_grad = jnp.concatenate([prefix_grad[:, 1:], arrived[:, None]], axis=1).reshape(8 * rim, inner)
    values_grad = jnp.concatenate([window_grad[8 * rim:count], window_grad[count:] + tail_grad], axis=0)
    values_grad = values_grad.astype(jnp.bfloat16)
    normed_part = dot_n(values_grad, layer.into[:, :inner]) + gate_through
    small = jnp.concatenate([taps_grad, shift_grad[None], bias_grad[None], decay_grad], axis=0)
    return normed_part, small, (values_grad, before_low, high, low), split_parts(start_grad, parts)[:, 0], prefix_grad[:, 0]


def thick_grads(kept, normed, lows):
    inputs, dt_low = kept[3], kept[4]
    values_grad, before_low, high, low = lows
    blocks = lax.axis_size("blk")
    x_grad = dot_t(high, inputs) + dot_t(low, inputs)
    return [eights(part.reshape(blocks, -1, part.shape[-1]))
            for part in (dot_t(normed, values_grad), x_grad, dot_t(dt_low, before_low))]


def eights(array):
    return jnp.pad(array, ((0, 0), (0, -array.shape[1] % 8), (0, 0)))


def norm_back(gain, normed_grad, residual, q):
    gain_grad = jnp.sum(normed_grad * (residual * q), axis=0)
    scaled = normed_grad * gain
    inner_mean = jnp.mean(scaled * residual, axis=-1, keepdims=True)
    return gain_grad, q * scaled - residual * (q * q * q * inner_mean)


def on_device(tokens, cotangent, *args):
    scan_init, conv_init = args[-2:]
    weights = args[:-2]
    blocks, index = lax.axis_size("blk"), lax.axis_index("blk")
    at_first = index == 0
    layer_total = weights[1].shape[0]
    seqs = tokens.shape[0]
    parts = 8 // seqs
    length = tokens.shape[1] // parts
    width = tokens.shape[2]
    layers = [Layer(l, weights) for l in range(layer_total)]
    last = layer_total - 1

    def arrange(array):
        return array.reshape(seqs, parts, length, width).transpose(2, 1, 0, 3).reshape(length * 8, width)

    def restore(array):
        array = array.reshape(length, parts, seqs, width).transpose(2, 1, 0, 3)
        return array.reshape(seqs, parts * length, width)

    residual = arrange(tokens).astype(jnp.float32)
    normed = lax.optimization_barrier((residual * inverse_rms(residual) * layers[0].gain).astype(jnp.bfloat16))
    residual = own_rows(residual)
    input_square = jnp.sum(residual * residual)
    grad = arrange(cotangent).astype(jnp.float32)
    grad_low = grad.astype(jnp.bfloat16)

    kept, scans, norms, finals, tails, squares = ([None] * layer_total for _ in range(6))
    starts, prefixes, smalls, gains = ([None] * layer_total for _ in range(4))
    for l, layer in enumerate(layers):
        norms[l] = (normed, residual)
        kept[l], local, tails[l] = front(
            layer, normed, jnp.moveaxis(conv_init[l], 1, 0), parts, at_first)
        totals = kept[l][-1]
        first = jnp.moveaxis(scan_init[l], 1, 0)
        if l == last:
            grads = back_gated(kept[l], late_gated)
            late = back_local(layer, kept[l], grads[1])
            start, end = exchange(layer, [local, late], totals, first, (False, True), layer_total + l)
        else:
            start, = exchange(layer, [local], totals, first, (False,), layer_total + l)
        scans[l], final = scanning(layer, kept[l], start)
        gated = scans[l][1]
        if l == last:
            gated, late_out = lax.optimization_barrier((gated, dot_t(grad_low, gated)))
        partial_sum = dot32(gated, layer.out)
        finals[l] = split_parts(final, parts)[:, -1]
        half = core_sum(partial_sum)
        if l < last:
            half, stored = lax.optimization_barrier((half, weights[1]))
            into = [stored[k].reshape(width, -1) for k in range(layer_total)]
            layers[l + 1].raw = stored[l + 1]
            late_gated = dot_n(grad_low, layers[last].out)
            got, into, grad_low, late_gated = lax.optimization_barrier((across(half), into, grad_low, late_gated))
            for each, array in zip(layers, into):
                each.into = array
            branch = half + got
            following = residual + branch
            squares[l] = jnp.stack([jnp.sum(branch * branch), jnp.sum(following * following)])
            residual = following
            unscaled = all_rows(residual * inverse_rms(residual))
            normed = (unscaled * layers[l + 1].gain).astype(jnp.bfloat16)

    thins, scattered = [], [None] * layer_total
    for l in reversed(range(layer_total)):
        layer = layers[l]
        normed, base = norms[l]
        if l < last:
            grads, out_grad = lax.optimization_barrier(
                (back_gated(kept[l], dot_n(grad_low, layer.out)), dot_t(grad_low, scans[l][1])))
            scattered[l] = [blk_scatter(out_grad)]
            late = back_local(layer, kept[l], grads[1])
            end, = exchange(layer, [late], kept[l][-1], jnp.zeros_like(late[:, 0]), (True,), 2 + 2 * layer_total + l)
        else:
            out_grad = late_out
        side = back_side(layer, kept[l], normed, scans[l], grads, grad_low)
        middle = half.shape[0] // 2
        if l == last:
            scattered[l] = [blk_scatter(out_grad), blk_scatter(side[0])]
            end, side, half = lax.optimization_barrier((end, side, half))
            scan_out, got = lax.optimization_barrier(
                (back_scan(layer, kept[l], scans[l], grads, end), across(half[:middle])))
        else:
            scattered[l].append(blk_scatter(side[0]))
            end, side, half, scattered[last] = lax.optimization_barrier((end, side, half, scattered[last]))
            stacked_last = jnp.stack([scattered[last][2], scattered[last][1]], axis=1)
            scan_out, got_rest = lax.optimization_barrier(
                (back_scan(layer, kept[l], scans[l], grads, end), across(half[middle:])))
            branch = half + jnp.concatenate([got, got_rest], axis=0)
            following = residual + branch
            squares[last] = jnp.stack([jnp.sum(branch * branch), jnp.sum(following * following)])
            out = restore((2.0 * all_rows(0.5 * following)).astype(jnp.bfloat16))
        gate_grad, gate_through, skip_grad = side
        normed_part, smalls[l], lows, starts[l], prefixes[l] = back_rest(
            layer, kept[l], grads, scan_out, gate_through)
        smalls[l] = jnp.concatenate([smalls[l], skip_grad[None]], axis=0)
        thick = thick_grads(kept[l], normed, lows)
        inner = smalls[l].shape[-1]
        if l == last:
            thins = thick[1:] + thins
            joint, scattered[l][0] = lax.optimization_barrier((joint_sums(
                normed_part, base, layer.gain, [rows(thick[0])], (0,), smalls[l], l), scattered[l][0]))
            change, gains[l], thick, smalls[l] = joint
            scattered[l].append(thick[0])
        else:
            thins = thick[1:] + thins
            cuts = [part.shape[1] for part in thins]
            extra = jnp.concatenate([jnp.stack(squares).reshape(-1), input_square.reshape(1)])
            extra = jnp.pad(extra, (0, inner - extra.shape[0]))[None]
            shared = rows_sum(jnp.concatenate(
                [extra] + [gain.reshape(-1, inner) for gain in gains[1:]], axis=0))
            own_count = smalls[l].shape[0]
            small = jnp.concatenate([smalls[l], shared], axis=0)
            small = jnp.pad(small, ((0, -small.shape[0] % 8), (0, 0)))
            normed_part, thins, out, stacked_last = lax.optimization_barrier((normed_part, thins, out, stacked_last))
            change, gains[l], thick, small = joint_sums(
                normed_part, base, layer.gain, [rows(thick[0]), rows(jnp.concatenate(thins, axis=1))], (0, inner),
                small, l)
            scattered[l].append(thick[0])
            smalls[l], rest = small[:own_count], small[own_count:]
        grad = grad + change
        grad_low = grad.astype(jnp.bfloat16)
        if l:
            grad_low = lax.optimization_barrier(grad_low)
    first_gain = blk_sum(rows_sum(gains[0].reshape(-1, inner)))
    input_grad = restore(grad_low)

    small = jnp.stack(smalls)
    gain_rows = first_gain.shape[0] * layer_total
    gain_grad = jnp.concatenate([first_gain, rest[1:1 + gain_rows - first_gain.shape[0]]], axis=0)
    gain_grad = gain_grad.reshape(layer_total, width)
    taps = weights[2].shape[1]
    row_total = tokens.shape[0] * tokens.shape[1] * width * blocks
    squares = rest[0] / row_total
    rms_stats = jnp.sqrt(squares[:2 * layer_total]).reshape(layer_total, 2)
    input_rms = jnp.sqrt(squares[2 * layer_total:2 * layer_total + 1])
    pieces, at = [], 0
    for cut in cuts:
        pieces.append(thick[1][at:at + cut])
        at += cut
    into_out = jnp.stack([jnp.stack([part[2], part[1]], axis=1) for part in scattered[:-1]] + [stacked_last])

    def stacked(parts_):
        return jnp.stack([jnp.moveaxis(part, 0, 1) for part in parts_])[:, :, None]

    return (
        out,
        stacked(finals),
        stacked(tails),
        input_grad,
        stacked(starts),
        stacked(prefixes),
        gain_grad,
        into_out,
        small[:, :taps],
        small[:, taps],
        jnp.stack([part[:weights[4].shape[-1] // blocks].T for part in pieces[0::2]]),
        jnp.stack([part[:RANK // blocks] for part in pieces[1::2]]),
        small[:, taps + 1],
        small[:, taps + 2:-1],
        small[:, -1],
        jnp.stack([part[0].T for part in scattered]),
        rms_stats,
        input_rms,
    )


def solution(mesh):
    placed = (
        P(None, "blk", None),
        P(None, "blk", None),
        P(),
        P(None, None, None, "tensor"),
        P(None, None, "tensor"),
        P(None, "tensor"),
        P(None, "tensor", None),
        P(None, None, "tensor"),
        P(None, "tensor"),
        P(None, None, "tensor"),
        P(None, "tensor"),
        P(None, "tensor", None),
        P(None, None, None, "tensor"),
        P(None, None, None, "tensor"),
    )
    return jax.shard_map(
        on_device,
        mesh=mesh,
        in_specs=placed,
        out_specs=(
            P(None, "blk", None),
            P(None, None, "blk", None, "tensor"),
            P(None, None, "blk", None, "tensor"),
            P(None, "blk", None),
            P(None, None, "blk", None, "tensor"),
            P(None, None, "blk", None, "tensor"),
            P(),
            P(None, "blk", None, "tensor"),
            P(None, None, "tensor"),
            P(None, "tensor"),
            P(None, "tensor", "blk"),
            P(None, "blk", "tensor"),
            P(None, "tensor"),
            P(None, None, "tensor"),
            P(None, "tensor"),
            P(None, "tensor", "blk"),
            P(),
            P(),
        ),
        check_vma=False,
    )
```

```python
import math
from functools import partial
import jax
import jax.numpy as jnp
from jax import lax
from jax.experimental import pallas as pl
from jax.experimental.pallas import tpu as pltpu

from jax.sharding import PartitionSpec as P

STATE = 16
RANK = 128
EPSILON = 1e-05
LANES=128
LOG2E=math.log2(math.e)

def cost(step, passes):
    return pl.CostEstimate(flops=passes * STATE * step.size, bytes_accessed=passes * STATE * step.size, transcendentals=0)

def cp(limit):
    return pltpu.CompilerParams(dimension_semantics=("arbitrary",), vmem_limit_bytes=limit)

def spread(ref_value, out, first):
    for n in range(STATE):
        for t in range(out.shape[0]):
            out[t, n] = jnp.broadcast_to(ref_value[t, :, first + n:first + n + 1], out.shape[2:])

def rates(rate_ref, lanes, n):
    return jnp.broadcast_to(rate_ref[pl.ds(n, 1), lanes], (8, LANES))

def end_body(blocks, width, held, step_ref, push_ref, coef_ref, rate_ref, end_ref, write):
    @pl.when(pl.program_id(0) == 0)
    def _():
        end_ref[...] = jnp.zeros_like(end_ref)
    spread(coef_ref, write, 0)
    def group(g, _):
        cols = [pl.ds(pl.multiple_of((g * width + k) * LANES, LANES), LANES) for k in range(width)]
        for low in range(0, STATE, held):
            span = range(low, low + held)
            state = {(k, n): end_ref[n, :, cols[k]] for k in range(width) for n in span}
            rate = {(k, n): rates(rate_ref, cols[k], n) for k in range(width) for n in span}
            for t in range(step_ref.shape[0]):
                step = [step_ref[t, :, c] for c in cols]
                push = [push_ref[t, :, c] for c in cols]
                for n in span:
                    w = write[t, n]
                    for k in range(width):
                        state[k, n] = jnp.exp2(step[k] * rate[k, n]) * state[k, n] + push[k] * w
            for k in range(width):
                for n in span:
                    end_ref[n, :, cols[k]] = state[k, n]
        return 0
    lax.fori_loop(0, blocks // width, group, 0)

def end_states(step, push, coef, rate, tb=16, width=2, held=8, limit=48*2**20):
    T, _, C = step.shape
    return pl.pallas_call(
        partial(end_body, C // LANES, width, held),
        grid=(T // tb,),
        in_specs=[pl.BlockSpec((tb, 8, C), lambda i: (i, 0, 0)), pl.BlockSpec((tb, 8, C), lambda i: (i, 0, 0)),
                  pl.BlockSpec((tb, 8, 2 * STATE), lambda i: (i, 0, 0)), pl.BlockSpec((STATE, C), lambda i: (0, 0))],
        out_specs=pl.BlockSpec((STATE, 8, C), lambda i: (0, 0, 0)),
        out_shape=jax.ShapeDtypeStruct((STATE, 8, C), jnp.float32),
        scratch_shapes=[pltpu.VMEM((tb, STATE, 8, LANES), jnp.float32)],
        compiler_params=cp(limit), cost_estimate=cost(step, 4), name="end_states")(step, push, coef, rate)

def scan_body(blocks, width, held, step_ref, push_ref, coef_ref, rate_ref, start_ref, out_ref, states_ref, final_ref, write, read):
    @pl.when(pl.program_id(0) == 0)
    def _():
        final_ref[...] = start_ref[...]
    spread(coef_ref, write, 0)
    spread(coef_ref, read, STATE)
    def group(g, _):
        cols = [pl.ds(pl.multiple_of((g * width + k) * LANES, LANES), LANES) for k in range(width)]
        for low in range(0, STATE, held):
            span = range(low, low + held)
            state = {(k, n): final_ref[n, :, cols[k]] for k in range(width) for n in span}
            rate = {(k, n): rates(rate_ref, cols[k], n) for k in range(width) for n in span}
            for t in range(step_ref.shape[0]):
                step = [step_ref[t, :, c] for c in cols]
                push = [push_ref[t, :, c] for c in cols]
                total = [None] * width
                for n in span:
                    w, r = write[t, n], read[t, n]
                    for k in range(width):
                        s = jnp.exp2(step[k] * rate[k, n]) * state[k, n] + push[k] * w
                        state[k, n] = s
                        states_ref[t, n, :, cols[k]] = s
                        total[k] = r * s if total[k] is None else total[k] + r * s
                for k in range(width):
                    if low == 0:
                        out_ref[t, :, cols[k]] = total[k]
                    else:
                        out_ref[t, :, cols[k]] += total[k]
            for k in range(width):
                for n in span:
                    final_ref[n, :, cols[k]] = state[k, n]
        return 0
    lax.fori_loop(0, blocks // width, group, 0)

def scan_forward(step, push, coef, rate, start, tb=16, width=2, held=8, limit=48*2**20):
    T, _, C = step.shape
    row = pl.BlockSpec((tb, 8, C), lambda i: (i, 0, 0))
    whole = pl.BlockSpec((STATE, 8, C), lambda i: (0, 0, 0))
    f32 = jnp.float32
    return pl.pallas_call(
        partial(scan_body, C // LANES, width, held),
        grid=(T // tb,),
        in_specs=[row, row, pl.BlockSpec((tb, 8, 2 * STATE), lambda i: (i, 0, 0)), pl.BlockSpec((STATE, C), lambda i: (0, 0)), whole],
        out_specs=[row, pl.BlockSpec((tb, STATE, 8, C), lambda i: (i, 0, 0, 0)), whole],
        out_shape=[jax.ShapeDtypeStruct((T, 8, C), f32), jax.ShapeDtypeStruct((T, STATE, 8, C), f32),
                   jax.ShapeDtypeStruct((STATE, 8, C), f32)],
        scratch_shapes=[pltpu.VMEM((tb, STATE, 8, LANES), f32)] * 2,
        compiler_params=cp(limit), cost_estimate=cost(step, 7), name="scan_forward")(step, push, coef, rate, start)

def start_body(blocks, width, held, step_ref, grad_ref, coef_ref, rate_ref, start_ref, read):
    @pl.when(pl.program_id(0) == 0)
    def _():
        start_ref[...] = jnp.zeros_like(start_ref)
    spread(coef_ref, read, STATE)
    def group(g, _):
        cols = [pl.ds(pl.multiple_of((g * width + k) * LANES, LANES), LANES) for k in range(width)]
        for low in range(0, STATE, held):
            span = range(low, low + held)
            state = {(k, n): start_ref[n, :, cols[k]] for k in range(width) for n in span}
            rate = {(k, n): rates(rate_ref, cols[k], n) for k in range(width) for n in span}
            for t in reversed(range(step_ref.shape[0])):
                step = [step_ref[t, :, c] for c in cols]
                grad = [grad_ref[t, :, c] for c in cols]
                for n in span:
                    r = read[t, n]
                    for k in range(width):
                        state[k, n] = jnp.exp2(step[k] * rate[k, n]) * (state[k, n] + r * grad[k])
            for k in range(width):
                for n in span:
                    start_ref[n, :, cols[k]] = state[k, n]
        return 0
    lax.fori_loop(0, blocks // width, group, 0)

def start_grads(step, grad, coef, rate, tb=16, width=2, held=8, limit=48*2**20):
    T, _, C = step.shape
    last = T // tb - 1
    row = pl.BlockSpec((tb, 8, C), lambda i: (last - i, 0, 0))
    return pl.pallas_call(
        partial(start_body, C // LANES, width, held),
        grid=(T // tb,),
        in_specs=[row, row, pl.BlockSpec((tb, 8, 2 * STATE), lambda i: (last - i, 0, 0)), pl.BlockSpec((STATE, C), lambda i: (0, 0))],
        out_specs=pl.BlockSpec((STATE, 8, C), lambda i: (0, 0, 0)),
        out_shape=jax.ShapeDtypeStruct((STATE, 8, C), jnp.float32),
        scratch_shapes=[pltpu.VMEM((tb, STATE, 8, LANES), jnp.float32)],
        compiler_params=cp(limit), cost_estimate=cost(step, 4), name="start_grads")(step, grad, coef, rate)

def back_body(blocks, width, held, step_ref, push_ref, grad_ref, coef_ref, rate_ref, states_ref, prior_ref, begin_ref, end_ref,
              decay_out, push_out, coef_out, start_ref, speed_ref, write, read, write_sum, read_sum):
    @pl.when(pl.program_id(0) == 0)
    def _():
        start_ref[...] = end_ref[...]
        speed_ref[...] = jnp.zeros_like(speed_ref)
    spread(coef_ref, write, 0)
    spread(coef_ref, read, STATE)
    tb = step_ref.shape[0]
    begins = pl.program_id(0) == pl.num_programs(0) - 1
    def group(g, first):
        cols = [pl.ds((g * width + k) * LANES if first else pl.multiple_of((g * width + k) * LANES, LANES), LANES)
                for k in range(width)]
        for low in range(0, STATE, held):
            span = range(low, low + held)
            carry = {(k, n): start_ref[n, :, cols[k]] for k in range(width) for n in span}
            speed = {(k, n): speed_ref[n, :, cols[k]] for k in range(width) for n in span}
            rate = {(k, n): rates(rate_ref, cols[k], n) for k in range(width) for n in span}
            enter = {(k, n): jnp.where(begins, begin_ref[n, :, cols[k]], prior_ref[0, n, :, cols[k]])
                     for k in range(width) for n in span}
            for t in reversed(range(tb)):
                step = [step_ref[t, :, c] for c in cols]
                push = [push_ref[t, :, c] for c in cols]
                grad = [grad_ref[t, :, c] for c in cols]
                decays = [None] * width
                pushes = [None] * width
                for n in span:
                    w, r = write[t, n], read[t, n]
                    wsum, rsum = None, None
                    for k in range(width):
                        before = states_ref[t - 1, n, :, cols[k]] if t else enter[k, n]
                        back = carry[k, n] + r * grad[k]
                        onward = jnp.exp2(step[k] * rate[k, n]) * back
                        carry[k, n] = onward
                        q = onward * before
                        speed[k, n] = speed[k, n] + step[k] * q
                        rq, bw = rate[k, n] * q, back * w
                        decays[k] = rq if decays[k] is None else decays[k] + rq
                        pushes[k] = bw if pushes[k] is None else pushes[k] + bw
                        bp, gs = back * push[k], grad[k] * states_ref[t, n, :, cols[k]]
                        wsum = bp if wsum is None else wsum + bp
                        rsum = gs if rsum is None else rsum + gs
                    if first:
                        write_sum[t, n] = wsum
                        read_sum[t, n] = rsum
                    else:
                        write_sum[t, n] += wsum
                        read_sum[t, n] += rsum
                for k in range(width):
                    if low == 0:
                        decay_out[t, :, cols[k]] = decays[k]
                        push_out[t, :, cols[k]] = pushes[k]
                    else:
                        decay_out[t, :, cols[k]] += decays[k]
                        push_out[t, :, cols[k]] += pushes[k]
            for k in range(width):
                for n in span:
                    start_ref[n, :, cols[k]] = carry[k, n]
                    speed_ref[n, :, cols[k]] = speed[k, n]
        return 0
    group(0, True)
    lax.fori_loop(1, blocks // width, lambda g, _: group(g, False), 0)
    lane = lax.broadcasted_iota(jnp.int32, (8, 2 * STATE), 1)
    for t in range(tb):
        row = jnp.zeros((8, 2 * STATE), jnp.float32)
        for n in range(STATE):
            row = jnp.where(lane == n, jnp.sum(write_sum[t, n], axis=-1, keepdims=True), row)
            row = jnp.where(lane == STATE + n, jnp.sum(read_sum[t, n], axis=-1, keepdims=True), row)
        coef_out[t] = row

def scan_backward(step, push, grad, coef, rate, states, begin, end, tb=8, width=2, held=4, limit=48*2**20):
    T, _, C = step.shape
    last = T // tb - 1
    f32 = jnp.float32
    row = pl.BlockSpec((tb, 8, C), lambda i: (last - i, 0, 0))
    thin = pl.BlockSpec((tb, 8, 2 * STATE), lambda i: (last - i, 0, 0))
    whole = pl.BlockSpec((STATE, 8, C), lambda i: (0, 0, 0))
    return pl.pallas_call(
        partial(back_body, C // LANES, width, held),
        grid=(T // tb,),
        in_specs=[row, row, row, thin, pl.BlockSpec((STATE, C), lambda i: (0, 0)),
                  pl.BlockSpec((tb, STATE, 8, C), lambda i: (last - i, 0, 0, 0)),
                  pl.BlockSpec((1, STATE, 8, C), lambda i: (jnp.maximum((last - i) * tb - 1, 0), 0, 0, 0)), whole, whole],
        out_specs=[row, row, thin, whole, whole],
        out_shape=[jax.ShapeDtypeStruct((T, 8, C), f32)] * 2 + [jax.ShapeDtypeStruct((T, 8, 2 * STATE), f32)]
          + [jax.ShapeDtypeStruct((STATE, 8, C), f32)] * 2,
        scratch_shapes=[pltpu.VMEM((tb, STATE, 8, LANES), f32)] * 4,
        compiler_params=cp(limit), cost_estimate=cost(step, 13), name="scan_backward")(step, push, grad, coef, rate, states, states, begin, end)


HALVES_OF_CHIP = 2


def silu_slope(argument):
    sigmoid_value = jax.nn.sigmoid(argument)
    return sigmoid_value * (1.0 + argument * (1.0 - sigmoid_value))


def half_of(array, index):
    size = array.shape[0] // 2
    return lax.dynamic_slice_in_dim(array, index * size, size, 0)


def ordered(index, mine, other):
    first = jnp.where(index == 0, mine, other)
    second = jnp.where(index == 0, other, mine)
    return jnp.concatenate([first, second], axis=0)


BESIDE = [(0, 1), (1, 0), (2, 3), (3, 2)]
ACROSS = [(0, 2), (2, 0), (1, 3), (3, 1)]


def paired():
    return lax.axis_size("tensor") == 4


def tensor_sum(array):
    if not paired():
        return lax.psum(array, "tensor")
    core = lax.axis_index("tensor") % 2
    half = half_of(array, core) + lax.ppermute(half_of(array, 1 - core), "tensor", BESIDE)
    half = half + lax.ppermute(half, "tensor", ACROSS)
    return ordered(core, half, lax.ppermute(half, "tensor", BESIDE))


def pair_body(chunks, count, *refs):
    ins, outs, refs = refs[:count], refs[count:2 * count], refs[2 * count:]
    buffers, sems = refs[:5 * count], refs[5 * count:]
    blk, tensor = lax.axis_index("blk"), lax.axis_index("tensor")
    core = tensor % 2
    beside, far = (blk, tensor + 1 - 2 * core), (blk, (tensor + 2) % 4)
    barrier = pltpu.get_barrier_semaphore()
    for device in (beside, far):
        pl.semaphore_signal(barrier, inc=1, device_id=device, device_id_type=pl.DeviceIdType.MESH)
    pl.semaphore_wait(barrier, 2)
    parts = [(k, i) for k in range(chunks) for i in range(count)]
    firsts, seconds, thirds = {}, {}, {}

    def rows_of(i, k, side):
        size = ins[i].shape[0] // 2 // chunks
        return pl.ds(pl.multiple_of((side * chunks + k) * size, size), size)

    for at, (k, i) in enumerate(parts):
        firsts[k, i] = remote(ins[i].at[rows_of(i, k, 1 - core)], buffers[5 * i].at[k], sems[0], sems[1], at, beside)
        firsts[k, i].start()
    for at, (k, i) in enumerate(parts):
        firsts[k, i].wait_recv()
        buffers[5 * i + 1][k] = ins[i][rows_of(i, k, core), :] + buffers[5 * i][k]
        seconds[k, i] = remote(buffers[5 * i + 1].at[k], buffers[5 * i + 2].at[k], sems[2], sems[3], at, far)
        seconds[k, i].start()
    for at, (k, i) in enumerate(parts):
        seconds[k, i].wait_recv()
        total = buffers[5 * i + 1][k] + buffers[5 * i + 2][k]
        buffers[5 * i + 3][k] = total
        outs[i][rows_of(i, k, core), :] = total
        thirds[k, i] = remote(buffers[5 * i + 3].at[k], buffers[5 * i + 4].at[k], sems[4], sems[5], at, beside)
        thirds[k, i].start()
    for k, i in parts:
        thirds[k, i].wait_recv()
        outs[i][rows_of(i, k, 1 - core), :] = buffers[5 * i + 4][k]
    for group in (firsts, seconds, thirds):
        for copy in group.values():
            copy.wait_send()


def pair_sums(arrays, collective_id):
    if not paired() or lax.axis_size("blk") != 8:
        return [lax.psum(array, "tensor") for array in arrays]
    chunks, count = 2, len(arrays)
    f32 = jnp.float32
    spec = pl.BlockSpec(memory_space=pltpu.VMEM)
    scratch = []
    for array in arrays:
        scratch += [pltpu.VMEM((chunks, array.shape[0] // 2 // chunks, array.shape[1]), f32)] * 5
    return pl.pallas_call(
        partial(pair_body, chunks, count),
        in_specs=[spec] * count,
        out_specs=[spec] * count,
        out_shape=[jax.ShapeDtypeStruct(array.shape, f32) for array in arrays],
        scratch_shapes=scratch + [pltpu.SemaphoreType.DMA((chunks * count,))] * 6,
        compiler_params=pltpu.CompilerParams(
            collective_id=collective_id, has_side_effects=True, vmem_limit_bytes=24 * 2**20),
        cost_estimate=pl.CostEstimate(flops=0, bytes_accessed=40 * 2**20, transcendentals=0),
        name="pair_sums",
    )(*arrays)


def own_rows(array):
    if not paired():
        size = array.shape[0] // lax.axis_size("tensor")
        return lax.dynamic_slice_in_dim(array, lax.axis_index("tensor") * size, size, 0)
    return half_of(array, lax.axis_index("tensor") % 2)


def core_sum(array):
    if not paired():
        return lax.psum_scatter(array, "tensor", scatter_dimension=0, tiled=True)
    core = lax.axis_index("tensor") % 2
    return half_of(array, core) + lax.ppermute(half_of(array, 1 - core), "tensor", BESIDE)


def across(half):
    if not paired():
        return jnp.zeros_like(half)
    return lax.ppermute(half, "tensor", ACROSS)


def all_rows(array, finish=lambda part: part):
    if not paired():
        return finish(lax.optimization_barrier(lax.all_gather(array, "tensor", tiled=True)))
    other = lax.optimization_barrier(lax.ppermute(array, "tensor", BESIDE))
    return ordered(lax.axis_index("tensor") % 2, finish(array), finish(other))


def rows_sum(array):
    if not paired():
        return lax.psum(array, "tensor")
    return array + lax.ppermute(array, "tensor", BESIDE)


def blk_sum(array):
    if lax.axis_size("blk") != 8:
        return lax.psum(array, "blk")
    for bit in (1, 2, 4):
        array = array + lax.ppermute(array, "blk", [(j, j ^ bit) for j in range(8)])
    return array


def blk_scatter(array):
    return lax.psum_scatter(array, "blk", scatter_dimension=0, tiled=True)


def add_rows(total, other, count):
    slab = 8

    def body(i, _):
        at = pl.ds(pl.multiple_of(i * slab, slab), slab)
        total[at, :] = total[at, :] + other[at, :]
        return 0

    lax.fori_loop(0, count // slab, body, 0)


def remote(src, dst, sends, recvs, at, device):
    return pltpu.make_async_remote_copy(
        src_ref=src, dst_ref=dst, send_sem=sends.at[at], recv_sem=recvs.at[at], device_id=device,
        device_id_type=pl.DeviceIdType.MESH)


def joint_body(plan, chunks, sum_ref, base_ref, gain_ref, *refs):
    count = 1 + max(job[0] for job in plan)
    thick_refs, small_ref, refs = refs[:count], refs[count], refs[count + 1:]
    change_out, gain_out, refs = refs[0], refs[1], refs[2:]
    thick_outs, small_out, refs = refs[:count], refs[count], refs[1 + count:]
    own_half, core_half, far_half, base, came, small_in, refs = refs[0], refs[1], refs[2], refs[3], refs[4], refs[5], refs[6:]
    gain_in, gain_send, gain_recv, refs = refs[0], refs[1], refs[2], refs[3:]
    core_send, core_recv, far_send, far_recv, back_send, back_recv, local_sem, base_sem, out_sem, came_sem = refs[:10]
    small_send, small_recv = refs[10:12]
    refs = refs[12:]
    blk, tensor = lax.axis_index("blk"), lax.axis_index("tensor")
    bits = {1: blk % 2, 2: (blk // 2) % 2, 4: blk // 4}
    core = tensor % 2
    beside = (blk, tensor + 1 - 2 * core)
    far = (blk, (tensor + 2) % 4)
    peers = {bit: (blk + bit - 2 * bit * bits[bit], tensor) for bit in bits}
    barrier = pltpu.get_barrier_semaphore()
    for device in (beside, far, peers[1], peers[2], peers[4]):
        pl.semaphore_signal(barrier, inc=1, device_id=device, device_id_type=pl.DeviceIdType.MESH)
    pl.semaphore_wait(barrier, 5)

    rows_each, width = own_half.shape[1:]
    smalls, core_copies, local_copies, base_copies, far_copies, back_copies, outs = [], [], [], [], [], [], []

    def small_step(i):
        copy = remote(small_out, small_in.at[i], small_send, small_recv, i, peers[1 << i])
        copy.start()
        smalls.append(copy)

    def small_end(i):
        smalls[i].wait()
        small_out[...] = small_out[...] + small_in[i]

    small_out[...] = small_ref[...]
    small_step(0)
    for k in range(chunks):
        give = pl.ds(pl.multiple_of((1 - core) * rows_each * chunks + k * rows_each, rows_each), rows_each)
        keep = pl.ds(pl.multiple_of(core * rows_each * chunks + k * rows_each, rows_each), rows_each)
        copy = remote(sum_ref.at[give], core_half.at[k], core_send, core_recv, k, beside)
        copy.start()
        core_copies.append(copy)
        copy = pltpu.make_async_copy(sum_ref.at[keep], own_half.at[k], local_sem.at[k])
        copy.start()
        local_copies.append(copy)
        copy = pltpu.make_async_copy(base_ref.at[pl.ds(k * rows_each, rows_each)], base.at[k], base_sem.at[k])
        copy.start()
        base_copies.append(copy)
    gain_out[...] = jnp.zeros_like(gain_out)

    class Job:
        def __init__(self, which, low, wide, order, refs):
            (self.own, self.first, self.second, self.third, self.sems) = refs[0], refs[1], refs[2], refs[3], refs[4:]
            self.order = order
            self.count = thick_refs[which].shape[3]
            self.out = thick_outs[which].at[:, pl.ds(low, wide)]
            lead, (u, v) = bits[order[0]], (bits[order[1]], bits[order[2]])
            self.parts = [(1 - u, 1 - v), (1 - u, v), (u, 1 - v), (u, v)]
            self.firsts, self.owns, self.seconds = [], [], []
            for i, part in enumerate(self.parts):
                at = {order[1]: part[0], order[2]: part[1]}

                def source(mine):
                    index = dict(at)
                    index[order[0]] = mine
                    return thick_refs[which].at[index[4], index[2], index[1], :, pl.ds(low, wide)]

                copy = remote(source(1 - lead), self.first.at[part], self.sems[0], self.sems[1], i, peers[order[0]])
                copy.start()
                self.firsts.append(copy)
                copy = pltpu.make_async_copy(source(lead), self.own.at[part], self.sems[2].at[i])
                copy.start()
                self.owns.append(copy)

        def first_end(self, i):
            self.owns[i].wait()
            self.firsts[i].wait_recv()
            add_rows(self.own.at[self.parts[i]], self.first.at[self.parts[i]], self.count)
            if i < 2:
                copy = remote(self.own.at[self.parts[i]], self.second.at[i], self.sems[3], self.sems[4], i,
                              peers[self.order[1]])
                copy.start()
                self.seconds.append(copy)
                return
            self.seconds[i - 2].wait_recv()
            add_rows(self.own.at[self.parts[i]], self.second.at[i - 2], self.count)
            if i == 2:
                self.last = remote(self.own.at[self.parts[i]], self.third, self.sems[5], self.sems[6], 0,
                                   peers[self.order[2]])
                self.last.start()

        def end(self):
            self.last.wait_recv()
            add_rows(self.own.at[self.parts[3]], self.third, self.count)
            copy = pltpu.make_async_copy(self.own.at[self.parts[3]], self.out, self.sems[7].at[0])
            copy.start()
            outs.append(copy)

        def sent(self):
            return self.firsts + self.seconds + [self.last]

    jobs = [Job(*job, refs[12 * i:12 * i + 12]) for i, job in enumerate(plan)]
    gains = []

    def gain_step(i):
        device = beside if i == 0 else peers[1 << (i - 1)]
        copy = remote(gain_out, gain_in.at[i], gain_send, gain_recv, i, device)
        copy.start()
        gains.append(copy)

    def gain_end(i):
        gains[i].wait()
        gain_out[...] = gain_out[...] + gain_in[i]

    def core_end(k):
        local_copies[k].wait()
        core_copies[k].wait()
        add_rows(own_half.at[k], core_half.at[k], rows_each)
        copy = remote(own_half.at[k], far_half.at[k], far_send, far_recv, k, far)
        copy.start()
        far_copies.append(copy)

    def far_end(k):
        far_copies[k].wait_recv()
        base_copies[k].wait()

        def slab(i, _):
            at = pl.ds(pl.multiple_of(i * 8, 8), 8)
            residual = base[k, at, :]
            normed_grad = far_half[k, at, :] + own_half[k, at, :]
            q = lax.rsqrt(jnp.sum(residual * residual, axis=-1, keepdims=True) * (1.0 / width) + EPSILON)
            part = residual * q
            gain_out[...] += normed_grad * part
            scaled = normed_grad * gain_ref[...]
            inner = jnp.sum(scaled * part, axis=-1, keepdims=True) * (1.0 / width)
            far_half[k, at, :] = q * (scaled - part * inner)
            return 0

        lax.fori_loop(0, rows_each // 8, slab, 0)
        copy = remote(far_half.at[k], came.at[k], back_send, back_recv, k, beside)
        copy.start()
        back_copies.append(copy)
        own_rows_at = pl.ds(pl.multiple_of((core * chunks + k) * rows_each, rows_each), rows_each)
        copy = pltpu.make_async_copy(far_half.at[k], change_out.at[own_rows_at], out_sem.at[k])
        copy.start()
        outs.append(copy)

    def back_end(k):
        back_copies[k].wait_recv()
        other_rows_at = pl.ds(pl.multiple_of(((1 - core) * chunks + k) * rows_each, rows_each), rows_each)
        copy = pltpu.make_async_copy(came.at[k], change_out.at[other_rows_at], came_sem.at[k])
        copy.start()
        outs.append(copy)

    for k in range(chunks):
        core_end(k)
    small_end(0)
    small_step(1)
    for i in range(4):
        for job in jobs:
            job.first_end(i)
        if i in (0, 1):
            small_end(i + 1)
            if i == 0:
                small_step(2)
        far_end(i)
    gain_step(0)
    for k in range(chunks):
        back_end(k)
    for i in range(4):
        gain_end(i)
        if i < 3:
            gain_step(i + 1)
    for job in jobs:
        job.end()
    for copy in far_copies + back_copies + [each for job in jobs for each in job.sent()]:
        copy.wait_send()
    for copy in outs:
        copy.wait()


def joint_sums(array, base, gain, thick, late, small, collective_id):
    if not paired() or lax.axis_size("blk") != 8:
        normed_grad = lax.psum_scatter(array, "tensor", scatter_dimension=0, tiled=True)
        gain_grad, change = norm_back(gain, normed_grad, base, inverse_rms(base))
        return all_rows(change), lax.psum(rows_sum(gain_grad), "blk"), [blk_scatter(part) for part in thick], lax.psum(small, "blk")
    R, N = array.shape
    C = thick[0].shape[1]
    chunks = 4
    f32 = jnp.float32
    dma = pltpu.SemaphoreType.DMA
    any_spec = pl.BlockSpec(memory_space=pl.ANY)
    vmem_spec = pl.BlockSpec(memory_space=pltpu.VMEM)
    plan = [(i, 0, C - each, (1, 2, 4)) for i, each in enumerate(late) if each < C]
    plan += [(i, C - each, each, (2, 4, 1)) for i, each in enumerate(late) if each]
    scratch = []
    for which, _, wide, _ in plan:
        count = thick[which].shape[0] // 8
        scratch += [pltpu.VMEM((2, 2, count, wide), f32), pltpu.VMEM((2, 2, count, wide), f32),
                    pltpu.VMEM((2, count, wide), f32), pltpu.VMEM((count, wide), f32),
                    dma((4,)), dma((4,)), dma((4,)), dma((2,)), dma((2,)), dma((1,)), dma((1,)), dma((1,))]
    half = pltpu.VMEM((chunks, R // 2 // chunks, N), f32)
    out = pl.pallas_call(
        partial(joint_body, plan, chunks),
        in_specs=[any_spec, any_spec, vmem_spec] + [any_spec] * len(thick) + [vmem_spec],
        out_specs=[any_spec, vmem_spec] + [any_spec] * len(thick) + [vmem_spec],
        out_shape=[jax.ShapeDtypeStruct((R, N), f32), jax.ShapeDtypeStruct((8, N), f32)]
        + [jax.ShapeDtypeStruct((part.shape[0] // 8, C), f32) for part in thick]
        + [jax.ShapeDtypeStruct(small.shape, f32)],
        scratch_shapes=[half] * 5 + [pltpu.VMEM((3,) + small.shape, f32), pltpu.VMEM((4, 8, N), f32), dma((4,)), dma((4,))]
        + [dma((chunks,))] * 10 + [dma((3,)), dma((3,))] + scratch,
        compiler_params=pltpu.CompilerParams(
            collective_id=collective_id, has_side_effects=True, vmem_limit_bytes=52 * 2**20),
        cost_estimate=pl.CostEstimate(flops=0, bytes_accessed=50 * R * N * 4, transcendentals=0),
        name="joint_sums",
    )(array, base, gain[None], *[part.reshape(2, 2, 2, part.shape[0] // 8, C) for part in thick], small)
    return out[0], jnp.sum(out[1], axis=0), list(out[2:-1]), out[-1]


def neighbour(value, steps):
    count = lax.axis_size("blk")
    first, last = max(0, -steps), min(count, count - steps)
    return lax.ppermute(value, "blk", [(j, j + steps) for j in range(first, last)])


def entering_any(total, local, rate, first, reverse):
    peers, index = lax.axis_size("blk"), lax.axis_index("blk")
    totals, locals_ = lax.all_gather(total, "blk"), lax.all_gather(local, "blk")

    def step(k, state):
        at = peers - 1 - k if reverse else k
        reached = at > index if reverse else at < index
        return jnp.where(reached, jnp.exp2(totals[at][None] * rate) * state + locals_[at], state)

    return lax.fori_loop(0, peers, step, first)


def hop_body(reverses, groups, total_ref, rate_ref, *refs):
    ways = len(reverses)
    locals_, first_ref, refs = refs[:ways], refs[ways], refs[ways + 1:]
    outs, refs = refs[:ways], refs[ways:]
    beside_total, total_send, total_recv, refs = refs[0], refs[1], refs[2], refs[3:]
    blk, tensor = lax.axis_index("blk"), lax.axis_index("tensor")
    y, z = blk % 2, blk // 2
    beside = (blk + 1 - 2 * y, tensor)
    up, down = ((blk + 2) % 8, tensor), ((blk + 6) % 8, tensor)
    barrier = pltpu.get_barrier_semaphore()

    def greet(device):
        pl.semaphore_signal(barrier, inc=1, device_id=device, device_id_type=pl.DeviceIdType.MESH)

    greet(beside)
    pl.when(z < 3)(lambda: greet(up))
    pl.when(z > 0)(lambda: greet(down))
    pl.semaphore_wait(barrier, 3 - z // 3 - (3 - z) // 3)

    total = total_ref[...]
    copy_total = remote(total_ref, beside_total, total_send, total_recv, 0, beside)
    copy_total.start()
    size = STATE // 2 // groups

    class Way:
        def __init__(self, reverse, local, out, refs):
            self.own, self.other, self.came, self.goes, self.gives, self.gets = refs[:6]
            self.sems, self.out, self.reverse = refs[6:], out, reverse
            self.y, self.z = (1 - y, 3 - z) if reverse else (y, z)
            self.following = down if reverse else up
            self.at_a, self.begins = self.y == 0, self.z == 0
            self.firsts = []
            for n in range(STATE):
                value = local[n]
                if not reverse:
                    decay = jnp.exp2(total * rate_ref[pl.ds(n, 1), :])
                    value = value + jnp.where(jnp.logical_and(self.begins, self.at_a), decay * first_ref[n], 0.0)
                self.own[n] = value
            for k in range(groups):
                give = pl.ds((1 - self.y) * (STATE // 2) + k * size, size)
                copy = remote(self.own.at[give], self.other.at[pl.ds(k * size, size)], self.sems[0], self.sems[1], k, beside)
                copy.start()
                self.firsts.append(copy)

        def chain(self, k):
            part = pl.ds(k * size, size)
            return remote(self.goes.at[part], self.came.at[part], self.sems[2], self.sems[3], k, self.following)

        def middle(self, k, total_a, total_b):
            self.firsts[k].wait()
            pl.when(self.z > 0)(lambda: self.chain(k).wait_recv())
            for i in range(k * size, k * size + size):
                n = self.y * (STATE // 2) + i
                rate = rate_ref[pl.ds(n, 1), :]
                mine, got = self.own[n], self.other[i]
                local_a, local_b = jnp.where(self.at_a, mine, got), jnp.where(self.at_a, got, mine)
                enter = jnp.where(self.begins, 0.0, self.came[i])
                after_a = local_a + jnp.exp2(total_a * rate) * enter
                self.goes[i] = local_b + jnp.exp2(total_b * rate) * after_a
                self.gives[i] = jnp.where(self.at_a, after_a, enter)
                self.out[n] = jnp.where(self.at_a, enter, after_a)
            pl.when(self.z < 3)(lambda: self.chain(k).start())
            self.last(k).start()

        def last(self, k):
            part = pl.ds(k * size, size)
            return remote(self.gives.at[part], self.gets.at[part], self.sems[4], self.sems[5], k, beside)

        def all(self):
            other_total = beside_total[...]
            total_a, total_b = jnp.where(self.at_a, total, other_total), jnp.where(self.at_a, other_total, total)
            for k in range(groups):
                self.middle(k, total_a, total_b)

        def end(self, k):
            self.last(k).wait()
            for i in range(k * size, k * size + size):
                self.out[(1 - self.y) * (STATE // 2) + i] = self.gets[i]
            pl.when(self.z < 3)(lambda: self.chain(k).wait_send())

        def begin(self):
            starts = jnp.logical_and(self.begins, self.at_a)
            for n in range(STATE):
                first = 0.0 if self.reverse else first_ref[n]
                self.out[n] = jnp.where(starts, first, self.out[n])

    each = 6 + 6
    jobs = [Way(reverse, locals_[i], outs[i], refs[each * i:each * i + each]) for i, reverse in enumerate(reverses)]
    copy_total.wait()
    if ways == 1:
        jobs[0].all()
    else:

        def in_turn(order):
            for job in order:
                job.all()

        pl.when(z < 2)(lambda: in_turn(jobs))
        pl.when(z >= 2)(lambda: in_turn(jobs[::-1]))
    for k in range(groups):
        for job in jobs:
            job.end(k)
    for job in jobs:
        job.begin()


def hops(total, locals_, rate, first, reverses, collective_id):
    C = total.shape[-1]
    groups = 4
    f32 = jnp.float32
    dma = pltpu.SemaphoreType.DMA
    spec = pl.BlockSpec(memory_space=pltpu.VMEM)
    whole, half = pltpu.VMEM((STATE, 8, C), f32), pltpu.VMEM((STATE // 2, 8, C), f32)
    return pl.pallas_call(
        partial(hop_body, reverses, groups),
        in_specs=[spec] * (3 + len(locals_)),
        out_specs=[spec] * len(locals_),
        out_shape=[jax.ShapeDtypeStruct((STATE, 8, C), f32)] * len(locals_),
        scratch_shapes=[pltpu.VMEM((8, C), f32), dma((1,)), dma((1,))]
        + ([whole] + [half] * 5 + [dma((groups,))] * 6) * len(locals_),
        compiler_params=pltpu.CompilerParams(
            collective_id=collective_id, has_side_effects=True, vmem_limit_bytes=32 * 2**20),
        cost_estimate=pl.CostEstimate(flops=0, bytes_accessed=100 * total.size * 32, transcendentals=0),
        name="hops",
    )(total, rate, *locals_, first)


def rows(array):
    return array.reshape(-1, array.shape[-1])


def by_step(array):
    return array.reshape(-1, 8, array.shape[-1])


def dot32(left, right):
    return jnp.dot(left, right, preferred_element_type=jnp.float32)


def dot_t(left, right):
    return lax.dot_general(left, right, (((0,), (0,)), ((), ())), preferred_element_type=jnp.float32)


def dot_n(left, right):
    return lax.dot_general(left, right, (((1,), (1,)), ((), ())), preferred_element_type=jnp.float32)


def two_parts(array):
    high = lax.optimization_barrier(array.astype(jnp.bfloat16))
    return high, (array - high.astype(jnp.float32)).astype(jnp.bfloat16)


def split_parts(array, parts):
    return array.reshape(array.shape[:-2] + (parts, 8 // parts) + array.shape[-1:])


class Layer:
    def __init__(self, index, args):
        (norm_gain, in_weight, conv_weight, conv_bias, x_weight, dt_weight, dt_bias, decay_log,
         skip_weight, out_weight) = args
        self.gain = norm_gain[index]
        self.raw = in_weight[index] if index == 0 else None
        self.taps = conv_weight[index]
        self.shift = conv_bias[index]
        self.x = x_weight[index]
        self.dt = dt_weight[index]
        self.dt_bias = dt_bias[index]
        self.rate = -jnp.exp(decay_log[index])
        self.rate2 = self.rate * LOG2E
        self.skip = skip_weight[index]
        self.out = out_weight[index]


def inverse_rms(residual):
    return lax.rsqrt(jnp.mean(residual * residual, axis=-1, keepdims=True) + EPSILON)


def front(layer, normed, conv_first, parts, at_first, collective_id):
    mixed = jnp.einsum("rd,dkc->krc", normed, layer.raw, preferred_element_type=jnp.float32)
    values, gate = mixed[0], mixed[1]
    inner = values.shape[-1]
    count = values.shape[0]
    rim = layer.taps.shape[0] - 1
    tails = split_parts(by_step(values[count - 8 * rim:]), parts)
    arrived = jnp.where(at_first, conv_first, neighbour(tails[:, -1], 1))
    prefix = jnp.concatenate([arrived[:, None], tails[:, :-1]], axis=1).reshape(rim * 8, inner)
    window = jnp.concatenate([prefix, values], axis=0)
    conv_out = layer.shift + sum(layer.taps[k] * window[8 * k:8 * k + count] for k in range(rim + 1))
    inputs = lax.optimization_barrier(jax.nn.silu(conv_out).astype(jnp.bfloat16))
    ranks, coef = pair_sums(
        [dot32(inputs, layer.x[:, :RANK]), lax.dot_general(
            layer.x[:, RANK:], inputs, (((0,), (1,)), ((), ())), preferred_element_type=jnp.float32)], collective_id)
    dt_low = ranks.astype(jnp.bfloat16)
    coef = by_step(coef.T)
    step = jax.nn.softplus(dot32(dt_low, layer.dt) + layer.dt_bias)
    push = step * inputs.astype(jnp.float32)
    local = split_parts(end_states(by_step(step), by_step(push), coef, layer.rate2), parts)
    totals = split_parts(jnp.sum(by_step(step), axis=0), parts)
    return (window, gate, conv_out, inputs, dt_low, coef, step, push, totals), local, tails[:, -1]


def join(local, totals, rate, reverse):
    order = range(local.shape[1])
    order = list(reversed(order)) if reverse else list(order)
    joined, total = local[:, order[0]], totals[order[0]]
    for p in order[1:]:
        joined = local[:, p] + jnp.exp2(totals[p][None] * rate) * joined
        total = total + totals[p]
    return total, joined


def each_part(state, local, totals, rate, reverse):
    order = range(local.shape[1])
    order = list(reversed(order)) if reverse else list(order)
    states = {order[0]: state}
    for p, following in zip(order[:-1], order[1:]):
        states[following] = local[:, p] + jnp.exp2(totals[p][None] * rate) * states[p]
    state = jnp.stack([states[p] for p in range(local.shape[1])], axis=1)
    return state.reshape(STATE, 8, state.shape[-1])


def exchange(layer, locals_, totals, first, reverses, collective_id):
    rate = layer.rate2[:, None]
    if lax.axis_size("blk") == 8 and totals.shape[0] == 1:
        return hops(totals[0], [local[:, 0] for local in locals_], layer.rate2, first, reverses, collective_id)
    states = []
    for local, reverse in zip(locals_, reverses):
        total, joined = join(local, totals, rate, reverse)
        state = entering_any(total, joined, rate, jnp.zeros_like(first) if reverse else first, reverse)
        states.append(each_part(state, local, totals, rate, reverse))
    return states


def scanning(layer, kept, start):
    window, gate, conv_out, inputs, dt_low, coef, step, push, totals = kept
    scanned, states, final = scan_forward(by_step(step), by_step(push), coef, layer.rate2, start)
    result = rows(scanned) + layer.skip * inputs.astype(jnp.float32)
    gated = (result * jax.nn.silu(gate)).astype(jnp.bfloat16)
    return (result, gated, states, start), final


def back_gated(kept, grad_gated):
    gate = kept[1]
    return grad_gated, grad_gated * jax.nn.silu(gate)


def back_local(layer, kept, grad_result):
    window, gate, conv_out, inputs, dt_low, coef, step, push, totals = kept
    local = start_grads(by_step(step), by_step(grad_result), coef, layer.rate2)
    return split_parts(local, totals.shape[0])


def back_side(layer, kept, normed, scans, grads, grad_low):
    window, gate, conv_out, inputs, dt_low, coef, step, push, totals = kept
    result, gated, states, start = scans
    grad_gated, grad_result = grads
    inner = gate.shape[1]
    grad_gate = (grad_gated * result * silu_slope(gate)).astype(jnp.bfloat16)
    gate_grad = dot_t(normed, grad_gate)
    gate_through = dot_n(grad_gate, layer.into[:, inner:])
    skip_grad = jnp.sum(grad_result * inputs.astype(jnp.float32), axis=0)
    return gate_grad, gate_through, skip_grad


def back_scan(layer, kept, scans, grads, end):
    window, gate, conv_out, inputs, dt_low, coef, step, push, totals = kept
    result, gated, states, start = scans
    grad_gated, grad_result = grads
    return scan_backward(
        by_step(step), by_step(push), by_step(grad_result), coef, layer.rate2, states, start, end)


def back_rest(layer, kept, grads, scan_out, gate_through, collective_id):
    window, gate, conv_out, inputs, dt_low, coef, step, push, totals = kept
    grad_gated, grad_result = grads
    count, inner = gate.shape
    parts = totals.shape[0]
    rim = layer.taps.shape[0] - 1
    wide = inputs.astype(jnp.float32)
    decays, pushes, coef_grad, start_grad, speed = scan_out
    pushes = rows(pushes)
    step_grad = rows(decays) * (1.0 / LOG2E) + wide * pushes
    before_grad = step_grad * -jnp.expm1(-step)
    bias_grad = jnp.sum(before_grad, axis=0)
    decay_grad = layer.rate * jnp.sum(speed, axis=1)
    before_low = before_grad.astype(jnp.bfloat16)
    ranks_grad, coef_grad = pair_sums([dot_n(before_low, layer.dt), rows(coef_grad).T], collective_id)
    high, low = two_parts(jnp.concatenate([ranks_grad, coef_grad.T], axis=-1))
    through = dot_n(jnp.concatenate([high, low], axis=-1), jnp.concatenate([layer.x, layer.x], axis=-1))
    inputs_grad = grad_result * layer.skip + step * pushes + through
    conv_grad = inputs_grad * silu_slope(conv_out)
    taps_grad = jnp.stack([jnp.sum(conv_grad * window[8 * k:8 * k + count], axis=0) for k in range(rim + 1)])
    shift_grad = jnp.sum(conv_grad, axis=0)
    margin = jnp.zeros((8 * rim, inner), jnp.float32)
    padded = jnp.concatenate([margin, conv_grad, margin], axis=0)
    window_grad = sum(
        layer.taps[k] * padded[8 * (rim - k):8 * (rim - k) + count + 8 * rim] for k in range(rim + 1))
    prefix_grad = split_parts(by_step(window_grad[:8 * rim]), parts)
    arrived = neighbour(prefix_grad[:, 0], -1)
    tail_grad = jnp.concatenate([prefix_grad[:, 1:], arrived[:, None]], axis=1).reshape(8 * rim, inner)
    values_grad = jnp.concatenate([window_grad[8 * rim:count], window_grad[count:] + tail_grad], axis=0)
    values_grad = values_grad.astype(jnp.bfloat16)
    normed_part = dot_n(values_grad, layer.into[:, :inner]) + gate_through
    small = jnp.concatenate([taps_grad, shift_grad[None], bias_grad[None], decay_grad], axis=0)
    return normed_part, small, (values_grad, before_low, high, low), split_parts(start_grad, parts)[:, 0], prefix_grad[:, 0]


def thick_grads(kept, normed, lows):
    inputs, dt_low = kept[3], kept[4]
    values_grad, before_low, high, low = lows
    blocks = lax.axis_size("blk")
    x_grad = dot_t(high, inputs) + dot_t(low, inputs)
    return [eights(part.reshape(blocks, -1, part.shape[-1]))
            for part in (dot_t(normed, values_grad), x_grad, dot_t(dt_low, before_low))]


def eights(array):
    return jnp.pad(array, ((0, 0), (0, -array.shape[1] % 8), (0, 0)))


def norm_back(gain, normed_grad, residual, q):
    gain_grad = jnp.sum(normed_grad * (residual * q), axis=0)
    scaled = normed_grad * gain
    inner_mean = jnp.mean(scaled * residual, axis=-1, keepdims=True)
    return gain_grad, q * scaled - residual * (q * q * q * inner_mean)


def on_device(tokens, cotangent, *args):
    scan_init, conv_init = args[-2:]
    weights = args[:-2]
    blocks, index = lax.axis_size("blk"), lax.axis_index("blk")
    at_first = index == 0
    layer_total = weights[1].shape[0]
    seqs = tokens.shape[0]
    parts = 8 // seqs
    length = tokens.shape[1] // parts
    width = tokens.shape[2]
    layers = [Layer(l, weights) for l in range(layer_total)]
    last = layer_total - 1

    def arrange(array):
        return array.reshape(seqs, parts, length, width).transpose(2, 1, 0, 3).reshape(length * 8, width)

    def restore(array):
        array = array.reshape(length, parts, seqs, width).transpose(2, 1, 0, 3)
        return array.reshape(seqs, parts * length, width)

    residual = arrange(tokens).astype(jnp.float32)
    normed = lax.optimization_barrier((residual * inverse_rms(residual) * layers[0].gain).astype(jnp.bfloat16))
    residual = own_rows(residual)
    input_square = jnp.sum(residual * residual)
    grad = arrange(cotangent).astype(jnp.float32)
    grad_low = grad.astype(jnp.bfloat16)

    kept, scans, norms, finals, tails, squares = ([None] * layer_total for _ in range(6))
    starts, prefixes, smalls, gains = ([None] * layer_total for _ in range(4))
    for l, layer in enumerate(layers):
        norms[l] = (normed, residual)
        kept[l], local, tails[l] = front(
            layer, normed, jnp.moveaxis(conv_init[l], 1, 0), parts, at_first, 4 * layer_total + l)
        totals = kept[l][-1]
        first = jnp.moveaxis(scan_init[l], 1, 0)
        if l == last:
            grads = back_gated(kept[l], late_gated)
            late = back_local(layer, kept[l], grads[1])
            start, end = exchange(layer, [local, late], totals, first, (False, True), layer_total + l)
        else:
            start, = exchange(layer, [local], totals, first, (False,), layer_total + l)
        scans[l], final = scanning(layer, kept[l], start)
        gated = scans[l][1]
        if l == last:
            gated, late_out = lax.optimization_barrier((gated, dot_t(grad_low, gated)))
        partial_sum = dot32(gated, layer.out)
        finals[l] = split_parts(final, parts)[:, -1]
        half = core_sum(partial_sum)
        if l < last:
            half, stored = lax.optimization_barrier((half, weights[1]))
            into = [stored[k].reshape(width, -1) for k in range(layer_total)]
            layers[l + 1].raw = stored[l + 1]
            late_gated = dot_n(grad_low, layers[last].out)
            got, into, grad_low, late_gated = lax.optimization_barrier((across(half), into, grad_low, late_gated))
            for each, array in zip(layers, into):
                each.into = array
            branch = half + got
            following = residual + branch
            squares[l] = jnp.stack([jnp.sum(branch * branch), jnp.sum(following * following)])
            residual = following
            gain = layers[l + 1].gain
            normed = all_rows(residual * inverse_rms(residual), lambda part: (part * gain).astype(jnp.bfloat16))

    thins, scattered = [], [None] * layer_total
    for l in reversed(range(layer_total)):
        layer = layers[l]
        normed, base = norms[l]
        if l < last:
            grads, out_grad, half = lax.optimization_barrier(
                (back_gated(kept[l], dot_n(grad_low, layer.out)), dot_t(grad_low, scans[l][1]), half))
            scattered[l] = [blk_scatter(out_grad)]
            late = back_local(layer, kept[l], grads[1])
            end, = exchange(layer, [late], kept[l][-1], jnp.zeros_like(late[:, 0]), (True,), 2 + 2 * layer_total + l)
            end, got_rest = lax.optimization_barrier((end, across(half[half.shape[0] // 2:])))
            branch = half + jnp.concatenate([got, got_rest], axis=0)
            following = residual + branch
            squares[last] = jnp.stack([jnp.sum(branch * branch), jnp.sum(following * following)])
            out = restore(all_rows(0.5 * following, lambda part: (2.0 * part).astype(jnp.bfloat16)))
        else:
            out_grad = late_out
        side = back_side(layer, kept[l], normed, scans[l], grads, grad_low)
        if l == last:
            scattered[l] = [blk_scatter(out_grad), blk_scatter(side[0])]
            end, side, half = lax.optimization_barrier((end, side, half))
            scan_out, got = lax.optimization_barrier(
                (back_scan(layer, kept[l], scans[l], grads, end), across(half[:half.shape[0] // 2])))
        else:
            scattered[l].append(blk_scatter(side[0]))
            end, side, scattered[last] = lax.optimization_barrier((end, side, scattered[last]))
            stacked_last = jnp.stack([scattered[last][2], scattered[last][1]], axis=1)
            scan_out = lax.optimization_barrier(back_scan(layer, kept[l], scans[l], grads, end))
        gate_grad, gate_through, skip_grad = side
        normed_part, smalls[l], lows, starts[l], prefixes[l] = back_rest(
            layer, kept[l], grads, scan_out, gate_through, 5 * layer_total + l)
        smalls[l] = jnp.concatenate([smalls[l], skip_grad[None]], axis=0)
        thick = thick_grads(kept[l], normed, lows)
        inner = smalls[l].shape[-1]
        if l == last:
            thins = thick[1:] + thins
            joint, scattered[l][0] = lax.optimization_barrier((joint_sums(
                normed_part, base, layer.gain, [rows(thick[0])], (0,), smalls[l], l), scattered[l][0]))
            change, gains[l], thick, smalls[l] = joint
            scattered[l].append(thick[0])
        else:
            thins = thick[1:] + thins
            cuts = [part.shape[1] for part in thins]
            extra = jnp.concatenate([jnp.stack(squares).reshape(-1), input_square.reshape(1)])
            extra = jnp.pad(extra, (0, inner - extra.shape[0]))[None]
            shared = rows_sum(extra)
            own_count = smalls[l].shape[0]
            small = jnp.concatenate([smalls[l], shared], axis=0)
            small = jnp.pad(small, ((0, -small.shape[0] % 8), (0, 0)))
            normed_part, thins, out, stacked_last = lax.optimization_barrier((normed_part, thins, out, stacked_last))
            change, gains[l], thick, small = joint_sums(
                normed_part, base, layer.gain, [rows(thick[0]), rows(jnp.concatenate(thins, axis=1))], (0, inner),
                small, l)
            scattered[l].append(thick[0])
            smalls[l], rest = small[:own_count], small[own_count:]
        grad = grad + change
        grad_low = grad.astype(jnp.bfloat16)
        if l:
            grad_low = lax.optimization_barrier(grad_low)
    input_grad = restore(grad_low)

    small = jnp.stack(smalls)
    gain_grad = jnp.stack(gains)
    taps = weights[2].shape[1]
    row_total = tokens.shape[0] * tokens.shape[1] * width * blocks
    squares = rest[0] / row_total
    rms_stats = jnp.sqrt(squares[:2 * layer_total]).reshape(layer_total, 2)
    input_rms = jnp.sqrt(squares[2 * layer_total:2 * layer_total + 1])
    pieces, at = [], 0
    for cut in cuts:
        pieces.append(thick[1][at:at + cut])
        at += cut
    into_out = jnp.stack([jnp.stack([part[2], part[1]], axis=1) for part in scattered[:-1]] + [stacked_last])

    def stacked(parts_):
        return jnp.stack([jnp.moveaxis(part, 0, 1) for part in parts_])[:, :, None]

    return (
        out,
        stacked(finals),
        stacked(tails),
        input_grad,
        stacked(starts),
        stacked(prefixes),
        gain_grad,
        into_out,
        small[:, :taps],
        small[:, taps],
        jnp.stack([part[:weights[4].shape[-1] // blocks].T for part in pieces[0::2]]),
        jnp.stack([part[:RANK // blocks] for part in pieces[1::2]]),
        small[:, taps + 1],
        small[:, taps + 2:-1],
        small[:, -1],
        jnp.stack([part[0].T for part in scattered]),
        rms_stats,
        input_rms,
    )


def solution(mesh):
    placed = (
        P(None, "blk", None),
        P(None, "blk", None),
        P(),
        P(None, None, None, "tensor"),
        P(None, None, "tensor"),
        P(None, "tensor"),
        P(None, "tensor", None),
        P(None, None, "tensor"),
        P(None, "tensor"),
        P(None, None, "tensor"),
        P(None, "tensor"),
        P(None, "tensor", None),
        P(None, None, None, "tensor"),
        P(None, None, None, "tensor"),
    )
    return jax.shard_map(
        on_device,
        mesh=mesh,
        in_specs=placed,
        out_specs=(
            P(None, "blk", None),
            P(None, None, "blk", None, "tensor"),
            P(None, None, "blk", None, "tensor"),
            P(None, "blk", None),
            P(None, None, "blk", None, "tensor"),
            P(None, None, "blk", None, "tensor"),
            P(),
            P(None, "blk", None, "tensor"),
            P(None, None, "tensor"),
            P(None, "tensor"),
            P(None, "tensor", "blk"),
            P(None, "blk", "tensor"),
            P(None, "tensor"),
            P(None, None, "tensor"),
            P(None, "tensor"),
            P(None, "tensor", "blk"),
            P(),
            P(),
        ),
        check_vma=False,
    )
```

```python
import math
from functools import partial
import jax
import jax.numpy as jnp
from jax import lax
from jax.experimental import pallas as pl
from jax.experimental.pallas import tpu as pltpu

from jax.sharding import PartitionSpec as P

STATE = 16
RANK = 128
EPSILON = 1e-05
LANES=128
LOG2E=math.log2(math.e)

def cost(step, passes):
    return pl.CostEstimate(flops=passes * STATE * step.size, bytes_accessed=passes * STATE * step.size, transcendentals=0)

def cp(limit):
    return pltpu.CompilerParams(dimension_semantics=("arbitrary",), vmem_limit_bytes=limit)

def spread(ref_value, out, first):
    for n in range(STATE):
        for t in range(out.shape[0]):
            out[t, n] = jnp.broadcast_to(ref_value[t, :, first + n:first + n + 1], out.shape[2:])

def rates(rate_ref, lanes, n):
    return jnp.broadcast_to(rate_ref[pl.ds(n, 1), lanes], (8, LANES))

def end_body(blocks, width, held, step_ref, push_ref, coef_ref, rate_ref, end_ref, write):
    @pl.when(pl.program_id(0) == 0)
    def _():
        end_ref[...] = jnp.zeros_like(end_ref)
    spread(coef_ref, write, 0)
    def group(g, _):
        cols = [pl.ds(pl.multiple_of((g * width + k) * LANES, LANES), LANES) for k in range(width)]
        for low in range(0, STATE, held):
            span = range(low, low + held)
            state = {(k, n): end_ref[n, :, cols[k]] for k in range(width) for n in span}
            rate = {(k, n): rates(rate_ref, cols[k], n) for k in range(width) for n in span}
            for t in range(step_ref.shape[0]):
                step = [step_ref[t, :, c] for c in cols]
                push = [push_ref[t, :, c] for c in cols]
                for n in span:
                    w = write[t, n]
                    for k in range(width):
                        state[k, n] = jnp.exp2(step[k] * rate[k, n]) * state[k, n] + push[k] * w
            for k in range(width):
                for n in span:
                    end_ref[n, :, cols[k]] = state[k, n]
        return 0
    lax.fori_loop(0, blocks // width, group, 0)

def end_states(step, push, coef, rate, tb=16, width=2, held=8, limit=48*2**20):
    T, _, C = step.shape
    return pl.pallas_call(
        partial(end_body, C // LANES, width, held),
        grid=(T // tb,),
        in_specs=[pl.BlockSpec((tb, 8, C), lambda i: (i, 0, 0)), pl.BlockSpec((tb, 8, C), lambda i: (i, 0, 0)),
                  pl.BlockSpec((tb, 8, 2 * STATE), lambda i: (i, 0, 0)), pl.BlockSpec((STATE, C), lambda i: (0, 0))],
        out_specs=pl.BlockSpec((STATE, 8, C), lambda i: (0, 0, 0)),
        out_shape=jax.ShapeDtypeStruct((STATE, 8, C), jnp.float32),
        scratch_shapes=[pltpu.VMEM((tb, STATE, 8, LANES), jnp.float32)],
        compiler_params=cp(limit), cost_estimate=cost(step, 4), name="end_states")(step, push, coef, rate)

def scan_body(blocks, width, held, step_ref, push_ref, coef_ref, rate_ref, start_ref, out_ref, states_ref, final_ref, write, read):
    @pl.when(pl.program_id(0) == 0)
    def _():
        final_ref[...] = start_ref[...]
    spread(coef_ref, write, 0)
    spread(coef_ref, read, STATE)
    def group(g, _):
        cols = [pl.ds(pl.multiple_of((g * width + k) * LANES, LANES), LANES) for k in range(width)]
        for low in range(0, STATE, held):
            span = range(low, low + held)
            state = {(k, n): final_ref[n, :, cols[k]] for k in range(width) for n in span}
            rate = {(k, n): rates(rate_ref, cols[k], n) for k in range(width) for n in span}
            for t in range(step_ref.shape[0]):
                step = [step_ref[t, :, c] for c in cols]
                push = [push_ref[t, :, c] for c in cols]
                total = [None] * width
                for n in span:
                    w, r = write[t, n], read[t, n]
                    for k in range(width):
                        s = jnp.exp2(step[k] * rate[k, n]) * state[k, n] + push[k] * w
                        state[k, n] = s
                        states_ref[t, n, :, cols[k]] = s
                        total[k] = r * s if total[k] is None else total[k] + r * s
                for k in range(width):
                    if low == 0:
                        out_ref[t, :, cols[k]] = total[k]
                    else:
                        out_ref[t, :, cols[k]] += total[k]
            for k in range(width):
                for n in span:
                    final_ref[n, :, cols[k]] = state[k, n]
        return 0
    lax.fori_loop(0, blocks // width, group, 0)

def scan_forward(step, push, coef, rate, start, tb=16, width=2, held=8, limit=48*2**20):
    T, _, C = step.shape
    row = pl.BlockSpec((tb, 8, C), lambda i: (i, 0, 0))
    whole = pl.BlockSpec((STATE, 8, C), lambda i: (0, 0, 0))
    f32 = jnp.float32
    return pl.pallas_call(
        partial(scan_body, C // LANES, width, held),
        grid=(T // tb,),
        in_specs=[row, row, pl.BlockSpec((tb, 8, 2 * STATE), lambda i: (i, 0, 0)), pl.BlockSpec((STATE, C), lambda i: (0, 0)), whole],
        out_specs=[row, pl.BlockSpec((tb, STATE, 8, C), lambda i: (i, 0, 0, 0)), whole],
        out_shape=[jax.ShapeDtypeStruct((T, 8, C), f32), jax.ShapeDtypeStruct((T, STATE, 8, C), f32),
                   jax.ShapeDtypeStruct((STATE, 8, C), f32)],
        scratch_shapes=[pltpu.VMEM((tb, STATE, 8, LANES), f32)] * 2,
        compiler_params=cp(limit), cost_estimate=cost(step, 7), name="scan_forward")(step, push, coef, rate, start)

def start_body(blocks, width, held, step_ref, grad_ref, coef_ref, rate_ref, start_ref, read):
    @pl.when(pl.program_id(0) == 0)
    def _():
        start_ref[...] = jnp.zeros_like(start_ref)
    spread(coef_ref, read, STATE)
    def group(g, _):
        cols = [pl.ds(pl.multiple_of((g * width + k) * LANES, LANES), LANES) for k in range(width)]
        for low in range(0, STATE, held):
            span = range(low, low + held)
            state = {(k, n): start_ref[n, :, cols[k]] for k in range(width) for n in span}
            rate = {(k, n): rates(rate_ref, cols[k], n) for k in range(width) for n in span}
            for t in reversed(range(step_ref.shape[0])):
                step = [step_ref[t, :, c] for c in cols]
                grad = [grad_ref[t, :, c] for c in cols]
                for n in span:
                    r = read[t, n]
                    for k in range(width):
                        state[k, n] = jnp.exp2(step[k] * rate[k, n]) * (state[k, n] + r * grad[k])
            for k in range(width):
                for n in span:
                    start_ref[n, :, cols[k]] = state[k, n]
        return 0
    lax.fori_loop(0, blocks // width, group, 0)

def start_grads(step, grad, coef, rate, tb=16, width=2, held=8, limit=48*2**20):
    T, _, C = step.shape
    last = T // tb - 1
    row = pl.BlockSpec((tb, 8, C), lambda i: (last - i, 0, 0))
    return pl.pallas_call(
        partial(start_body, C // LANES, width, held),
        grid=(T // tb,),
        in_specs=[row, row, pl.BlockSpec((tb, 8, 2 * STATE), lambda i: (last - i, 0, 0)), pl.BlockSpec((STATE, C), lambda i: (0, 0))],
        out_specs=pl.BlockSpec((STATE, 8, C), lambda i: (0, 0, 0)),
        out_shape=jax.ShapeDtypeStruct((STATE, 8, C), jnp.float32),
        scratch_shapes=[pltpu.VMEM((tb, STATE, 8, LANES), jnp.float32)],
        compiler_params=cp(limit), cost_estimate=cost(step, 4), name="start_grads")(step, grad, coef, rate)

def back_body(blocks, width, held, step_ref, push_ref, grad_ref, coef_ref, rate_ref, states_ref, prior_ref, begin_ref, end_ref,
              decay_out, push_out, coef_out, start_ref, speed_ref, write, read, write_sum, read_sum):
    @pl.when(pl.program_id(0) == 0)
    def _():
        start_ref[...] = end_ref[...]
        speed_ref[...] = jnp.zeros_like(speed_ref)
    spread(coef_ref, write, 0)
    spread(coef_ref, read, STATE)
    tb = step_ref.shape[0]
    begins = pl.program_id(0) == pl.num_programs(0) - 1
    def group(g, first):
        cols = [pl.ds((g * width + k) * LANES if first else pl.multiple_of((g * width + k) * LANES, LANES), LANES)
                for k in range(width)]
        for low in range(0, STATE, held):
            span = range(low, low + held)
            carry = {(k, n): start_ref[n, :, cols[k]] for k in range(width) for n in span}
            speed = {(k, n): speed_ref[n, :, cols[k]] for k in range(width) for n in span}
            rate = {(k, n): rates(rate_ref, cols[k], n) for k in range(width) for n in span}
            enter = {(k, n): jnp.where(begins, begin_ref[n, :, cols[k]], prior_ref[0, n, :, cols[k]])
                     for k in range(width) for n in span}
            for t in reversed(range(tb)):
                step = [step_ref[t, :, c] for c in cols]
                push = [push_ref[t, :, c] for c in cols]
                grad = [grad_ref[t, :, c] for c in cols]
                decays = [None] * width
                pushes = [None] * width
                for n in span:
                    w, r = write[t, n], read[t, n]
                    wsum, rsum = None, None
                    for k in range(width):
                        before = states_ref[t - 1, n, :, cols[k]] if t else enter[k, n]
                        back = carry[k, n] + r * grad[k]
                        onward = jnp.exp2(step[k] * rate[k, n]) * back
                        carry[k, n] = onward
                        q = onward * before
                        speed[k, n] = speed[k, n] + step[k] * q
                        rq, bw = rate[k, n] * q, back * w
                        decays[k] = rq if decays[k] is None else decays[k] + rq
                        pushes[k] = bw if pushes[k] is None else pushes[k] + bw
                        bp, gs = back * push[k], grad[k] * states_ref[t, n, :, cols[k]]
                        wsum = bp if wsum is None else wsum + bp
                        rsum = gs if rsum is None else rsum + gs
                    if first:
                        write_sum[t, n] = wsum
                        read_sum[t, n] = rsum
                    else:
                        write_sum[t, n] += wsum
                        read_sum[t, n] += rsum
                for k in range(width):
                    if low == 0:
                        decay_out[t, :, cols[k]] = decays[k]
                        push_out[t, :, cols[k]] = pushes[k]
                    else:
                        decay_out[t, :, cols[k]] += decays[k]
                        push_out[t, :, cols[k]] += pushes[k]
            for k in range(width):
                for n in span:
                    start_ref[n, :, cols[k]] = carry[k, n]
                    speed_ref[n, :, cols[k]] = speed[k, n]
        return 0
    group(0, True)
    lax.fori_loop(1, blocks // width, lambda g, _: group(g, False), 0)
    lane = lax.broadcasted_iota(jnp.int32, (8, 2 * STATE), 1)
    for t in range(tb):
        row = jnp.zeros((8, 2 * STATE), jnp.float32)
        for n in range(STATE):
            row = jnp.where(lane == n, jnp.sum(write_sum[t, n], axis=-1, keepdims=True), row)
            row = jnp.where(lane == STATE + n, jnp.sum(read_sum[t, n], axis=-1, keepdims=True), row)
        coef_out[t] = row

def scan_backward(step, push, grad, coef, rate, states, begin, end, tb=8, width=2, held=4, limit=48*2**20):
    T, _, C = step.shape
    last = T // tb - 1
    f32 = jnp.float32
    row = pl.BlockSpec((tb, 8, C), lambda i: (last - i, 0, 0))
    thin = pl.BlockSpec((tb, 8, 2 * STATE), lambda i: (last - i, 0, 0))
    whole = pl.BlockSpec((STATE, 8, C), lambda i: (0, 0, 0))
    return pl.pallas_call(
        partial(back_body, C // LANES, width, held),
        grid=(T // tb,),
        in_specs=[row, row, row, thin, pl.BlockSpec((STATE, C), lambda i: (0, 0)),
                  pl.BlockSpec((tb, STATE, 8, C), lambda i: (last - i, 0, 0, 0)),
                  pl.BlockSpec((1, STATE, 8, C), lambda i: (jnp.maximum((last - i) * tb - 1, 0), 0, 0, 0)), whole, whole],
        out_specs=[row, row, thin, whole, whole],
        out_shape=[jax.ShapeDtypeStruct((T, 8, C), f32)] * 2 + [jax.ShapeDtypeStruct((T, 8, 2 * STATE), f32)]
          + [jax.ShapeDtypeStruct((STATE, 8, C), f32)] * 2,
        scratch_shapes=[pltpu.VMEM((tb, STATE, 8, LANES), f32)] * 4,
        compiler_params=cp(limit), cost_estimate=cost(step, 13), name="scan_backward")(step, push, grad, coef, rate, states, states, begin, end)


HALVES_OF_CHIP = 2


def silu_slope(argument):
    sigmoid_value = jax.nn.sigmoid(argument)
    return sigmoid_value * (1.0 + argument * (1.0 - sigmoid_value))


def half_of(array, index):
    size = array.shape[0] // 2
    return lax.dynamic_slice_in_dim(array, index * size, size, 0)


def ordered(index, mine, other):
    first = jnp.where(index == 0, mine, other)
    second = jnp.where(index == 0, other, mine)
    return jnp.concatenate([first, second], axis=0)


BESIDE = [(0, 1), (1, 0), (2, 3), (3, 2)]
ACROSS = [(0, 2), (2, 0), (1, 3), (3, 1)]


def paired():
    return lax.axis_size("tensor") == 4


def tensor_sum(array):
    if not paired():
        return lax.psum(array, "tensor")
    core = lax.axis_index("tensor") % 2
    half = half_of(array, core) + lax.ppermute(half_of(array, 1 - core), "tensor", BESIDE)
    half = half + lax.ppermute(half, "tensor", ACROSS)
    return ordered(core, half, lax.ppermute(half, "tensor", BESIDE))


def pair_body(chunks, count, *refs):
    ins, outs, refs = refs[:count], refs[count:2 * count], refs[2 * count:]
    buffers, sems = refs[:5 * count], refs[5 * count:]
    blk, tensor = lax.axis_index("blk"), lax.axis_index("tensor")
    core = tensor % 2
    beside, far = (blk, tensor + 1 - 2 * core), (blk, (tensor + 2) % 4)
    barrier = pltpu.get_barrier_semaphore()
    for device in (beside, far):
        pl.semaphore_signal(barrier, inc=1, device_id=device, device_id_type=pl.DeviceIdType.MESH)
    pl.semaphore_wait(barrier, 2)
    parts = [(k, i) for k in range(chunks) for i in range(count)]
    firsts, seconds, thirds = {}, {}, {}

    def rows_of(i, k, side):
        size = ins[i].shape[0] // 2 // chunks
        return pl.ds(pl.multiple_of((side * chunks + k) * size, size), size)

    for at, (k, i) in enumerate(parts):
        firsts[k, i] = remote(ins[i].at[rows_of(i, k, 1 - core)], buffers[5 * i].at[k], sems[0], sems[1], at, beside)
        firsts[k, i].start()
    for at, (k, i) in enumerate(parts):
        firsts[k, i].wait_recv()
        buffers[5 * i + 1][k] = ins[i][rows_of(i, k, core), :] + buffers[5 * i][k]
        seconds[k, i] = remote(buffers[5 * i + 1].at[k], buffers[5 * i + 2].at[k], sems[2], sems[3], at, far)
        seconds[k, i].start()
    for at, (k, i) in enumerate(parts):
        seconds[k, i].wait_recv()
        total = buffers[5 * i + 1][k] + buffers[5 * i + 2][k]
        buffers[5 * i + 3][k] = total
        outs[i][rows_of(i, k, core), :] = total
        thirds[k, i] = remote(buffers[5 * i + 3].at[k], buffers[5 * i + 4].at[k], sems[4], sems[5], at, beside)
        thirds[k, i].start()
    for k, i in parts:
        thirds[k, i].wait_recv()
        outs[i][rows_of(i, k, 1 - core), :] = buffers[5 * i + 4][k]
    for group in (firsts, seconds, thirds):
        for copy in group.values():
            copy.wait_send()


def pair_sums(arrays, collective_id):
    if not paired() or lax.axis_size("blk") != 8:
        first, second = arrays
        total = lax.psum(jnp.concatenate([first, second.T], axis=-1), "tensor")
        return [total[:, :first.shape[1]], total[:, first.shape[1]:].T]
    chunks, count = 2, len(arrays)
    f32 = jnp.float32
    spec = pl.BlockSpec(memory_space=pltpu.VMEM)
    scratch = []
    for array in arrays:
        scratch += [pltpu.VMEM((chunks, array.shape[0] // 2 // chunks, array.shape[1]), f32)] * 5
    return pl.pallas_call(
        partial(pair_body, chunks, count),
        in_specs=[spec] * count,
        out_specs=[spec] * count,
        out_shape=[jax.ShapeDtypeStruct(array.shape, f32) for array in arrays],
        scratch_shapes=scratch + [pltpu.SemaphoreType.DMA((chunks * count,))] * 6,
        compiler_params=pltpu.CompilerParams(
            collective_id=collective_id, has_side_effects=True, vmem_limit_bytes=24 * 2**20),
        cost_estimate=pl.CostEstimate(flops=0, bytes_accessed=40 * 2**20, transcendentals=0),
        name="pair_sums",
    )(*arrays)


def own_rows(array):
    if not paired():
        size = array.shape[0] // lax.axis_size("tensor")
        return lax.dynamic_slice_in_dim(array, lax.axis_index("tensor") * size, size, 0)
    return half_of(array, lax.axis_index("tensor") % 2)


def core_sum(array):
    if not paired():
        return lax.psum_scatter(array, "tensor", scatter_dimension=0, tiled=True)
    core = lax.axis_index("tensor") % 2
    return half_of(array, core) + lax.ppermute(half_of(array, 1 - core), "tensor", BESIDE)


def across(half):
    if not paired():
        return jnp.zeros_like(half)
    return lax.ppermute(half, "tensor", ACROSS)


def all_rows(array, finish=lambda part: part):
    if not paired():
        return finish(lax.optimization_barrier(lax.all_gather(array, "tensor", tiled=True)))
    other = lax.optimization_barrier(lax.ppermute(array, "tensor", BESIDE))
    return ordered(lax.axis_index("tensor") % 2, finish(array), finish(other))


def rows_sum(array):
    if not paired():
        return lax.psum(array, "tensor")
    return array + lax.ppermute(array, "tensor", BESIDE)


def blk_sum(array):
    if lax.axis_size("blk") != 8:
        return lax.psum(array, "blk")
    for bit in (1, 2, 4):
        array = array + lax.ppermute(array, "blk", [(j, j ^ bit) for j in range(8)])
    return array


def blk_scatter(array):
    return lax.psum_scatter(array, "blk", scatter_dimension=0, tiled=True)


def add_rows(total, other, count):
    slab = 8

    def body(i, _):
        at = pl.ds(pl.multiple_of(i * slab, slab), slab)
        total[at, :] = total[at, :] + other[at, :]
        return 0

    lax.fori_loop(0, count // slab, body, 0)


def remote(src, dst, sends, recvs, at, device):
    return pltpu.make_async_remote_copy(
        src_ref=src, dst_ref=dst, send_sem=sends.at[at], recv_sem=recvs.at[at], device_id=device,
        device_id_type=pl.DeviceIdType.MESH)


def joint_body(plan, chunks, sum_gain, sum_ref, base_ref, gain_ref, *refs):
    count = 1 + max(job[0] for job in plan)
    thick_refs, small_ref, refs = refs[:count], refs[count], refs[count + 1:]
    change_out, gain_out, refs = refs[0], refs[1], refs[2:]
    thick_outs, small_out, refs = refs[:count], refs[count], refs[1 + count:]
    own_half, core_half, far_half, base, came, small_in, refs = refs[0], refs[1], refs[2], refs[3], refs[4], refs[5], refs[6:]
    gain_in, gain_send, gain_recv, refs = refs[0], refs[1], refs[2], refs[3:]
    core_send, core_recv, far_send, far_recv, back_send, back_recv, local_sem, base_sem, out_sem, came_sem = refs[:10]
    small_send, small_recv = refs[10:12]
    refs = refs[12:]
    blk, tensor = lax.axis_index("blk"), lax.axis_index("tensor")
    bits = {1: blk % 2, 2: (blk // 2) % 2, 4: blk // 4}
    core = tensor % 2
    beside = (blk, tensor + 1 - 2 * core)
    far = (blk, (tensor + 2) % 4)
    peers = {bit: (blk + bit - 2 * bit * bits[bit], tensor) for bit in bits}
    barrier = pltpu.get_barrier_semaphore()
    for device in (beside, far, peers[1], peers[2], peers[4]):
        pl.semaphore_signal(barrier, inc=1, device_id=device, device_id_type=pl.DeviceIdType.MESH)
    pl.semaphore_wait(barrier, 5)

    rows_each, width = own_half.shape[1:]
    smalls, core_copies, local_copies, base_copies, far_copies, back_copies, outs = [], [], [], [], [], [], []

    def small_step(i):
        copy = remote(small_out, small_in.at[i], small_send, small_recv, i, peers[1 << i])
        copy.start()
        smalls.append(copy)

    def small_end(i):
        smalls[i].wait()
        small_out[...] = small_out[...] + small_in[i]

    small_out[...] = small_ref[...]
    small_step(0)
    for k in range(chunks):
        give = pl.ds(pl.multiple_of((1 - core) * rows_each * chunks + k * rows_each, rows_each), rows_each)
        keep = pl.ds(pl.multiple_of(core * rows_each * chunks + k * rows_each, rows_each), rows_each)
        copy = remote(sum_ref.at[give], core_half.at[k], core_send, core_recv, k, beside)
        copy.start()
        core_copies.append(copy)
        copy = pltpu.make_async_copy(sum_ref.at[keep], own_half.at[k], local_sem.at[k])
        copy.start()
        local_copies.append(copy)
        copy = pltpu.make_async_copy(base_ref.at[pl.ds(k * rows_each, rows_each)], base.at[k], base_sem.at[k])
        copy.start()
        base_copies.append(copy)
    gain_out[...] = jnp.zeros_like(gain_out)

    class Job:
        def __init__(self, which, low, wide, order, refs):
            (self.own, self.first, self.second, self.third, self.sems) = refs[0], refs[1], refs[2], refs[3], refs[4:]
            self.order = order
            self.count = thick_refs[which].shape[3]
            self.out = thick_outs[which].at[:, pl.ds(low, wide)]
            lead, (u, v) = bits[order[0]], (bits[order[1]], bits[order[2]])
            self.parts = [(1 - u, 1 - v), (1 - u, v), (u, 1 - v), (u, v)]
            self.firsts, self.owns, self.seconds = [], [], []
            for i, part in enumerate(self.parts):
                at = {order[1]: part[0], order[2]: part[1]}

                def source(mine):
                    index = dict(at)
                    index[order[0]] = mine
                    return thick_refs[which].at[index[4], index[2], index[1], :, pl.ds(low, wide)]

                copy = remote(source(1 - lead), self.first.at[part], self.sems[0], self.sems[1], i, peers[order[0]])
                copy.start()
                self.firsts.append(copy)
                copy = pltpu.make_async_copy(source(lead), self.own.at[part], self.sems[2].at[i])
                copy.start()
                self.owns.append(copy)

        def first_end(self, i):
            self.owns[i].wait()
            self.firsts[i].wait_recv()
            add_rows(self.own.at[self.parts[i]], self.first.at[self.parts[i]], self.count)
            if i < 2:
                copy = remote(self.own.at[self.parts[i]], self.second.at[i], self.sems[3], self.sems[4], i,
                              peers[self.order[1]])
                copy.start()
                self.seconds.append(copy)
                return
            self.seconds[i - 2].wait_recv()
            add_rows(self.own.at[self.parts[i]], self.second.at[i - 2], self.count)
            if i == 2:
                self.last = remote(self.own.at[self.parts[i]], self.third, self.sems[5], self.sems[6], 0,
                                   peers[self.order[2]])
                self.last.start()

        def end(self):
            self.last.wait_recv()
            add_rows(self.own.at[self.parts[3]], self.third, self.count)
            copy = pltpu.make_async_copy(self.own.at[self.parts[3]], self.out, self.sems[7].at[0])
            copy.start()
            outs.append(copy)

        def sent(self):
            return self.firsts + self.seconds + [self.last]

    jobs = [Job(*job, refs[12 * i:12 * i + 12]) for i, job in enumerate(plan)]
    gains = []

    def gain_step(i):
        device = beside if i == 0 else peers[1 << (i - 1)]
        copy = remote(gain_out, gain_in.at[i], gain_send, gain_recv, i, device)
        copy.start()
        gains.append(copy)

    def gain_end(i):
        gains[i].wait()
        gain_out[...] = gain_out[...] + gain_in[i]

    def core_end(k):
        local_copies[k].wait()
        core_copies[k].wait()
        add_rows(own_half.at[k], core_half.at[k], rows_each)
        copy = remote(own_half.at[k], far_half.at[k], far_send, far_recv, k, far)
        copy.start()
        far_copies.append(copy)

    def far_end(k):
        far_copies[k].wait_recv()
        base_copies[k].wait()

        def slab(i, _):
            at = pl.ds(pl.multiple_of(i * 8, 8), 8)
            residual = base[k, at, :]
            normed_grad = far_half[k, at, :] + own_half[k, at, :]
            q = lax.rsqrt(jnp.sum(residual * residual, axis=-1, keepdims=True) * (1.0 / width) + EPSILON)
            part = residual * q
            gain_out[...] += normed_grad * part
            scaled = normed_grad * gain_ref[...]
            inner = jnp.sum(scaled * part, axis=-1, keepdims=True) * (1.0 / width)
            far_half[k, at, :] = q * (scaled - part * inner)
            return 0

        lax.fori_loop(0, rows_each // 8, slab, 0)
        copy = remote(far_half.at[k], came.at[k], back_send, back_recv, k, beside)
        copy.start()
        back_copies.append(copy)
        own_rows_at = pl.ds(pl.multiple_of((core * chunks + k) * rows_each, rows_each), rows_each)
        copy = pltpu.make_async_copy(far_half.at[k], change_out.at[own_rows_at], out_sem.at[k])
        copy.start()
        outs.append(copy)

    def back_end(k):
        back_copies[k].wait_recv()
        other_rows_at = pl.ds(pl.multiple_of(((1 - core) * chunks + k) * rows_each, rows_each), rows_each)
        copy = pltpu.make_async_copy(came.at[k], change_out.at[other_rows_at], came_sem.at[k])
        copy.start()
        outs.append(copy)

    for k in range(chunks):
        core_end(k)
    small_end(0)
    small_step(1)
    for i in range(4):
        for job in jobs:
            job.first_end(i)
        if i in (0, 1):
            small_end(i + 1)
            if i == 0:
                small_step(2)
        far_end(i)
    if sum_gain:
        gain_step(0)
    for k in range(chunks):
        back_end(k)
    if sum_gain:
        for i in range(4):
            gain_end(i)
            if i < 3:
                gain_step(i + 1)
    for job in jobs:
        job.end()
    for copy in far_copies + back_copies + [each for job in jobs for each in job.sent()]:
        copy.wait_send()
    for copy in outs:
        copy.wait()


def joint_sums(array, base, gain, thick, late, small, sum_gain, collective_id):
    if not paired() or lax.axis_size("blk") != 8:
        normed_grad = lax.psum_scatter(array, "tensor", scatter_dimension=0, tiled=True)
        gain_grad, change = norm_back(gain, normed_grad, base, inverse_rms(base))
        if sum_gain:
            gain_grad = lax.psum(rows_sum(gain_grad), "blk")
        return all_rows(change), gain_grad, [blk_scatter(part) for part in thick], lax.psum(small, "blk")
    R, N = array.shape
    C = thick[0].shape[1]
    chunks = 4
    f32 = jnp.float32
    dma = pltpu.SemaphoreType.DMA
    any_spec = pl.BlockSpec(memory_space=pl.ANY)
    vmem_spec = pl.BlockSpec(memory_space=pltpu.VMEM)
    plan = [(i, 0, C - each, (1, 2, 4)) for i, each in enumerate(late) if each < C]
    plan += [(i, C - each, each, (2, 4, 1)) for i, each in enumerate(late) if each]
    scratch = []
    for which, _, wide, _ in plan:
        count = thick[which].shape[0] // 8
        scratch += [pltpu.VMEM((2, 2, count, wide), f32), pltpu.VMEM((2, 2, count, wide), f32),
                    pltpu.VMEM((2, count, wide), f32), pltpu.VMEM((count, wide), f32),
                    dma((4,)), dma((4,)), dma((4,)), dma((2,)), dma((2,)), dma((1,)), dma((1,)), dma((1,))]
    half = pltpu.VMEM((chunks, R // 2 // chunks, N), f32)
    out = pl.pallas_call(
        partial(joint_body, plan, chunks, sum_gain),
        in_specs=[any_spec, any_spec, vmem_spec] + [any_spec] * len(thick) + [vmem_spec],
        out_specs=[any_spec, vmem_spec] + [any_spec] * len(thick) + [vmem_spec],
        out_shape=[jax.ShapeDtypeStruct((R, N), f32), jax.ShapeDtypeStruct((8, N), f32)]
        + [jax.ShapeDtypeStruct((part.shape[0] // 8, C), f32) for part in thick]
        + [jax.ShapeDtypeStruct(small.shape, f32)],
        scratch_shapes=[half] * 5 + [pltpu.VMEM((3,) + small.shape, f32), pltpu.VMEM((4, 8, N), f32), dma((4,)), dma((4,))]
        + [dma((chunks,))] * 10 + [dma((3,)), dma((3,))] + scratch,
        compiler_params=pltpu.CompilerParams(
            collective_id=collective_id, has_side_effects=True, vmem_limit_bytes=52 * 2**20),
        cost_estimate=pl.CostEstimate(flops=0, bytes_accessed=50 * R * N * 4, transcendentals=0),
        name="joint_sums",
    )(array, base, gain[None], *[part.reshape(2, 2, 2, part.shape[0] // 8, C) for part in thick], small)
    return out[0], jnp.sum(out[1], axis=0), list(out[2:-1]), out[-1]


def neighbour(value, steps):
    count = lax.axis_size("blk")
    first, last = max(0, -steps), min(count, count - steps)
    return lax.ppermute(value, "blk", [(j, j + steps) for j in range(first, last)])


def entering_any(total, local, rate, first, reverse):
    peers, index = lax.axis_size("blk"), lax.axis_index("blk")
    totals, locals_ = lax.all_gather(total, "blk"), lax.all_gather(local, "blk")

    def step(k, state):
        at = peers - 1 - k if reverse else k
        reached = at > index if reverse else at < index
        return jnp.where(reached, jnp.exp2(totals[at][None] * rate) * state + locals_[at], state)

    return lax.fori_loop(0, peers, step, first)


def hop_body(reverses, groups, total_ref, rate_ref, *refs):
    ways = len(reverses)
    locals_, first_ref, refs = refs[:ways], refs[ways], refs[ways + 1:]
    outs, refs = refs[:ways], refs[ways:]
    beside_total, total_send, total_recv, refs = refs[0], refs[1], refs[2], refs[3:]
    blk, tensor = lax.axis_index("blk"), lax.axis_index("tensor")
    y, z = blk % 2, blk // 2
    beside = (blk + 1 - 2 * y, tensor)
    up, down = ((blk + 2) % 8, tensor), ((blk + 6) % 8, tensor)
    barrier = pltpu.get_barrier_semaphore()

    def greet(device):
        pl.semaphore_signal(barrier, inc=1, device_id=device, device_id_type=pl.DeviceIdType.MESH)

    greet(beside)
    pl.when(z < 3)(lambda: greet(up))
    pl.when(z > 0)(lambda: greet(down))
    pl.semaphore_wait(barrier, 3 - z // 3 - (3 - z) // 3)

    total = total_ref[...]
    copy_total = remote(total_ref, beside_total, total_send, total_recv, 0, beside)
    copy_total.start()
    size = STATE // 2 // groups

    class Way:
        def __init__(self, reverse, local, out, refs):
            self.own, self.other, self.came, self.goes, self.gives, self.gets = refs[:6]
            self.sems, self.out, self.reverse = refs[6:], out, reverse
            self.y, self.z = (1 - y, 3 - z) if reverse else (y, z)
            self.following = down if reverse else up
            self.at_a, self.begins = self.y == 0, self.z == 0
            self.firsts = []
            for n in range(STATE):
                value = local[n]
                if not reverse:
                    decay = jnp.exp2(total * rate_ref[pl.ds(n, 1), :])
                    value = value + jnp.where(jnp.logical_and(self.begins, self.at_a), decay * first_ref[n], 0.0)
                self.own[n] = value
            for k in range(groups):
                give = pl.ds((1 - self.y) * (STATE // 2) + k * size, size)
                copy = remote(self.own.at[give], self.other.at[pl.ds(k * size, size)], self.sems[0], self.sems[1], k, beside)
                copy.start()
                self.firsts.append(copy)

        def chain(self, k):
            part = pl.ds(k * size, size)
            return remote(self.goes.at[part], self.came.at[part], self.sems[2], self.sems[3], k, self.following)

        def middle(self, k, total_a, total_b):
            self.firsts[k].wait()
            pl.when(self.z > 0)(lambda: self.chain(k).wait_recv())
            for i in range(k * size, k * size + size):
                n = self.y * (STATE // 2) + i
                rate = rate_ref[pl.ds(n, 1), :]
                mine, got = self.own[n], self.other[i]
                local_a, local_b = jnp.where(self.at_a, mine, got), jnp.where(self.at_a, got, mine)
                enter = jnp.where(self.begins, 0.0, self.came[i])
                after_a = local_a + jnp.exp2(total_a * rate) * enter
                self.goes[i] = local_b + jnp.exp2(total_b * rate) * after_a
                self.gives[i] = jnp.where(self.at_a, after_a, enter)
                self.out[n] = jnp.where(self.at_a, enter, after_a)
            pl.when(self.z < 3)(lambda: self.chain(k).start())
            self.last(k).start()

        def last(self, k):
            part = pl.ds(k * size, size)
            return remote(self.gives.at[part], self.gets.at[part], self.sems[4], self.sems[5], k, beside)

        def all(self):
            other_total = beside_total[...]
            total_a, total_b = jnp.where(self.at_a, total, other_total), jnp.where(self.at_a, other_total, total)
            for k in range(groups):
                self.middle(k, total_a, total_b)

        def end(self, k):
            self.last(k).wait()
            for i in range(k * size, k * size + size):
                self.out[(1 - self.y) * (STATE // 2) + i] = self.gets[i]
            pl.when(self.z < 3)(lambda: self.chain(k).wait_send())

        def begin(self):
            starts = jnp.logical_and(self.begins, self.at_a)
            for n in range(STATE):
                first = 0.0 if self.reverse else first_ref[n]
                self.out[n] = jnp.where(starts, first, self.out[n])

    each = 6 + 6
    jobs = [Way(reverse, locals_[i], outs[i], refs[each * i:each * i + each]) for i, reverse in enumerate(reverses)]
    copy_total.wait()
    if ways == 1:
        jobs[0].all()
    else:

        def in_turn(order):
            for job in order:
                job.all()

        pl.when(z < 2)(lambda: in_turn(jobs))
        pl.when(z >= 2)(lambda: in_turn(jobs[::-1]))
    for k in range(groups):
        for job in jobs:
            job.end(k)
    for job in jobs:
        job.begin()


def hops(total, locals_, rate, first, reverses, collective_id):
    C = total.shape[-1]
    groups = 4
    f32 = jnp.float32
    dma = pltpu.SemaphoreType.DMA
    spec = pl.BlockSpec(memory_space=pltpu.VMEM)
    whole, half = pltpu.VMEM((STATE, 8, C), f32), pltpu.VMEM((STATE // 2, 8, C), f32)
    return pl.pallas_call(
        partial(hop_body, reverses, groups),
        in_specs=[spec] * (3 + len(locals_)),
        out_specs=[spec] * len(locals_),
        out_shape=[jax.ShapeDtypeStruct((STATE, 8, C), f32)] * len(locals_),
        scratch_shapes=[pltpu.VMEM((8, C), f32), dma((1,)), dma((1,))]
        + ([whole] + [half] * 5 + [dma((groups,))] * 6) * len(locals_),
        compiler_params=pltpu.CompilerParams(
            collective_id=collective_id, has_side_effects=True, vmem_limit_bytes=32 * 2**20),
        cost_estimate=pl.CostEstimate(flops=0, bytes_accessed=100 * total.size * 32, transcendentals=0),
        name="hops",
    )(total, rate, *locals_, first)


def rows(array):
    return array.reshape(-1, array.shape[-1])


def by_step(array):
    return array.reshape(-1, 8, array.shape[-1])


def dot32(left, right):
    return jnp.dot(left, right, preferred_element_type=jnp.float32)


def dot_t(left, right):
    return lax.dot_general(left, right, (((0,), (0,)), ((), ())), preferred_element_type=jnp.float32)


def dot_n(left, right):
    return lax.dot_general(left, right, (((1,), (1,)), ((), ())), preferred_element_type=jnp.float32)


def two_parts(array):
    high = lax.optimization_barrier(array.astype(jnp.bfloat16))
    return high, (array - high.astype(jnp.float32)).astype(jnp.bfloat16)


def split_parts(array, parts):
    return array.reshape(array.shape[:-2] + (parts, 8 // parts) + array.shape[-1:])


class Layer:
    def __init__(self, index, args):
        (norm_gain, in_weight, conv_weight, conv_bias, x_weight, dt_weight, dt_bias, decay_log,
         skip_weight, out_weight) = args
        self.gain = norm_gain[index]
        self.raw = in_weight[index] if index == 0 else None
        self.taps = conv_weight[index]
        self.shift = conv_bias[index]
        self.x = x_weight[index]
        self.dt = dt_weight[index]
        self.dt_bias = dt_bias[index]
        self.rate = -jnp.exp(decay_log[index])
        self.rate2 = self.rate * LOG2E
        self.skip = skip_weight[index]
        self.out = out_weight[index]


def norm_body(rows_ref, gain_ref, out_ref):
    value = rows_ref[...].astype(jnp.float32)
    q = lax.rsqrt(jnp.mean(value * value, axis=-1, keepdims=True) + EPSILON)
    out_ref[...] = (value * q * gain_ref[...]).astype(jnp.bfloat16)


def norm_rows(array, gain):
    R, N = array.shape
    block = 128
    return pl.pallas_call(
        norm_body,
        grid=(R // block,),
        in_specs=[pl.BlockSpec((block, N), lambda i: (i, 0)), pl.BlockSpec((1, N), lambda i: (0, 0))],
        out_specs=pl.BlockSpec((block, N), lambda i: (i, 0)),
        out_shape=jax.ShapeDtypeStruct((R, N), jnp.bfloat16),
        compiler_params=cp(24 * 2**20),
        cost_estimate=pl.CostEstimate(flops=4 * R * N, bytes_accessed=4 * R * N, transcendentals=R),
        name="norm_rows",
    )(array, gain[None])


def inverse_rms(residual):
    return lax.rsqrt(jnp.mean(residual * residual, axis=-1, keepdims=True) + EPSILON)


def front(layer, normed, conv_first, parts, at_first, collective_id):
    mixed = jnp.einsum("rd,dkc->krc", normed, layer.raw, preferred_element_type=jnp.float32)
    values, gate = mixed[0], mixed[1]
    inner = values.shape[-1]
    count = values.shape[0]
    rim = layer.taps.shape[0] - 1
    tails = split_parts(by_step(values[count - 8 * rim:]), parts)
    arrived = jnp.where(at_first, conv_first, neighbour(tails[:, -1], 1))
    prefix = jnp.concatenate([arrived[:, None], tails[:, :-1]], axis=1).reshape(rim * 8, inner)
    window = jnp.concatenate([prefix, values], axis=0)
    conv_out = layer.shift + sum(layer.taps[k] * window[8 * k:8 * k + count] for k in range(rim + 1))
    inputs = lax.optimization_barrier(jax.nn.silu(conv_out).astype(jnp.bfloat16))
    ranks, coef = pair_sums(
        [dot32(inputs, layer.x[:, :RANK]), lax.dot_general(
            layer.x[:, RANK:], inputs, (((0,), (1,)), ((), ())), preferred_element_type=jnp.float32)], collective_id)
    dt_low = ranks.astype(jnp.bfloat16)
    coef = by_step(coef.T)
    step = jax.nn.softplus(dot32(dt_low, layer.dt) + layer.dt_bias)
    push = step * inputs.astype(jnp.float32)
    local = split_parts(end_states(by_step(step), by_step(push), coef, layer.rate2), parts)
    totals = split_parts(jnp.sum(by_step(step), axis=0), parts)
    return (window, gate, conv_out, inputs, dt_low, coef, step, push, totals), local, tails[:, -1]


def join(local, totals, rate, reverse):
    order = range(local.shape[1])
    order = list(reversed(order)) if reverse else list(order)
    joined, total = local[:, order[0]], totals[order[0]]
    for p in order[1:]:
        joined = local[:, p] + jnp.exp2(totals[p][None] * rate) * joined
        total = total + totals[p]
    return total, joined


def each_part(state, local, totals, rate, reverse):
    order = range(local.shape[1])
    order = list(reversed(order)) if reverse else list(order)
    states = {order[0]: state}
    for p, following in zip(order[:-1], order[1:]):
        states[following] = local[:, p] + jnp.exp2(totals[p][None] * rate) * states[p]
    state = jnp.stack([states[p] for p in range(local.shape[1])], axis=1)
    return state.reshape(STATE, 8, state.shape[-1])


def exchange(layer, locals_, totals, first, reverses, collective_id):
    rate = layer.rate2[:, None]
    if lax.axis_size("blk") == 8 and totals.shape[0] == 1:
        return hops(totals[0], [local[:, 0] for local in locals_], layer.rate2, first, reverses, collective_id)
    states = []
    for local, reverse in zip(locals_, reverses):
        total, joined = join(local, totals, rate, reverse)
        state = entering_any(total, joined, rate, jnp.zeros_like(first) if reverse else first, reverse)
        states.append(each_part(state, local, totals, rate, reverse))
    return states


def scanning(layer, kept, start):
    window, gate, conv_out, inputs, dt_low, coef, step, push, totals = kept
    scanned, states, final = scan_forward(by_step(step), by_step(push), coef, layer.rate2, start)
    result = rows(scanned) + layer.skip * inputs.astype(jnp.float32)
    gated = (result * jax.nn.silu(gate)).astype(jnp.bfloat16)
    return (result, gated, states, start), final


def back_gated(kept, grad_gated):
    gate = kept[1]
    return grad_gated, grad_gated * jax.nn.silu(gate)


def back_local(layer, kept, grad_result):
    window, gate, conv_out, inputs, dt_low, coef, step, push, totals = kept
    local = start_grads(by_step(step), by_step(grad_result), coef, layer.rate2)
    return split_parts(local, totals.shape[0])


def back_side(layer, kept, normed, scans, grads, grad_low):
    window, gate, conv_out, inputs, dt_low, coef, step, push, totals = kept
    result, gated, states, start = scans
    grad_gated, grad_result = grads
    grad_gate = (grad_gated * result * silu_slope(gate)).astype(jnp.bfloat16)
    gate_grad = dot_t(normed, grad_gate)
    skip_grad = jnp.sum(grad_result * inputs.astype(jnp.float32), axis=0)
    return gate_grad, grad_gate, skip_grad


def back_scan(layer, kept, scans, grads, end):
    window, gate, conv_out, inputs, dt_low, coef, step, push, totals = kept
    result, gated, states, start = scans
    grad_gated, grad_result = grads
    return scan_backward(
        by_step(step), by_step(push), by_step(grad_result), coef, layer.rate2, states, start, end)


def back_rest(layer, kept, grads, scan_out, grad_gate, collective_id):
    window, gate, conv_out, inputs, dt_low, coef, step, push, totals = kept
    grad_gated, grad_result = grads
    count, inner = gate.shape
    parts = totals.shape[0]
    rim = layer.taps.shape[0] - 1
    wide = inputs.astype(jnp.float32)
    decays, pushes, coef_grad, start_grad, speed = scan_out
    pushes = rows(pushes)
    step_grad = rows(decays) * (1.0 / LOG2E) + wide * pushes
    before_grad = step_grad * -jnp.expm1(-step)
    bias_grad = jnp.sum(before_grad, axis=0)
    decay_grad = layer.rate * jnp.sum(speed, axis=1)
    before_low = before_grad.astype(jnp.bfloat16)
    ranks_grad, coef_grad = pair_sums([dot_n(before_low, layer.dt), rows(coef_grad).T], collective_id)
    high, low = two_parts(jnp.concatenate([ranks_grad, coef_grad.T], axis=-1))
    through = dot_n(jnp.concatenate([high, low], axis=-1), jnp.concatenate([layer.x, layer.x], axis=-1))
    inputs_grad = grad_result * layer.skip + step * pushes + through
    conv_grad = inputs_grad * silu_slope(conv_out)
    taps_grad = jnp.stack([jnp.sum(conv_grad * window[8 * k:8 * k + count], axis=0) for k in range(rim + 1)])
    shift_grad = jnp.sum(conv_grad, axis=0)
    margin = jnp.zeros((8 * rim, inner), jnp.float32)
    padded = jnp.concatenate([margin, conv_grad, margin], axis=0)
    window_grad = sum(
        layer.taps[k] * padded[8 * (rim - k):8 * (rim - k) + count + 8 * rim] for k in range(rim + 1))
    prefix_grad = split_parts(by_step(window_grad[:8 * rim]), parts)
    arrived = neighbour(prefix_grad[:, 0], -1)
    tail_grad = jnp.concatenate([prefix_grad[:, 1:], arrived[:, None]], axis=1).reshape(8 * rim, inner)
    values_grad = jnp.concatenate([window_grad[8 * rim:count], window_grad[count:] + tail_grad], axis=0)
    values_grad = values_grad.astype(jnp.bfloat16)
    normed_part = dot_n(jnp.concatenate([values_grad, grad_gate], axis=-1), layer.into)
    small = jnp.concatenate([taps_grad, shift_grad[None], bias_grad[None], decay_grad], axis=0)
    return normed_part, small, (values_grad, before_low, high, low), split_parts(start_grad, parts)[:, 0], prefix_grad[:, 0]


def thick_grads(kept, normed, lows):
    inputs, dt_low = kept[3], kept[4]
    values_grad, before_low, high, low = lows
    blocks = lax.axis_size("blk")
    x_grad = dot_t(high, inputs) + dot_t(low, inputs)
    return [eights(part.reshape(blocks, -1, part.shape[-1]))
            for part in (dot_t(normed, values_grad), x_grad, dot_t(dt_low, before_low))]


def eights(array):
    return jnp.pad(array, ((0, 0), (0, -array.shape[1] % 8), (0, 0)))


def norm_back(gain, normed_grad, residual, q):
    gain_grad = jnp.sum(normed_grad * (residual * q), axis=0)
    scaled = normed_grad * gain
    inner_mean = jnp.mean(scaled * residual, axis=-1, keepdims=True)
    return gain_grad, q * scaled - residual * (q * q * q * inner_mean)


def on_device(tokens, cotangent, *args):
    scan_init, conv_init = args[-2:]
    weights = args[:-2]
    blocks, index = lax.axis_size("blk"), lax.axis_index("blk")
    at_first = index == 0
    layer_total = weights[1].shape[0]
    seqs = tokens.shape[0]
    parts = 8 // seqs
    length = tokens.shape[1] // parts
    width = tokens.shape[2]
    layers = [Layer(l, weights) for l in range(layer_total)]
    last = layer_total - 1

    def arrange(array):
        return array.reshape(seqs, parts, length, width).transpose(2, 1, 0, 3).reshape(length * 8, width)

    def restore(array):
        array = array.reshape(length, parts, seqs, width).transpose(2, 1, 0, 3)
        return array.reshape(seqs, parts * length, width)

    rows_low = arrange(tokens)
    normed = norm_rows(rows_low, layers[0].gain)
    residual = own_rows(rows_low).astype(jnp.float32)
    grad = arrange(cotangent).astype(jnp.float32)
    grad_low = grad.astype(jnp.bfloat16)

    kept, scans, norms, finals, tails, squares = ([None] * layer_total for _ in range(6))
    starts, prefixes, smalls, gains = ([None] * layer_total for _ in range(4))
    for l, layer in enumerate(layers):
        norms[l] = (normed, residual)
        kept[l], local, tails[l] = front(
            layer, normed, jnp.moveaxis(conv_init[l], 1, 0), parts, at_first, 4 * layer_total + l)
        totals = kept[l][-1]
        first = jnp.moveaxis(scan_init[l], 1, 0)
        if l == last:
            grads = back_gated(kept[l], late_gated)
            late = back_local(layer, kept[l], grads[1])
            start, end = exchange(layer, [local, late], totals, first, (False, True), layer_total + l)
        else:
            start, = exchange(layer, [local], totals, first, (False,), layer_total + l)
        scans[l], final = scanning(layer, kept[l], start)
        gated = scans[l][1]
        if l == last:
            gated, late_out = lax.optimization_barrier((gated, dot_t(grad_low, gated)))
        partial_sum = dot32(gated, layer.out)
        finals[l] = split_parts(final, parts)[:, -1]
        half = core_sum(partial_sum)
        if l < last:
            if l == 0:
                half, residual = lax.optimization_barrier((half, residual))
                input_square = jnp.sum(residual * residual)
            half, stored = lax.optimization_barrier((half, weights[1]))
            into = [stored[k].reshape(width, -1) for k in range(layer_total)]
            layers[l + 1].raw = stored[l + 1]
            late_gated = dot_n(grad_low, layers[last].out)
            got, into, grad_low, late_gated, input_square = lax.optimization_barrier(
                (across(half), into, grad_low, late_gated, input_square))
            for each, array in zip(layers, into):
                each.into = array
            branch = half + got
            following = residual + branch
            squares[l] = jnp.stack([jnp.sum(branch * branch), jnp.sum(following * following)])
            residual = following
            gain = layers[l + 1].gain
            normed = all_rows(residual * inverse_rms(residual), lambda part: (part * gain).astype(jnp.bfloat16))

    thins, scattered = [], [None] * layer_total
    for l in reversed(range(layer_total)):
        layer = layers[l]
        normed, base = norms[l]
        if l < last:
            grads, out_grad, half = lax.optimization_barrier(
                (back_gated(kept[l], dot_n(grad_low, layer.out)), dot_t(grad_low, scans[l][1]), half))
            scattered[l] = [blk_scatter(out_grad)]
            late = back_local(layer, kept[l], grads[1])
            end, = exchange(layer, [late], kept[l][-1], jnp.zeros_like(late[:, 0]), (True,), 2 + 2 * layer_total + l)
            end, got_rest = lax.optimization_barrier((end, across(half[half.shape[0] // 2:])))
            branch = half + jnp.concatenate([got, got_rest], axis=0)
            following = residual + branch
            squares[last] = jnp.stack([jnp.sum(branch * branch), jnp.sum(following * following)])
            out = restore(all_rows(0.5 * following, lambda part: (2.0 * part).astype(jnp.bfloat16)))
        else:
            out_grad = late_out
        side = back_side(layer, kept[l], normed, scans[l], grads, grad_low)
        if l == last:
            scattered[l] = [blk_scatter(out_grad), blk_scatter(side[0])]
            end, side, half = lax.optimization_barrier((end, side, half))
            scan_out, got = lax.optimization_barrier(
                (back_scan(layer, kept[l], scans[l], grads, end), across(half[:half.shape[0] // 2])))
        else:
            scattered[l].append(blk_scatter(side[0]))
            end, side, scattered[last] = lax.optimization_barrier((end, side, scattered[last]))
            stacked_last = jnp.stack([scattered[last][2], scattered[last][1]], axis=1)
            scan_out = lax.optimization_barrier(back_scan(layer, kept[l], scans[l], grads, end))
        gate_grad, grad_gate, skip_grad = side
        normed_part, smalls[l], lows, starts[l], prefixes[l] = back_rest(
            layer, kept[l], grads, scan_out, grad_gate, 5 * layer_total + l)
        smalls[l] = jnp.concatenate([smalls[l], skip_grad[None]], axis=0)
        thick = thick_grads(kept[l], normed, lows)
        inner = smalls[l].shape[-1]
        if l == last:
            thins = thick[1:] + thins
            joint, scattered[l][0] = lax.optimization_barrier((joint_sums(
                normed_part, base, layer.gain, [rows(thick[0])], (0,), smalls[l], False, l), scattered[l][0]))
            change, gains[l], thick, smalls[l] = joint
            scattered[l].append(thick[0])
        else:
            thins = thick[1:] + thins
            cuts = [part.shape[1] for part in thins]
            extra = jnp.concatenate([jnp.stack(squares).reshape(-1), input_square.reshape(1)])
            extra = jnp.pad(extra, (0, inner - extra.shape[0]))[None]
            shared = rows_sum(jnp.concatenate(
                [extra] + [gain.reshape(-1, inner) for gain in gains[1:]], axis=0))
            own_count = smalls[l].shape[0]
            small = jnp.concatenate([smalls[l], shared], axis=0)
            small = jnp.pad(small, ((0, -small.shape[0] % 8), (0, 0)))
            normed_part, thins, out, stacked_last = lax.optimization_barrier((normed_part, thins, out, stacked_last))
            change, gains[l], thick, small = joint_sums(
                normed_part, base, layer.gain, [rows(thick[0]), rows(jnp.concatenate(thins, axis=1))], (0, inner),
                small, True, l)
            scattered[l].append(thick[0])
            smalls[l], rest = small[:own_count], small[own_count:]
        grad = grad + change
        grad_low = grad.astype(jnp.bfloat16)
        if l:
            grad_low = lax.optimization_barrier(grad_low)
    input_grad = restore(grad_low)

    small = jnp.stack(smalls)
    gain_rows = width // inner
    gain_grad = jnp.concatenate([gains[0].reshape(-1, inner), rest[1:1 + gain_rows * last]], axis=0)
    gain_grad = gain_grad.reshape(layer_total, width)
    taps = weights[2].shape[1]
    row_total = tokens.shape[0] * tokens.shape[1] * width * blocks
    squares = rest[0] / row_total
    rms_stats = jnp.sqrt(squares[:2 * layer_total]).reshape(layer_total, 2)
    input_rms = jnp.sqrt(squares[2 * layer_total:2 * layer_total + 1])
    pieces, at = [], 0
    for cut in cuts:
        pieces.append(thick[1][at:at + cut])
        at += cut
    into_out = jnp.stack([jnp.stack([part[2], part[1]], axis=1) for part in scattered[:-1]] + [stacked_last])

    def stacked(parts_):
        return jnp.stack([jnp.moveaxis(part, 0, 1) for part in parts_])[:, :, None]

    return (
        out,
        stacked(finals),
        stacked(tails),
        input_grad,
        stacked(starts),
        stacked(prefixes),
        gain_grad,
        into_out,
        small[:, :taps],
        small[:, taps],
        jnp.stack([part[:weights[4].shape[-1] // blocks].T for part in pieces[0::2]]),
        jnp.stack([part[:RANK // blocks] for part in pieces[1::2]]),
        small[:, taps + 1],
        small[:, taps + 2:-1],
        small[:, -1],
        jnp.stack([part[0].T for part in scattered]),
        rms_stats,
        input_rms,
    )


def solution(mesh):
    placed = (
        P(None, "blk", None),
        P(None, "blk", None),
        P(),
        P(None, None, None, "tensor"),
        P(None, None, "tensor"),
        P(None, "tensor"),
        P(None, "tensor", None),
        P(None, None, "tensor"),
        P(None, "tensor"),
        P(None, None, "tensor"),
        P(None, "tensor"),
        P(None, "tensor", None),
        P(None, None, None, "tensor"),
        P(None, None, None, "tensor"),
    )
    return jax.shard_map(
        on_device,
        mesh=mesh,
        in_specs=placed,
        out_specs=(
            P(None, "blk", None),
            P(None, None, "blk", None, "tensor"),
            P(None, None, "blk", None, "tensor"),
            P(None, "blk", None),
            P(None, None, "blk", None, "tensor"),
            P(None, None, "blk", None, "tensor"),
            P(),
            P(None, "blk", None, "tensor"),
            P(None, None, "tensor"),
            P(None, "tensor"),
            P(None, "tensor", "blk"),
            P(None, "blk", "tensor"),
            P(None, "tensor"),
            P(None, None, "tensor"),
            P(None, "tensor"),
            P(None, "tensor", "blk"),
            P(),
            P(),
        ),
        check_vma=False,
    )
```
